32 devices in a mesh: tile: 4 (over x, core), lev: 4 (over z), sec: 2 (over y).
Axes of the slice: x: 2, y: 2, z: 4, core: 2. Of those that a mesh axis runs over, the one named last changes fastest.
Arguments:
- forcing: float32 [8, 72, 160, 384], P('sec', 'lev', 'tile'), may hold values from -6 to 6
- courant_x: bfloat16 [72, 160, 384], P('lev', 'tile'), may hold values from -0.44921875 to 0.44921875
- courant_y: bfloat16 [72, 160, 384], P('lev', 'tile'), may hold values from -0.44921875 to 0.44921875
- mass_flux: bfloat16 [72, 160, 384], P('lev', 'tile'), may hold values from 0 to 0.59765625
- limiter_code: int32 [72, 160, 384], P('lev', 'tile'), may hold values from 0 to 15
- seam_code: int32 [4, 2], replicated, may hold values from 0 to 1
- level_weight: float32 [72], P('lev'), may hold values from 0.02 to 0.5
- sector_share: float32 [8, 160, 384], P('sec', 'tile'), may hold values from 0.1 to 1
- flux_cell: int32 [16, 3840], P('tile'), may hold values from 0 to 15359
Outputs:
- adjoint_start: float32 [8, 72, 160, 384], P('sec', 'lev', 'tile')
- flux_sensitivity: float32 [61440], P('tile')
The draws below stay inside these ranges and needn't reach their ends.
All inputs are finite; a program needn't handle non-finite values.
Results may differ from the reference program's by a relative error of at most 0.0003.
Values sent between devices are 32-bit elements; how exact they have to be, the bound alone decides.
No kernel may reach another device: no remote copies, remote signals or barrier semaphores. Data moves between devices by JAX's collectives and lax.ppermute only.
A program may use at most 128 MiB of HBM per device.

```python
import math
import jax
import jax.numpy as jnp
from jax import lax

SECTORS = 8
LEVELS = 72
CX = 40
CY = 384
TILES = 4
NX = 160
SHARE = 3840
FL_DEV = 15360
FLUX = 61440


def set_ends(result, rng, smallest, largest):
    place = [jax.random.randint(jax.random.fold_in(rng, axis), (), 0, length) for axis, length in enumerate(result.shape)]
    widest = result.shape.index(max(result.shape))
    beside = place[:widest] + [(place[widest] + 1) % result.shape[widest]] + place[widest + 1:]
    return result.at[tuple(place)].set(smallest).at[tuple(beside)].set(largest)


def levels(rng, extent, cuts, least, high):
    factor_of = 1.0
    for position, blocks in cuts:
        heights = jax.random.uniform(jax.random.fold_in(jax.random.fold_in(rng, 6), position), (blocks,), jnp.float32, least / len(cuts), high / len(cuts))
        factor_of = factor_of * jnp.repeat(jnp.exp(heights), extent[position] // blocks).reshape((-1,) + (1,) * (len(extent) - 1 - position))
    return factor_of


def noise(key, extent, scale, limit, cuts=(), kind=jnp.bfloat16):
    drawn = jax.random.normal(key, extent, jnp.float32) * scale
    if len(cuts) > 0:
        drawn = levels(key, extent, cuts, -0.22, 0.18) * drawn
    return jnp.clip(drawn, min=-limit, max=limit).astype(kind)


def setup_inputs(seed: int = 0) -> dict:
    arg_keys = jax.random.split(jax.random.key(seed), 10)
    return {
        "forcing": noise(arg_keys[0], (SECTORS, LEVELS, NX, CY), 1.0, 6.0, ((0, 2), (1, 4), (2, 4)), jnp.float32),
        "courant_x": jnp.clip(jax.random.uniform(arg_keys[1], (LEVELS, NX, CY), jnp.float32, -0.44921875, 0.44921875) * levels(arg_keys[1], (LEVELS, NX, CY), ((0, 4), (1, 4)), -0.4, 0.0), -0.44921875, 0.44921875).astype(jnp.bfloat16),
        "courant_y": jnp.clip(jax.random.uniform(arg_keys[2], (LEVELS, NX, CY), jnp.float32, -0.44921875, 0.44921875) * levels(arg_keys[2], (LEVELS, NX, CY), ((0, 4), (1, 4)), -0.4, 0.0), -0.44921875, 0.44921875).astype(jnp.bfloat16),
        "mass_flux": jnp.clip(0.59765625 * jax.random.uniform(arg_keys[3], (LEVELS, NX, CY), jnp.float32) ** levels(arg_keys[3], (LEVELS, NX, CY), ((0, 4), (1, 4)), -0.2, 0.2), 0.0, 0.59765625).astype(jnp.bfloat16),
        "limiter_code": set_ends(jax.random.randint(arg_keys[4], (LEVELS, NX, CY), 0, 16), jax.random.fold_in(arg_keys[4], 1), 0, 15).astype(jnp.int32),
        "seam_code": set_ends(jax.random.randint(arg_keys[5], (TILES, 2), 0, 2), jax.random.fold_in(arg_keys[5], 1), 0, 1).astype(jnp.int32),
        "level_weight": jnp.clip(jnp.exp(math.log(0.5) - 3.218876 * jax.random.uniform(arg_keys[6], (LEVELS,), jnp.float32) ** levels(arg_keys[6], (LEVELS,), ((0, 4),), -0.2, 0.2)), 0.02, 0.5),
        "sector_share": jnp.clip(jnp.exp(math.log(1.0) - 2.3025851 * jax.random.uniform(arg_keys[7], (SECTORS, NX, CY), jnp.float32) ** levels(arg_keys[7], (SECTORS, NX, CY), ((0, 2), (1, 4)), -0.2, 0.2)), 0.1, 1.0),
        "flux_cell": set_ends(jax.random.randint(arg_keys[8], (TILES * TILES, SHARE), 0, FL_DEV), jax.random.fold_in(arg_keys[8], 1), 0, FL_DEV - 1).astype(jnp.int32),
    }


def coefficients(courant, codes, bit):
    value = courant.astype(jnp.float32)
    limited = jnp.bitwise_and(jnp.right_shift(codes, bit), 1).astype(jnp.float32)
    spread = 0.5 * jnp.abs(value) * (1.0 - jnp.abs(value))
    ahead = jnp.maximum(value, 0.0) - limited * spread
    behind = jnp.minimum(value, 0.0) + limited * spread
    return ahead, behind


def vertical(adjoint, mixing):
    upper = jnp.concatenate([adjoint[1:], adjoint[-1:]], axis=0)
    return adjoint + mixing * (upper - adjoint)


def sweep_second(adjoint, courant, codes, bit):
    ahead, behind = coefficients(courant, codes, bit)
    following = jnp.concatenate([adjoint[..., 1:], adjoint[..., -1:]], axis=-1)
    previous = jnp.concatenate([adjoint[..., :1], adjoint[..., :-1]], axis=-1)
    return adjoint + ahead * (following - adjoint) + behind * (adjoint - previous)


def sweep_first(adjoint, courant, codes, bit, seam_code):
    ahead, behind = coefficients(courant, codes, bit)
    depth = adjoint.shape[0]
    width = adjoint.shape[2]
    blocks = adjoint.reshape(depth, TILES, CX, width)
    left_rim = jnp.roll(blocks[:, :, -1, :], 1, axis=1)
    right_rim = jnp.roll(blocks[:, :, 0, :], -1, axis=1)
    flip_left = (seam_code[:, 0] == 1)[None, :, None]
    flip_right = (seam_code[:, 1] == 1)[None, :, None]
    left_rim = jnp.where(flip_left, left_rim[..., ::-1], left_rim)
    right_rim = jnp.where(flip_right, right_rim[..., ::-1], right_rim)
    following = jnp.concatenate([blocks[:, :, 1:], right_rim[:, :, None]], axis=2).reshape(adjoint.shape)
    previous = jnp.concatenate([left_rim[:, :, None], blocks[:, :, :-1]], axis=2).reshape(adjoint.shape)
    return adjoint + ahead * (following - adjoint) + behind * (adjoint - previous)


def reference(forcing, courant_x, courant_y, mass_flux, limiter_code, seam_code, level_weight, sector_share, flux_cell):
    mixing = mass_flux.astype(jnp.float32)

    def one_sector(total, item):
        adjoint, share = item
        for turn_index in (1, 0):
            adjoint = vertical(adjoint, mixing)
            adjoint = sweep_second(adjoint, courant_y, limiter_code, 2 * turn_index + 1)
            adjoint = sweep_first(adjoint, courant_x, limiter_code, 2 * turn_index, seam_code)
        column_sum = jnp.einsum("l,lxy->xy", level_weight, adjoint, precision=lax.Precision.HIGHEST)
        return total + share * column_sum, adjoint

    start = jnp.zeros((NX, CY), jnp.float32)
    sensitivity, adjoint_start = lax.scan(one_sector, start, (forcing, sector_share))
    grouped = sensitivity.reshape(TILES, TILES, SHARE)
    cells = flux_cell.reshape(TILES, TILES, SHARE).transpose(1, 0, 2)
    offsets = (jnp.arange(TILES, dtype=jnp.int32) * FL_DEV)[None, :, None]
    target = (cells + offsets).astype(jnp.int32)
    flux_sensitivity = jax.ops.segment_sum(grouped.reshape(-1), target.reshape(-1), num_segments=FLUX)
    return adjoint_start, flux_sensitivity
```

```python
import jax
import jax.numpy as jnp
from jax import lax
from jax.experimental import pallas as pl
from jax.experimental.pallas import tpu as pltpu
from jax.sharding import PartitionSpec as P

FL_DEV = 15360


def from_behind(value, axis, steps):
    count = lax.axis_size(axis)
    initial, last = (max(0, -steps), min(count, count - steps))
    return lax.ppermute(value, axis, [(source, source + steps) for source in range(initial, last)])


def extended_2(value, sides, width):
    for axis, dim in sides:
        devices, length = (lax.axis_size(axis), value.shape[dim])
        up = [(i, (i + 1) % devices) for i in range(devices)]
        down = [(j, i) for i, j in up]
        last = lax.slice_in_dim(value, length - width, length, axis=dim)
        initial = lax.slice_in_dim(value, 0, width, axis=dim)
        before = lax.ppermute(last, axis, up)
        after = lax.ppermute(initial, axis, down)
        value = jnp.concatenate([before, value, after], axis=dim)
    return value


def coefficients(courant, codes, bit):
    value = courant.astype(jnp.float32)
    limited = jnp.bitwise_and(jnp.right_shift(codes, bit), 1).astype(jnp.float32)
    spread = 0.5 * jnp.abs(value) * (1.0 - jnp.abs(value))
    ahead = jnp.maximum(value, 0.0) - limited * spread
    behind = jnp.minimum(value, 0.0) + limited * spread
    return (ahead, behind)


def flipped(rim, flag):
    return jnp.where(flag, rim[..., ::-1], rim)


def vertical(adjoint, mixing, at_top):
    above = from_behind(adjoint[:, :1], "lev", -1)
    above = jnp.where(at_top, adjoint[:, -1:], above)
    upper = jnp.concatenate([adjoint[:, 1:], above], axis=1)
    return adjoint + mixing * (upper - adjoint)


def sweep_second(adjoint, courant, codes, bit):
    ahead, behind = coefficients(courant, codes, bit)
    following = jnp.concatenate([adjoint[..., 1:], adjoint[..., -1:]], axis=-1)
    previous = jnp.concatenate([adjoint[..., :1], adjoint[..., :-1]], axis=-1)
    return adjoint + ahead * (following - adjoint) + behind * (adjoint - previous)


def sweep_first(adjoint, courant, codes, bit, flip_left, flip_right):
    ahead, behind = coefficients(courant, codes, bit)
    extended = extended_2(adjoint, (("tile", 2),), 1)
    left_rim = flipped(extended[:, :, :1], flip_left)
    right_rim = flipped(extended[:, :, -1:], flip_right)
    following = jnp.concatenate([adjoint[:, :, 1:], right_rim], axis=2)
    previous = jnp.concatenate([left_rim, adjoint[:, :, :-1]], axis=2)
    return adjoint + ahead * (following - adjoint) + behind * (adjoint - previous)


def scatter_kernel(cells_ref, values_ref, out_ref):
    rows, lanes = out_ref.shape
    count = cells_ref.shape[0]
    high_iota = lax.broadcasted_iota(jnp.int32, (rows, lanes), 0)
    low_iota = lax.broadcasted_iota(jnp.int32, (lanes, lanes), 0)
    total = jnp.zeros((2 * rows, lanes), jnp.float32)
    for pair in range(0, count, 2):
        lefts, rights = [], []
        for row in (pair, pair + 1):
            cells = cells_ref[row : row + 1, :]
            value = values_ref[row : row + 1, :]
            coarse = value.astype(jnp.bfloat16).astype(jnp.float32)
            fine = value - coarse
            here = jnp.right_shift(cells, 7) == high_iota
            lefts.append(
                jnp.concatenate(
                    [jnp.where(here, coarse, 0.0), jnp.where(here, fine, 0.0)], axis=0
                ).astype(jnp.bfloat16)
            )
            match = jnp.bitwise_and(cells, 127) == low_iota
            rights.append(jnp.where(match, 1.0, 0.0).astype(jnp.bfloat16))
        total += lax.dot_general(
            jnp.concatenate(lefts, axis=1),
            jnp.concatenate(rights, axis=1),
            (((1,), (1,)), ((), ())),
            preferred_element_type=jnp.float32,
        )
    out_ref[...] = total[:rows] + total[rows:]


def remapped(partial_value, flux_cell):
    tiles, share = flux_cell.shape
    group = lax.axis_size("lev") * lax.axis_size("sec")
    piece = share // group
    sent = partial_value.reshape(tiles * group, piece)
    received = lax.all_to_all(
        sent, ("tile", "lev", "sec"), split_axis=0, concat_axis=0, tiled=True
    )
    summed = jnp.sum(received.reshape(tiles, group, piece), axis=1)
    gathered = lax.all_gather(summed, ("lev", "sec"))
    cells = flux_cell.reshape(tiles, group, piece).transpose(1, 0, 2)
    out = pl.pallas_call(
        scatter_kernel,
        out_shape=jax.ShapeDtypeStruct((FL_DEV // 128, 128), jnp.float32),
        compiler_params=pltpu.CompilerParams(vmem_limit_bytes=48 * 2**20),
    )(cells.reshape(-1, 128), gathered.reshape(-1, 128))
    return out.reshape(-1)


def shards(
    forcing,
    courant_x,
    courant_y,
    mass_flux,
    limiter_code,
    seam_code,
    level_weight,
    sector_share,
    flux_cell,
):
    mixing = mass_flux.astype(jnp.float32)
    at_top = lax.axis_index("lev") == lax.axis_size("lev") - 1
    tile_count = lax.axis_size("tile")
    tile_rank = lax.axis_index("tile")
    place = jnp.remainder(tile_rank + tile_count, tile_count)
    seams_here = lax.dynamic_index_in_dim(seam_code, place, 0, keepdims=False) == 1
    adjoint = forcing
    for turn_index in (1, 0):
        adjoint = vertical(adjoint, mixing, at_top)
        adjoint = sweep_second(adjoint, courant_y, limiter_code, 2 * turn_index + 1)
        adjoint = sweep_first(
            adjoint, courant_x, limiter_code, 2 * turn_index, seams_here[0], seams_here[1]
        )
    partial_value = jnp.einsum(
        "sxy,l,slxy->xy", sector_share, level_weight, adjoint, precision=lax.Precision.HIGHEST
    )
    flux_sensitivity = remapped(partial_value, flux_cell)
    return (adjoint, flux_sensitivity)


def solution(mesh):
    placed = (
        P("sec", "lev", "tile", None),
        P("lev", "tile", None),
        P("lev", "tile", None),
        P("lev", "tile", None),
        P("lev", "tile", None),
        P(),
        P("lev"),
        P("sec", "tile", None),
        P("tile", None),
    )
    return jax.shard_map(
        shards,
        mesh=mesh,
        in_specs=placed,
        out_specs=(P("sec", "lev", "tile", None), P("tile")),
        check_vma=False,
    )
```

```python
import functools

import jax
import jax.numpy as jnp
from jax import lax
from jax.experimental import pallas as pl
from jax.experimental.pallas import tpu as pltpu
from jax.sharding import PartitionSpec as P

FL_DEV = 15360
LANES = 128
ROWS = 8
MIB = 2**20
VM = pl.BlockSpec(memory_space=pltpu.VMEM)
HBM = pl.BlockSpec(memory_space=pltpu.HBM)


def call(kernel, out_shape, in_specs, out_specs, operands, scratch=(), mib=16):
    return pl.pallas_call(
        kernel,
        out_shape=out_shape,
        in_specs=in_specs,
        out_specs=out_specs,
        scratch_shapes=list(scratch),
        compiler_params=pltpu.CompilerParams(vmem_limit_bytes=mib * MIB),
    )(*operands)


def f32(*shape):
    return jax.ShapeDtypeStruct(shape, jnp.float32)


def cut(value, xt, j):
    return value[xt * ROWS : (xt + 1) * ROWS, j * LANES : (j + 1) * LANES]


def weights(courant, codes, bit):
    size = jnp.abs(courant)
    half = (0.5 * size) * (1.0 - size)
    limited = jnp.where(jnp.bitwise_and(codes, 1 << bit) != 0, half, 0.0)
    ahead = jnp.maximum(courant, 0.0) - limited
    back = jnp.maximum(-courant, 0.0) - limited
    return ahead, back


def second_weights(cy, codes, bit, xt, tiles):
    lane = lax.broadcasted_iota(jnp.int32, (ROWS, LANES), 1)
    out = []
    for j in range(tiles):
        ahead, back = weights(cut(cy, xt, j), cut(codes, xt, j), bit)
        if j == 0:
            back = jnp.where(lane == 0, 0.0, back)
        if j == tiles - 1:
            ahead = jnp.where(lane == LANES - 1, 0.0, ahead)
        out.append((ahead, back, (1.0 - ahead) - back))
    return out


def second_sweep(parts, factors):
    lane = lax.broadcasted_iota(jnp.int32, (ROWS, LANES), 1)
    tiles = len(parts)
    later = [pltpu.roll(part, LANES - 1, 1) for part in parts]
    sooner = [pltpu.roll(part, 1, 1) for part in parts]
    out = []
    for j in range(tiles):
        following, previous = later[j], sooner[j]
        if j + 1 < tiles:
            following = jnp.where(lane == LANES - 1, later[j + 1], following)
        if j > 0:
            previous = jnp.where(lane == 0, sooner[j - 1], previous)
        ahead, back, own = factors[j]
        out.append(own * parts[j] + ahead * following + back * previous)
    return out


def first_sweep(field, s, j, xt, last, factors, left_row, right_row):
    start = ROWS * (xt + 1)
    sub = lax.broadcasted_iota(jnp.int32, (ROWS, LANES), 0)
    own_value = field(s, j, start)
    following = field(s, j, start + 1)
    previous = field(s, j, start - 1)
    if xt == 0:
        previous = jnp.where(sub == 0, left_row(s, j), previous)
    if xt == last:
        following = jnp.where(sub == ROWS - 1, right_row(s, j), following)
    ahead, back, own = factors
    return own * own_value + ahead * following + back * previous


def turned(source_ref, flag, target_ref):
    tiles, rows, _ = source_ref.shape
    for j in range(tiles):
        for start in range(0, rows, ROWS):
            count = min(ROWS, rows - start)
            index = (LANES - 1) - lax.broadcasted_iota(jnp.int32, (count, LANES), 1)
            straight = source_ref[j, start : start + count, :]
            other = source_ref[tiles - 1 - j, start : start + count, :]
            mirrored = jnp.take_along_axis(other, index, axis=1, mode="promise_in_bounds")
            target_ref[j, start : start + count, :] = jnp.where(flag[:count], mirrored, straight)


def store_padded(ref, index, s, j, xt, value):
    start = ROWS * (xt + 1)
    ref[(*index, s, j, slice(start, start + ROWS), slice(None))] = value


def store_rims(first_ref, last_ref, row, j, xt, last, value):
    if xt == 0:
        first_ref[j, pl.ds(row, 1), :] = value[:1]
    if xt == last:
        last_ref[j, pl.ds(row, 1), :] = value[ROWS - 1 :]


def flags(seam_ref):
    return seam_ref[0] == 1, seam_ref[1] == 1


def lower_kernel(
    f_hbm, mf_hbm, cy_hbm, code_hbm,
    v_ref, first_ref, last_ref, top_ref,
    f_ref, mf_ref, cy_ref, code_ref, sems,
):
    sectors, levels, columns, width = f_hbm.shape
    tiles, strips = width // LANES, columns // ROWS

    def fetch(k):
        return pltpu.make_async_copy(f_hbm.at[:, k], f_ref.at[k], sems.at[0, k])

    def fetch_code(k):
        return pltpu.make_async_copy(code_hbm.at[k], code_ref.at[k], sems.at[1, k])

    fetch_mf = pltpu.make_async_copy(mf_hbm, mf_ref, sems.at[2, 0])
    fetch_cy = pltpu.make_async_copy(cy_hbm, cy_ref, sems.at[2, 1])
    fetch(0).start()
    fetch_mf.start()
    fetch_cy.start()
    for k in range(levels - 1):
        fetch_code(k).start()
        fetch(k + 1).start()
    fetch(0).wait()
    fetch_mf.wait()
    fetch_cy.wait()

    def level(k, _):
        fetch_code(k).wait()
        fetch(k + 1).wait()
        mf = mf_ref[k].astype(jnp.float32)
        cy = cy_ref[k].astype(jnp.float32)
        codes = code_ref[k]
        for xt in range(strips):
            factors = second_weights(cy, codes, 3, xt, tiles)
            rows = slice(xt * ROWS, (xt + 1) * ROWS)
            for s in range(sectors):
                parts = []
                for j in range(tiles):
                    lanes = slice(j * LANES, (j + 1) * LANES)
                    here = f_ref[k, s, rows, lanes]
                    upper = f_ref[k + 1, s, rows, lanes]
                    parts.append(here + cut(mf, xt, j) * (upper - here))
                for j, value in enumerate(second_sweep(parts, factors)):
                    store_padded(v_ref, (k,), s, j, xt, value)
                    store_rims(first_ref, last_ref, k * sectors + s, j, xt, strips - 1, value)
        return 0

    lax.fori_loop(0, levels - 1, level, 0)
    top_ref[...] = f_ref[levels - 1]


def upper_kernel(bit, here_ref, above_ref, mf_ref, cy_ref, code_ref, v_ref, first_ref, last_ref):
    sectors, columns, width = above_ref.shape
    level = mf_ref.shape[0] - 1
    tiles, strips = width // LANES, columns // ROWS
    at_top = lax.axis_index("lev") == lax.axis_size("lev") - 1
    mf = mf_ref[level].astype(jnp.float32)
    cy = cy_ref[level].astype(jnp.float32)
    codes = code_ref[level]
    for xt in range(strips):
        factors = second_weights(cy, codes, bit, xt, tiles)
        rows = slice(xt * ROWS, (xt + 1) * ROWS)
        for s in range(sectors):
            parts = []
            for j in range(tiles):
                lanes = slice(j * LANES, (j + 1) * LANES)
                here = here_ref[s, rows, lanes]
                upper = jnp.where(at_top, here, above_ref[s, rows, lanes])
                parts.append(here + cut(mf, xt, j) * (upper - here))
            for j, value in enumerate(second_sweep(parts, factors)):
                store_padded(v_ref, (), s, j, xt, value)
                store_rims(first_ref, last_ref, s, j, xt, strips - 1, value)


def first_weights(cx, codes, bit, xt, j):
    ahead, back = weights(cut(cx, xt, j), cut(codes, xt, j), bit)
    return ahead, back, (1.0 - ahead) - back


def lowest_kernel(v_ref, left_ref, right_ref, seam_ref, cx_ref, code_ref, out_ref, lrow_ref, rrow_ref):
    _, sectors, tiles, _, _ = v_ref.shape
    columns = out_ref.shape[1]
    strips = columns // ROWS
    flip_left, flip_right = flags(seam_ref)
    turned(left_ref.at[:, :ROWS], flip_left, lrow_ref)
    turned(right_ref.at[:, :ROWS], flip_right, rrow_ref)
    cx = cx_ref[0].astype(jnp.float32)
    codes = code_ref[0]
    for xt in range(strips):
        for j in range(tiles):
            factors = first_weights(cx, codes, 2, xt, j)
            for s in range(sectors):
                value = first_sweep(
                    lambda s, j, start: v_ref[0, s, j, start : start + ROWS, :],
                    s, j, xt, strips - 1, factors,
                    lambda s, j: lrow_ref[j, s : s + 1, :],
                    lambda s, j: rrow_ref[j, s : s + 1, :],
                )
                out_ref[s, xt * ROWS : (xt + 1) * ROWS, j * LANES : (j + 1) * LANES] = value


def middle_kernel(
    v_ref, vt_ref, left_ref, right_ref, left_top_ref, right_top_ref, seam_ref,
    cx_ref, mf_ref, cy_ref, code_ref,
    out_ref, first_ref, last_ref, top_ref,
    lrow_ref, rrow_ref, ltop_ref, rtop_ref, a_ref,
):
    below, sectors, tiles, padded, _ = v_ref.shape
    strips = (padded - 2 * ROWS) // ROWS
    flip_left, flip_right = flags(seam_ref)
    turned(left_ref, flip_left, lrow_ref)
    turned(right_ref, flip_right, rrow_ref)
    turned(left_top_ref, flip_left, ltop_ref)
    turned(right_top_ref, flip_right, rtop_ref)

    cx = cx_ref[below].astype(jnp.float32)
    codes = code_ref[below]
    for xt in range(strips):
        for j in range(tiles):
            factors = first_weights(cx, codes, 2, xt, j)
            for s in range(sectors):
                value = first_sweep(
                    lambda s, j, start: vt_ref[s, j, start : start + ROWS, :],
                    s, j, xt, strips - 1, factors,
                    lambda s, j: ltop_ref[j, s : s + 1, :],
                    lambda s, j: rtop_ref[j, s : s + 1, :],
                )
                a_ref[below, s, j, xt * ROWS : (xt + 1) * ROWS, :] = value
                top_ref[s, xt * ROWS : (xt + 1) * ROWS, j * LANES : (j + 1) * LANES] = value

    def level(step, _):
        k = below - 1 - step
        cx = cx_ref[k].astype(jnp.float32)
        mf = mf_ref[k].astype(jnp.float32)
        cy = cy_ref[k].astype(jnp.float32)
        codes = code_ref[k]
        for xt in range(strips):
            along = [first_weights(cx, codes, 2, xt, j) for j in range(tiles)]
            across = second_weights(cy, codes, 1, xt, tiles)
            rows = slice(xt * ROWS, (xt + 1) * ROWS)
            for s in range(sectors):
                parts = []
                for j in range(tiles):
                    here = first_sweep(
                        lambda s, j, start: v_ref[k, s, j, start : start + ROWS, :],
                        s, j, xt, strips - 1, along[j],
                        lambda s, j: lrow_ref[j, pl.ds(k * sectors + s, 1), :],
                        lambda s, j: rrow_ref[j, pl.ds(k * sectors + s, 1), :],
                    )
                    upper = a_ref[k + 1, s, j, rows, :]
                    a_ref[k, s, j, rows, :] = here
                    parts.append(here + cut(mf, xt, j) * (upper - here))
                for j, value in enumerate(second_sweep(parts, across)):
                    store_padded(out_ref, (k,), s, j, xt, value)
                    store_rims(first_ref, last_ref, k * sectors + s, j, xt, strips - 1, value)
        return 0

    lax.fori_loop(0, below, level, 0)


def final_kernel(
    v_ref, vt_ref, left_ref, right_ref, left_top_ref, right_top_ref, seam_ref,
    cx_ref, code_ref, weight_ref, share_ref,
    out_hbm, sens_ref,
    lrow_ref, rrow_ref, ltop_ref, rtop_ref, out_ref, sems,
):
    below, sectors, tiles, padded, _ = v_ref.shape
    strips = (padded - 2 * ROWS) // ROWS
    flip_left, flip_right = flags(seam_ref)
    turned(left_ref, flip_left, lrow_ref)
    turned(right_ref, flip_right, rrow_ref)
    turned(left_top_ref, flip_left, ltop_ref)
    turned(right_top_ref, flip_right, rtop_ref)

    def send(k):
        return pltpu.make_async_copy(out_ref.at[k], out_hbm.at[:, k], sems.at[k])

    def level(k, field, left_row, right_row, start_sum):
        cx = cx_ref[k].astype(jnp.float32)
        codes = code_ref[k]
        factor = weight_ref[pl.ds(k, 1), :]
        for xt in range(strips):
            rows = slice(xt * ROWS, (xt + 1) * ROWS)
            for j in range(tiles):
                lanes = slice(j * LANES, (j + 1) * LANES)
                factors = first_weights(cx, codes, 0, xt, j)
                total = 0.0
                for s in range(sectors):
                    value = first_sweep(
                        field, s, j, xt, strips - 1, factors, left_row, right_row
                    )
                    out_ref[k, s, rows, lanes] = value
                    total = total + share_ref[s, rows, lanes] * value
                if start_sum:
                    sens_ref[rows, lanes] = factor * total
                else:
                    sens_ref[rows, lanes] += factor * total
        send(k).start()

    level(
        below,
        lambda s, j, start: vt_ref[s, j, start : start + ROWS, :],
        lambda s, j: ltop_ref[j, s : s + 1, :],
        lambda s, j: rtop_ref[j, s : s + 1, :],
        True,
    )

    def step(k, _):
        level(
            k,
            lambda s, j, start: v_ref[k, s, j, start : start + ROWS, :],
            lambda s, j: lrow_ref[j, pl.ds(k * sectors + s, 1), :],
            lambda s, j: rrow_ref[j, pl.ds(k * sectors + s, 1), :],
            False,
        )
        return 0

    lax.fori_loop(0, below, step, 0)
    for k in range(below + 1):
        send(k).wait()


def scatter_kernel(cells_ref, values_ref, out_ref):
    rows, lanes = out_ref.shape
    count = cells_ref.shape[0]
    high_iota = lax.broadcasted_iota(jnp.int32, (rows, lanes), 0)
    low_iota = lax.broadcasted_iota(jnp.int32, (lanes, lanes), 0)
    total = jnp.zeros((2 * rows, lanes), jnp.float32)
    for pair in range(0, count, 2):
        lefts, rights = [], []
        for row in (pair, pair + 1):
            cells = cells_ref[row : row + 1, :]
            value = values_ref[row : row + 1, :]
            coarse = value.astype(jnp.bfloat16).astype(jnp.float32)
            fine = value - coarse
            here = jnp.right_shift(cells, 7) == high_iota
            lefts.append(
                jnp.concatenate(
                    [jnp.where(here, coarse, 0.0), jnp.where(here, fine, 0.0)], axis=0
                ).astype(jnp.bfloat16)
            )
            match = jnp.bitwise_and(cells, 127) == low_iota
            rights.append(jnp.where(match, 1.0, 0.0).astype(jnp.bfloat16))
        total += lax.dot_general(
            jnp.concatenate(lefts, axis=1),
            jnp.concatenate(rights, axis=1),
            (((1,), (1,)), ((), ())),
            preferred_element_type=jnp.float32,
        )
    out_ref[...] = total[:rows] + total[rows:]


def remapped(partial_value, flux_cell):
    tiles, share = flux_cell.shape
    group = lax.axis_size("lev") * lax.axis_size("sec")
    piece = share // group
    sent = partial_value.reshape(tiles * group, piece)
    received = lax.all_to_all(
        sent, ("tile", "lev", "sec"), split_axis=0, concat_axis=0, tiled=True
    )
    summed = jnp.sum(received.reshape(tiles, group, piece), axis=1)
    copies = jnp.broadcast_to(summed.reshape(1, tiles * piece), (group, tiles * piece))
    gathered = lax.all_to_all(copies, ("lev", "sec"), split_axis=0, concat_axis=0, tiled=True)
    cells = flux_cell.reshape(tiles, group, piece).transpose(1, 0, 2)
    out = call(
        scatter_kernel,
        f32(FL_DEV // LANES, LANES),
        [VM, VM],
        VM,
        (cells.reshape(-1, LANES), gathered.reshape(-1, LANES)),
    )
    return out.reshape(-1)


def around(first, last):
    count = lax.axis_size("tile")
    up = [(i, (i + 1) % count) for i in range(count)]
    down = [(j, i) for i, j in up]
    return lax.ppermute(last, "tile", up), lax.ppermute(first, "tile", down)


def from_above(value):
    count = lax.axis_size("lev")
    return lax.ppermute(value, "lev", [(i + 1, i) for i in range(count - 1)])


def shards(
    forcing, courant_x, courant_y, mass_flux, limiter_code, seam_code, level_weight, sector_share, flux_cell
):
    sectors, levels, columns, width = forcing.shape
    tiles, below = width // LANES, levels - 1
    padded = columns + 2 * ROWS
    field = f32(below, sectors, tiles, padded, LANES)
    field_top = f32(sectors, tiles, padded, LANES)
    plane = f32(sectors, columns, width)
    rim = f32(tiles, below * sectors, LANES)
    rim_top = f32(tiles, sectors, LANES)
    rim_scratch = pltpu.VMEM(rim.shape, jnp.float32)
    top_scratch = pltpu.VMEM(rim_top.shape, jnp.float32)

    seam = lax.dynamic_index_in_dim(seam_code, lax.axis_index("tile"), 0, keepdims=False)
    seam = jnp.broadcast_to(seam[:, None, None], (2, ROWS, LANES))
    weight = jnp.broadcast_to(level_weight[:, None], (levels, LANES))

    above = from_above(forcing[:, 0])
    v, first, last, top = call(
        lower_kernel,
        (field, rim, rim, plane),
        [HBM] * 4,
        [VM] * 4,
        (forcing, mass_flux, courant_y, limiter_code),
        [
            pltpu.VMEM((levels, sectors, columns, width), jnp.float32),
            pltpu.VMEM((levels, columns, width), jnp.bfloat16),
            pltpu.VMEM((levels, columns, width), jnp.bfloat16),
            pltpu.VMEM((below, columns, width), jnp.int32),
            pltpu.SemaphoreType.DMA((3, levels)),
        ],
    )
    left, right = around(first, last)
    lowest = call(
        lowest_kernel,
        plane,
        [VM] * 6,
        VM,
        (v, left, right, seam, courant_x, limiter_code),
        [pltpu.VMEM((tiles, ROWS, LANES), jnp.float32)] * 2,
    )
    vt, first_top, last_top = call(
        functools.partial(upper_kernel, 3),
        (field_top, rim_top, rim_top),
        [VM] * 5,
        [VM] * 3,
        (top, above, mass_flux, courant_y, limiter_code),
    )
    left_top, right_top = around(first_top, last_top)
    above = from_above(lowest)

    v, first, last, top = call(
        middle_kernel,
        (field, rim, rim, plane),
        [VM] * 11,
        [VM] * 4,
        (
            v, vt, left, right, left_top, right_top, seam,
            courant_x, mass_flux, courant_y, limiter_code,
        ),
        [
            rim_scratch, rim_scratch, top_scratch, top_scratch,
            pltpu.VMEM((levels, sectors, tiles, columns, LANES), jnp.float32),
        ],
    )
    left, right = around(first, last)
    vt, first_top, last_top = call(
        functools.partial(upper_kernel, 1),
        (field_top, rim_top, rim_top),
        [VM] * 5,
        [VM] * 3,
        (top, above, mass_flux, courant_y, limiter_code),
    )
    left_top, right_top = around(first_top, last_top)
    adjoint, sensitivity = call(
        final_kernel,
        (f32(*forcing.shape), f32(columns, width)),
        [VM] * 11,
        [HBM, VM],
        (
            v, vt, left, right, left_top, right_top, seam,
            courant_x, limiter_code, weight, sector_share,
        ),
        [
            rim_scratch, rim_scratch, top_scratch, top_scratch,
            pltpu.VMEM((levels, sectors, columns, width), jnp.float32),
            pltpu.SemaphoreType.DMA((levels,)),
        ],
    )
    return (adjoint, remapped(sensitivity, flux_cell))


def solution(mesh):
    placed = (
        P("sec", "lev", "tile", None),
        P("lev", "tile", None),
        P("lev", "tile", None),
        P("lev", "tile", None),
        P("lev", "tile", None),
        P(),
        P("lev"),
        P("sec", "tile", None),
        P("tile", None),
    )
    return jax.shard_map(
        shards,
        mesh=mesh,
        in_specs=placed,
        out_specs=(P("sec", "lev", "tile", None), P("tile")),
        check_vma=False,
    )
```

```python
import functools

import jax
import jax.numpy as jnp
from jax import lax
from jax.experimental import pallas as pl
from jax.experimental.pallas import tpu as pltpu
from jax.sharding import PartitionSpec as P

FL_DEV = 15360
LANES = 128
ROWS = 8
MIB = 2**20
VM = pl.BlockSpec(memory_space=pltpu.VMEM)
HBM = pl.BlockSpec(memory_space=pltpu.HBM)


def call(kernel, out_shape, in_specs, out_specs, operands, scratch=(), mib=16):
    return pl.pallas_call(
        kernel,
        out_shape=out_shape,
        in_specs=in_specs,
        out_specs=out_specs,
        scratch_shapes=list(scratch),
        cost_estimate=pl.CostEstimate(flops=1, transcendentals=0, bytes_accessed=1),
        compiler_params=pltpu.CompilerParams(vmem_limit_bytes=mib * MIB),
    )(*operands)


def in_hbm(*arrays):
    return tuple(pltpu.with_memory_space_constraint(a, pltpu.HBM) for a in arrays)


def kept(*shape):
    return pltpu.VMEM(shape, jnp.float32)


def f32(*shape):
    return jax.ShapeDtypeStruct(shape, jnp.float32)


def cut(value, xt, j):
    return value[xt * ROWS : (xt + 1) * ROWS, j * LANES : (j + 1) * LANES]


def weights(courant, codes, bit):
    size = jnp.abs(courant)
    half = (0.5 * size) * (1.0 - size)
    limited = jnp.where(jnp.bitwise_and(codes, 1 << bit) != 0, half, 0.0)
    ahead = jnp.maximum(courant, 0.0) - limited
    back = jnp.maximum(-courant, 0.0) - limited
    return ahead, back


def second_weights(cy, codes, bit, xt, tiles):
    lane = lax.broadcasted_iota(jnp.int32, (ROWS, LANES), 1)
    out = []
    for j in range(tiles):
        ahead, back = weights(cut(cy, xt, j), cut(codes, xt, j), bit)
        if j == 0:
            back = jnp.where(lane == 0, 0.0, back)
        if j == tiles - 1:
            ahead = jnp.where(lane == LANES - 1, 0.0, ahead)
        out.append((ahead, back, (1.0 - ahead) - back))
    return out


def second_sweep(parts, factors):
    lane = lax.broadcasted_iota(jnp.int32, (ROWS, LANES), 1)
    tiles = len(parts)
    later = [pltpu.roll(part, LANES - 1, 1) for part in parts]
    sooner = [pltpu.roll(part, 1, 1) for part in parts]
    out = []
    for j in range(tiles):
        following, previous = later[j], sooner[j]
        if j + 1 < tiles:
            following = jnp.where(lane == LANES - 1, later[j + 1], following)
        if j > 0:
            previous = jnp.where(lane == 0, sooner[j - 1], previous)
        ahead, back, own = factors[j]
        out.append(own * parts[j] + ahead * following + back * previous)
    return out


def first_sweep(field, s, j, xt, last, factors, left_row, right_row):
    start = ROWS * (xt + 1)
    sub = lax.broadcasted_iota(jnp.int32, (ROWS, LANES), 0)
    own_value = field(s, j, start)
    following = field(s, j, start + 1)
    previous = field(s, j, start - 1)
    if xt == 0:
        previous = jnp.where(sub == 0, left_row(s, j), previous)
    if xt == last:
        following = jnp.where(sub == ROWS - 1, right_row(s, j), following)
    ahead, back, own = factors
    return own * own_value + ahead * following + back * previous


def turned(source_ref, flag, target_ref):
    tiles, rows, _ = source_ref.shape
    for j in range(tiles):
        for start in range(0, rows, ROWS):
            count = min(ROWS, rows - start)
            index = (LANES - 1) - lax.broadcasted_iota(jnp.int32, (count, LANES), 1)
            straight = source_ref[j, start : start + count, :]
            other = source_ref[tiles - 1 - j, start : start + count, :]
            mirrored = jnp.take_along_axis(other, index, axis=1, mode="promise_in_bounds")
            target_ref[j, start : start + count, :] = jnp.where(flag[:count], mirrored, straight)


def store_padded(ref, index, s, j, xt, value):
    start = ROWS * (xt + 1)
    ref[(*index, s, j, slice(start, start + ROWS), slice(None))] = value


def store_rims(first_ref, last_ref, row, j, xt, last, value):
    if xt == 0:
        first_ref[j, pl.ds(row, 1), :] = value[:1]
    if xt == last:
        last_ref[j, pl.ds(row, 1), :] = value[ROWS - 1 :]


def flags(seam_ref):
    return seam_ref[0] == 1, seam_ref[1] == 1


def lower_kernel(
    f_hbm, mf_hbm, cy_hbm, code_hbm, cx_hbm,
    v_ref, first_ref, last_ref, top_ref, mf_ref, cy_ref, code_ref, cx_ref,
    f_ref, sems,
):
    sectors, levels, columns, width = f_hbm.shape
    tiles, strips = width // LANES, columns // ROWS

    def fetch(k):
        return pltpu.make_async_copy(f_hbm.at[:, k], f_ref.at[k], sems.at[0, k])

    def fetch_code(k):
        return pltpu.make_async_copy(code_hbm.at[k], code_ref.at[k], sems.at[1, k])

    fetch_mf = pltpu.make_async_copy(mf_hbm, mf_ref, sems.at[2, 0])
    fetch_cy = pltpu.make_async_copy(cy_hbm, cy_ref, sems.at[2, 1])
    fetch_cx = pltpu.make_async_copy(cx_hbm, cx_ref, sems.at[2, 2])
    fetch(0).start()
    fetch_mf.start()
    fetch_cy.start()
    for k in range(levels - 1):
        fetch_code(k).start()
        fetch(k + 1).start()
    fetch_code(levels - 1).start()
    fetch_cx.start()
    fetch(0).wait()
    fetch_mf.wait()
    fetch_cy.wait()

    def level(k, _):
        fetch_code(k).wait()
        fetch(k + 1).wait()
        mf = mf_ref[k].astype(jnp.float32)
        cy = cy_ref[k].astype(jnp.float32)
        codes = code_ref[k]
        for xt in range(strips):
            factors = second_weights(cy, codes, 3, xt, tiles)
            rows = slice(xt * ROWS, (xt + 1) * ROWS)
            for s in range(sectors):
                parts = []
                for j in range(tiles):
                    lanes = slice(j * LANES, (j + 1) * LANES)
                    here = f_ref[k, s, rows, lanes]
                    upper = f_ref[k + 1, s, rows, lanes]
                    parts.append(here + cut(mf, xt, j) * (upper - here))
                for j, value in enumerate(second_sweep(parts, factors)):
                    store_padded(v_ref, (k,), s, j, xt, value)
                    store_rims(first_ref, last_ref, k * sectors + s, j, xt, strips - 1, value)
        return 0

    lax.fori_loop(0, levels - 1, level, 0)
    top_ref[...] = f_ref[levels - 1]
    fetch_code(levels - 1).wait()
    fetch_cx.wait()


def first_weights(cx, codes, bit, xt, j):
    ahead, back = weights(cut(cx, xt, j), cut(codes, xt, j), bit)
    return ahead, back, (1.0 - ahead) - back


def ends_kernel(
    v_ref, left_ref, right_ref, seam_ref, cx_ref, code_ref, here_ref, above_ref, mf_ref, cy_ref,
    out_ref, top_ref, first_ref, last_ref,
    lrow_ref, rrow_ref,
):
    _, sectors, tiles, _, _ = v_ref.shape
    columns = out_ref.shape[1]
    strips = columns // ROWS
    flip_left, flip_right = flags(seam_ref)
    turned(left_ref.at[:, :ROWS], flip_left, lrow_ref)
    turned(right_ref.at[:, :ROWS], flip_right, rrow_ref)
    cx = cx_ref[0].astype(jnp.float32)
    codes = code_ref[0]
    for xt in range(strips):
        for j in range(tiles):
            factors = first_weights(cx, codes, 2, xt, j)
            for s in range(sectors):
                value = first_sweep(
                    lambda s, j, start: v_ref[0, s, j, start : start + ROWS, :],
                    s, j, xt, strips - 1, factors,
                    lambda s, j: lrow_ref[j, s : s + 1, :],
                    lambda s, j: rrow_ref[j, s : s + 1, :],
                )
                out_ref[s, xt * ROWS : (xt + 1) * ROWS, j * LANES : (j + 1) * LANES] = value

    level = mf_ref.shape[0] - 1
    at_top = lax.axis_index("lev") == lax.axis_size("lev") - 1
    mf = mf_ref[level].astype(jnp.float32)
    cy = cy_ref[level].astype(jnp.float32)
    codes = code_ref[level]
    for xt in range(strips):
        factors = second_weights(cy, codes, 3, xt, tiles)
        rows = slice(xt * ROWS, (xt + 1) * ROWS)
        for s in range(sectors):
            parts = []
            for j in range(tiles):
                lanes = slice(j * LANES, (j + 1) * LANES)
                here = here_ref[s, rows, lanes]
                upper = jnp.where(at_top, here, above_ref[s, rows, lanes])
                parts.append(here + cut(mf, xt, j) * (upper - here))
            for j, value in enumerate(second_sweep(parts, factors)):
                store_padded(top_ref, (), s, j, xt, value)
                store_rims(first_ref, last_ref, s, j, xt, strips - 1, value)


def middle_kernel(
    v_ref, left_ref, right_ref, lowest_ref, seam_ref, cx_ref, mf_ref, cy_ref, code_ref,
    out_ref, first_ref, last_ref, top_ref,
    lrow_ref, rrow_ref, a_ref,
):
    below, sectors, tiles, padded, _ = v_ref.shape
    strips = (padded - 2 * ROWS) // ROWS
    flip_left, flip_right = flags(seam_ref)
    turned(left_ref, flip_left, lrow_ref)
    turned(right_ref, flip_right, rrow_ref)
    for s in range(sectors):
        for j in range(tiles):
            a_ref[0, s, j] = lowest_ref[s, :, j * LANES : (j + 1) * LANES]

    def level(k, _):
        cx = cx_ref[k + 1].astype(jnp.float32)
        mf = mf_ref[k].astype(jnp.float32)
        cy = cy_ref[k].astype(jnp.float32)
        codes_x = code_ref[k + 1]
        codes_y = code_ref[k]
        slot = lax.rem(k, 2)
        for xt in range(strips):
            along = [first_weights(cx, codes_x, 2, xt, j) for j in range(tiles)]
            across = second_weights(cy, codes_y, 1, xt, tiles)
            rows = slice(xt * ROWS, (xt + 1) * ROWS)
            for s in range(sectors):
                parts = []
                for j in range(tiles):
                    upper = first_sweep(
                        lambda s, j, start: v_ref[k + 1, s, j, start : start + ROWS, :],
                        s, j, xt, strips - 1, along[j],
                        lambda s, j: lrow_ref[j, pl.ds((k + 1) * sectors + s, 1), :],
                        lambda s, j: rrow_ref[j, pl.ds((k + 1) * sectors + s, 1), :],
                    )
                    here = a_ref[slot, s, j, rows, :]
                    a_ref[1 - slot, s, j, rows, :] = upper
                    parts.append(here + cut(mf, xt, j) * (upper - here))
                for j, value in enumerate(second_sweep(parts, across)):
                    store_padded(out_ref, (k,), s, j, xt, value)
                    store_rims(first_ref, last_ref, k * sectors + s, j, xt, strips - 1, value)
        return 0

    lax.fori_loop(0, below - 1, level, 0)
    top_ref[...] = a_ref[(below - 1) % 2]


def highest_kernel(
    vt_ref, left_ref, right_ref, lower_ref, above_ref, seam_ref, cx_ref, mf_ref, cy_ref, code_ref,
    out_ref, first_ref, last_ref,
    lrow_ref, rrow_ref,
):
    sectors, tiles, padded, _ = vt_ref.shape
    strips = (padded - 2 * ROWS) // ROWS
    top = mf_ref.shape[0] - 1
    at_top = lax.axis_index("lev") == lax.axis_size("lev") - 1
    flip_left, flip_right = flags(seam_ref)
    turned(left_ref, flip_left, lrow_ref)
    turned(right_ref, flip_right, rrow_ref)
    cx = cx_ref[top].astype(jnp.float32)
    mixing = [mf_ref[top - 1].astype(jnp.float32), mf_ref[top].astype(jnp.float32)]
    cys = [cy_ref[top - 1].astype(jnp.float32), cy_ref[top].astype(jnp.float32)]
    codes = [code_ref[top - 1], code_ref[top]]
    for xt in range(strips):
        along = [first_weights(cx, codes[1], 2, xt, j) for j in range(tiles)]
        across = [second_weights(cys[i], codes[i], 1, xt, tiles) for i in range(2)]
        rows = slice(xt * ROWS, (xt + 1) * ROWS)
        for s in range(sectors):
            low, high = [], []
            for j in range(tiles):
                here = first_sweep(
                    lambda s, j, start: vt_ref[s, j, start : start + ROWS, :],
                    s, j, xt, strips - 1, along[j],
                    lambda s, j: lrow_ref[j, s : s + 1, :],
                    lambda s, j: rrow_ref[j, s : s + 1, :],
                )
                lower = lower_ref[s, j, rows, :]
                low.append(lower + cut(mixing[0], xt, j) * (here - lower))
                upper = above_ref[s, rows, j * LANES : (j + 1) * LANES]
                upper = jnp.where(at_top, here, upper)
                high.append(here + cut(mixing[1], xt, j) * (upper - here))
            for i, parts in enumerate((low, high)):
                for j, value in enumerate(second_sweep(parts, across[i])):
                    store_padded(out_ref, (i,), s, j, xt, value)
                    store_rims(first_ref, last_ref, i * sectors + s, j, xt, strips - 1, value)


def final_kernel(
    v_ref, vt_ref, left_ref, right_ref, left_top_ref, right_top_ref, seam_ref,
    cx_ref, code_ref, weight_ref, share_ref,
    out_hbm, sens_ref,
    lrow_ref, rrow_ref, ltop_ref, rtop_ref, out_ref, sems,
):
    below, sectors, tiles, padded, _ = v_ref.shape
    strips = (padded - 2 * ROWS) // ROWS
    flip_left, flip_right = flags(seam_ref)
    turned(left_ref, flip_left, lrow_ref)
    turned(right_ref, flip_right, rrow_ref)
    turned(left_top_ref, flip_left, ltop_ref)
    turned(right_top_ref, flip_right, rtop_ref)

    def send(k):
        return pltpu.make_async_copy(out_ref.at[k], out_hbm.at[:, k], sems.at[k])

    def level(k, field, left_row, right_row, start_sum):
        cx = cx_ref[k].astype(jnp.float32)
        codes = code_ref[k]
        factor = weight_ref[pl.ds(k, 1), :]
        for xt in range(strips):
            rows = slice(xt * ROWS, (xt + 1) * ROWS)
            for j in range(tiles):
                lanes = slice(j * LANES, (j + 1) * LANES)
                factors = first_weights(cx, codes, 0, xt, j)
                total = 0.0
                for s in range(sectors):
                    value = first_sweep(
                        field, s, j, xt, strips - 1, factors, left_row, right_row
                    )
                    out_ref[k, s, rows, lanes] = value
                    total = total + share_ref[s, rows, lanes] * value
                if start_sum:
                    sens_ref[rows, lanes] = factor * total
                else:
                    sens_ref[rows, lanes] += factor * total
        send(k).start()

    for i in range(2):
        level(
            below + i,
            lambda s, j, start: vt_ref[i, s, j, start : start + ROWS, :],
            lambda s, j: ltop_ref[j, i * sectors + s : i * sectors + s + 1, :],
            lambda s, j: rtop_ref[j, i * sectors + s : i * sectors + s + 1, :],
            i == 0,
        )

    def step(k, _):
        level(
            k,
            lambda s, j, start: v_ref[k, s, j, start : start + ROWS, :],
            lambda s, j: lrow_ref[j, pl.ds(k * sectors + s, 1), :],
            lambda s, j: rrow_ref[j, pl.ds(k * sectors + s, 1), :],
            False,
        )
        return 0

    lax.fori_loop(0, below, step, 0)
    for k in range(below + 2):
        send(k).wait()


def scatter_kernel(cells_ref, *refs):
    *value_refs, out_ref = refs
    rows, lanes = out_ref.shape
    count = cells_ref.shape[0]
    high_iota = lax.broadcasted_iota(jnp.int32, (rows, lanes), 0)
    low_iota = lax.broadcasted_iota(jnp.int32, (lanes, lanes), 0)
    total = jnp.zeros((2 * rows, lanes), jnp.float32)
    for pair in range(0, count, 2):
        lefts, rights = [], []
        for row in (pair, pair + 1):
            cells = cells_ref[row : row + 1, :]
            part, line = divmod(row, value_refs[0].shape[0])
            value = value_refs[part][line : line + 1, :]
            coarse = value.astype(jnp.bfloat16).astype(jnp.float32)
            fine = value - coarse
            here = jnp.right_shift(cells, 7) == high_iota
            lefts.append(
                jnp.concatenate(
                    [jnp.where(here, coarse, 0.0), jnp.where(here, fine, 0.0)], axis=0
                ).astype(jnp.bfloat16)
            )
            match = jnp.bitwise_and(cells, 127) == low_iota
            rights.append(jnp.where(match, 1.0, 0.0).astype(jnp.bfloat16))
        total += lax.dot_general(
            jnp.concatenate(lefts, axis=1),
            jnp.concatenate(rights, axis=1),
            (((1,), (1,)), ((), ())),
            preferred_element_type=jnp.float32,
        )
    out_ref[...] = total[:rows] + total[rows:]


def remapped(partial_value, flux_cell):
    tiles, share = flux_cell.shape
    group = lax.axis_size("lev") * lax.axis_size("sec")
    piece = share // group
    sent = partial_value.reshape(tiles * group, piece)
    received = lax.all_to_all(
        sent, ("tile", "lev", "sec"), split_axis=0, concat_axis=0, tiled=True
    )
    summed = jnp.sum(received.reshape(tiles, group, piece), axis=1)
    own = summed.reshape(-1, LANES)
    rank = lax.axis_index(("lev", "sec"))
    parts = [own]
    for apart in range(1, group):
        pairs = [(i, i ^ apart) for i in range(group)]
        parts.append(lax.ppermute(own, ("lev", "sec"), pairs))
    cells = flux_cell.reshape(tiles, group, piece).transpose(1, 0, 2).reshape(group, -1, LANES)
    order = jnp.bitwise_xor(rank, jnp.arange(group, dtype=jnp.int32))
    cells = jnp.concatenate(
        [lax.dynamic_slice_in_dim(cells, order[i], 1, axis=0)[0] for i in range(group)], axis=0
    )
    out = call(
        scatter_kernel,
        f32(FL_DEV // LANES, LANES),
        [VM] * (group + 1),
        VM,
        (cells, *parts),
    )
    return out.reshape(-1)


def around(first, last):
    count = lax.axis_size("tile")
    up = [(i, (i + 1) % count) for i in range(count)]
    down = [(j, i) for i, j in up]
    return lax.ppermute(last, "tile", up), lax.ppermute(first, "tile", down)


def from_above(value):
    count = lax.axis_size("lev")
    return lax.ppermute(value, "lev", [(i + 1, i) for i in range(count - 1)])


def shards(
    forcing, courant_x, courant_y, mass_flux, limiter_code, seam_code, level_weight, sector_share, flux_cell
):
    sectors, levels, columns, width = forcing.shape
    tiles, below = width // LANES, levels - 1
    padded = columns + 2 * ROWS
    field = kept(below, sectors, tiles, padded, LANES)
    field_top = kept(sectors, tiles, padded, LANES)
    plane = kept(sectors, columns, width)
    rim = kept(tiles, below * sectors, LANES)
    rim_top = kept(tiles, sectors, LANES)
    rim_next = kept(tiles, (below - 1) * sectors, LANES)
    rim_pair = kept(tiles, 2 * sectors, LANES)
    rim_scratch = pltpu.VMEM((tiles, below * sectors, LANES), jnp.float32)

    seam = lax.dynamic_index_in_dim(seam_code, lax.axis_index("tile"), 0, keepdims=False)
    seam = jnp.broadcast_to(seam[:, None, None], (2, ROWS, LANES))
    weight = jnp.broadcast_to(level_weight[:, None], (levels, LANES))

    above = from_above(forcing[:, 0])
    narrow = pltpu.VMEM((levels, columns, width), jnp.bfloat16)
    v, first, last, top, mass_flux, courant_y, limiter_code, courant_x = call(
        lower_kernel,
        (
            field, rim, rim, plane,
            narrow, narrow, pltpu.VMEM((levels, columns, width), jnp.int32), narrow,
        ),
        [HBM] * 5,
        [VM] * 8,
        in_hbm(forcing, mass_flux, courant_y, limiter_code, courant_x),
        [
            pltpu.VMEM((levels, sectors, columns, width), jnp.float32),
            pltpu.SemaphoreType.DMA((3, levels)),
        ],
    )
    left, right = around(first, last)
    lowest, vt, first_top, last_top = call(
        ends_kernel,
        (plane, field_top, rim_top, rim_top),
        [VM] * 10,
        [VM] * 4,
        (
            v, left, right, seam, courant_x, limiter_code, top, above, mass_flux, courant_y,
        ),
        [pltpu.VMEM((tiles, ROWS, LANES), jnp.float32)] * 2,
    )
    above = from_above(lowest)
    left_top, right_top = around(first_top, last_top)

    v, first, last, top = call(
        middle_kernel,
        (
            kept(below - 1, sectors, tiles, padded, LANES),
            rim_next,
            rim_next,
            kept(sectors, tiles, columns, LANES),
        ),
        [VM] * 9,
        [VM] * 4,
        (v, left, right, lowest, seam, courant_x, mass_flux, courant_y, limiter_code),
        [rim_scratch, rim_scratch, pltpu.VMEM((2, sectors, tiles, columns, LANES), jnp.float32)],
    )
    left, right = around(first, last)
    vt, first_top, last_top = call(
        highest_kernel,
        (kept(2, sectors, tiles, padded, LANES), rim_pair, rim_pair),
        [VM] * 10,
        [VM] * 3,
        (
            vt, left_top, right_top, top, above, seam,
            courant_x, mass_flux, courant_y, limiter_code,
        ),
        [pltpu.VMEM((tiles, sectors, LANES), jnp.float32)] * 2,
    )
    left_top, right_top = around(first_top, last_top)
    adjoint, sensitivity = call(
        final_kernel,
        (f32(*forcing.shape), f32(columns, width)),
        [VM] * 11,
        [HBM, VM],
        (
            v, vt, left, right, left_top, right_top, seam,
            courant_x, limiter_code, weight, sector_share,
        ),
        [
            pltpu.VMEM((tiles, (below - 1) * sectors, LANES), jnp.float32),
            pltpu.VMEM((tiles, (below - 1) * sectors, LANES), jnp.float32),
            pltpu.VMEM((tiles, 2 * sectors, LANES), jnp.float32),
            pltpu.VMEM((tiles, 2 * sectors, LANES), jnp.float32),
            pltpu.VMEM((levels, sectors, columns, width), jnp.float32),
            pltpu.SemaphoreType.DMA((levels,)),
        ],
    )
    return (adjoint, remapped(sensitivity, flux_cell))


def solution(mesh):
    placed = (
        P("sec", "lev", "tile", None),
        P("lev", "tile", None),
        P("lev", "tile", None),
        P("lev", "tile", None),
        P("lev", "tile", None),
        P(),
        P("lev"),
        P("sec", "tile", None),
        P("tile", None),
    )
    return jax.shard_map(
        shards,
        mesh=mesh,
        in_specs=placed,
        out_specs=(P("sec", "lev", "tile", None), P("tile")),
        check_vma=False,
    )
```

```python
import functools

import jax
import jax.numpy as jnp
from jax import lax
from jax.experimental import pallas as pl
from jax.experimental.pallas import tpu as pltpu
from jax.sharding import PartitionSpec as P

FL_DEV = 15360
LANES = 128
ROWS = 8
MIB = 2**20
VM = pl.BlockSpec(memory_space=pltpu.VMEM)
HBM = pl.BlockSpec(memory_space=pltpu.HBM)


def call(kernel, out_shape, in_specs, out_specs, operands, scratch=(), mib=16):
    return pl.pallas_call(
        kernel,
        out_shape=out_shape,
        in_specs=in_specs,
        out_specs=out_specs,
        scratch_shapes=list(scratch),
        cost_estimate=pl.CostEstimate(flops=1, transcendentals=0, bytes_accessed=1),
        compiler_params=pltpu.CompilerParams(vmem_limit_bytes=mib * MIB),
    )(*operands)


def in_hbm(*arrays):
    return tuple(pltpu.with_memory_space_constraint(a, pltpu.HBM) for a in arrays)


def kept(*shape):
    return pltpu.VMEM(shape, jnp.float32)


def f32(*shape):
    return jax.ShapeDtypeStruct(shape, jnp.float32)


def cut(value, xt, j):
    return value[xt * ROWS : (xt + 1) * ROWS, j * LANES : (j + 1) * LANES]


def weights(courant, codes, bit):
    size = jnp.abs(courant)
    half = (0.5 * size) * (1.0 - size)
    limited = jnp.where(jnp.bitwise_and(codes, 1 << bit) != 0, half, 0.0)
    ahead = jnp.maximum(courant, 0.0) - limited
    back = jnp.maximum(-courant, 0.0) - limited
    return ahead, back


def second_weights(cy, codes, bit, xt, tiles):
    lane = lax.broadcasted_iota(jnp.int32, (ROWS, LANES), 1)
    out = []
    for j in range(tiles):
        ahead, back = weights(cut(cy, xt, j), cut(codes, xt, j), bit)
        if j == 0:
            back = jnp.where(lane == 0, 0.0, back)
        if j == tiles - 1:
            ahead = jnp.where(lane == LANES - 1, 0.0, ahead)
        out.append((ahead, back, (1.0 - ahead) - back))
    return out


def second_sweep(parts, factors):
    lane = lax.broadcasted_iota(jnp.int32, (ROWS, LANES), 1)
    tiles = len(parts)
    later = [pltpu.roll(part, LANES - 1, 1) for part in parts]
    sooner = [pltpu.roll(part, 1, 1) for part in parts]
    out = []
    for j in range(tiles):
        following, previous = later[j], sooner[j]
        if j + 1 < tiles:
            following = jnp.where(lane == LANES - 1, later[j + 1], following)
        if j > 0:
            previous = jnp.where(lane == 0, sooner[j - 1], previous)
        ahead, back, own = factors[j]
        out.append(own * parts[j] + ahead * following + back * previous)
    return out


def first_sweep(field, s, j, xt, last, factors, left_row, right_row):
    start = ROWS * (xt + 1)
    sub = lax.broadcasted_iota(jnp.int32, (ROWS, LANES), 0)
    own_value = field(s, j, start)
    following = field(s, j, start + 1)
    previous = field(s, j, start - 1)
    if xt == 0:
        previous = jnp.where(sub == 0, left_row(s, j), previous)
    if xt == last:
        following = jnp.where(sub == ROWS - 1, right_row(s, j), following)
    ahead, back, own = factors
    return own * own_value + ahead * following + back * previous


def turned(source_ref, flag, target_ref):
    tiles, rows, _ = source_ref.shape
    for j in range(tiles):
        for start in range(0, rows, ROWS):
            count = min(ROWS, rows - start)
            index = (LANES - 1) - lax.broadcasted_iota(jnp.int32, (count, LANES), 1)
            straight = source_ref[j, start : start + count, :]
            other = source_ref[tiles - 1 - j, start : start + count, :]
            mirrored = jnp.take_along_axis(other, index, axis=1, mode="promise_in_bounds")
            target_ref[j, start : start + count, :] = jnp.where(flag, mirrored, straight)


def store_padded(ref, index, s, j, xt, value):
    start = ROWS * (xt + 1)
    ref[(*index, s, j, slice(start, start + ROWS), slice(None))] = value


def store_rims(first_ref, last_ref, row, j, xt, last, value):
    if xt == 0:
        first_ref[j, pl.ds(row, 1), :] = value[:1]
    if xt == last:
        last_ref[j, pl.ds(row, 1), :] = value[ROWS - 1 :]


def flags(seam_ref):
    tile = lax.axis_index("tile")
    return seam_ref[tile, 0:1, :] == 1, seam_ref[tile, 1:2, :] == 1


def start_kernel(f_hbm, out_ref, sem):
    copy = pltpu.make_async_copy(f_hbm.at[:, 0], out_ref, sem)
    copy.start()
    copy.wait()


def lower_kernel(
    f_hbm, mf_hbm, cy_hbm, code_hbm, cx_hbm,
    v_ref, first_ref, last_ref, top_ref, mf_ref, cy_ref, code_ref, cx_ref,
    f_ref, sems,
):
    sectors, levels, columns, width = f_hbm.shape
    tiles, strips = width // LANES, columns // ROWS

    def fetch(k):
        return pltpu.make_async_copy(f_hbm.at[:, k], f_ref.at[k], sems.at[0, k])

    def fetch_code(k):
        return pltpu.make_async_copy(code_hbm.at[k], code_ref.at[k], sems.at[1, k])

    def fetch_mf(k):
        return pltpu.make_async_copy(mf_hbm.at[k], mf_ref.at[k], sems.at[2, k])

    def fetch_cy(k):
        return pltpu.make_async_copy(cy_hbm.at[k], cy_ref.at[k], sems.at[3, k])

    fetch_cx = pltpu.make_async_copy(cx_hbm, cx_ref, sems.at[4, 0])
    fetch(0).start()
    for k in range(levels):
        fetch_mf(k).start()
        fetch_cy(k).start()
        fetch_code(k).start()
        if k < levels - 1:
            fetch(k + 1).start()
    fetch_cx.start()
    fetch(0).wait()

    def level(k, _):
        fetch_mf(k).wait()
        fetch_cy(k).wait()
        fetch_code(k).wait()
        fetch(k + 1).wait()
        mf = mf_ref[k].astype(jnp.float32)
        cy = cy_ref[k].astype(jnp.float32)
        codes = code_ref[k]
        for xt in range(strips):
            factors = second_weights(cy, codes, 3, xt, tiles)
            rows = slice(xt * ROWS, (xt + 1) * ROWS)
            for s in range(sectors):
                parts = []
                for j in range(tiles):
                    lanes = slice(j * LANES, (j + 1) * LANES)
                    here = f_ref[k, s, rows, lanes]
                    upper = f_ref[k + 1, s, rows, lanes]
                    parts.append(here + cut(mf, xt, j) * (upper - here))
                for j, value in enumerate(second_sweep(parts, factors)):
                    store_padded(v_ref, (k,), s, j, xt, value)
                    store_rims(first_ref, last_ref, k * sectors + s, j, xt, strips - 1, value)
        return 0

    lax.fori_loop(0, levels - 1, level, 0)
    top_ref[...] = f_ref[levels - 1]
    fetch_mf(levels - 1).wait()
    fetch_cy(levels - 1).wait()
    fetch_code(levels - 1).wait()
    fetch_cx.wait()


def first_weights(cx, codes, bit, xt, j):
    ahead, back = weights(cut(cx, xt, j), cut(codes, xt, j), bit)
    return ahead, back, (1.0 - ahead) - back


def ends_kernel(
    v_ref, left_ref, right_ref, seam_ref, cx_ref, code_ref, here_ref, above_ref, mf_ref, cy_ref,
    out_ref, top_ref, first_ref, last_ref,
    lrow_ref, rrow_ref,
):
    _, sectors, tiles, _, _ = v_ref.shape
    columns = out_ref.shape[1]
    strips = columns // ROWS
    flip_left, flip_right = flags(seam_ref)
    turned(left_ref.at[:, :ROWS], flip_left, lrow_ref)
    turned(right_ref.at[:, :ROWS], flip_right, rrow_ref)
    cx = cx_ref[0].astype(jnp.float32)
    codes = code_ref[0]
    for xt in range(strips):
        for j in range(tiles):
            factors = first_weights(cx, codes, 2, xt, j)
            for s in range(sectors):
                value = first_sweep(
                    lambda s, j, start: v_ref[0, s, j, start : start + ROWS, :],
                    s, j, xt, strips - 1, factors,
                    lambda s, j: lrow_ref[j, s : s + 1, :],
                    lambda s, j: rrow_ref[j, s : s + 1, :],
                )
                out_ref[s, xt * ROWS : (xt + 1) * ROWS, j * LANES : (j + 1) * LANES] = value

    level = mf_ref.shape[0] - 1
    at_top = lax.axis_index("lev") == lax.axis_size("lev") - 1
    mf = mf_ref[level].astype(jnp.float32)
    cy = cy_ref[level].astype(jnp.float32)
    codes = code_ref[level]
    for xt in range(strips):
        factors = second_weights(cy, codes, 3, xt, tiles)
        rows = slice(xt * ROWS, (xt + 1) * ROWS)
        for s in range(sectors):
            parts = []
            for j in range(tiles):
                lanes = slice(j * LANES, (j + 1) * LANES)
                here = here_ref[s, rows, lanes]
                upper = jnp.where(at_top, here, above_ref[s, rows, lanes])
                parts.append(here + cut(mf, xt, j) * (upper - here))
            for j, value in enumerate(second_sweep(parts, factors)):
                store_padded(top_ref, (), s, j, xt, value)
                store_rims(first_ref, last_ref, s, j, xt, strips - 1, value)


def middle_kernel(
    v_ref, left_ref, right_ref, lowest_ref, seam_ref, cx_ref, mf_ref, cy_ref, code_ref,
    out_ref, first_ref, last_ref, top_ref,
    lrow_ref, rrow_ref, a_ref,
):
    below, sectors, tiles, padded, _ = v_ref.shape
    strips = (padded - 2 * ROWS) // ROWS
    flip_left, flip_right = flags(seam_ref)
    turned(left_ref, flip_left, lrow_ref)
    turned(right_ref, flip_right, rrow_ref)
    for s in range(sectors):
        for j in range(tiles):
            a_ref[0, s, j] = lowest_ref[s, :, j * LANES : (j + 1) * LANES]

    def level(k, _):
        cx = cx_ref[k + 1].astype(jnp.float32)
        mf = mf_ref[k].astype(jnp.float32)
        cy = cy_ref[k].astype(jnp.float32)
        codes_x = code_ref[k + 1]
        codes_y = code_ref[k]
        slot = lax.rem(k, 2)
        for xt in range(strips):
            along = [first_weights(cx, codes_x, 2, xt, j) for j in range(tiles)]
            across = second_weights(cy, codes_y, 1, xt, tiles)
            rows = slice(xt * ROWS, (xt + 1) * ROWS)
            for s in range(sectors):
                parts = []
                for j in range(tiles):
                    upper = first_sweep(
                        lambda s, j, start: v_ref[k + 1, s, j, start : start + ROWS, :],
                        s, j, xt, strips - 1, along[j],
                        lambda s, j: lrow_ref[j, pl.ds((k + 1) * sectors + s, 1), :],
                        lambda s, j: rrow_ref[j, pl.ds((k + 1) * sectors + s, 1), :],
                    )
                    here = a_ref[slot, s, j, rows, :]
                    a_ref[1 - slot, s, j, rows, :] = upper
                    parts.append(here + cut(mf, xt, j) * (upper - here))
                for j, value in enumerate(second_sweep(parts, across)):
                    store_padded(out_ref, (k,), s, j, xt, value)
                    store_rims(first_ref, last_ref, k * sectors + s, j, xt, strips - 1, value)
        return 0

    lax.fori_loop(0, below - 1, level, 0)
    top_ref[...] = a_ref[(below - 1) % 2]


def second_last_kernel(
    vt_ref, left_ref, right_ref, lower_ref, first_in, last_in, seam_ref, cx_ref, mf_ref, cy_ref, code_ref,
    out_ref, first_ref, last_ref, top_ref,
    lrow_ref, rrow_ref,
):
    sectors, tiles, padded, _ = vt_ref.shape
    strips = (padded - 2 * ROWS) // ROWS
    top = mf_ref.shape[0] - 1
    done = first_in.shape[1]
    flip_left, flip_right = flags(seam_ref)
    turned(left_ref, flip_left, lrow_ref)
    turned(right_ref, flip_right, rrow_ref)
    first_ref[:, :done] = first_in[...]
    last_ref[:, :done] = last_in[...]
    cx = cx_ref[top].astype(jnp.float32)
    mf = mf_ref[top - 1].astype(jnp.float32)
    cy = cy_ref[top - 1].astype(jnp.float32)
    for xt in range(strips):
        along = [first_weights(cx, code_ref[top], 2, xt, j) for j in range(tiles)]
        across = second_weights(cy, code_ref[top - 1], 1, xt, tiles)
        rows = slice(xt * ROWS, (xt + 1) * ROWS)
        for s in range(sectors):
            parts = []
            for j in range(tiles):
                upper = first_sweep(
                    lambda s, j, start: vt_ref[s, j, start : start + ROWS, :],
                    s, j, xt, strips - 1, along[j],
                    lambda s, j: lrow_ref[j, s : s + 1, :],
                    lambda s, j: rrow_ref[j, s : s + 1, :],
                )
                top_ref[s, j, rows, :] = upper
                here = lower_ref[s, j, rows, :]
                parts.append(here + cut(mf, xt, j) * (upper - here))
            for j, value in enumerate(second_sweep(parts, across)):
                store_padded(out_ref, (), s, j, xt, value)
                store_rims(first_ref, last_ref, done + s, j, xt, strips - 1, value)


def highest_kernel(here_ref, above_ref, mf_ref, cy_ref, code_ref, out_ref, first_ref, last_ref):
    sectors, tiles, columns, _ = here_ref.shape
    strips = columns // ROWS
    top = mf_ref.shape[0] - 1
    at_top = lax.axis_index("lev") == lax.axis_size("lev") - 1
    mf = mf_ref[top].astype(jnp.float32)
    cy = cy_ref[top].astype(jnp.float32)
    for xt in range(strips):
        across = second_weights(cy, code_ref[top], 1, xt, tiles)
        rows = slice(xt * ROWS, (xt + 1) * ROWS)
        for s in range(sectors):
            parts = []
            for j in range(tiles):
                here = here_ref[s, j, rows, :]
                upper = above_ref[s, rows, j * LANES : (j + 1) * LANES]
                upper = jnp.where(at_top, here, upper)
                parts.append(here + cut(mf, xt, j) * (upper - here))
            for j, value in enumerate(second_sweep(parts, across)):
                store_padded(out_ref, (), s, j, xt, value)
                store_rims(first_ref, last_ref, s, j, xt, strips - 1, value)


def final_kernel(
    v_ref, vs_ref, vt_ref, left_ref, right_ref, left_top_ref, right_top_ref, seam_ref,
    cx_ref, code_ref, weight_ref, share_ref,
    out_hbm, *refs,
):
    *piece_refs, lrow_ref, rrow_ref, ltop_ref, rtop_ref, out_ref, sens_ref, packed_ref, sems = refs
    below, sectors, tiles, padded, _ = v_ref.shape
    strips = (padded - 2 * ROWS) // ROWS
    flip_left, flip_right = flags(seam_ref)
    turned(left_ref, flip_left, lrow_ref)
    turned(right_ref, flip_right, rrow_ref)
    turned(left_top_ref, flip_left, ltop_ref)
    turned(right_top_ref, flip_right, rtop_ref)

    def send(k):
        return pltpu.make_async_copy(out_ref.at[k], out_hbm.at[:, k], sems.at[k])

    def level(k, field, left_row, right_row, start_sum):
        cx = cx_ref[k].astype(jnp.float32)
        codes = code_ref[k]
        factor = weight_ref[pl.ds(k, 1), :]
        for xt in range(strips):
            rows = slice(xt * ROWS, (xt + 1) * ROWS)
            for j in range(tiles):
                lanes = slice(j * LANES, (j + 1) * LANES)
                factors = first_weights(cx, codes, 0, xt, j)
                total = 0.0
                for s in range(sectors):
                    value = first_sweep(
                        field, s, j, xt, strips - 1, factors, left_row, right_row
                    )
                    out_ref[k, s, rows, lanes] = value
                    total = total + share_ref[s, rows, lanes] * value
                if start_sum:
                    sens_ref[rows, lanes] = factor * total
                else:
                    sens_ref[rows, lanes] += factor * total
        send(k).start()

    level(
        below + 1,
        lambda s, j, start: vt_ref[s, j, start : start + ROWS, :],
        lambda s, j: ltop_ref[j, s : s + 1, :],
        lambda s, j: rtop_ref[j, s : s + 1, :],
        True,
    )
    level(
        below,
        lambda s, j, start: vs_ref[s, j, start : start + ROWS, :],
        lambda s, j: lrow_ref[j, below * sectors + s : below * sectors + s + 1, :],
        lambda s, j: rrow_ref[j, below * sectors + s : below * sectors + s + 1, :],
        False,
    )

    def step(k, _):
        level(
            k,
            lambda s, j, start: v_ref[k, s, j, start : start + ROWS, :],
            lambda s, j: lrow_ref[j, pl.ds(k * sectors + s, 1), :],
            lambda s, j: rrow_ref[j, pl.ds(k * sectors + s, 1), :],
            False,
        )
        return 0

    lax.fori_loop(0, below, step, 0)
    if len(piece_refs) == 1:
        piece_refs[0][...] = sens_ref[...]
    else:
        owners, group, depth, _ = packed_ref.shape
        share = strips * ROWS * tiles // owners
        rank = lax.axis_index("lev")
        for o in range(owners):
            for place in range(group * depth):
                piece, line = divmod(place, depth)
                if place < share:
                    x, j = divmod(o * share + place, tiles)
                    row = sens_ref[x : x + 1, j * LANES : (j + 1) * LANES]
                else:
                    row = jnp.zeros((1, LANES), jnp.float32)
                packed_ref[o, piece, line : line + 1, :] = row
        for apart, ref in enumerate(piece_refs):
            ref[...] = packed_ref[:, jnp.bitwise_xor(rank, apart)]
    for k in range(below + 2):
        send(k).wait()


def scatter_kernel(cells_ref, *refs):
    *value_refs, out_ref = refs
    rows, lanes = out_ref.shape
    group, owners, depth, _ = cells_ref.shape
    tile, rank = lax.axis_index("tile"), lax.axis_index("lev")
    high_iota = lax.broadcasted_iota(jnp.int32, (rows, lanes), 0)
    low_iota = lax.broadcasted_iota(jnp.int32, (lanes, lanes), 0)
    total = jnp.zeros((2 * rows, lanes), jnp.float32)
    lines = [(i, o, r) for i in range(group) for o in range(owners) for r in range(depth)]
    for pair in range(0, len(lines), 2):
        lefts, rights = [], []
        for part, owner, line in lines[pair : pair + 2]:
            source = lax.rem(tile + owners - owner, owners)
            cells = cells_ref[jnp.bitwise_xor(rank, part), source, line : line + 1, :]
            value = value_refs[part][owner, line : line + 1, :]
            coarse = value.astype(jnp.bfloat16).astype(jnp.float32)
            fine = value - coarse
            here = jnp.right_shift(cells, 7) == high_iota
            lefts.append(
                jnp.concatenate(
                    [jnp.where(here, coarse, 0.0), jnp.where(here, fine, 0.0)], axis=0
                ).astype(jnp.bfloat16)
            )
            match = jnp.bitwise_and(cells, 127) == low_iota
            rights.append(jnp.where(match, 1.0, 0.0).astype(jnp.bfloat16))
        total += lax.dot_general(
            jnp.concatenate(lefts, axis=1),
            jnp.concatenate(rights, axis=1),
            (((1,), (1,)), ((), ())),
            preferred_element_type=jnp.float32,
        )
    out_ref[...] = total[:rows] + total[rows:]


def choose_kernel(mine_ref, other_ref, *out_refs):
    owners = mine_ref.shape[0]
    tile = lax.axis_index("tile")
    for apart, ref in enumerate(out_refs):
        owner = lax.rem(tile + apart, owners)
        ref[...] = mine_ref[owner] + other_ref[owner]


def exchanged(value, axis, apart):
    count = lax.axis_size(axis)
    return lax.ppermute(value, axis, [(i, i ^ apart) for i in range(count)])


def remapped(pieces, flux_cell):
    owners, share = flux_cell.shape
    group = lax.axis_size("lev")
    depth = pieces[0].shape[1]
    mine = pieces[0]
    arrived = [exchanged(pieces[d], "lev", d) for d in range(1, group)]
    for other in arrived:
        mine = mine + other
    other = exchanged(mine, "sec", 1)
    if owners <= 8:
        sent = call(
            choose_kernel, (f32(depth, LANES),) * owners, [VM] * 2, [VM] * owners, (mine, other)
        )
        got = [sent[0]]
        for d in range(1, owners):
            hops = [(i, (i + d) % owners) for i in range(owners)]
            got.append(lax.ppermute(sent[d], "tile", hops))
        own = jnp.stack(got)
    else:
        own = lax.all_to_all(mine + other, "tile", split_axis=0, concat_axis=0, tiled=True)
        order = jnp.remainder(lax.axis_index("tile") - jnp.arange(owners), owners)
        own = jnp.take(own, order, axis=0)
    parts = [own] + [exchanged(own, "lev", d) for d in range(1, group)]
    cells = jnp.pad(flux_cell, ((0, 0), (0, group * depth * LANES - share)))
    cells = cells.reshape(owners, group, depth, LANES).transpose(1, 0, 2, 3)
    out = call(
        scatter_kernel, f32(FL_DEV // LANES, LANES), [VM] * (group + 1), VM, (cells, *parts)
    )
    return out.reshape(-1)


def around(first, last):
    count = lax.axis_size("tile")
    up = [(i, (i + 1) % count) for i in range(count)]
    down = [(j, i) for i, j in up]
    return lax.ppermute(last, "tile", up), lax.ppermute(first, "tile", down)


def from_above(value):
    count = lax.axis_size("lev")
    return lax.ppermute(value, "lev", [(i + 1, i) for i in range(count - 1)])


def shards(
    forcing, courant_x, courant_y, mass_flux, limiter_code, seam_code, level_weight, sector_share, flux_cell
):
    sectors, levels, columns, width = forcing.shape
    tiles, below = width // LANES, levels - 1
    padded = columns + 2 * ROWS
    field = kept(below, sectors, tiles, padded, LANES)
    field_top = kept(sectors, tiles, padded, LANES)
    plane = kept(sectors, columns, width)
    rim = kept(tiles, below * sectors, LANES)
    rim_top = kept(tiles, sectors, LANES)
    rim_next = kept(tiles, (below - 1) * sectors, LANES)
    rim_scratch = pltpu.VMEM((tiles, below * sectors, LANES), jnp.float32)

    seam = jnp.broadcast_to(seam_code[:, :, None], (*seam_code.shape, LANES))
    weight = jnp.broadcast_to(level_weight[:, None], (levels, LANES))

    above = from_above(
        call(start_kernel, plane, [HBM], VM, in_hbm(forcing), [pltpu.SemaphoreType.DMA])
    )
    narrow = pltpu.VMEM((levels, columns, width), jnp.bfloat16)
    v, first, last, top, mass_flux, courant_y, limiter_code, courant_x = call(
        lower_kernel,
        (
            field, rim, rim, plane,
            narrow, narrow, pltpu.VMEM((levels, columns, width), jnp.int32), narrow,
        ),
        [HBM] * 5,
        [VM] * 8,
        in_hbm(forcing, mass_flux, courant_y, limiter_code, courant_x),
        [
            pltpu.VMEM((levels, sectors, columns, width), jnp.float32),
            pltpu.SemaphoreType.DMA((5, levels)),
        ],
    )
    left, right = around(first, last)
    lowest, vt, first_top, last_top = call(
        ends_kernel,
        (plane, field_top, rim_top, rim_top),
        [VM] * 10,
        [VM] * 4,
        (
            v, left, right, seam, courant_x, limiter_code, top, above, mass_flux, courant_y,
        ),
        [pltpu.VMEM((tiles, ROWS, LANES), jnp.float32)] * 2,
    )
    above = from_above(lowest)
    left_top, right_top = around(first_top, last_top)

    v, first, last, top = call(
        middle_kernel,
        (
            kept(below - 1, sectors, tiles, padded, LANES),
            rim_next,
            rim_next,
            kept(sectors, tiles, columns, LANES),
        ),
        [VM] * 9,
        [VM] * 4,
        (v, left, right, lowest, seam, courant_x, mass_flux, courant_y, limiter_code),
        [rim_scratch, rim_scratch, pltpu.VMEM((2, sectors, tiles, columns, LANES), jnp.float32)],
    )
    vs, first, last, top = call(
        second_last_kernel,
        (field_top, rim, rim, kept(sectors, tiles, columns, LANES)),
        [VM] * 11,
        [VM] * 4,
        (
            vt, left_top, right_top, top, first, last, seam,
            courant_x, mass_flux, courant_y, limiter_code,
        ),
        [pltpu.VMEM((tiles, sectors, LANES), jnp.float32)] * 2,
    )
    left, right = around(first, last)
    vt, first_top, last_top = call(
        highest_kernel,
        (field_top, rim_top, rim_top),
        [VM] * 5,
        [VM] * 3,
        (top, above, mass_flux, courant_y, limiter_code),
    )
    left_top, right_top = around(first_top, last_top)

    owners, share = flux_cell.shape
    group = lax.axis_size("lev")
    depth = -(-share // (group * LANES))
    aligned = share % LANES == 0 and width % LANES == 0
    pieces = (f32(owners, depth, LANES),) * group if aligned else (f32(columns, width),)
    adjoint, *pieces = call(
        final_kernel,
        (f32(*forcing.shape), *pieces),
        [VM] * 12,
        [HBM] + [VM] * len(pieces),
        (
            v, vs, vt, left, right, left_top, right_top, seam,
            courant_x, limiter_code, weight, sector_share,
        ),
        [
            rim_scratch, rim_scratch,
            pltpu.VMEM((tiles, sectors, LANES), jnp.float32),
            pltpu.VMEM((tiles, sectors, LANES), jnp.float32),
            pltpu.VMEM((levels, sectors, columns, width), jnp.float32),
            pltpu.VMEM((columns, width), jnp.float32),
            pltpu.VMEM((owners, group, depth, LANES), jnp.float32),
            pltpu.SemaphoreType.DMA((levels,)),
        ],
    )
    if not aligned:
        packed = jnp.pad(
            pieces[0].reshape(owners, share), ((0, 0), (0, group * depth * LANES - share))
        ).reshape(owners, group, depth, LANES)
        rank = lax.axis_index("lev")
        pieces = [
            lax.dynamic_index_in_dim(packed, jnp.bitwise_xor(rank, d), 1, keepdims=False)
            for d in range(group)
        ]
    flux_cell, pieces = lax.optimization_barrier((flux_cell, pieces))
    return (adjoint, remapped(pieces, flux_cell))


def solution(mesh):
    placed = (
        P("sec", "lev", "tile", None),
        P("lev", "tile", None),
        P("lev", "tile", None),
        P("lev", "tile", None),
        P("lev", "tile", None),
        P(),
        P("lev"),
        P("sec", "tile", None),
        P("tile", None),
    )
    return jax.shard_map(
        shards,
        mesh=mesh,
        in_specs=placed,
        out_specs=(P("sec", "lev", "tile", None), P("tile")),
        check_vma=False,
    )
```

```python
import functools

import jax
import jax.numpy as jnp
from jax import lax
from jax.experimental import pallas as pl
from jax.experimental.pallas import tpu as pltpu
from jax.sharding import PartitionSpec as P

FL_DEV = 15360
LANES = 128
ROWS = 8
MIB = 2**20
VM = pl.BlockSpec(memory_space=pltpu.VMEM)
HBM = pl.BlockSpec(memory_space=pltpu.HBM)


def call(kernel, out_shape, in_specs, out_specs, operands, scratch=(), mib=16):
    return pl.pallas_call(
        kernel,
        out_shape=out_shape,
        in_specs=in_specs,
        out_specs=out_specs,
        scratch_shapes=list(scratch),
        cost_estimate=pl.CostEstimate(flops=1, transcendentals=0, bytes_accessed=1),
        compiler_params=pltpu.CompilerParams(vmem_limit_bytes=mib * MIB),
    )(*operands)


def in_hbm(*arrays):
    return tuple(pltpu.with_memory_space_constraint(a, pltpu.HBM) for a in arrays)


def kept(*shape):
    return pltpu.VMEM(shape, jnp.float32)


def f32(*shape):
    return jax.ShapeDtypeStruct(shape, jnp.float32)


def cut(value, xt, j):
    return value[xt * ROWS : (xt + 1) * ROWS, j * LANES : (j + 1) * LANES]


def weights(courant, codes, bit):
    size = jnp.abs(courant)
    half = (0.5 * size) * (1.0 - size)
    limited = jnp.where(jnp.bitwise_and(codes, 1 << bit) != 0, half, 0.0)
    ahead = jnp.maximum(courant, 0.0) - limited
    back = jnp.maximum(-courant, 0.0) - limited
    return ahead, back


def second_weights(cy, codes, bit, xt, tiles):
    lane = lax.broadcasted_iota(jnp.int32, (ROWS, LANES), 1)
    out = []
    for j in range(tiles):
        ahead, back = weights(cut(cy, xt, j), cut(codes, xt, j), bit)
        if j == 0:
            back = jnp.where(lane == 0, 0.0, back)
        if j == tiles - 1:
            ahead = jnp.where(lane == LANES - 1, 0.0, ahead)
        out.append((ahead, back, (1.0 - ahead) - back))
    return out


def second_sweep(parts, factors):
    lane = lax.broadcasted_iota(jnp.int32, (ROWS, LANES), 1)
    tiles = len(parts)
    later = [pltpu.roll(part, LANES - 1, 1) for part in parts]
    sooner = [pltpu.roll(part, 1, 1) for part in parts]
    out = []
    for j in range(tiles):
        following, previous = later[j], sooner[j]
        if j + 1 < tiles:
            following = jnp.where(lane == LANES - 1, later[j + 1], following)
        if j > 0:
            previous = jnp.where(lane == 0, sooner[j - 1], previous)
        ahead, back, own = factors[j]
        out.append(own * parts[j] + ahead * following + back * previous)
    return out


def first_sweep(field, s, j, xt, last, factors, left_row, right_row):
    start = ROWS * (xt + 1)
    sub = lax.broadcasted_iota(jnp.int32, (ROWS, LANES), 0)
    own_value = field(s, j, start)
    following = field(s, j, start + 1)
    previous = field(s, j, start - 1)
    if xt == 0:
        previous = jnp.where(sub == 0, left_row(s, j), previous)
    if xt == last:
        following = jnp.where(sub == ROWS - 1, right_row(s, j), following)
    ahead, back, own = factors
    return own * own_value + ahead * following + back * previous


def turned(source_ref, flag, target_ref):
    tiles, rows, _ = source_ref.shape
    for j in range(tiles):
        for start in range(0, rows, ROWS):
            count = min(ROWS, rows - start)
            index = (LANES - 1) - lax.broadcasted_iota(jnp.int32, (count, LANES), 1)
            straight = source_ref[j, start : start + count, :]
            other = source_ref[tiles - 1 - j, start : start + count, :]
            mirrored = jnp.take_along_axis(other, index, axis=1, mode="promise_in_bounds")
            target_ref[j, start : start + count, :] = jnp.where(flag, mirrored, straight)


def store_padded(ref, index, s, j, xt, value):
    start = ROWS * (xt + 1)
    ref[(*index, s, j, slice(start, start + ROWS), slice(None))] = value


def store_rims(first_ref, last_ref, row, j, xt, last, value):
    if xt == 0:
        first_ref[j, pl.ds(row, 1), :] = value[:1]
    if xt == last:
        last_ref[j, pl.ds(row, 1), :] = value[ROWS - 1 :]


def flags(seam_ref):
    tile = lax.axis_index("tile")
    return seam_ref[0, pl.ds(tile, 1), :] == 1, seam_ref[1, pl.ds(tile, 1), :] == 1


def start_kernel(f_hbm, out_ref, sem):
    copy = pltpu.make_async_copy(f_hbm.at[:, 0], out_ref, sem)
    copy.start()
    copy.wait()


def lower_kernel(
    f_hbm, mf_hbm, cy_hbm, code_hbm, cx_hbm,
    v_ref, first_ref, last_ref, top_ref, mf_ref, cy_ref, code_ref, cx_ref,
    f_ref, sems,
):
    sectors, levels, columns, width = f_hbm.shape
    tiles, strips = width // LANES, columns // ROWS

    def fetch(k):
        return pltpu.make_async_copy(f_hbm.at[:, k], f_ref.at[k], sems.at[0, k])

    def fetch_code(k):
        return pltpu.make_async_copy(code_hbm.at[k], code_ref.at[k], sems.at[1, k])

    def fetch_mf(k):
        return pltpu.make_async_copy(mf_hbm.at[k], mf_ref.at[k], sems.at[2, k])

    def fetch_cy(k):
        return pltpu.make_async_copy(cy_hbm.at[k], cy_ref.at[k], sems.at[3, k])

    fetch_cx = pltpu.make_async_copy(cx_hbm, cx_ref, sems.at[4, 0])
    fetch(0).start()
    for k in range(levels):
        fetch_mf(k).start()
        fetch_cy(k).start()
        fetch_code(k).start()
        if k < levels - 1:
            fetch(k + 1).start()
    fetch_cx.start()
    fetch(0).wait()

    def level(k, _):
        fetch_mf(k).wait()
        fetch_cy(k).wait()
        fetch_code(k).wait()
        fetch(k + 1).wait()
        mf = mf_ref[k].astype(jnp.float32)
        cy = cy_ref[k].astype(jnp.float32)
        codes = code_ref[k]
        for xt in range(strips):
            factors = second_weights(cy, codes, 3, xt, tiles)
            rows = slice(xt * ROWS, (xt + 1) * ROWS)
            for s in range(sectors):
                parts = []
                for j in range(tiles):
                    lanes = slice(j * LANES, (j + 1) * LANES)
                    here = f_ref[k, s, rows, lanes]
                    upper = f_ref[k + 1, s, rows, lanes]
                    parts.append(here + cut(mf, xt, j) * (upper - here))
                for j, value in enumerate(second_sweep(parts, factors)):
                    store_padded(v_ref, (k,), s, j, xt, value)
                    store_rims(first_ref, last_ref, k * sectors + s, j, xt, strips - 1, value)
        return 0

    lax.fori_loop(0, levels - 1, level, 0)
    top_ref[...] = f_ref[levels - 1]
    fetch_mf(levels - 1).wait()
    fetch_cy(levels - 1).wait()
    fetch_code(levels - 1).wait()
    fetch_cx.wait()


def first_weights(cx, codes, bit, xt, j):
    ahead, back = weights(cut(cx, xt, j), cut(codes, xt, j), bit)
    return ahead, back, (1.0 - ahead) - back


def ends_kernel(
    v_ref, left_ref, right_ref, seam_ref, cx_ref, code_ref, here_ref, above_ref, mf_ref, cy_ref,
    out_ref, top_ref, first_ref, last_ref,
    lrow_ref, rrow_ref,
):
    _, sectors, tiles, _, _ = v_ref.shape
    columns = out_ref.shape[1]
    strips = columns // ROWS
    flip_left, flip_right = flags(seam_ref)
    turned(left_ref.at[:, :ROWS], flip_left, lrow_ref)
    turned(right_ref.at[:, :ROWS], flip_right, rrow_ref)
    cx = cx_ref[0].astype(jnp.float32)
    codes = code_ref[0]
    for xt in range(strips):
        for j in range(tiles):
            factors = first_weights(cx, codes, 2, xt, j)
            for s in range(sectors):
                value = first_sweep(
                    lambda s, j, start: v_ref[0, s, j, start : start + ROWS, :],
                    s, j, xt, strips - 1, factors,
                    lambda s, j: lrow_ref[j, s : s + 1, :],
                    lambda s, j: rrow_ref[j, s : s + 1, :],
                )
                out_ref[s, xt * ROWS : (xt + 1) * ROWS, j * LANES : (j + 1) * LANES] = value

    level = mf_ref.shape[0] - 1
    at_top = lax.axis_index("lev") == lax.axis_size("lev") - 1
    mf = mf_ref[level].astype(jnp.float32)
    cy = cy_ref[level].astype(jnp.float32)
    codes = code_ref[level]
    for xt in range(strips):
        factors = second_weights(cy, codes, 3, xt, tiles)
        rows = slice(xt * ROWS, (xt + 1) * ROWS)
        for s in range(sectors):
            parts = []
            for j in range(tiles):
                lanes = slice(j * LANES, (j + 1) * LANES)
                here = here_ref[s, rows, lanes]
                upper = jnp.where(at_top, here, above_ref[s, rows, lanes])
                parts.append(here + cut(mf, xt, j) * (upper - here))
            for j, value in enumerate(second_sweep(parts, factors)):
                store_padded(top_ref, (), s, j, xt, value)
                store_rims(first_ref, last_ref, s, j, xt, strips - 1, value)


def middle_kernel(
    v_ref, left_ref, right_ref, lowest_ref, seam_ref, cx_ref, mf_ref, cy_ref, code_ref,
    out_ref, first_ref, last_ref, top_ref,
    lrow_ref, rrow_ref, a_ref,
):
    below, sectors, tiles, padded, _ = v_ref.shape
    strips = (padded - 2 * ROWS) // ROWS
    flip_left, flip_right = flags(seam_ref)
    turned(left_ref, flip_left, lrow_ref)
    turned(right_ref, flip_right, rrow_ref)
    for s in range(sectors):
        for j in range(tiles):
            a_ref[0, s, j] = lowest_ref[s, :, j * LANES : (j + 1) * LANES]

    def level(k, _):
        cx = cx_ref[k + 1].astype(jnp.float32)
        mf = mf_ref[k].astype(jnp.float32)
        cy = cy_ref[k].astype(jnp.float32)
        codes_x = code_ref[k + 1]
        codes_y = code_ref[k]
        slot = lax.rem(k, 2)
        for xt in range(strips):
            along = [first_weights(cx, codes_x, 2, xt, j) for j in range(tiles)]
            across = second_weights(cy, codes_y, 1, xt, tiles)
            rows = slice(xt * ROWS, (xt + 1) * ROWS)
            for s in range(sectors):
                parts = []
                for j in range(tiles):
                    upper = first_sweep(
                        lambda s, j, start: v_ref[k + 1, s, j, start : start + ROWS, :],
                        s, j, xt, strips - 1, along[j],
                        lambda s, j: lrow_ref[j, pl.ds((k + 1) * sectors + s, 1), :],
                        lambda s, j: rrow_ref[j, pl.ds((k + 1) * sectors + s, 1), :],
                    )
                    here = a_ref[slot, s, j, rows, :]
                    a_ref[1 - slot, s, j, rows, :] = upper
                    parts.append(here + cut(mf, xt, j) * (upper - here))
                for j, value in enumerate(second_sweep(parts, across)):
                    store_padded(out_ref, (k,), s, j, xt, value)
                    store_rims(first_ref, last_ref, k * sectors + s, j, xt, strips - 1, value)
        return 0

    lax.fori_loop(0, below - 1, level, 0)
    top_ref[...] = a_ref[(below - 1) % 2]


def second_last_kernel(
    vt_ref, left_ref, right_ref, lower_ref, first_in, last_in, seam_ref, cx_ref, mf_ref, cy_ref, code_ref,
    out_ref, first_ref, last_ref, top_ref,
    lrow_ref, rrow_ref,
):
    sectors, tiles, padded, _ = vt_ref.shape
    strips = (padded - 2 * ROWS) // ROWS
    top = mf_ref.shape[0] - 1
    done = first_in.shape[1]
    flip_left, flip_right = flags(seam_ref)
    turned(left_ref, flip_left, lrow_ref)
    turned(right_ref, flip_right, rrow_ref)
    first_ref[:, :done] = first_in[...]
    last_ref[:, :done] = last_in[...]
    cx = cx_ref[top].astype(jnp.float32)
    mf = mf_ref[top - 1].astype(jnp.float32)
    cy = cy_ref[top - 1].astype(jnp.float32)
    for xt in range(strips):
        along = [first_weights(cx, code_ref[top], 2, xt, j) for j in range(tiles)]
        across = second_weights(cy, code_ref[top - 1], 1, xt, tiles)
        rows = slice(xt * ROWS, (xt + 1) * ROWS)
        for s in range(sectors):
            parts = []
            for j in range(tiles):
                upper = first_sweep(
                    lambda s, j, start: vt_ref[s, j, start : start + ROWS, :],
                    s, j, xt, strips - 1, along[j],
                    lambda s, j: lrow_ref[j, s : s + 1, :],
                    lambda s, j: rrow_ref[j, s : s + 1, :],
                )
                top_ref[s, j, rows, :] = upper
                here = lower_ref[s, j, rows, :]
                parts.append(here + cut(mf, xt, j) * (upper - here))
            for j, value in enumerate(second_sweep(parts, across)):
                store_padded(out_ref, (), s, j, xt, value)
                store_rims(first_ref, last_ref, done + s, j, xt, strips - 1, value)


def highest_kernel(here_ref, above_ref, mf_ref, cy_ref, code_ref, out_ref, first_ref, last_ref):
    sectors, tiles, columns, _ = here_ref.shape
    strips = columns // ROWS
    top = mf_ref.shape[0] - 1
    at_top = lax.axis_index("lev") == lax.axis_size("lev") - 1
    mf = mf_ref[top].astype(jnp.float32)
    cy = cy_ref[top].astype(jnp.float32)
    for xt in range(strips):
        across = second_weights(cy, code_ref[top], 1, xt, tiles)
        rows = slice(xt * ROWS, (xt + 1) * ROWS)
        for s in range(sectors):
            parts = []
            for j in range(tiles):
                here = here_ref[s, j, rows, :]
                upper = above_ref[s, rows, j * LANES : (j + 1) * LANES]
                upper = jnp.where(at_top, here, upper)
                parts.append(here + cut(mf, xt, j) * (upper - here))
            for j, value in enumerate(second_sweep(parts, across)):
                store_padded(out_ref, (), s, j, xt, value)
                store_rims(first_ref, last_ref, s, j, xt, strips - 1, value)


def final_kernel(
    v_ref, vs_ref, vt_ref, left_ref, right_ref, left_top_ref, right_top_ref, seam_ref,
    cx_ref, code_ref, weight_ref, share_ref,
    out_hbm, *refs,
):
    *piece_refs, lrow_ref, rrow_ref, ltop_ref, rtop_ref, out_ref, sens_ref, sems = refs
    below, sectors, tiles, padded, _ = v_ref.shape
    strips = (padded - 2 * ROWS) // ROWS
    flip_left, flip_right = flags(seam_ref)
    turned(left_ref, flip_left, lrow_ref)
    turned(right_ref, flip_right, rrow_ref)
    turned(left_top_ref, flip_left, ltop_ref)
    turned(right_top_ref, flip_right, rtop_ref)

    def send(k):
        return pltpu.make_async_copy(out_ref.at[k], out_hbm.at[:, k], sems.at[k])

    def level(k, field, left_row, right_row, start_sum):
        cx = cx_ref[k].astype(jnp.float32)
        codes = code_ref[k]
        factor = weight_ref[pl.ds(k, 1), :]
        for xt in range(strips):
            rows = slice(xt * ROWS, (xt + 1) * ROWS)
            for j in range(tiles):
                lanes = slice(j * LANES, (j + 1) * LANES)
                factors = first_weights(cx, codes, 0, xt, j)
                total = 0.0
                for s in range(sectors):
                    value = first_sweep(
                        field, s, j, xt, strips - 1, factors, left_row, right_row
                    )
                    out_ref[k, s, rows, lanes] = value
                    total = total + share_ref[s, rows, lanes] * value
                if start_sum:
                    sens_ref[rows, lanes] = factor * total
                else:
                    sens_ref[rows, lanes] += factor * total
        send(k).start()

    level(
        below + 1,
        lambda s, j, start: vt_ref[s, j, start : start + ROWS, :],
        lambda s, j: ltop_ref[j, s : s + 1, :],
        lambda s, j: rtop_ref[j, s : s + 1, :],
        True,
    )
    level(
        below,
        lambda s, j, start: vs_ref[s, j, start : start + ROWS, :],
        lambda s, j: lrow_ref[j, below * sectors + s : below * sectors + s + 1, :],
        lambda s, j: rrow_ref[j, below * sectors + s : below * sectors + s + 1, :],
        False,
    )

    def step(k, _):
        level(
            k,
            lambda s, j, start: v_ref[k, s, j, start : start + ROWS, :],
            lambda s, j: lrow_ref[j, pl.ds(k * sectors + s, 1), :],
            lambda s, j: rrow_ref[j, pl.ds(k * sectors + s, 1), :],
            False,
        )
        return 0

    lax.fori_loop(0, below, step, 0)
    (piece_ref,) = piece_refs
    if len(piece_ref.shape) == 2:
        piece_ref[...] = sens_ref[...]
    else:
        owners, group, copies, depth, _ = piece_ref.shape
        share = strips * ROWS * tiles // owners
        for o in range(owners):
            for place in range(group * depth):
                piece, line = divmod(place, depth)
                if place < share:
                    x, j = divmod(o * share + place, tiles)
                    row = sens_ref[x : x + 1, j * LANES : (j + 1) * LANES]
                else:
                    row = jnp.zeros((1, LANES), jnp.float32)
                for i in range(copies):
                    piece_ref[o, piece, i, line : line + 1, :] = row
    for k in range(below + 2):
        send(k).wait()


def scatter_kernel(cells_ref, *refs):
    *value_refs, out_ref = refs
    rows, lanes = out_ref.shape
    group, owners, depth, _ = cells_ref.shape
    rank = lax.axis_index("lev")
    high_iota = lax.broadcasted_iota(jnp.int32, (rows, lanes), 0)
    low_iota = lax.broadcasted_iota(jnp.int32, (lanes, lanes), 0)
    total = jnp.zeros((2 * rows, lanes), jnp.float32)
    lines = [(i, o, r) for i in range(group) for o in range(owners) for r in range(depth)]
    for pair in range(0, len(lines), 2):
        lefts, rights = [], []
        for part, owner, line in lines[pair : pair + 2]:
            cells = cells_ref[jnp.bitwise_xor(rank, part), owner, line : line + 1, :]
            value = value_refs[part][owner, line : line + 1, :]
            coarse = value.astype(jnp.bfloat16).astype(jnp.float32)
            fine = value - coarse
            here = jnp.right_shift(cells, 7) == high_iota
            lefts.append(
                jnp.concatenate(
                    [jnp.where(here, coarse, 0.0), jnp.where(here, fine, 0.0)], axis=0
                ).astype(jnp.bfloat16)
            )
            match = jnp.bitwise_and(cells, 127) == low_iota
            rights.append(jnp.where(match, 1.0, 0.0).astype(jnp.bfloat16))
        total += lax.dot_general(
            jnp.concatenate(lefts, axis=1),
            jnp.concatenate(rights, axis=1),
            (((1,), (1,)), ((), ())),
            preferred_element_type=jnp.float32,
        )
    out_ref[...] = total[:rows] + total[rows:]


def exchanged(value, axis, apart):
    count = lax.axis_size(axis)
    return lax.ppermute(value, axis, [(i, i ^ apart) for i in range(count)])


def remapped(pieces, flux_cell):
    owners, share = flux_cell.shape
    _, group, copies, depth, _ = pieces.shape
    sent = pieces.reshape(-1, depth, LANES)
    arrived = lax.all_to_all(
        sent, ("tile", "lev", "sec"), split_axis=0, concat_axis=0, tiled=True
    )
    own = jnp.sum(arrived.reshape(owners, group * copies, depth, LANES), axis=1)
    parts = [own] + [exchanged(own, "lev", d) for d in range(1, group)]
    cells = jnp.pad(flux_cell, ((0, 0), (0, group * depth * LANES - share)))
    cells = cells.reshape(owners, group, depth, LANES).transpose(1, 0, 2, 3)
    out = call(
        scatter_kernel, f32(FL_DEV // LANES, LANES), [VM] * (group + 1), VM, (cells, *parts)
    )
    return out.reshape(-1)


def around(first, last):
    count = lax.axis_size("tile")
    up = [(i, (i + 1) % count) for i in range(count)]
    down = [(j, i) for i, j in up]
    return lax.ppermute(last, "tile", up), lax.ppermute(first, "tile", down)


def from_above(value):
    count = lax.axis_size("lev")
    return lax.ppermute(value, "lev", [(i + 1, i) for i in range(count - 1)])


def shards(
    forcing, courant_x, courant_y, mass_flux, limiter_code, seam_code, level_weight, sector_share, flux_cell
):
    sectors, levels, columns, width = forcing.shape
    tiles, below = width // LANES, levels - 1
    padded = columns + 2 * ROWS
    field = kept(below, sectors, tiles, padded, LANES)
    field_top = kept(sectors, tiles, padded, LANES)
    plane = kept(sectors, columns, width)
    rim = kept(tiles, below * sectors, LANES)
    rim_top = kept(tiles, sectors, LANES)
    rim_next = kept(tiles, (below - 1) * sectors, LANES)
    rim_scratch = pltpu.VMEM((tiles, below * sectors, LANES), jnp.float32)

    seam = jnp.broadcast_to(seam_code.T[:, :, None], (*seam_code.T.shape, LANES))
    weight = jnp.broadcast_to(level_weight[:, None], (levels, LANES))

    above = from_above(
        call(start_kernel, plane, [HBM], VM, in_hbm(forcing), [pltpu.SemaphoreType.DMA])
    )
    narrow = pltpu.VMEM((levels, columns, width), jnp.bfloat16)
    v, first, last, top, mass_flux, courant_y, limiter_code, courant_x = call(
        lower_kernel,
        (
            field, rim, rim, plane,
            narrow, narrow, pltpu.VMEM((levels, columns, width), jnp.int32), narrow,
        ),
        [HBM] * 5,
        [VM] * 8,
        in_hbm(forcing, mass_flux, courant_y, limiter_code, courant_x),
        [
            pltpu.VMEM((levels, sectors, columns, width), jnp.float32),
            pltpu.SemaphoreType.DMA((5, levels)),
        ],
    )
    left, right = around(first, last)
    lowest, vt, first_top, last_top = call(
        ends_kernel,
        (plane, field_top, rim_top, rim_top),
        [VM] * 10,
        [VM] * 4,
        (
            v, left, right, seam, courant_x, limiter_code, top, above, mass_flux, courant_y,
        ),
        [pltpu.VMEM((tiles, ROWS, LANES), jnp.float32)] * 2,
    )
    above = from_above(lowest)
    left_top, right_top = around(first_top, last_top)

    v, first, last, top = call(
        middle_kernel,
        (
            kept(below - 1, sectors, tiles, padded, LANES),
            rim_next,
            rim_next,
            kept(sectors, tiles, columns, LANES),
        ),
        [VM] * 9,
        [VM] * 4,
        (v, left, right, lowest, seam, courant_x, mass_flux, courant_y, limiter_code),
        [rim_scratch, rim_scratch, pltpu.VMEM((2, sectors, tiles, columns, LANES), jnp.float32)],
    )
    vs, first, last, top = call(
        second_last_kernel,
        (field_top, rim, rim, kept(sectors, tiles, columns, LANES)),
        [VM] * 11,
        [VM] * 4,
        (
            vt, left_top, right_top, top, first, last, seam,
            courant_x, mass_flux, courant_y, limiter_code,
        ),
        [pltpu.VMEM((tiles, sectors, LANES), jnp.float32)] * 2,
    )
    left, right = around(first, last)
    vt, first_top, last_top = call(
        highest_kernel,
        (field_top, rim_top, rim_top),
        [VM] * 5,
        [VM] * 3,
        (top, above, mass_flux, courant_y, limiter_code),
    )
    left_top, right_top = around(first_top, last_top)

    owners, share = flux_cell.shape
    group, copies = lax.axis_size("lev"), lax.axis_size("sec")
    depth = -(-share // (group * LANES))
    aligned = share % LANES == 0
    packed = (owners, group, copies, depth, LANES)
    adjoint, pieces = call(
        final_kernel,
        (f32(*forcing.shape), f32(*packed) if aligned else f32(columns, width)),
        [VM] * 12,
        [HBM, VM],
        (
            v, vs, vt, left, right, left_top, right_top, seam,
            courant_x, limiter_code, weight, sector_share,
        ),
        [
            rim_scratch, rim_scratch,
            pltpu.VMEM((tiles, sectors, LANES), jnp.float32),
            pltpu.VMEM((tiles, sectors, LANES), jnp.float32),
            pltpu.VMEM((levels, sectors, columns, width), jnp.float32),
            pltpu.VMEM((columns, width), jnp.float32),
            pltpu.SemaphoreType.DMA((levels,)),
        ],
    )
    if not aligned:
        pieces = jnp.pad(
            pieces.reshape(owners, share), ((0, 0), (0, group * depth * LANES - share))
        ).reshape(owners, group, 1, depth, LANES)
        pieces = jnp.broadcast_to(pieces, packed)
    flux_cell, pieces = lax.optimization_barrier((flux_cell, pieces))
    return (adjoint, remapped(pieces, flux_cell))


def solution(mesh):
    placed = (
        P("sec", "lev", "tile", None),
        P("lev", "tile", None),
        P("lev", "tile", None),
        P("lev", "tile", None),
        P("lev", "tile", None),
        P(),
        P("lev"),
        P("sec", "tile", None),
        P("tile", None),
    )
    return jax.shard_map(
        shards,
        mesh=mesh,
        in_specs=placed,
        out_specs=(P("sec", "lev", "tile", None), P("tile")),
        check_vma=False,
    )
```

```python
import functools

import jax
import jax.numpy as jnp
from jax import lax
from jax.experimental import pallas as pl
from jax.experimental.pallas import tpu as pltpu
from jax.sharding import PartitionSpec as P

FL_DEV = 15360
LANES = 128
ROWS = 8
MIB = 2**20
VM = pl.BlockSpec(memory_space=pltpu.VMEM)
HBM = pl.BlockSpec(memory_space=pltpu.HBM)


def call(kernel, out_shape, in_specs, out_specs, operands, scratch=(), mib=16, aliases={}):
    return pl.pallas_call(
        kernel,
        out_shape=out_shape,
        in_specs=in_specs,
        out_specs=out_specs,
        scratch_shapes=list(scratch),
        input_output_aliases=aliases,
        cost_estimate=pl.CostEstimate(flops=1, transcendentals=0, bytes_accessed=1),
        compiler_params=pltpu.CompilerParams(vmem_limit_bytes=mib * MIB),
    )(*operands)


def in_hbm(*arrays):
    return tuple(pltpu.with_memory_space_constraint(a, pltpu.HBM) for a in arrays)


def kept(*shape):
    return pltpu.VMEM(shape, jnp.float32)


def f32(*shape):
    return jax.ShapeDtypeStruct(shape, jnp.float32)


def cut(value, xt, j):
    return value[xt * ROWS : (xt + 1) * ROWS, j * LANES : (j + 1) * LANES]


def weights(courant, codes, bit):
    size = jnp.abs(courant)
    half = (0.5 * size) * (1.0 - size)
    limited = jnp.where(jnp.bitwise_and(codes, 1 << bit) != 0, half, 0.0)
    ahead = jnp.maximum(courant, 0.0) - limited
    back = jnp.maximum(-courant, 0.0) - limited
    return ahead, back


def second_weights(cy, codes, bit, xt, tiles):
    lane = lax.broadcasted_iota(jnp.int32, (ROWS, LANES), 1)
    out = []
    for j in range(tiles):
        ahead, back = weights(cut(cy, xt, j), cut(codes, xt, j), bit)
        if j == 0:
            back = jnp.where(lane == 0, 0.0, back)
        if j == tiles - 1:
            ahead = jnp.where(lane == LANES - 1, 0.0, ahead)
        out.append((ahead, back, (1.0 - ahead) - back))
    return out


def second_sweep(parts, factors):
    lane = lax.broadcasted_iota(jnp.int32, (ROWS, LANES), 1)
    tiles = len(parts)
    later = [pltpu.roll(part, LANES - 1, 1) for part in parts]
    sooner = [pltpu.roll(part, 1, 1) for part in parts]
    out = []
    for j in range(tiles):
        following, previous = later[j], sooner[j]
        if j + 1 < tiles:
            following = jnp.where(lane == LANES - 1, later[j + 1], following)
        if j > 0:
            previous = jnp.where(lane == 0, sooner[j - 1], previous)
        ahead, back, own = factors[j]
        out.append(own * parts[j] + ahead * following + back * previous)
    return out


def first_sweep(field, s, j, xt, last, factors, left_row, right_row):
    start = ROWS * (xt + 1)
    sub = lax.broadcasted_iota(jnp.int32, (ROWS, LANES), 0)
    own_value = field(s, j, start)
    following = field(s, j, start + 1)
    previous = field(s, j, start - 1)
    if xt == 0:
        previous = jnp.where(sub == 0, left_row(s, j), previous)
    if xt == last:
        following = jnp.where(sub == ROWS - 1, right_row(s, j), following)
    ahead, back, own = factors
    return own * own_value + ahead * following + back * previous


def turned(source_ref, flag, target_ref):
    tiles, rows, _ = source_ref.shape
    for j in range(tiles):
        for start in range(0, rows, ROWS):
            count = min(ROWS, rows - start)
            index = (LANES - 1) - lax.broadcasted_iota(jnp.int32, (count, LANES), 1)
            straight = source_ref[j, start : start + count, :]
            other = source_ref[tiles - 1 - j, start : start + count, :]
            mirrored = jnp.take_along_axis(other, index, axis=1, mode="promise_in_bounds")
            target_ref[j, start : start + count, :] = jnp.where(flag, mirrored, straight)


def store_padded(ref, index, s, j, xt, value):
    start = ROWS * (xt + 1)
    ref[(*index, s, j, slice(start, start + ROWS), slice(None))] = value


def store_rims(first_ref, last_ref, row, j, xt, last, value):
    if xt == 0:
        first_ref[j, pl.ds(row, 1), :] = value[:1]
    if xt == last:
        last_ref[j, pl.ds(row, 1), :] = value[ROWS - 1 :]


def flags(seam_ref):
    tile = lax.axis_index("tile")
    return seam_ref[0, pl.ds(tile, 1), :] == 1, seam_ref[1, pl.ds(tile, 1), :] == 1


def start_kernel(f_hbm, out_ref, sem):
    copy = pltpu.make_async_copy(f_hbm.at[:, 0], out_ref, sem)
    copy.start()
    copy.wait()


def lower_kernel(
    f_hbm, mf_hbm, cy_hbm, code_hbm, cx_hbm,
    v_ref, first_ref, last_ref, top_ref, mf_ref, cy_ref, code_ref, cx_ref,
    f_ref, sems,
):
    sectors, levels, columns, width = f_hbm.shape
    tiles, strips = width // LANES, columns // ROWS

    def fetch(k):
        return pltpu.make_async_copy(f_hbm.at[:, k], f_ref.at[k], sems.at[0, k])

    def fetch_code(k):
        return pltpu.make_async_copy(code_hbm.at[k], code_ref.at[k], sems.at[1, k])

    def fetch_mf(k):
        return pltpu.make_async_copy(mf_hbm.at[k], mf_ref.at[k], sems.at[2, k])

    def fetch_cy(k):
        return pltpu.make_async_copy(cy_hbm.at[k], cy_ref.at[k], sems.at[3, k])

    fetch_cx = pltpu.make_async_copy(cx_hbm, cx_ref, sems.at[4, 0])
    fetch(0).start()
    for k in range(levels):
        fetch_mf(k).start()
        fetch_cy(k).start()
        fetch_code(k).start()
        if k < levels - 1:
            fetch(k + 1).start()
    fetch_cx.start()
    fetch(0).wait()

    def level(k, _):
        fetch_mf(k).wait()
        fetch_cy(k).wait()
        fetch_code(k).wait()
        fetch(k + 1).wait()
        mf = mf_ref[k].astype(jnp.float32)
        cy = cy_ref[k].astype(jnp.float32)
        codes = code_ref[k]
        for xt in range(strips):
            factors = second_weights(cy, codes, 3, xt, tiles)
            rows = slice(xt * ROWS, (xt + 1) * ROWS)
            for s in range(sectors):
                parts = []
                for j in range(tiles):
                    lanes = slice(j * LANES, (j + 1) * LANES)
                    here = f_ref[k, s, rows, lanes]
                    upper = f_ref[k + 1, s, rows, lanes]
                    parts.append(here + cut(mf, xt, j) * (upper - here))
                for j, value in enumerate(second_sweep(parts, factors)):
                    store_padded(v_ref, (k,), s, j, xt, value)
                    store_rims(first_ref, last_ref, k * sectors + s, j, xt, strips - 1, value)
        return 0

    lax.fori_loop(0, levels - 1, level, 0)
    top_ref[...] = f_ref[levels - 1]
    fetch_mf(levels - 1).wait()
    fetch_cy(levels - 1).wait()
    fetch_code(levels - 1).wait()
    fetch_cx.wait()


def first_weights(cx, codes, bit, xt, j):
    ahead, back = weights(cut(cx, xt, j), cut(codes, xt, j), bit)
    return ahead, back, (1.0 - ahead) - back


def ends_kernel(
    v_ref, inner_ref, left_ref, right_ref, seam_ref, cx_ref, code_ref, here_ref, above_ref,
    mf_ref, cy_ref,
    out_ref, top_ref, first_ref, last_ref,
    lrow_ref, rrow_ref,
):
    _, sectors, tiles, _, _ = v_ref.shape
    columns = out_ref.shape[1]
    strips = columns // ROWS
    flip_left, flip_right = flags(seam_ref)
    turned(left_ref.at[:, :ROWS], flip_left, lrow_ref)
    turned(right_ref.at[:, :ROWS], flip_right, rrow_ref)
    cx = cx_ref[0].astype(jnp.float32)
    codes = code_ref[0]
    for s in range(sectors):
        for j in range(tiles):
            lanes = slice(j * LANES, (j + 1) * LANES)
            out_ref[s, ROWS : columns - ROWS, lanes] = inner_ref[s, j, ROWS : columns - ROWS]
    for xt in (0, strips - 1):
        for j in range(tiles):
            factors = first_weights(cx, codes, 2, xt, j)
            for s in range(sectors):
                value = first_sweep(
                    lambda s, j, start: v_ref[0, s, j, start : start + ROWS, :],
                    s, j, xt, strips - 1, factors,
                    lambda s, j: lrow_ref[j, s : s + 1, :],
                    lambda s, j: rrow_ref[j, s : s + 1, :],
                )
                out_ref[s, xt * ROWS : (xt + 1) * ROWS, j * LANES : (j + 1) * LANES] = value

    level = mf_ref.shape[0] - 1
    at_top = lax.axis_index("lev") == lax.axis_size("lev") - 1
    mf = mf_ref[level].astype(jnp.float32)
    cy = cy_ref[level].astype(jnp.float32)
    codes = code_ref[level]
    for xt in range(strips):
        factors = second_weights(cy, codes, 3, xt, tiles)
        rows = slice(xt * ROWS, (xt + 1) * ROWS)
        for s in range(sectors):
            parts = []
            for j in range(tiles):
                lanes = slice(j * LANES, (j + 1) * LANES)
                here = here_ref[s, rows, lanes]
                upper = jnp.where(at_top, here, above_ref[s, rows, lanes])
                parts.append(here + cut(mf, xt, j) * (upper - here))
            for j, value in enumerate(second_sweep(parts, factors)):
                store_padded(top_ref, (), s, j, xt, value)
                store_rims(first_ref, last_ref, s, j, xt, strips - 1, value)


def middle_levels(
    chosen, v_ref, lrow_ref, rrow_ref, cx_ref, mf_ref, cy_ref, code_ref, out_ref, a_ref, rims=None
):
    below, sectors, tiles, padded, _ = v_ref.shape
    strips = (padded - 2 * ROWS) // ROWS

    def level(k, _):
        cx = cx_ref[k + 1].astype(jnp.float32)
        mf = mf_ref[k].astype(jnp.float32)
        cy = cy_ref[k].astype(jnp.float32)
        codes_x = code_ref[k + 1]
        codes_y = code_ref[k]
        slot = lax.rem(k, 2)
        for xt in chosen:
            along = [first_weights(cx, codes_x, 2, xt, j) for j in range(tiles)]
            across = second_weights(cy, codes_y, 1, xt, tiles)
            rows = slice(xt * ROWS, (xt + 1) * ROWS)
            for s in range(sectors):
                parts = []
                for j in range(tiles):
                    upper = first_sweep(
                        lambda s, j, start: v_ref[k + 1, s, j, start : start + ROWS, :],
                        s, j, xt, strips - 1, along[j],
                        lambda s, j: lrow_ref[j, pl.ds((k + 1) * sectors + s, 1), :],
                        lambda s, j: rrow_ref[j, pl.ds((k + 1) * sectors + s, 1), :],
                    )
                    here = a_ref[slot, s, j, rows, :]
                    a_ref[1 - slot, s, j, rows, :] = upper
                    parts.append(here + cut(mf, xt, j) * (upper - here))
                for j, value in enumerate(second_sweep(parts, across)):
                    store_padded(out_ref, (k,), s, j, xt, value)
                    if rims is not None:
                        store_rims(*rims, k * sectors + s, j, xt, strips - 1, value)
        return 0

    lax.fori_loop(0, below - 1, level, 0)


def inner_middle_kernel(
    v_ref, cx_ref, mf_ref, cy_ref, code_ref, out_ref, lowest_ref, top_ref, a_ref
):
    below, sectors, tiles, padded, _ = v_ref.shape
    strips = (padded - 2 * ROWS) // ROWS
    cx = cx_ref[0].astype(jnp.float32)
    for xt in range(1, strips - 1):
        for j in range(tiles):
            factors = first_weights(cx, code_ref[0], 2, xt, j)
            for s in range(sectors):
                value = first_sweep(
                    lambda s, j, start: v_ref[0, s, j, start : start + ROWS, :],
                    s, j, xt, strips - 1, factors, None, None,
                )
                a_ref[0, s, j, xt * ROWS : (xt + 1) * ROWS, :] = value
                lowest_ref[s, j, xt * ROWS : (xt + 1) * ROWS, :] = value
    middle_levels(
        range(1, strips - 1), v_ref, None, None, cx_ref, mf_ref, cy_ref, code_ref, out_ref, a_ref
    )
    inner = slice(ROWS, (strips - 1) * ROWS)
    top_ref[:, :, inner] = a_ref[(below - 1) % 2, :, :, inner]


def outer_middle_kernel(
    v_ref, inner_ref, inner_top_ref, left_ref, right_ref, lowest_ref, seam_ref,
    cx_ref, mf_ref, cy_ref, code_ref,
    out_ref, first_ref, last_ref, top_ref,
    lrow_ref, rrow_ref, a_ref,
):
    below, sectors, tiles, padded, _ = v_ref.shape
    strips = (padded - 2 * ROWS) // ROWS
    ends = (0, strips - 1)
    flip_left, flip_right = flags(seam_ref)
    turned(left_ref, flip_left, lrow_ref)
    turned(right_ref, flip_right, rrow_ref)
    for s in range(sectors):
        for j in range(tiles):
            for xt in ends:
                rows = slice(xt * ROWS, (xt + 1) * ROWS)
                a_ref[0, s, j, rows] = lowest_ref[s, rows, j * LANES : (j + 1) * LANES]
    middle_levels(
        ends, v_ref, lrow_ref, rrow_ref, cx_ref, mf_ref, cy_ref, code_ref, out_ref, a_ref,
        (first_ref, last_ref),
    )
    for xt in ends:
        rows = slice(xt * ROWS, (xt + 1) * ROWS)
        top_ref[:, :, rows] = a_ref[(below - 1) % 2, :, :, rows]
    inner = slice(ROWS, (strips - 1) * ROWS)
    top_ref[:, :, inner] = inner_top_ref[:, :, inner]
    inner = slice(2 * ROWS, strips * ROWS)

    def copy(k, _):
        out_ref[k, :, :, inner] = inner_ref[k, :, :, inner]
        return 0

    lax.fori_loop(0, below - 1, copy, 0)


def second_last_kernel(
    vt_ref, left_ref, right_ref, lower_ref, first_in, last_in, seam_ref, cx_ref, mf_ref, cy_ref, code_ref,
    out_ref, first_ref, last_ref, top_ref,
    lrow_ref, rrow_ref,
):
    sectors, tiles, padded, _ = vt_ref.shape
    strips = (padded - 2 * ROWS) // ROWS
    top = mf_ref.shape[0] - 1
    done = first_in.shape[1]
    flip_left, flip_right = flags(seam_ref)
    turned(left_ref, flip_left, lrow_ref)
    turned(right_ref, flip_right, rrow_ref)
    first_ref[:, :done] = first_in[...]
    last_ref[:, :done] = last_in[...]
    cx = cx_ref[top].astype(jnp.float32)
    mf = mf_ref[top - 1].astype(jnp.float32)
    cy = cy_ref[top - 1].astype(jnp.float32)
    for xt in range(strips):
        along = [first_weights(cx, code_ref[top], 2, xt, j) for j in range(tiles)]
        across = second_weights(cy, code_ref[top - 1], 1, xt, tiles)
        rows = slice(xt * ROWS, (xt + 1) * ROWS)
        for s in range(sectors):
            parts = []
            for j in range(tiles):
                upper = first_sweep(
                    lambda s, j, start: vt_ref[s, j, start : start + ROWS, :],
                    s, j, xt, strips - 1, along[j],
                    lambda s, j: lrow_ref[j, s : s + 1, :],
                    lambda s, j: rrow_ref[j, s : s + 1, :],
                )
                top_ref[s, j, rows, :] = upper
                here = lower_ref[s, j, rows, :]
                parts.append(here + cut(mf, xt, j) * (upper - here))
            for j, value in enumerate(second_sweep(parts, across)):
                store_padded(out_ref, (), s, j, xt, value)
                store_rims(first_ref, last_ref, done + s, j, xt, strips - 1, value)


def highest_kernel(here_ref, above_ref, mf_ref, cy_ref, code_ref, out_ref, first_ref, last_ref):
    sectors, tiles, columns, _ = here_ref.shape
    strips = columns // ROWS
    top = mf_ref.shape[0] - 1
    at_top = lax.axis_index("lev") == lax.axis_size("lev") - 1
    mf = mf_ref[top].astype(jnp.float32)
    cy = cy_ref[top].astype(jnp.float32)
    for xt in range(strips):
        across = second_weights(cy, code_ref[top], 1, xt, tiles)
        rows = slice(xt * ROWS, (xt + 1) * ROWS)
        for s in range(sectors):
            parts = []
            for j in range(tiles):
                here = here_ref[s, j, rows, :]
                upper = above_ref[s, rows, j * LANES : (j + 1) * LANES]
                upper = jnp.where(at_top, here, upper)
                parts.append(here + cut(mf, xt, j) * (upper - here))
            for j, value in enumerate(second_sweep(parts, across)):
                store_padded(out_ref, (), s, j, xt, value)
                store_rims(first_ref, last_ref, s, j, xt, strips - 1, value)


def final_level(
    k, chosen, strips, field, left_row, right_row, refs, out_ref, sens_ref, start_sum
):
    cx_ref, code_ref, weight_ref, share_ref = refs
    sectors, _, width = share_ref.shape
    cx = cx_ref[k].astype(jnp.float32)
    codes = code_ref[k]
    factor = weight_ref[pl.ds(k, 1), :]
    for xt in chosen:
        rows = slice(xt * ROWS, (xt + 1) * ROWS)
        for j in range(width // LANES):
            lanes = slice(j * LANES, (j + 1) * LANES)
            factors = first_weights(cx, codes, 0, xt, j)
            total = 0.0
            for s in range(sectors):
                value = first_sweep(field, s, j, xt, strips - 1, factors, left_row, right_row)
                out_ref[k, s, rows, lanes] = value
                total = total + share_ref[s, rows, lanes] * value
            if start_sum:
                sens_ref[rows, lanes] = factor * total
            else:
                sens_ref[rows, lanes] += factor * total


def inner_final_kernel(
    v_ref, vs_ref, cx_ref, code_ref, weight_ref, share_ref, out_hbm, sens_ref, out_ref, sems
):
    below, _, _, padded, _ = v_ref.shape
    strips = (padded - 2 * ROWS) // ROWS
    refs = (cx_ref, code_ref, weight_ref, share_ref)
    inner = pl.ds(ROWS, (strips - 2) * ROWS)

    def send(k):
        return pltpu.make_async_copy(out_ref.at[k, :, inner], out_hbm.at[:, k, inner], sems.at[k])

    final_level(
        below, range(1, strips - 1), strips,
        lambda s, j, start: vs_ref[s, j, start : start + ROWS, :],
        None, None, refs, out_ref, sens_ref, True,
    )
    send(below).start()

    def step(k, _):
        final_level(
            k, range(1, strips - 1), strips,
            lambda s, j, start: v_ref[k, s, j, start : start + ROWS, :],
            None, None, refs, out_ref, sens_ref, False,
        )
        send(k).start()
        return 0

    lax.fori_loop(0, below, step, 0)
    for k in range(below + 1):
        send(k).wait()


def outer_final_kernel(
    v_ref, vs_ref, vt_ref, left_ref, right_ref, left_top_ref, right_top_ref, seam_ref,
    cx_ref, code_ref, weight_ref, share_ref, inner_ref, done_hbm,
    out_hbm, piece_ref,
    lrow_ref, rrow_ref, ltop_ref, rtop_ref, out_ref, sens_ref, flat_ref, sems,
):
    below, sectors, tiles, padded, _ = v_ref.shape
    strips = (padded - 2 * ROWS) // ROWS
    ends = (0, strips - 1)
    refs = (cx_ref, code_ref, weight_ref, share_ref)
    flip_left, flip_right = flags(seam_ref)
    turned(left_ref, flip_left, lrow_ref)
    turned(right_ref, flip_right, rrow_ref)
    turned(left_top_ref, flip_left, ltop_ref)
    turned(right_top_ref, flip_right, rtop_ref)

    def send(k, i):
        rows = pl.ds(ends[i] * ROWS, ROWS)
        return pltpu.make_async_copy(out_ref.at[k, :, rows], out_hbm.at[:, k, rows], sems.at[i, k])

    send_top = pltpu.make_async_copy(
        out_ref.at[below + 1], out_hbm.at[:, below + 1], sems.at[0, below + 1]
    )
    final_level(
        below + 1, range(strips), strips,
        lambda s, j, start: vt_ref[s, j, start : start + ROWS, :],
        lambda s, j: ltop_ref[j, s : s + 1, :],
        lambda s, j: rtop_ref[j, s : s + 1, :],
        refs, out_ref, sens_ref, True,
    )
    send_top.start()
    final_level(
        below, ends, strips,
        lambda s, j, start: vs_ref[s, j, start : start + ROWS, :],
        lambda s, j: lrow_ref[j, below * sectors + s : below * sectors + s + 1, :],
        lambda s, j: rrow_ref[j, below * sectors + s : below * sectors + s + 1, :],
        refs, out_ref, sens_ref, False,
    )
    for i in range(2):
        send(below, i).start()

    def step(k, _):
        final_level(
            k, ends, strips,
            lambda s, j, start: v_ref[k, s, j, start : start + ROWS, :],
            lambda s, j: lrow_ref[j, pl.ds(k * sectors + s, 1), :],
            lambda s, j: rrow_ref[j, pl.ds(k * sectors + s, 1), :],
            refs, out_ref, sens_ref, False,
        )
        for i in range(2):
            send(k, i).start()
        return 0

    lax.fori_loop(0, below, step, 0)
    inner = slice(ROWS, (strips - 1) * ROWS)
    sens_ref[inner] += inner_ref[inner]
    if len(piece_ref.shape) == 2:
        piece_ref[...] = sens_ref[...]
    else:
        owners, group, copies, depth, _ = piece_ref.shape
        share = strips * ROWS * tiles // owners
        for xt in range(strips):
            for j in range(tiles):
                value = sens_ref[xt * ROWS : (xt + 1) * ROWS, j * LANES : (j + 1) * LANES]
                flat_ref[pl.ds(xt * ROWS * tiles + j, ROWS, stride=tiles), :] = value
        for o in range(owners):
            for piece in range(group):
                start = piece * depth
                used = max(0, min(depth, share - start))
                value = jnp.zeros((depth, LANES), jnp.float32)
                if used:
                    start += o * share
                    value = flat_ref[start : start + depth, :]
                    if used < depth:
                        line = lax.broadcasted_iota(jnp.int32, (depth, LANES), 0)
                        value = jnp.where(line < used, value, 0.0)
                for i in range(copies):
                    piece_ref[o, piece, i] = value
    send_top.wait()
    for k in range(below + 1):
        for i in range(2):
            send(k, i).wait()


def scatter_kernel(cells_ref, *refs):
    *value_refs, out_ref = refs
    rows, lanes = out_ref.shape
    group, owners, depth, _ = cells_ref.shape
    rank = lax.axis_index("lev")
    high_iota = lax.broadcasted_iota(jnp.int32, (rows, lanes), 0)
    low_iota = lax.broadcasted_iota(jnp.int32, (lanes, lanes), 0)
    total = jnp.zeros((2 * rows, lanes), jnp.float32)
    lines = [(i, o, r) for i in range(group) for o in range(owners) for r in range(depth)]
    for pair in range(0, len(lines), 2):
        lefts, rights = [], []
        for part, owner, line in lines[pair : pair + 2]:
            cells = cells_ref[jnp.bitwise_xor(rank, part), owner, line : line + 1, :]
            value = value_refs[part][owner, line : line + 1, :]
            coarse = value.astype(jnp.bfloat16).astype(jnp.float32)
            fine = value - coarse
            here = jnp.right_shift(cells, 7) == high_iota
            lefts.append(
                jnp.concatenate(
                    [jnp.where(here, coarse, 0.0), jnp.where(here, fine, 0.0)], axis=0
                ).astype(jnp.bfloat16)
            )
            match = jnp.bitwise_and(cells, 127) == low_iota
            rights.append(jnp.where(match, 1.0, 0.0).astype(jnp.bfloat16))
        total += lax.dot_general(
            jnp.concatenate(lefts, axis=1),
            jnp.concatenate(rights, axis=1),
            (((1,), (1,)), ((), ())),
            preferred_element_type=jnp.float32,
        )
    out_ref[...] = total[:rows] + total[rows:]


def exchanged(value, axis, apart):
    count = lax.axis_size(axis)
    return lax.ppermute(value, axis, [(i, i ^ apart) for i in range(count)])


def remapped(pieces, flux_cell):
    owners, share = flux_cell.shape
    _, group, copies, depth, _ = pieces.shape
    sent = pieces.reshape(-1, depth, LANES)
    arrived = lax.all_to_all(
        sent, ("tile", "lev", "sec"), split_axis=0, concat_axis=0, tiled=True
    )
    own = jnp.sum(arrived.reshape(owners, group * copies, depth, LANES), axis=1)
    parts = [own] + [exchanged(own, "lev", d) for d in range(1, group)]
    cells = jnp.pad(flux_cell, ((0, 0), (0, group * depth * LANES - share)))
    cells = cells.reshape(owners, group, depth, LANES).transpose(1, 0, 2, 3)
    out = call(
        scatter_kernel, f32(FL_DEV // LANES, LANES), [VM] * (group + 1), VM, (cells, *parts)
    )
    return out.reshape(-1)


def around(first, last):
    count = lax.axis_size("tile")
    up = [(i, (i + 1) % count) for i in range(count)]
    down = [(j, i) for i, j in up]
    return lax.ppermute(last, "tile", up), lax.ppermute(first, "tile", down)


def from_above(value):
    count = lax.axis_size("lev")
    return lax.ppermute(value, "lev", [(i + 1, i) for i in range(count - 1)])


def shards(
    forcing, courant_x, courant_y, mass_flux, limiter_code, seam_code, level_weight, sector_share, flux_cell
):
    sectors, levels, columns, width = forcing.shape
    tiles, below = width // LANES, levels - 1
    padded = columns + 2 * ROWS
    field = kept(below, sectors, tiles, padded, LANES)
    field_top = kept(sectors, tiles, padded, LANES)
    plane = kept(sectors, columns, width)
    rim = kept(tiles, below * sectors, LANES)
    rim_top = kept(tiles, sectors, LANES)
    rim_next = kept(tiles, (below - 1) * sectors, LANES)
    rim_scratch = pltpu.VMEM((tiles, below * sectors, LANES), jnp.float32)

    seam = jnp.broadcast_to(seam_code.T[:, :, None], (*seam_code.T.shape, LANES))
    weight = jnp.broadcast_to(level_weight[:, None], (levels, LANES))

    above = from_above(
        call(start_kernel, plane, [HBM], VM, in_hbm(forcing), [pltpu.SemaphoreType.DMA])
    )
    narrow = pltpu.VMEM((levels, columns, width), jnp.bfloat16)
    v, first, last, top, mass_flux, courant_y, limiter_code, courant_x = call(
        lower_kernel,
        (
            field, rim, rim, plane,
            narrow, narrow, pltpu.VMEM((levels, columns, width), jnp.int32), narrow,
        ),
        [HBM] * 5,
        [VM] * 8,
        in_hbm(forcing, mass_flux, courant_y, limiter_code, courant_x),
        [
            pltpu.VMEM((levels, sectors, columns, width), jnp.float32),
            pltpu.SemaphoreType.DMA((5, levels)),
        ],
    )
    left, right = around(first, last)
    lines = kept(sectors, tiles, columns, LANES)
    inner_field = kept(below - 1, sectors, tiles, padded, LANES)
    a_scratch = pltpu.VMEM((2, sectors, tiles, columns, LANES), jnp.float32)
    inner, inner_lowest, inner_top = call(
        inner_middle_kernel,
        (inner_field, lines, lines),
        [VM] * 5,
        [VM] * 3,
        (v, courant_x, mass_flux, courant_y, limiter_code),
        [a_scratch],
    )
    lowest, vt, first_top, last_top = call(
        ends_kernel,
        (plane, field_top, rim_top, rim_top),
        [VM] * 11,
        [VM] * 4,
        (
            v, inner_lowest, left, right, seam, courant_x, limiter_code, top, above,
            mass_flux, courant_y,
        ),
        [pltpu.VMEM((tiles, ROWS, LANES), jnp.float32)] * 2,
    )
    above = from_above(lowest)
    left_top, right_top = around(first_top, last_top)

    v, first, last, top = call(
        outer_middle_kernel,
        (inner_field, rim_next, rim_next, lines),
        [VM] * 11,
        [VM] * 4,
        (
            v, inner, inner_top, left, right, lowest, seam,
            courant_x, mass_flux, courant_y, limiter_code,
        ),
        [rim_scratch, rim_scratch, a_scratch],
    )
    vs, first, last, top = call(
        second_last_kernel,
        (field_top, rim, rim, kept(sectors, tiles, columns, LANES)),
        [VM] * 11,
        [VM] * 4,
        (
            vt, left_top, right_top, top, first, last, seam,
            courant_x, mass_flux, courant_y, limiter_code,
        ),
        [pltpu.VMEM((tiles, sectors, LANES), jnp.float32)] * 2,
    )
    left, right = around(first, last)
    vt, first_top, last_top = call(
        highest_kernel,
        (field_top, rim_top, rim_top),
        [VM] * 5,
        [VM] * 3,
        (top, above, mass_flux, courant_y, limiter_code),
    )
    left_top, right_top = around(first_top, last_top)

    owners, share = flux_cell.shape
    group, copies = lax.axis_size("lev"), lax.axis_size("sec")
    depth = -(-share // (group * LANES))
    aligned = share % LANES == 0
    packed = (owners, group, copies, depth, LANES)
    stage = pltpu.VMEM((levels, sectors, columns, width), jnp.float32)
    adjoint, inner = call(
        inner_final_kernel,
        (f32(*forcing.shape), kept(columns, width)),
        [VM] * 6,
        [HBM, VM],
        (v, vs, courant_x, limiter_code, weight, sector_share),
        [stage, pltpu.SemaphoreType.DMA((levels,))],
    )
    adjoint, pieces = call(
        outer_final_kernel,
        (f32(*forcing.shape), f32(*packed) if aligned else f32(columns, width)),
        [VM] * 13 + [HBM],
        [HBM, VM],
        (
            v, vs, vt, left, right, left_top, right_top, seam,
            courant_x, limiter_code, weight, sector_share, inner, adjoint,
        ),
        [
            rim_scratch, rim_scratch,
            pltpu.VMEM((tiles, sectors, LANES), jnp.float32),
            pltpu.VMEM((tiles, sectors, LANES), jnp.float32),
            stage,
            pltpu.VMEM((columns, width), jnp.float32),
            pltpu.VMEM((columns * tiles + ROWS, LANES), jnp.float32),
            pltpu.SemaphoreType.DMA((2, levels)),
        ],
        aliases={13: 0},
    )
    if not aligned:
        pieces = jnp.pad(
            pieces.reshape(owners, share), ((0, 0), (0, group * depth * LANES - share))
        ).reshape(owners, group, 1, depth, LANES)
        pieces = jnp.broadcast_to(pieces, packed)
    flux_cell, pieces = lax.optimization_barrier((flux_cell, pieces))
    return (adjoint, remapped(pieces, flux_cell))


def solution(mesh):
    placed = (
        P("sec", "lev", "tile", None),
        P("lev", "tile", None),
        P("lev", "tile", None),
        P("lev", "tile", None),
        P("lev", "tile", None),
        P(),
        P("lev"),
        P("sec", "tile", None),
        P("tile", None),
    )
    return jax.shard_map(
        shards,
        mesh=mesh,
        in_specs=placed,
        out_specs=(P("sec", "lev", "tile", None), P("tile")),
        check_vma=False,
    )
```

```python
import functools

import jax
import jax.numpy as jnp
from jax import lax
from jax.experimental import pallas as pl
from jax.experimental.pallas import tpu as pltpu
from jax.sharding import PartitionSpec as P

FL_DEV = 15360
LANES = 128
ROWS = 8
MIB = 2**20
VM = pl.BlockSpec(memory_space=pltpu.VMEM)
HBM = pl.BlockSpec(memory_space=pltpu.HBM)


def call(kernel, out_shape, in_specs, out_specs, operands, scratch=(), mib=16, aliases={}):
    return pl.pallas_call(
        kernel,
        out_shape=out_shape,
        in_specs=in_specs,
        out_specs=out_specs,
        scratch_shapes=list(scratch),
        input_output_aliases=aliases,
        cost_estimate=pl.CostEstimate(flops=1, transcendentals=0, bytes_accessed=1),
        compiler_params=pltpu.CompilerParams(vmem_limit_bytes=mib * MIB),
    )(*operands)


def in_hbm(*arrays):
    return tuple(pltpu.with_memory_space_constraint(a, pltpu.HBM) for a in arrays)


def kept(*shape):
    return pltpu.VMEM(shape, jnp.float32)


def f32(*shape):
    return jax.ShapeDtypeStruct(shape, jnp.float32)


def cut(value, xt, j):
    return value[xt * ROWS : (xt + 1) * ROWS, j * LANES : (j + 1) * LANES]


def weights(courant, codes, bit):
    size = jnp.abs(courant)
    half = (0.5 * size) * (1.0 - size)
    limited = jnp.where(jnp.bitwise_and(codes, 1 << bit) != 0, half, 0.0)
    ahead = jnp.maximum(courant, 0.0) - limited
    back = jnp.maximum(-courant, 0.0) - limited
    return ahead, back


def second_weights(cy, codes, bit, xt, tiles):
    lane = lax.broadcasted_iota(jnp.int32, (ROWS, LANES), 1)
    out = []
    for j in range(tiles):
        ahead, back = weights(cut(cy, xt, j), cut(codes, xt, j), bit)
        if j == 0:
            back = jnp.where(lane == 0, 0.0, back)
        if j == tiles - 1:
            ahead = jnp.where(lane == LANES - 1, 0.0, ahead)
        out.append((ahead, back, (1.0 - ahead) - back))
    return out


def second_sweep(parts, factors):
    lane = lax.broadcasted_iota(jnp.int32, (ROWS, LANES), 1)
    tiles = len(parts)
    later = [pltpu.roll(part, LANES - 1, 1) for part in parts]
    sooner = [pltpu.roll(part, 1, 1) for part in parts]
    out = []
    for j in range(tiles):
        following, previous = later[j], sooner[j]
        if j + 1 < tiles:
            following = jnp.where(lane == LANES - 1, later[j + 1], following)
        if j > 0:
            previous = jnp.where(lane == 0, sooner[j - 1], previous)
        ahead, back, own = factors[j]
        out.append(own * parts[j] + ahead * following + back * previous)
    return out


def first_sweep(field, s, j, xt, last, factors, left_row, right_row):
    start = ROWS * (xt + 1)
    sub = lax.broadcasted_iota(jnp.int32, (ROWS, LANES), 0)
    own_value = field(s, j, start)
    following = field(s, j, start + 1)
    previous = field(s, j, start - 1)
    if xt == 0:
        previous = jnp.where(sub == 0, left_row(s, j), previous)
    if xt == last:
        following = jnp.where(sub == ROWS - 1, right_row(s, j), following)
    ahead, back, own = factors
    return own * own_value + ahead * following + back * previous


def turned(source_ref, flag, target_ref):
    tiles, rows, _ = source_ref.shape
    for j in range(tiles):
        for start in range(0, rows, ROWS):
            count = min(ROWS, rows - start)
            index = (LANES - 1) - lax.broadcasted_iota(jnp.int32, (count, LANES), 1)
            straight = source_ref[j, start : start + count, :]
            other = source_ref[tiles - 1 - j, start : start + count, :]
            mirrored = jnp.take_along_axis(other, index, axis=1, mode="promise_in_bounds")
            target_ref[j, start : start + count, :] = jnp.where(flag, mirrored, straight)


def store_padded(ref, index, s, j, xt, value):
    start = ROWS * (xt + 1)
    ref[(*index, s, j, slice(start, start + ROWS), slice(None))] = value


def store_rims(first_ref, last_ref, row, j, xt, last, value):
    if xt == 0:
        first_ref[j, pl.ds(row, 1), :] = value[:1]
    if xt == last:
        last_ref[j, pl.ds(row, 1), :] = value[ROWS - 1 :]


def flags(seam_ref):
    tile = lax.axis_index("tile")
    return seam_ref[0, pl.ds(tile, 1), :] == 1, seam_ref[1, pl.ds(tile, 1), :] == 1


def start_kernel(f_hbm, out_ref, sem):
    copy = pltpu.make_async_copy(f_hbm.at[:, 0], out_ref, sem)
    copy.start()
    copy.wait()


def lower_kernel(
    f_ref, mf_hbm, cy_hbm, code_hbm, cx_hbm,
    v_ref, first_ref, last_ref, top_ref, mf_ref, cy_ref, code_ref, cx_ref,
    sems,
):
    sectors, levels, columns, width = f_ref.shape
    tiles, strips = width // LANES, columns // ROWS

    def fetch_code(k):
        return pltpu.make_async_copy(code_hbm.at[k], code_ref.at[k], sems.at[1, k])

    def fetch_mf(k):
        return pltpu.make_async_copy(mf_hbm.at[k], mf_ref.at[k], sems.at[2, k])

    def fetch_cy(k):
        return pltpu.make_async_copy(cy_hbm.at[k], cy_ref.at[k], sems.at[3, k])

    fetch_cx = pltpu.make_async_copy(cx_hbm, cx_ref, sems.at[4, 0])
    for k in range(levels):
        fetch_mf(k).start()
        fetch_cy(k).start()
        fetch_code(k).start()
    fetch_cx.start()

    def level(k, _):
        fetch_mf(k).wait()
        fetch_cy(k).wait()
        fetch_code(k).wait()
        mf = mf_ref[k].astype(jnp.float32)
        cy = cy_ref[k].astype(jnp.float32)
        codes = code_ref[k]
        for xt in range(strips):
            factors = second_weights(cy, codes, 3, xt, tiles)
            rows = slice(xt * ROWS, (xt + 1) * ROWS)
            for s in range(sectors):
                parts = []
                for j in range(tiles):
                    lanes = slice(j * LANES, (j + 1) * LANES)
                    here = f_ref[s, k, rows, lanes]
                    upper = f_ref[s, k + 1, rows, lanes]
                    parts.append(here + cut(mf, xt, j) * (upper - here))
                for j, value in enumerate(second_sweep(parts, factors)):
                    store_padded(v_ref, (k,), s, j, xt, value)
                    store_rims(first_ref, last_ref, k * sectors + s, j, xt, strips - 1, value)
        return 0

    lax.fori_loop(0, levels - 1, level, 0)
    top_ref[...] = f_ref[:, levels - 1]
    fetch_mf(levels - 1).wait()
    fetch_cy(levels - 1).wait()
    fetch_code(levels - 1).wait()
    fetch_cx.wait()


def first_weights(cx, codes, bit, xt, j):
    ahead, back = weights(cut(cx, xt, j), cut(codes, xt, j), bit)
    return ahead, back, (1.0 - ahead) - back


def ends_kernel(
    v_ref, inner_ref, left_ref, right_ref, seam_ref, cx_ref, code_ref, here_ref, above_ref,
    mf_ref, cy_ref,
    out_ref, top_ref, first_ref, last_ref,
    lrow_ref, rrow_ref,
):
    _, sectors, tiles, _, _ = v_ref.shape
    columns = out_ref.shape[1]
    strips = columns // ROWS
    flip_left, flip_right = flags(seam_ref)
    turned(left_ref.at[:, :ROWS], flip_left, lrow_ref)
    turned(right_ref.at[:, :ROWS], flip_right, rrow_ref)
    cx = cx_ref[0].astype(jnp.float32)
    codes = code_ref[0]
    for s in range(sectors):
        for j in range(tiles):
            lanes = slice(j * LANES, (j + 1) * LANES)
            out_ref[s, ROWS : columns - ROWS, lanes] = inner_ref[s, j, ROWS : columns - ROWS]
    for xt in (0, strips - 1):
        for j in range(tiles):
            factors = first_weights(cx, codes, 2, xt, j)
            for s in range(sectors):
                value = first_sweep(
                    lambda s, j, start: v_ref[0, s, j, start : start + ROWS, :],
                    s, j, xt, strips - 1, factors,
                    lambda s, j: lrow_ref[j, s : s + 1, :],
                    lambda s, j: rrow_ref[j, s : s + 1, :],
                )
                out_ref[s, xt * ROWS : (xt + 1) * ROWS, j * LANES : (j + 1) * LANES] = value

    level = mf_ref.shape[0] - 1
    at_top = lax.axis_index("lev") == lax.axis_size("lev") - 1
    mf = mf_ref[level].astype(jnp.float32)
    cy = cy_ref[level].astype(jnp.float32)
    codes = code_ref[level]
    for xt in range(strips):
        factors = second_weights(cy, codes, 3, xt, tiles)
        rows = slice(xt * ROWS, (xt + 1) * ROWS)
        for s in range(sectors):
            parts = []
            for j in range(tiles):
                lanes = slice(j * LANES, (j + 1) * LANES)
                here = here_ref[s, rows, lanes]
                upper = jnp.where(at_top, here, above_ref[s, rows, lanes])
                parts.append(here + cut(mf, xt, j) * (upper - here))
            for j, value in enumerate(second_sweep(parts, factors)):
                store_padded(top_ref, (), s, j, xt, value)
                store_rims(first_ref, last_ref, s, j, xt, strips - 1, value)


def middle_levels(
    chosen, v_ref, lrow_ref, rrow_ref, cx_ref, mf_ref, cy_ref, code_ref, out_ref, a_ref, rims=None
):
    below, sectors, tiles, padded, _ = v_ref.shape
    strips = (padded - 2 * ROWS) // ROWS

    def level(k, _):
        cx = cx_ref[k + 1].astype(jnp.float32)
        mf = mf_ref[k].astype(jnp.float32)
        cy = cy_ref[k].astype(jnp.float32)
        codes_x = code_ref[k + 1]
        codes_y = code_ref[k]
        slot = lax.rem(k, 2)
        for xt in chosen:
            along = [first_weights(cx, codes_x, 2, xt, j) for j in range(tiles)]
            across = second_weights(cy, codes_y, 1, xt, tiles)
            rows = slice(xt * ROWS, (xt + 1) * ROWS)
            for s in range(sectors):
                parts = []
                for j in range(tiles):
                    upper = first_sweep(
                        lambda s, j, start: v_ref[k + 1, s, j, start : start + ROWS, :],
                        s, j, xt, strips - 1, along[j],
                        lambda s, j: lrow_ref[j, pl.ds((k + 1) * sectors + s, 1), :],
                        lambda s, j: rrow_ref[j, pl.ds((k + 1) * sectors + s, 1), :],
                    )
                    here = a_ref[slot, s, j, rows, :]
                    a_ref[1 - slot, s, j, rows, :] = upper
                    parts.append(here + cut(mf, xt, j) * (upper - here))
                for j, value in enumerate(second_sweep(parts, across)):
                    store_padded(out_ref, (k,), s, j, xt, value)
                    if rims is not None:
                        store_rims(*rims, k * sectors + s, j, xt, strips - 1, value)
        return 0

    lax.fori_loop(0, below - 1, level, 0)


def inner_middle_kernel(
    v_ref, cx_ref, mf_ref, cy_ref, code_ref, out_ref, lowest_ref, top_ref, a_ref
):
    below, sectors, tiles, padded, _ = v_ref.shape
    strips = (padded - 2 * ROWS) // ROWS
    cx = cx_ref[0].astype(jnp.float32)
    for xt in range(1, strips - 1):
        for j in range(tiles):
            factors = first_weights(cx, code_ref[0], 2, xt, j)
            for s in range(sectors):
                value = first_sweep(
                    lambda s, j, start: v_ref[0, s, j, start : start + ROWS, :],
                    s, j, xt, strips - 1, factors, None, None,
                )
                a_ref[0, s, j, xt * ROWS : (xt + 1) * ROWS, :] = value
                lowest_ref[s, j, xt * ROWS : (xt + 1) * ROWS, :] = value
    middle_levels(
        range(1, strips - 1), v_ref, None, None, cx_ref, mf_ref, cy_ref, code_ref, out_ref, a_ref
    )
    inner = slice(ROWS, (strips - 1) * ROWS)
    top_ref[:, :, inner] = a_ref[(below - 1) % 2, :, :, inner]


def outer_middle_kernel(
    v_ref, inner_ref, inner_top_ref, left_ref, right_ref, lowest_ref, seam_ref,
    cx_ref, mf_ref, cy_ref, code_ref,
    out_ref, first_ref, last_ref, top_ref,
    lrow_ref, rrow_ref, a_ref,
):
    below, sectors, tiles, padded, _ = v_ref.shape
    strips = (padded - 2 * ROWS) // ROWS
    ends = (0, strips - 1)
    flip_left, flip_right = flags(seam_ref)
    turned(left_ref, flip_left, lrow_ref)
    turned(right_ref, flip_right, rrow_ref)
    for s in range(sectors):
        for j in range(tiles):
            for xt in ends:
                rows = slice(xt * ROWS, (xt + 1) * ROWS)
                a_ref[0, s, j, rows] = lowest_ref[s, rows, j * LANES : (j + 1) * LANES]
    middle_levels(
        ends, v_ref, lrow_ref, rrow_ref, cx_ref, mf_ref, cy_ref, code_ref, out_ref, a_ref,
        (first_ref, last_ref),
    )
    for xt in ends:
        rows = slice(xt * ROWS, (xt + 1) * ROWS)
        top_ref[:, :, rows] = a_ref[(below - 1) % 2, :, :, rows]
    inner = slice(ROWS, (strips - 1) * ROWS)
    top_ref[:, :, inner] = inner_top_ref[:, :, inner]
    inner = slice(2 * ROWS, strips * ROWS)

    def copy(k, _):
        out_ref[k, :, :, inner] = inner_ref[k, :, :, inner]
        return 0

    lax.fori_loop(0, below - 1, copy, 0)


def second_last_kernel(
    vt_ref, left_ref, right_ref, lower_ref, first_in, last_in, seam_ref, cx_ref, mf_ref, cy_ref, code_ref,
    out_ref, first_ref, last_ref, top_ref,
    lrow_ref, rrow_ref,
):
    sectors, tiles, padded, _ = vt_ref.shape
    strips = (padded - 2 * ROWS) // ROWS
    top = mf_ref.shape[0] - 1
    done = first_in.shape[1]
    flip_left, flip_right = flags(seam_ref)
    turned(left_ref, flip_left, lrow_ref)
    turned(right_ref, flip_right, rrow_ref)
    first_ref[:, :done] = first_in[...]
    last_ref[:, :done] = last_in[...]
    cx = cx_ref[top].astype(jnp.float32)
    mf = mf_ref[top - 1].astype(jnp.float32)
    cy = cy_ref[top - 1].astype(jnp.float32)
    for xt in range(strips):
        along = [first_weights(cx, code_ref[top], 2, xt, j) for j in range(tiles)]
        across = second_weights(cy, code_ref[top - 1], 1, xt, tiles)
        rows = slice(xt * ROWS, (xt + 1) * ROWS)
        for s in range(sectors):
            parts = []
            for j in range(tiles):
                upper = first_sweep(
                    lambda s, j, start: vt_ref[s, j, start : start + ROWS, :],
                    s, j, xt, strips - 1, along[j],
                    lambda s, j: lrow_ref[j, s : s + 1, :],
                    lambda s, j: rrow_ref[j, s : s + 1, :],
                )
                top_ref[s, j, rows, :] = upper
                here = lower_ref[s, j, rows, :]
                parts.append(here + cut(mf, xt, j) * (upper - here))
            for j, value in enumerate(second_sweep(parts, across)):
                store_padded(out_ref, (), s, j, xt, value)
                store_rims(first_ref, last_ref, done + s, j, xt, strips - 1, value)


def highest_kernel(here_ref, above_ref, mf_ref, cy_ref, code_ref, out_ref, first_ref, last_ref):
    sectors, tiles, columns, _ = here_ref.shape
    strips = columns // ROWS
    top = mf_ref.shape[0] - 1
    at_top = lax.axis_index("lev") == lax.axis_size("lev") - 1
    mf = mf_ref[top].astype(jnp.float32)
    cy = cy_ref[top].astype(jnp.float32)
    for xt in range(strips):
        across = second_weights(cy, code_ref[top], 1, xt, tiles)
        rows = slice(xt * ROWS, (xt + 1) * ROWS)
        for s in range(sectors):
            parts = []
            for j in range(tiles):
                here = here_ref[s, j, rows, :]
                upper = above_ref[s, rows, j * LANES : (j + 1) * LANES]
                upper = jnp.where(at_top, here, upper)
                parts.append(here + cut(mf, xt, j) * (upper - here))
            for j, value in enumerate(second_sweep(parts, across)):
                store_padded(out_ref, (), s, j, xt, value)
                store_rims(first_ref, last_ref, s, j, xt, strips - 1, value)


def final_level(
    k, chosen, strips, field, left_row, right_row, refs, out_ref, sens_ref, start_sum
):
    cx_ref, code_ref, weight_ref, share_ref = refs
    sectors, _, width = share_ref.shape
    cx = cx_ref[k].astype(jnp.float32)
    codes = code_ref[k]
    factor = weight_ref[pl.ds(k, 1), :]
    for xt in chosen:
        rows = slice(xt * ROWS, (xt + 1) * ROWS)
        for j in range(width // LANES):
            lanes = slice(j * LANES, (j + 1) * LANES)
            factors = first_weights(cx, codes, 0, xt, j)
            total = 0.0
            for s in range(sectors):
                value = first_sweep(field, s, j, xt, strips - 1, factors, left_row, right_row)
                out_ref[k, s, rows, lanes] = value
                total = total + share_ref[s, rows, lanes] * value
            if start_sum:
                sens_ref[rows, lanes] = factor * total
            else:
                sens_ref[rows, lanes] += factor * total


def inner_final_kernel(
    v_ref, vs_ref, cx_ref, code_ref, weight_ref, share_ref, out_hbm, sens_ref, out_ref, sems
):
    below, _, _, padded, _ = v_ref.shape
    strips = (padded - 2 * ROWS) // ROWS
    refs = (cx_ref, code_ref, weight_ref, share_ref)
    inner = pl.ds(ROWS, (strips - 2) * ROWS)

    def send(k):
        return pltpu.make_async_copy(out_ref.at[k, :, inner], out_hbm.at[:, k, inner], sems.at[k])

    final_level(
        below, range(1, strips - 1), strips,
        lambda s, j, start: vs_ref[s, j, start : start + ROWS, :],
        None, None, refs, out_ref, sens_ref, True,
    )
    send(below).start()

    def step(k, _):
        final_level(
            k, range(1, strips - 1), strips,
            lambda s, j, start: v_ref[k, s, j, start : start + ROWS, :],
            None, None, refs, out_ref, sens_ref, False,
        )
        send(k).start()
        return 0

    lax.fori_loop(0, below, step, 0)
    for k in range(below + 1):
        send(k).wait()


def outer_final_kernel(
    v_ref, vs_ref, vt_ref, left_ref, right_ref, left_top_ref, right_top_ref, seam_ref,
    cx_ref, code_ref, weight_ref, share_ref, inner_ref,
    out_ref, piece_ref,
    lrow_ref, rrow_ref, ltop_ref, rtop_ref, sens_ref, flat_ref,
):
    below, sectors, tiles, padded, _ = v_ref.shape
    strips = (padded - 2 * ROWS) // ROWS
    ends = (0, strips - 1)
    refs = (cx_ref, code_ref, weight_ref, share_ref)
    flip_left, flip_right = flags(seam_ref)
    turned(left_ref, flip_left, lrow_ref)
    turned(right_ref, flip_right, rrow_ref)
    turned(left_top_ref, flip_left, ltop_ref)
    turned(right_top_ref, flip_right, rtop_ref)

    final_level(
        below + 1, range(strips), strips,
        lambda s, j, start: vt_ref[s, j, start : start + ROWS, :],
        lambda s, j: ltop_ref[j, s : s + 1, :],
        lambda s, j: rtop_ref[j, s : s + 1, :],
        refs, out_ref, sens_ref, True,
    )
    final_level(
        below, ends, strips,
        lambda s, j, start: vs_ref[s, j, start : start + ROWS, :],
        lambda s, j: lrow_ref[j, below * sectors + s : below * sectors + s + 1, :],
        lambda s, j: rrow_ref[j, below * sectors + s : below * sectors + s + 1, :],
        refs, out_ref, sens_ref, False,
    )

    def step(k, _):
        final_level(
            k, ends, strips,
            lambda s, j, start: v_ref[k, s, j, start : start + ROWS, :],
            lambda s, j: lrow_ref[j, pl.ds(k * sectors + s, 1), :],
            lambda s, j: rrow_ref[j, pl.ds(k * sectors + s, 1), :],
            refs, out_ref, sens_ref, False,
        )
        return 0

    lax.fori_loop(0, below, step, 0)
    inner = slice(ROWS, (strips - 1) * ROWS)
    sens_ref[inner] += inner_ref[inner]
    if len(piece_ref.shape) == 2:
        piece_ref[...] = sens_ref[...]
    else:
        owners, group, copies, depth, _ = piece_ref.shape
        share = strips * ROWS * tiles // owners
        for xt in range(strips):
            for j in range(tiles):
                value = sens_ref[xt * ROWS : (xt + 1) * ROWS, j * LANES : (j + 1) * LANES]
                flat_ref[pl.ds(xt * ROWS * tiles + j, ROWS, stride=tiles), :] = value
        for o in range(owners):
            for piece in range(group):
                start = piece * depth
                used = max(0, min(depth, share - start))
                value = jnp.zeros((depth, LANES), jnp.float32)
                if used:
                    start += o * share
                    value = flat_ref[start : start + depth, :]
                    if used < depth:
                        line = lax.broadcasted_iota(jnp.int32, (depth, LANES), 0)
                        value = jnp.where(line < used, value, 0.0)
                for i in range(copies):
                    piece_ref[o, piece, i] = value


def write_kernel(part_ref, done_hbm, out_hbm, sems):
    levels, _, columns, _ = part_ref.shape

    def send(k, i):
        rows = pl.ds(i * (columns - ROWS), ROWS)
        return pltpu.make_async_copy(part_ref.at[k, :, rows], out_hbm.at[:, k, rows], sems.at[i, k])

    top = levels - 1
    send_top = pltpu.make_async_copy(part_ref.at[top], out_hbm.at[:, top], sems.at[0, top])
    send_top.start()
    for k in range(top):
        for i in range(2):
            send(k, i).start()
    send_top.wait()
    for k in range(top):
        for i in range(2):
            send(k, i).wait()


def mark_kernel(cells_ref, high_ref, low_ref):
    pairs, tall, _ = low_ref.shape
    short = high_ref.shape[1]
    high_iota = lax.broadcasted_iota(jnp.int32, (short, LANES), 0)
    low_iota = lax.broadcasted_iota(jnp.int32, (tall, LANES), 0)

    def step(pair, _):
        for i in range(2):
            cells = cells_ref[pl.ds(2 * pair + i, 1), :]
            high = jnp.right_shift(cells, 8) == high_iota
            low = jnp.bitwise_and(cells, 255) == low_iota
            lanes = slice(i * LANES, (i + 1) * LANES)
            high_ref[pair, :, lanes] = jnp.where(high, 1.0, 0.0).astype(jnp.bfloat16)
            low_ref[pair, :, lanes] = jnp.where(low, 1.0, 0.0).astype(jnp.bfloat16)
        return 0

    lax.fori_loop(0, pairs, step, 0)


def total_kernel(arrived_ref, *refs):
    out_ref = refs[-1]
    owners, senders, _, _ = arrived_ref.shape
    for o in range(owners):
        total = arrived_ref[o, 0]
        for i in range(1, senders):
            total = total + arrived_ref[o, i]
        out_ref[o] = total


def scatter_kernel(high_ref, low_ref, *refs):
    *value_refs, out_ref = refs
    group = len(value_refs)
    pairs, short, _ = high_ref.shape
    each = pairs // group
    rank = lax.axis_index("lev")
    total = jnp.zeros((2 * short, low_ref.shape[1]), jnp.float32)
    for part, value_ref in enumerate(value_refs):
        base = jnp.bitwise_xor(rank, part) * each
        for pair in range(each):
            high = high_ref[base + pair]
            scaled = []
            value = jnp.concatenate(
                [value_ref[2 * pair + i : 2 * pair + i + 1, :] for i in range(2)], axis=1
            )
            coarse = value.astype(jnp.bfloat16)
            fine = (value - coarse.astype(jnp.float32)).astype(jnp.bfloat16)
            for bits in (coarse, fine):
                scaled.append(high * jnp.broadcast_to(bits, high.shape))
            total += lax.dot_general(
                jnp.concatenate(scaled, axis=0),
                low_ref[base + pair],
                (((1,), (1,)), ((), ())),
                preferred_element_type=jnp.float32,
            )
    total = total[:short] + total[short:]
    rows = out_ref.shape[0] // 2
    for i in range(2):
        out_ref[pl.ds(i, rows, stride=2), :] = total[:rows, i * LANES : (i + 1) * LANES]


def exchanged(value, axis, apart):
    count = lax.axis_size(axis)
    return lax.ppermute(value, axis, [(i, i ^ apart) for i in range(count)])


def remapped(pieces, flux_cell, adjoint):
    owners, share = flux_cell.shape
    _, group, copies, depth, _ = pieces.shape
    sent = pieces.reshape(-1, depth, LANES)
    arrived = lax.all_to_all(
        sent, ("tile", "lev", "sec"), split_axis=0, concat_axis=0, tiled=True
    )
    cells = jnp.pad(flux_cell, ((0, 0), (0, group * depth * LANES - share)))
    cells = cells.reshape(owners, group, depth, LANES).transpose(1, 0, 2, 3).reshape(-1, LANES)
    pairs = cells.shape[0] // 2
    high, low = call(
        mark_kernel,
        (
            pltpu.VMEM((pairs, FL_DEV // 256 + 4, 256), jnp.bfloat16),
            pltpu.VMEM((pairs, 256, 256), jnp.bfloat16),
        ),
        [VM],
        [VM] * 2,
        (cells,),
    )
    own = call(
        total_kernel,
        f32(owners, depth, LANES),
        [VM, VM, VM, HBM],
        VM,
        (arrived.reshape(owners, group * copies, depth, LANES), high, low, *in_hbm(adjoint)),
    ).reshape(owners * depth, LANES)
    parts = [own] + [exchanged(own, "lev", d) for d in range(1, group)]
    out = call(
        scatter_kernel, f32(FL_DEV // LANES, LANES), [VM] * (group + 2), VM, (high, low, *parts)
    )
    return out.reshape(-1)


def around(first, last):
    count = lax.axis_size("tile")
    up = [(i, (i + 1) % count) for i in range(count)]
    down = [(j, i) for i, j in up]
    return lax.ppermute(last, "tile", up), lax.ppermute(first, "tile", down)


def from_above(value):
    count = lax.axis_size("lev")
    return lax.ppermute(value, "lev", [(i + 1, i) for i in range(count - 1)])


def shards(
    forcing, courant_x, courant_y, mass_flux, limiter_code, seam_code, level_weight, sector_share, flux_cell
):
    sectors, levels, columns, width = forcing.shape
    tiles, below = width // LANES, levels - 1
    padded = columns + 2 * ROWS
    field = kept(below, sectors, tiles, padded, LANES)
    field_top = kept(sectors, tiles, padded, LANES)
    plane = kept(sectors, columns, width)
    rim = kept(tiles, below * sectors, LANES)
    rim_top = kept(tiles, sectors, LANES)
    rim_next = kept(tiles, (below - 1) * sectors, LANES)
    rim_scratch = pltpu.VMEM((tiles, below * sectors, LANES), jnp.float32)

    seam = jnp.broadcast_to(seam_code.T[:, :, None], (*seam_code.T.shape, LANES))
    weight = jnp.broadcast_to(level_weight[:, None], (levels, LANES))

    above = from_above(
        call(start_kernel, plane, [HBM], VM, in_hbm(forcing), [pltpu.SemaphoreType.DMA])
    )
    narrow = pltpu.VMEM((levels, columns, width), jnp.bfloat16)
    v, first, last, top, mass_flux, courant_y, limiter_code, courant_x = call(
        lower_kernel,
        (
            field, rim, rim, plane,
            narrow, narrow, pltpu.VMEM((levels, columns, width), jnp.int32), narrow,
        ),
        [VM] + [HBM] * 4,
        [VM] * 8,
        (forcing, *in_hbm(mass_flux, courant_y, limiter_code, courant_x)),
        [pltpu.SemaphoreType.DMA((5, levels))],
    )
    left, right = around(first, last)
    lines = kept(sectors, tiles, columns, LANES)
    inner_field = kept(below - 1, sectors, tiles, padded, LANES)
    a_scratch = pltpu.VMEM((2, sectors, tiles, columns, LANES), jnp.float32)
    inner, inner_lowest, inner_top = call(
        inner_middle_kernel,
        (inner_field, lines, lines),
        [VM] * 5,
        [VM] * 3,
        (v, courant_x, mass_flux, courant_y, limiter_code),
        [a_scratch],
    )
    lowest, vt, first_top, last_top = call(
        ends_kernel,
        (plane, field_top, rim_top, rim_top),
        [VM] * 11,
        [VM] * 4,
        (
            v, inner_lowest, left, right, seam, courant_x, limiter_code, top, above,
            mass_flux, courant_y,
        ),
        [pltpu.VMEM((tiles, ROWS, LANES), jnp.float32)] * 2,
    )
    above = from_above(lowest)
    left_top, right_top = around(first_top, last_top)

    v, first, last, top = call(
        outer_middle_kernel,
        (inner_field, rim_next, rim_next, lines),
        [VM] * 11,
        [VM] * 4,
        (
            v, inner, inner_top, left, right, lowest, seam,
            courant_x, mass_flux, courant_y, limiter_code,
        ),
        [rim_scratch, rim_scratch, a_scratch],
    )
    vs, first, last, top = call(
        second_last_kernel,
        (field_top, rim, rim, kept(sectors, tiles, columns, LANES)),
        [VM] * 11,
        [VM] * 4,
        (
            vt, left_top, right_top, top, first, last, seam,
            courant_x, mass_flux, courant_y, limiter_code,
        ),
        [pltpu.VMEM((tiles, sectors, LANES), jnp.float32)] * 2,
    )
    left, right = around(first, last)
    vt, first_top, last_top = call(
        highest_kernel,
        (field_top, rim_top, rim_top),
        [VM] * 5,
        [VM] * 3,
        (top, above, mass_flux, courant_y, limiter_code),
    )
    left_top, right_top = around(first_top, last_top)

    owners, share = flux_cell.shape
    group, copies = lax.axis_size("lev"), lax.axis_size("sec")
    depth = -(-share // (group * LANES))
    aligned = share % LANES == 0
    packed = (owners, group, copies, depth, LANES)
    stage = pltpu.VMEM((levels, sectors, columns, width), jnp.float32)
    adjoint, inner = call(
        inner_final_kernel,
        (f32(*forcing.shape), kept(columns, width)),
        [VM] * 6,
        [HBM, VM],
        (v, vs, courant_x, limiter_code, weight, sector_share),
        [stage, pltpu.SemaphoreType.DMA((levels,))],
    )
    part, pieces = call(
        outer_final_kernel,
        (
            kept(levels, sectors, columns, width),
            f32(*packed) if aligned else f32(columns, width),
        ),
        [VM] * 13,
        [VM, VM],
        (
            v, vs, vt, left, right, left_top, right_top, seam,
            courant_x, limiter_code, weight, sector_share, inner,
        ),
        [
            rim_scratch, rim_scratch,
            pltpu.VMEM((tiles, sectors, LANES), jnp.float32),
            pltpu.VMEM((tiles, sectors, LANES), jnp.float32),
            pltpu.VMEM((columns, width), jnp.float32),
            pltpu.VMEM((columns * tiles + ROWS, LANES), jnp.float32),
        ],
    )
    adjoint = call(
        write_kernel,
        f32(*forcing.shape),
        [VM, HBM],
        HBM,
        (part, adjoint),
        [pltpu.SemaphoreType.DMA((2, levels))],
        aliases={1: 0},
    )
    if not aligned:
        pieces = jnp.pad(
            pieces.reshape(owners, share), ((0, 0), (0, group * depth * LANES - share))
        ).reshape(owners, group, 1, depth, LANES)
        pieces = jnp.broadcast_to(pieces, packed)
    flux_cell, pieces = lax.optimization_barrier((flux_cell, pieces))
    return (adjoint, remapped(pieces, flux_cell, adjoint))


def solution(mesh):
    placed = (
        P("sec", "lev", "tile", None),
        P("lev", "tile", None),
        P("lev", "tile", None),
        P("lev", "tile", None),
        P("lev", "tile", None),
        P(),
        P("lev"),
        P("sec", "tile", None),
        P("tile", None),
    )
    return jax.shard_map(
        shards,
        mesh=mesh,
        in_specs=placed,
        out_specs=(P("sec", "lev", "tile", None), P("tile")),
        check_vma=False,
    )
```

```python
import functools

import jax
import jax.numpy as jnp
from jax import lax
from jax.experimental import pallas as pl
from jax.experimental.pallas import tpu as pltpu
from jax.sharding import PartitionSpec as P

FL_DEV = 15360
LANES = 128
ROWS = 8
MIB = 2**20
VM = pl.BlockSpec(memory_space=pltpu.VMEM)
HBM = pl.BlockSpec(memory_space=pltpu.HBM)


def call(kernel, out_shape, in_specs, out_specs, operands, scratch=(), mib=16, aliases={}):
    return pl.pallas_call(
        kernel,
        out_shape=out_shape,
        in_specs=in_specs,
        out_specs=out_specs,
        scratch_shapes=list(scratch),
        input_output_aliases=aliases,
        cost_estimate=pl.CostEstimate(flops=1, transcendentals=0, bytes_accessed=1),
        compiler_params=pltpu.CompilerParams(vmem_limit_bytes=mib * MIB),
    )(*operands)


def in_hbm(*arrays):
    return tuple(pltpu.with_memory_space_constraint(a, pltpu.HBM) for a in arrays)


def kept(*shape):
    return pltpu.VMEM(shape, jnp.float32)


def f32(*shape):
    return jax.ShapeDtypeStruct(shape, jnp.float32)


def cut(value, xt, j):
    return value[xt * ROWS : (xt + 1) * ROWS, j * LANES : (j + 1) * LANES]


def weights(courant, codes, bit):
    size = jnp.abs(courant)
    half = (0.5 * size) * (1.0 - size)
    limited = jnp.where(jnp.bitwise_and(codes, 1 << bit) != 0, half, 0.0)
    ahead = jnp.maximum(courant, 0.0) - limited
    back = jnp.maximum(-courant, 0.0) - limited
    return ahead, back


def second_weights(cy, codes, bit, xt, tiles):
    lane = lax.broadcasted_iota(jnp.int32, (ROWS, LANES), 1)
    out = []
    for j in range(tiles):
        ahead, back = weights(cut(cy, xt, j), cut(codes, xt, j), bit)
        if j == 0:
            back = jnp.where(lane == 0, 0.0, back)
        if j == tiles - 1:
            ahead = jnp.where(lane == LANES - 1, 0.0, ahead)
        out.append((ahead, back, (1.0 - ahead) - back))
    return out


def second_sweep(parts, factors):
    lane = lax.broadcasted_iota(jnp.int32, (ROWS, LANES), 1)
    tiles = len(parts)
    later = [pltpu.roll(part, LANES - 1, 1) for part in parts]
    sooner = [pltpu.roll(part, 1, 1) for part in parts]
    out = []
    for j in range(tiles):
        following, previous = later[j], sooner[j]
        if j + 1 < tiles:
            following = jnp.where(lane == LANES - 1, later[j + 1], following)
        if j > 0:
            previous = jnp.where(lane == 0, sooner[j - 1], previous)
        ahead, back, own = factors[j]
        out.append(own * parts[j] + ahead * following + back * previous)
    return out


def first_sweep(field, s, j, xt, last, factors, left_row, right_row):
    start = ROWS * (xt + 1)
    sub = lax.broadcasted_iota(jnp.int32, (ROWS, LANES), 0)
    own_value = field(s, j, start)
    following = field(s, j, start + 1)
    previous = field(s, j, start - 1)
    if xt == 0:
        previous = jnp.where(sub == 0, left_row(s, j), previous)
    if xt == last:
        following = jnp.where(sub == ROWS - 1, right_row(s, j), following)
    ahead, back, own = factors
    return own * own_value + ahead * following + back * previous


def turned(source_ref, flag, target_ref):
    tiles, rows, _ = source_ref.shape
    for j in range(tiles):
        for start in range(0, rows, ROWS):
            count = min(ROWS, rows - start)
            index = (LANES - 1) - lax.broadcasted_iota(jnp.int32, (count, LANES), 1)
            straight = source_ref[j, start : start + count, :]
            other = source_ref[tiles - 1 - j, start : start + count, :]
            mirrored = jnp.take_along_axis(other, index, axis=1, mode="promise_in_bounds")
            target_ref[j, start : start + count, :] = jnp.where(flag, mirrored, straight)


def store_padded(ref, index, s, j, xt, value):
    start = ROWS * (xt + 1)
    ref[(*index, s, j, slice(start, start + ROWS), slice(None))] = value


def store_rims(first_ref, last_ref, row, j, xt, last, value):
    if xt == 0:
        first_ref[j, pl.ds(row, 1), :] = value[:1]
    if xt == last:
        last_ref[j, pl.ds(row, 1), :] = value[ROWS - 1 :]


def flags(seam_ref):
    tile = lax.axis_index("tile")
    return seam_ref[0, pl.ds(tile, 1), :] == 1, seam_ref[1, pl.ds(tile, 1), :] == 1


def start_kernel(f_hbm, mf_hbm, cy_hbm, code_hbm, cx_hbm, out_ref, mf_ref, cy_ref, code_ref, cx_ref, sems):
    copies = [
        pltpu.make_async_copy(source, target, sems.at[i])
        for i, (source, target) in enumerate(
            (
                (f_hbm.at[:, 0], out_ref),
                (mf_hbm, mf_ref),
                (cy_hbm, cy_ref),
                (code_hbm, code_ref),
                (cx_hbm, cx_ref),
            )
        )
    ]
    for copy in copies:
        copy.start()
    for copy in copies:
        copy.wait()


def lower_kernel(f_ref, mf_ref, cy_ref, code_ref, v_ref, first_ref, last_ref, top_ref):
    sectors, levels, columns, width = f_ref.shape
    tiles, strips = width // LANES, columns // ROWS

    def level(k, _):
        mf = mf_ref[k].astype(jnp.float32)
        cy = cy_ref[k].astype(jnp.float32)
        codes = code_ref[k]
        for xt in range(strips):
            factors = second_weights(cy, codes, 3, xt, tiles)
            rows = slice(xt * ROWS, (xt + 1) * ROWS)
            for s in range(sectors):
                parts = []
                for j in range(tiles):
                    lanes = slice(j * LANES, (j + 1) * LANES)
                    here = f_ref[s, k, rows, lanes]
                    upper = f_ref[s, k + 1, rows, lanes]
                    parts.append(here + cut(mf, xt, j) * (upper - here))
                for j, value in enumerate(second_sweep(parts, factors)):
                    store_padded(v_ref, (k,), s, j, xt, value)
                    store_rims(first_ref, last_ref, k * sectors + s, j, xt, strips - 1, value)
        return 0

    lax.fori_loop(0, levels - 1, level, 0)
    top_ref[...] = f_ref[:, levels - 1]


def first_weights(cx, codes, bit, xt, j):
    ahead, back = weights(cut(cx, xt, j), cut(codes, xt, j), bit)
    return ahead, back, (1.0 - ahead) - back


def ends_kernel(
    v_ref, inner_ref, left_ref, right_ref, seam_ref, cx_ref, code_ref, here_ref, above_ref,
    mf_ref, cy_ref,
    out_ref, top_ref, first_ref, last_ref,
    lrow_ref, rrow_ref,
):
    _, sectors, tiles, _, _ = v_ref.shape
    columns = out_ref.shape[1]
    strips = columns // ROWS
    flip_left, flip_right = flags(seam_ref)
    turned(left_ref.at[:, :ROWS], flip_left, lrow_ref)
    turned(right_ref.at[:, :ROWS], flip_right, rrow_ref)
    cx = cx_ref[0].astype(jnp.float32)
    codes = code_ref[0]
    for s in range(sectors):
        for j in range(tiles):
            lanes = slice(j * LANES, (j + 1) * LANES)
            out_ref[s, ROWS : columns - ROWS, lanes] = inner_ref[s, j, ROWS : columns - ROWS]
    for xt in (0, strips - 1):
        for j in range(tiles):
            factors = first_weights(cx, codes, 2, xt, j)
            for s in range(sectors):
                value = first_sweep(
                    lambda s, j, start: v_ref[0, s, j, start : start + ROWS, :],
                    s, j, xt, strips - 1, factors,
                    lambda s, j: lrow_ref[j, s : s + 1, :],
                    lambda s, j: rrow_ref[j, s : s + 1, :],
                )
                out_ref[s, xt * ROWS : (xt + 1) * ROWS, j * LANES : (j + 1) * LANES] = value

    level = mf_ref.shape[0] - 1
    at_top = lax.axis_index("lev") == lax.axis_size("lev") - 1
    mf = mf_ref[level].astype(jnp.float32)
    cy = cy_ref[level].astype(jnp.float32)
    codes = code_ref[level]
    for xt in range(strips):
        factors = second_weights(cy, codes, 3, xt, tiles)
        rows = slice(xt * ROWS, (xt + 1) * ROWS)
        for s in range(sectors):
            parts = []
            for j in range(tiles):
                lanes = slice(j * LANES, (j + 1) * LANES)
                here = here_ref[s, rows, lanes]
                upper = jnp.where(at_top, here, above_ref[s, rows, lanes])
                parts.append(here + cut(mf, xt, j) * (upper - here))
            for j, value in enumerate(second_sweep(parts, factors)):
                store_padded(top_ref, (), s, j, xt, value)
                store_rims(first_ref, last_ref, s, j, xt, strips - 1, value)


def middle_levels(
    chosen, v_ref, lrow_ref, rrow_ref, cx_ref, mf_ref, cy_ref, code_ref, out_ref, a_ref, rims=None
):
    below, sectors, tiles, padded, _ = v_ref.shape
    strips = (padded - 2 * ROWS) // ROWS

    def level(k, _):
        cx = cx_ref[k + 1].astype(jnp.float32)
        mf = mf_ref[k].astype(jnp.float32)
        cy = cy_ref[k].astype(jnp.float32)
        codes_x = code_ref[k + 1]
        codes_y = code_ref[k]
        slot = lax.rem(k, 2)
        for xt in chosen:
            along = [first_weights(cx, codes_x, 2, xt, j) for j in range(tiles)]
            across = second_weights(cy, codes_y, 1, xt, tiles)
            rows = slice(xt * ROWS, (xt + 1) * ROWS)
            for s in range(sectors):
                parts = []
                for j in range(tiles):
                    upper = first_sweep(
                        lambda s, j, start: v_ref[k + 1, s, j, start : start + ROWS, :],
                        s, j, xt, strips - 1, along[j],
                        lambda s, j: lrow_ref[j, pl.ds((k + 1) * sectors + s, 1), :],
                        lambda s, j: rrow_ref[j, pl.ds((k + 1) * sectors + s, 1), :],
                    )
                    here = a_ref[slot, s, j, rows, :]
                    a_ref[1 - slot, s, j, rows, :] = upper
                    parts.append(here + cut(mf, xt, j) * (upper - here))
                for j, value in enumerate(second_sweep(parts, across)):
                    store_padded(out_ref, (k,), s, j, xt, value)
                    if rims is not None:
                        store_rims(*rims, k * sectors + s, j, xt, strips - 1, value)
        return 0

    lax.fori_loop(0, below - 1, level, 0)


def inner_middle_kernel(
    v_ref, cx_ref, mf_ref, cy_ref, code_ref, out_ref, lowest_ref, top_ref, a_ref
):
    below, sectors, tiles, padded, _ = v_ref.shape
    strips = (padded - 2 * ROWS) // ROWS
    cx = cx_ref[0].astype(jnp.float32)
    for xt in range(1, strips - 1):
        for j in range(tiles):
            factors = first_weights(cx, code_ref[0], 2, xt, j)
            for s in range(sectors):
                value = first_sweep(
                    lambda s, j, start: v_ref[0, s, j, start : start + ROWS, :],
                    s, j, xt, strips - 1, factors, None, None,
                )
                a_ref[0, s, j, xt * ROWS : (xt + 1) * ROWS, :] = value
                lowest_ref[s, j, xt * ROWS : (xt + 1) * ROWS, :] = value
    middle_levels(
        range(1, strips - 1), v_ref, None, None, cx_ref, mf_ref, cy_ref, code_ref, out_ref, a_ref
    )
    inner = slice(ROWS, (strips - 1) * ROWS)
    top_ref[:, :, inner] = a_ref[(below - 1) % 2, :, :, inner]


def outer_middle_kernel(
    v_ref, inner_ref, inner_top_ref, left_ref, right_ref, lowest_ref, seam_ref,
    cx_ref, mf_ref, cy_ref, code_ref,
    out_ref, first_ref, last_ref, top_ref,
    lrow_ref, rrow_ref, a_ref,
):
    below, sectors, tiles, padded, _ = v_ref.shape
    strips = (padded - 2 * ROWS) // ROWS
    ends = (0, strips - 1)
    flip_left, flip_right = flags(seam_ref)
    turned(left_ref, flip_left, lrow_ref)
    turned(right_ref, flip_right, rrow_ref)
    for s in range(sectors):
        for j in range(tiles):
            for xt in ends:
                rows = slice(xt * ROWS, (xt + 1) * ROWS)
                a_ref[0, s, j, rows] = lowest_ref[s, rows, j * LANES : (j + 1) * LANES]
    middle_levels(
        ends, v_ref, lrow_ref, rrow_ref, cx_ref, mf_ref, cy_ref, code_ref, out_ref, a_ref,
        (first_ref, last_ref),
    )
    for xt in ends:
        rows = slice(xt * ROWS, (xt + 1) * ROWS)
        top_ref[:, :, rows] = a_ref[(below - 1) % 2, :, :, rows]
    inner = slice(ROWS, (strips - 1) * ROWS)
    top_ref[:, :, inner] = inner_top_ref[:, :, inner]
    inner = slice(2 * ROWS, strips * ROWS)

    def copy(k, _):
        out_ref[k, :, :, inner] = inner_ref[k, :, :, inner]
        return 0

    lax.fori_loop(0, below - 1, copy, 0)


def second_last_kernel(
    vt_ref, left_ref, right_ref, lower_ref, first_in, last_in, seam_ref, cx_ref, mf_ref, cy_ref, code_ref,
    out_ref, first_ref, last_ref, top_ref,
    lrow_ref, rrow_ref,
):
    sectors, tiles, padded, _ = vt_ref.shape
    strips = (padded - 2 * ROWS) // ROWS
    top = mf_ref.shape[0] - 1
    done = first_in.shape[1]
    flip_left, flip_right = flags(seam_ref)
    turned(left_ref, flip_left, lrow_ref)
    turned(right_ref, flip_right, rrow_ref)
    first_ref[:, :done] = first_in[...]
    last_ref[:, :done] = last_in[...]
    cx = cx_ref[top].astype(jnp.float32)
    mf = mf_ref[top - 1].astype(jnp.float32)
    cy = cy_ref[top - 1].astype(jnp.float32)
    for xt in range(strips):
        along = [first_weights(cx, code_ref[top], 2, xt, j) for j in range(tiles)]
        across = second_weights(cy, code_ref[top - 1], 1, xt, tiles)
        rows = slice(xt * ROWS, (xt + 1) * ROWS)
        for s in range(sectors):
            parts = []
            for j in range(tiles):
                upper = first_sweep(
                    lambda s, j, start: vt_ref[s, j, start : start + ROWS, :],
                    s, j, xt, strips - 1, along[j],
                    lambda s, j: lrow_ref[j, s : s + 1, :],
                    lambda s, j: rrow_ref[j, s : s + 1, :],
                )
                top_ref[s, j, rows, :] = upper
                here = lower_ref[s, j, rows, :]
                parts.append(here + cut(mf, xt, j) * (upper - here))
            for j, value in enumerate(second_sweep(parts, across)):
                store_padded(out_ref, (), s, j, xt, value)
                store_rims(first_ref, last_ref, done + s, j, xt, strips - 1, value)


def highest_kernel(here_ref, above_ref, mf_ref, cy_ref, code_ref, out_ref, first_ref, last_ref):
    sectors, tiles, columns, _ = here_ref.shape
    strips = columns // ROWS
    top = mf_ref.shape[0] - 1
    at_top = lax.axis_index("lev") == lax.axis_size("lev") - 1
    mf = mf_ref[top].astype(jnp.float32)
    cy = cy_ref[top].astype(jnp.float32)
    for xt in range(strips):
        across = second_weights(cy, code_ref[top], 1, xt, tiles)
        rows = slice(xt * ROWS, (xt + 1) * ROWS)
        for s in range(sectors):
            parts = []
            for j in range(tiles):
                here = here_ref[s, j, rows, :]
                upper = above_ref[s, rows, j * LANES : (j + 1) * LANES]
                upper = jnp.where(at_top, here, upper)
                parts.append(here + cut(mf, xt, j) * (upper - here))
            for j, value in enumerate(second_sweep(parts, across)):
                store_padded(out_ref, (), s, j, xt, value)
                store_rims(first_ref, last_ref, s, j, xt, strips - 1, value)


def final_level(
    k, chosen, strips, field, left_row, right_row, refs, out_ref, sens_ref, start_sum
):
    cx_ref, code_ref, weight_ref, share_ref = refs
    sectors, _, width = share_ref.shape
    cx = cx_ref[k].astype(jnp.float32)
    codes = code_ref[k]
    factor = weight_ref[pl.ds(k, 1), :]
    for xt in chosen:
        rows = slice(xt * ROWS, (xt + 1) * ROWS)
        for j in range(width // LANES):
            lanes = slice(j * LANES, (j + 1) * LANES)
            factors = first_weights(cx, codes, 0, xt, j)
            total = 0.0
            for s in range(sectors):
                value = first_sweep(field, s, j, xt, strips - 1, factors, left_row, right_row)
                out_ref[k, s, rows, lanes] = value
                total = total + share_ref[s, rows, lanes] * value
            if start_sum:
                sens_ref[rows, lanes] = factor * total
            else:
                sens_ref[rows, lanes] += factor * total


def inner_final_kernel(
    v_ref, vs_ref, cx_ref, code_ref, weight_ref, share_ref, out_hbm, sens_ref, out_ref, sems
):
    below, _, _, padded, _ = v_ref.shape
    strips = (padded - 2 * ROWS) // ROWS
    refs = (cx_ref, code_ref, weight_ref, share_ref)
    inner = pl.ds(ROWS, (strips - 2) * ROWS)

    def send(k):
        return pltpu.make_async_copy(out_ref.at[k, :, inner], out_hbm.at[:, k, inner], sems.at[k])

    final_level(
        below, range(1, strips - 1), strips,
        lambda s, j, start: vs_ref[s, j, start : start + ROWS, :],
        None, None, refs, out_ref, sens_ref, True,
    )
    send(below).start()

    def step(k, _):
        final_level(
            k, range(1, strips - 1), strips,
            lambda s, j, start: v_ref[k, s, j, start : start + ROWS, :],
            None, None, refs, out_ref, sens_ref, False,
        )
        send(k).start()
        return 0

    lax.fori_loop(0, below, step, 0)
    for k in range(below + 1):
        send(k).wait()


def outer_final_kernel(
    v_ref, vs_ref, vt_ref, left_ref, right_ref, left_top_ref, right_top_ref, seam_ref,
    cx_ref, code_ref, weight_ref, share_ref, inner_ref, done_hbm,
    out_hbm, piece_ref,
    lrow_ref, rrow_ref, ltop_ref, rtop_ref, out_ref, sens_ref, flat_ref, sems,
):
    below, sectors, tiles, padded, _ = v_ref.shape
    strips = (padded - 2 * ROWS) // ROWS
    ends = (0, strips - 1)
    refs = (cx_ref, code_ref, weight_ref, share_ref)
    flip_left, flip_right = flags(seam_ref)
    turned(left_ref, flip_left, lrow_ref)
    turned(right_ref, flip_right, rrow_ref)
    turned(left_top_ref, flip_left, ltop_ref)
    turned(right_top_ref, flip_right, rtop_ref)

    def send(k, i):
        rows = pl.ds(ends[i] * ROWS, ROWS)
        return pltpu.make_async_copy(out_ref.at[k, :, rows], out_hbm.at[:, k, rows], sems.at[i, k])

    send_top = pltpu.make_async_copy(
        out_ref.at[below + 1], out_hbm.at[:, below + 1], sems.at[0, below + 1]
    )
    final_level(
        below + 1, range(strips), strips,
        lambda s, j, start: vt_ref[s, j, start : start + ROWS, :],
        lambda s, j: ltop_ref[j, s : s + 1, :],
        lambda s, j: rtop_ref[j, s : s + 1, :],
        refs, out_ref, sens_ref, True,
    )
    send_top.start()
    final_level(
        below, ends, strips,
        lambda s, j, start: vs_ref[s, j, start : start + ROWS, :],
        lambda s, j: lrow_ref[j, below * sectors + s : below * sectors + s + 1, :],
        lambda s, j: rrow_ref[j, below * sectors + s : below * sectors + s + 1, :],
        refs, out_ref, sens_ref, False,
    )
    for i in range(2):
        send(below, i).start()

    def step(k, _):
        final_level(
            k, ends, strips,
            lambda s, j, start: v_ref[k, s, j, start : start + ROWS, :],
            lambda s, j: lrow_ref[j, pl.ds(k * sectors + s, 1), :],
            lambda s, j: rrow_ref[j, pl.ds(k * sectors + s, 1), :],
            refs, out_ref, sens_ref, False,
        )
        for i in range(2):
            send(k, i).start()
        return 0

    lax.fori_loop(0, below, step, 0)
    inner = slice(ROWS, (strips - 1) * ROWS)
    sens_ref[inner] += inner_ref[inner]
    if len(piece_ref.shape) == 2:
        piece_ref[...] = sens_ref[...]
    else:
        owners, group, copies, depth, _ = piece_ref.shape
        share = strips * ROWS * tiles // owners
        for xt in range(strips):
            for j in range(tiles):
                value = sens_ref[xt * ROWS : (xt + 1) * ROWS, j * LANES : (j + 1) * LANES]
                flat_ref[pl.ds(xt * ROWS * tiles + j, ROWS, stride=tiles), :] = value
        for o in range(owners):
            for piece in range(group):
                start = piece * depth
                used = max(0, min(depth, share - start))
                value = jnp.zeros((depth, LANES), jnp.float32)
                if used:
                    start += o * share
                    value = flat_ref[start : start + depth, :]
                    if used < depth:
                        line = lax.broadcasted_iota(jnp.int32, (depth, LANES), 0)
                        value = jnp.where(line < used, value, 0.0)
                for i in range(copies):
                    piece_ref[o, piece, i] = value
    send_top.wait()
    for k in range(below + 1):
        for i in range(2):
            send(k, i).wait()


def scatter_kernel(cells_ref, *refs):
    *value_refs, out_ref = refs
    rows, lanes = out_ref.shape
    group, owners, depth, _ = cells_ref.shape
    rank = lax.axis_index("lev")
    half = jnp.bfloat16
    zero, one = jnp.zeros((), half), jnp.ones((), half)
    iota = lax.broadcasted_iota(jnp.int32, (lanes, lanes), 0).astype(jnp.float32).astype(half)
    total = jnp.zeros((2 * lanes, lanes), jnp.float32)
    lines = [(i, o, r) for i in range(group) for o in range(owners) for r in range(depth)]
    wide = 8

    def spread(row):
        return jnp.broadcast_to(row, (lanes, lanes)).astype(half)

    for start in range(0, len(lines), wide):
        lefts, rights = [], []
        for part, owner, line in lines[start : start + wide]:
            cells = cells_ref[jnp.bitwise_xor(rank, part), owner, line : line + 1, :]
            value = value_refs[part][owner, line : line + 1, :]
            coarse = value.astype(half).astype(jnp.float32)
            high = spread(jnp.right_shift(cells, 7).astype(jnp.float32)) == iota
            low = spread(jnp.bitwise_and(cells, 127).astype(jnp.float32)) == iota
            lefts.append(
                jnp.concatenate(
                    [
                        jnp.where(high, spread(coarse), zero),
                        jnp.where(high, spread(value - coarse), zero),
                    ],
                    axis=0,
                )
            )
            rights.append(jnp.where(low, one, zero))
        total += lax.dot_general(
            jnp.concatenate(lefts, axis=1),
            jnp.concatenate(rights, axis=1),
            (((1,), (1,)), ((), ())),
            preferred_element_type=jnp.float32,
        )
    out_ref[...] = total[:rows] + total[lanes : lanes + rows]


def exchanged(value, axis, apart):
    count = lax.axis_size(axis)
    return lax.ppermute(value, axis, [(i, i ^ apart) for i in range(count)])


def remapped(pieces, flux_cell):
    owners, share = flux_cell.shape
    _, group, copies, depth, _ = pieces.shape
    sent = pieces.reshape(-1, depth, LANES)
    arrived = lax.all_to_all(
        sent, ("tile", "lev", "sec"), split_axis=0, concat_axis=0, tiled=True
    )
    own = jnp.sum(arrived.reshape(owners, group * copies, depth, LANES), axis=1)
    parts = [own] + [exchanged(own, "lev", d) for d in range(1, group)]
    cells = jnp.pad(flux_cell, ((0, 0), (0, group * depth * LANES - share)))
    cells = cells.reshape(owners, group, depth, LANES).transpose(1, 0, 2, 3)
    out = call(
        scatter_kernel, f32(FL_DEV // LANES, LANES), [VM] * (group + 1), VM, (cells, *parts)
    )
    return out.reshape(-1)


def around(first, last):
    count = lax.axis_size("tile")
    up = [(i, (i + 1) % count) for i in range(count)]
    down = [(j, i) for i, j in up]
    return lax.ppermute(last, "tile", up), lax.ppermute(first, "tile", down)


def from_above(value):
    count = lax.axis_size("lev")
    return lax.ppermute(value, "lev", [(i + 1, i) for i in range(count - 1)])


def shards(
    forcing, courant_x, courant_y, mass_flux, limiter_code, seam_code, level_weight, sector_share, flux_cell
):
    sectors, levels, columns, width = forcing.shape
    tiles, below = width // LANES, levels - 1
    padded = columns + 2 * ROWS
    field = kept(below, sectors, tiles, padded, LANES)
    field_top = kept(sectors, tiles, padded, LANES)
    plane = kept(sectors, columns, width)
    rim = kept(tiles, below * sectors, LANES)
    rim_top = kept(tiles, sectors, LANES)
    rim_next = kept(tiles, (below - 1) * sectors, LANES)
    rim_scratch = pltpu.VMEM((tiles, below * sectors, LANES), jnp.float32)

    seam = jnp.broadcast_to(seam_code.T[:, :, None], (*seam_code.T.shape, LANES))
    weight = jnp.broadcast_to(level_weight[:, None], (levels, LANES))

    narrow = pltpu.VMEM((levels, columns, width), jnp.bfloat16)
    lowest, mass_flux, courant_y, limiter_code, courant_x = call(
        start_kernel,
        (plane, narrow, narrow, pltpu.VMEM((levels, columns, width), jnp.int32), narrow),
        [HBM] * 5,
        [VM] * 5,
        in_hbm(forcing, mass_flux, courant_y, limiter_code, courant_x),
        [pltpu.SemaphoreType.DMA((5,))],
    )
    above = from_above(lowest)
    v, first, last, top = call(
        lower_kernel,
        (field, rim, rim, plane),
        [VM] * 4,
        [VM] * 4,
        (forcing, mass_flux, courant_y, limiter_code),
    )
    left, right = around(first, last)
    lines = kept(sectors, tiles, columns, LANES)
    inner_field = kept(below - 1, sectors, tiles, padded, LANES)
    a_scratch = pltpu.VMEM((2, sectors, tiles, columns, LANES), jnp.float32)
    inner, inner_lowest, inner_top = call(
        inner_middle_kernel,
        (inner_field, lines, lines),
        [VM] * 5,
        [VM] * 3,
        (v, courant_x, mass_flux, courant_y, limiter_code),
        [a_scratch],
    )
    lowest, vt, first_top, last_top = call(
        ends_kernel,
        (plane, field_top, rim_top, rim_top),
        [VM] * 11,
        [VM] * 4,
        (
            v, inner_lowest, left, right, seam, courant_x, limiter_code, top, above,
            mass_flux, courant_y,
        ),
        [pltpu.VMEM((tiles, ROWS, LANES), jnp.float32)] * 2,
    )
    above = from_above(lowest)
    left_top, right_top = around(first_top, last_top)

    v, first, last, top = call(
        outer_middle_kernel,
        (inner_field, rim_next, rim_next, lines),
        [VM] * 11,
        [VM] * 4,
        (
            v, inner, inner_top, left, right, lowest, seam,
            courant_x, mass_flux, courant_y, limiter_code,
        ),
        [rim_scratch, rim_scratch, a_scratch],
    )
    vs, first, last, top = call(
        second_last_kernel,
        (field_top, rim, rim, kept(sectors, tiles, columns, LANES)),
        [VM] * 11,
        [VM] * 4,
        (
            vt, left_top, right_top, top, first, last, seam,
            courant_x, mass_flux, courant_y, limiter_code,
        ),
        [pltpu.VMEM((tiles, sectors, LANES), jnp.float32)] * 2,
    )
    left, right = around(first, last)
    vt, first_top, last_top = call(
        highest_kernel,
        (field_top, rim_top, rim_top),
        [VM] * 5,
        [VM] * 3,
        (top, above, mass_flux, courant_y, limiter_code),
    )
    left_top, right_top = around(first_top, last_top)

    owners, share = flux_cell.shape
    group, copies = lax.axis_size("lev"), lax.axis_size("sec")
    depth = -(-share // (group * LANES))
    aligned = share % LANES == 0
    packed = (owners, group, copies, depth, LANES)
    stage = pltpu.VMEM((levels, sectors, columns, width), jnp.float32)
    adjoint, inner = call(
        inner_final_kernel,
        (f32(*forcing.shape), kept(columns, width)),
        [VM] * 6,
        [HBM, VM],
        (v, vs, courant_x, limiter_code, weight, sector_share),
        [stage, pltpu.SemaphoreType.DMA((levels,))],
    )
    adjoint, pieces = call(
        outer_final_kernel,
        (f32(*forcing.shape), f32(*packed) if aligned else f32(columns, width)),
        [VM] * 13 + [HBM],
        [HBM, VM],
        (
            v, vs, vt, left, right, left_top, right_top, seam,
            courant_x, limiter_code, weight, sector_share, inner, adjoint,
        ),
        [
            rim_scratch, rim_scratch,
            pltpu.VMEM((tiles, sectors, LANES), jnp.float32),
            pltpu.VMEM((tiles, sectors, LANES), jnp.float32),
            stage,
            pltpu.VMEM((columns, width), jnp.float32),
            pltpu.VMEM((columns * tiles + ROWS, LANES), jnp.float32),
            pltpu.SemaphoreType.DMA((2, levels)),
        ],
        aliases={13: 0},
    )
    if not aligned:
        pieces = jnp.pad(
            pieces.reshape(owners, share), ((0, 0), (0, group * depth * LANES - share))
        ).reshape(owners, group, 1, depth, LANES)
        pieces = jnp.broadcast_to(pieces, packed)
    flux_cell, pieces = lax.optimization_barrier((flux_cell, pieces))
    return (adjoint, remapped(pieces, flux_cell))


def solution(mesh):
    placed = (
        P("sec", "lev", "tile", None),
        P("lev", "tile", None),
        P("lev", "tile", None),
        P("lev", "tile", None),
        P("lev", "tile", None),
        P(),
        P("lev"),
        P("sec", "tile", None),
        P("tile", None),
    )
    return jax.shard_map(
        shards,
        mesh=mesh,
        in_specs=placed,
        out_specs=(P("sec", "lev", "tile", None), P("tile")),
        check_vma=False,
    )
```

```python
import functools

import jax
import jax.numpy as jnp
from jax import lax
from jax.experimental import pallas as pl
from jax.experimental.pallas import tpu as pltpu
from jax.sharding import PartitionSpec as P

FL_DEV = 15360
LANES = 128
ROWS = 8
MIB = 2**20
VM = pl.BlockSpec(memory_space=pltpu.VMEM)
HBM = pl.BlockSpec(memory_space=pltpu.HBM)


def call(kernel, out_shape, in_specs, out_specs, operands, scratch=(), mib=16, aliases={}):
    if isinstance(out_shape, tuple):
        out_specs = tuple(
            tuple(spec for _ in part) if isinstance(part, tuple) else spec
            for spec, part in zip(out_specs, out_shape)
        )
    return pl.pallas_call(
        kernel,
        out_shape=out_shape,
        in_specs=[jax.tree.map(lambda _: spec, part) for spec, part in zip(in_specs, operands)],
        out_specs=out_specs,
        scratch_shapes=list(scratch),
        input_output_aliases={len(jax.tree.leaves(operands[:i])): o for i, o in aliases.items()},
        cost_estimate=pl.CostEstimate(flops=1, transcendentals=0, bytes_accessed=1),
        compiler_params=pltpu.CompilerParams(vmem_limit_bytes=mib * MIB),
    )(*operands)


def in_hbm(*arrays):
    return tuple(pltpu.with_memory_space_constraint(a, pltpu.HBM) for a in arrays)


def kept(*shape):
    return pltpu.VMEM(shape, jnp.float32)


def f32(*shape):
    return jax.ShapeDtypeStruct(shape, jnp.float32)


def half_of(halves, s):
    count = halves[0].shape[0]
    return halves[s // count], s % count


def cut(value, xt, j):
    return value[xt * ROWS : (xt + 1) * ROWS, j * LANES : (j + 1) * LANES]


def weights(courant, codes, bit):
    size = jnp.abs(courant)
    half = (0.5 * size) * (1.0 - size)
    limited = jnp.where(jnp.bitwise_and(codes, 1 << bit) != 0, half, 0.0)
    ahead = jnp.maximum(courant, 0.0) - limited
    back = jnp.maximum(-courant, 0.0) - limited
    return ahead, back


def second_weights(cy, codes, bit, xt, tiles):
    lane = lax.broadcasted_iota(jnp.int32, (ROWS, LANES), 1)
    out = []
    for j in range(tiles):
        ahead, back = weights(cut(cy, xt, j), cut(codes, xt, j), bit)
        if j == 0:
            back = jnp.where(lane == 0, 0.0, back)
        if j == tiles - 1:
            ahead = jnp.where(lane == LANES - 1, 0.0, ahead)
        out.append((ahead, back, (1.0 - ahead) - back))
    return out


def second_sweep(parts, factors):
    lane = lax.broadcasted_iota(jnp.int32, (ROWS, LANES), 1)
    tiles = len(parts)
    later = [pltpu.roll(part, LANES - 1, 1) for part in parts]
    sooner = [pltpu.roll(part, 1, 1) for part in parts]
    out = []
    for j in range(tiles):
        following, previous = later[j], sooner[j]
        if j + 1 < tiles:
            following = jnp.where(lane == LANES - 1, later[j + 1], following)
        if j > 0:
            previous = jnp.where(lane == 0, sooner[j - 1], previous)
        ahead, back, own = factors[j]
        out.append(own * parts[j] + ahead * following + back * previous)
    return out


def first_sweep(field, s, j, xt, last, factors, left_row, right_row):
    start = ROWS * (xt + 1)
    sub = lax.broadcasted_iota(jnp.int32, (ROWS, LANES), 0)
    own_value = field(s, j, start)
    following = field(s, j, start + 1)
    previous = field(s, j, start - 1)
    if xt == 0:
        previous = jnp.where(sub == 0, left_row(s, j), previous)
    if xt == last:
        following = jnp.where(sub == ROWS - 1, right_row(s, j), following)
    ahead, back, own = factors
    return own * own_value + ahead * following + back * previous


def turned(source_ref, flag, target_ref):
    tiles, rows, _ = source_ref.shape
    for j in range(tiles):
        for start in range(0, rows, ROWS):
            count = min(ROWS, rows - start)
            index = (LANES - 1) - lax.broadcasted_iota(jnp.int32, (count, LANES), 1)
            straight = source_ref[j, start : start + count, :]
            other = source_ref[tiles - 1 - j, start : start + count, :]
            mirrored = jnp.take_along_axis(other, index, axis=1, mode="promise_in_bounds")
            target_ref[j, start : start + count, :] = jnp.where(flag, mirrored, straight)


def store_padded(ref, index, s, j, xt, value):
    start = ROWS * (xt + 1)
    ref[(*index, s, j, slice(start, start + ROWS), slice(None))] = value


def store_rims(first_ref, last_ref, row, j, xt, last, value):
    if xt == 0:
        first_ref[j, pl.ds(row, 1), :] = value[:1]
    if xt == last:
        last_ref[j, pl.ds(row, 1), :] = value[ROWS - 1 :]


def flags(seam_ref):
    tile = lax.axis_index("tile")
    return seam_ref[0, pl.ds(tile, 1), :] == 1, seam_ref[1, pl.ds(tile, 1), :] == 1


def start_kernel(f_hbm, mf_hbm, cy_hbm, code_hbm, cx_hbm, out_ref, mf_ref, cy_ref, code_ref, cx_ref, sems):
    copies = [
        pltpu.make_async_copy(source, target, sems.at[i])
        for i, (source, target) in enumerate(
            (
                (f_hbm.at[: f_hbm.shape[0] // 2, 0], out_ref[0]),
                (f_hbm.at[f_hbm.shape[0] // 2 :, 0], out_ref[1]),
                (mf_hbm, mf_ref),
                (cy_hbm, cy_ref),
                (code_hbm, code_ref),
                (cx_hbm, cx_ref),
            )
        )
    ]
    for copy in copies:
        copy.start()
    for copy in copies:
        copy.wait()


def lower_kernel(f_ref, mf_ref, cy_ref, code_ref, v_ref, first_ref, last_ref, top_ref):
    sectors, levels, columns, width = f_ref.shape
    tiles, strips = width // LANES, columns // ROWS

    def level(k, _):
        mf = mf_ref[k].astype(jnp.float32)
        cy = cy_ref[k].astype(jnp.float32)
        codes = code_ref[k]
        for xt in range(strips):
            factors = second_weights(cy, codes, 3, xt, tiles)
            rows = slice(xt * ROWS, (xt + 1) * ROWS)
            for s in range(sectors):
                parts = []
                for j in range(tiles):
                    lanes = slice(j * LANES, (j + 1) * LANES)
                    here = f_ref[s, k, rows, lanes]
                    upper = f_ref[s, k + 1, rows, lanes]
                    parts.append(here + cut(mf, xt, j) * (upper - here))
                for j, value in enumerate(second_sweep(parts, factors)):
                    store_padded(v_ref, (k,), s, j, xt, value)
                    store_rims(first_ref, last_ref, k * sectors + s, j, xt, strips - 1, value)
        return 0

    lax.fori_loop(0, levels - 1, level, 0)
    top_ref[...] = f_ref[:, levels - 1]


def first_weights(cx, codes, bit, xt, j):
    ahead, back = weights(cut(cx, xt, j), cut(codes, xt, j), bit)
    return ahead, back, (1.0 - ahead) - back


def ends_kernel(
    v_ref, inner_ref, left_ref, right_ref, seam_ref, cx_ref, code_ref, here_ref, above_ref,
    mf_ref, cy_ref,
    out_ref, top_ref, first_ref, last_ref,
    lrow_ref, rrow_ref,
):
    _, sectors, tiles, _, _ = v_ref.shape
    columns = here_ref.shape[1]
    strips = columns // ROWS
    flip_left, flip_right = flags(seam_ref)
    turned(left_ref.at[:, :ROWS], flip_left, lrow_ref)
    turned(right_ref.at[:, :ROWS], flip_right, rrow_ref)
    cx = cx_ref[0].astype(jnp.float32)
    codes = code_ref[0]
    for s in range(sectors):
        for j in range(tiles):
            lanes = slice(j * LANES, (j + 1) * LANES)
            half, at = half_of(out_ref, s)
            half[at, ROWS : columns - ROWS, lanes] = inner_ref[s, j, ROWS : columns - ROWS]
    for xt in (0, strips - 1):
        for j in range(tiles):
            factors = first_weights(cx, codes, 2, xt, j)
            for s in range(sectors):
                value = first_sweep(
                    lambda s, j, start: v_ref[0, s, j, start : start + ROWS, :],
                    s, j, xt, strips - 1, factors,
                    lambda s, j: lrow_ref[j, s : s + 1, :],
                    lambda s, j: rrow_ref[j, s : s + 1, :],
                )
                half, at = half_of(out_ref, s)
                half[at, xt * ROWS : (xt + 1) * ROWS, j * LANES : (j + 1) * LANES] = value

    level = mf_ref.shape[0] - 1
    at_top = lax.axis_index("lev") == lax.axis_size("lev") - 1
    mf = mf_ref[level].astype(jnp.float32)
    cy = cy_ref[level].astype(jnp.float32)
    codes = code_ref[level]
    for xt in range(strips):
        factors = second_weights(cy, codes, 3, xt, tiles)
        rows = slice(xt * ROWS, (xt + 1) * ROWS)
        for s in range(sectors):
            parts = []
            for j in range(tiles):
                lanes = slice(j * LANES, (j + 1) * LANES)
                here = here_ref[s, rows, lanes]
                half, at = half_of(above_ref, s)
                upper = jnp.where(at_top, here, half[at, rows, lanes])
                parts.append(here + cut(mf, xt, j) * (upper - here))
            for j, value in enumerate(second_sweep(parts, factors)):
                store_padded(top_ref, (), s, j, xt, value)
                store_rims(first_ref, last_ref, s, j, xt, strips - 1, value)


def middle_levels(
    chosen, v_ref, lrow_ref, rrow_ref, cx_ref, mf_ref, cy_ref, code_ref, out_ref, a_ref, rims=None
):
    below, sectors, tiles, padded, _ = v_ref.shape
    strips = (padded - 2 * ROWS) // ROWS

    def level(k, _):
        cx = cx_ref[k + 1].astype(jnp.float32)
        mf = mf_ref[k].astype(jnp.float32)
        cy = cy_ref[k].astype(jnp.float32)
        codes_x = code_ref[k + 1]
        codes_y = code_ref[k]
        slot = lax.rem(k, 2)
        for xt in chosen:
            along = [first_weights(cx, codes_x, 2, xt, j) for j in range(tiles)]
            across = second_weights(cy, codes_y, 1, xt, tiles)
            rows = slice(xt * ROWS, (xt + 1) * ROWS)
            for s in range(sectors):
                parts = []
                for j in range(tiles):
                    upper = first_sweep(
                        lambda s, j, start: v_ref[k + 1, s, j, start : start + ROWS, :],
                        s, j, xt, strips - 1, along[j],
                        lambda s, j: lrow_ref[j, pl.ds((k + 1) * sectors + s, 1), :],
                        lambda s, j: rrow_ref[j, pl.ds((k + 1) * sectors + s, 1), :],
                    )
                    here = a_ref[slot, s, j, rows, :]
                    a_ref[1 - slot, s, j, rows, :] = upper
                    parts.append(here + cut(mf, xt, j) * (upper - here))
                for j, value in enumerate(second_sweep(parts, across)):
                    store_padded(out_ref, (k,), s, j, xt, value)
                    if rims is not None:
                        store_rims(*rims, k * sectors + s, j, xt, strips - 1, value)
        return 0

    lax.fori_loop(0, below - 1, level, 0)


def inner_middle_kernel(
    v_ref, cx_ref, mf_ref, cy_ref, code_ref, out_ref, lowest_ref, top_ref, a_ref
):
    below, sectors, tiles, padded, _ = v_ref.shape
    strips = (padded - 2 * ROWS) // ROWS
    cx = cx_ref[0].astype(jnp.float32)
    for xt in range(1, strips - 1):
        for j in range(tiles):
            factors = first_weights(cx, code_ref[0], 2, xt, j)
            for s in range(sectors):
                value = first_sweep(
                    lambda s, j, start: v_ref[0, s, j, start : start + ROWS, :],
                    s, j, xt, strips - 1, factors, None, None,
                )
                a_ref[0, s, j, xt * ROWS : (xt + 1) * ROWS, :] = value
                lowest_ref[s, j, xt * ROWS : (xt + 1) * ROWS, :] = value
    middle_levels(
        range(1, strips - 1), v_ref, None, None, cx_ref, mf_ref, cy_ref, code_ref, out_ref, a_ref
    )
    inner = slice(ROWS, (strips - 1) * ROWS)
    top_ref[:, :, inner] = a_ref[(below - 1) % 2, :, :, inner]


def outer_middle_kernel(
    v_ref, inner_ref, inner_top_ref, left_ref, right_ref, lowest_ref, seam_ref,
    cx_ref, mf_ref, cy_ref, code_ref,
    out_ref, first_ref, last_ref, top_ref,
    lrow_ref, rrow_ref, a_ref,
):
    below, sectors, tiles, padded, _ = v_ref.shape
    strips = (padded - 2 * ROWS) // ROWS
    ends = (0, strips - 1)
    flip_left, flip_right = flags(seam_ref)
    turned(left_ref, flip_left, lrow_ref)
    turned(right_ref, flip_right, rrow_ref)
    for s in range(sectors):
        for j in range(tiles):
            for xt in ends:
                rows = slice(xt * ROWS, (xt + 1) * ROWS)
                half, at = half_of(lowest_ref, s)
                a_ref[0, s, j, rows] = half[at, rows, j * LANES : (j + 1) * LANES]
    middle_levels(
        ends, v_ref, lrow_ref, rrow_ref, cx_ref, mf_ref, cy_ref, code_ref, out_ref, a_ref,
        (first_ref, last_ref),
    )
    for xt in ends:
        rows = slice(xt * ROWS, (xt + 1) * ROWS)
        top_ref[:, :, rows] = a_ref[(below - 1) % 2, :, :, rows]
    inner = slice(ROWS, (strips - 1) * ROWS)
    top_ref[:, :, inner] = inner_top_ref[:, :, inner]
    inner = slice(2 * ROWS, strips * ROWS)

    def copy(k, _):
        out_ref[k, :, :, inner] = inner_ref[k, :, :, inner]
        return 0

    lax.fori_loop(0, below - 1, copy, 0)


def second_last_kernel(
    vt_ref, left_ref, right_ref, lower_ref, first_in, last_in, seam_ref, cx_ref, mf_ref, cy_ref, code_ref,
    out_ref, first_ref, last_ref, top_ref,
    lrow_ref, rrow_ref,
):
    sectors, tiles, padded, _ = vt_ref.shape
    strips = (padded - 2 * ROWS) // ROWS
    top = mf_ref.shape[0] - 1
    done = first_in.shape[1]
    flip_left, flip_right = flags(seam_ref)
    turned(left_ref, flip_left, lrow_ref)
    turned(right_ref, flip_right, rrow_ref)
    first_ref[:, :done] = first_in[...]
    last_ref[:, :done] = last_in[...]
    cx = cx_ref[top].astype(jnp.float32)
    mf = mf_ref[top - 1].astype(jnp.float32)
    cy = cy_ref[top - 1].astype(jnp.float32)
    for xt in range(strips):
        along = [first_weights(cx, code_ref[top], 2, xt, j) for j in range(tiles)]
        across = second_weights(cy, code_ref[top - 1], 1, xt, tiles)
        rows = slice(xt * ROWS, (xt + 1) * ROWS)
        for s in range(sectors):
            parts = []
            for j in range(tiles):
                upper = first_sweep(
                    lambda s, j, start: vt_ref[s, j, start : start + ROWS, :],
                    s, j, xt, strips - 1, along[j],
                    lambda s, j: lrow_ref[j, s : s + 1, :],
                    lambda s, j: rrow_ref[j, s : s + 1, :],
                )
                top_ref[s, j, rows, :] = upper
                here = lower_ref[s, j, rows, :]
                parts.append(here + cut(mf, xt, j) * (upper - here))
            for j, value in enumerate(second_sweep(parts, across)):
                store_padded(out_ref, (), s, j, xt, value)
                store_rims(first_ref, last_ref, done + s, j, xt, strips - 1, value)


def highest_kernel(here_ref, above_ref, mf_ref, cy_ref, code_ref, out_ref, first_ref, last_ref):
    sectors, tiles, columns, _ = here_ref.shape
    strips = columns // ROWS
    top = mf_ref.shape[0] - 1
    at_top = lax.axis_index("lev") == lax.axis_size("lev") - 1
    mf = mf_ref[top].astype(jnp.float32)
    cy = cy_ref[top].astype(jnp.float32)
    for xt in range(strips):
        across = second_weights(cy, code_ref[top], 1, xt, tiles)
        rows = slice(xt * ROWS, (xt + 1) * ROWS)
        for s in range(sectors):
            parts = []
            for j in range(tiles):
                here = here_ref[s, j, rows, :]
                half, at = half_of(above_ref, s)
                upper = half[at, rows, j * LANES : (j + 1) * LANES]
                upper = jnp.where(at_top, here, upper)
                parts.append(here + cut(mf, xt, j) * (upper - here))
            for j, value in enumerate(second_sweep(parts, across)):
                store_padded(out_ref, (), s, j, xt, value)
                store_rims(first_ref, last_ref, s, j, xt, strips - 1, value)


def final_level(
    k, chosen, strips, field, left_row, right_row, refs, out_ref, sens_ref, start_sum
):
    cx_ref, code_ref, weight_ref, share_ref = refs
    sectors, _, width = share_ref.shape
    cx = cx_ref[k].astype(jnp.float32)
    codes = code_ref[k]
    factor = weight_ref[pl.ds(k, 1), :]
    for xt in chosen:
        rows = slice(xt * ROWS, (xt + 1) * ROWS)
        for j in range(width // LANES):
            lanes = slice(j * LANES, (j + 1) * LANES)
            factors = first_weights(cx, codes, 0, xt, j)
            total = 0.0
            for s in range(sectors):
                value = first_sweep(field, s, j, xt, strips - 1, factors, left_row, right_row)
                out_ref[k, s, rows, lanes] = value
                total = total + share_ref[s, rows, lanes] * value
            if start_sum:
                sens_ref[rows, lanes] = factor * total
            else:
                sens_ref[rows, lanes] += factor * total


def inner_final_kernel(
    v_ref, vs_ref, cx_ref, code_ref, weight_ref, share_ref, out_hbm, sens_ref, out_ref, sems
):
    below, _, _, padded, _ = v_ref.shape
    strips = (padded - 2 * ROWS) // ROWS
    refs = (cx_ref, code_ref, weight_ref, share_ref)
    inner = pl.ds(ROWS, (strips - 2) * ROWS)

    def send(k):
        return pltpu.make_async_copy(out_ref.at[k, :, inner], out_hbm.at[:, k, inner], sems.at[k])

    final_level(
        below, range(1, strips - 1), strips,
        lambda s, j, start: vs_ref[s, j, start : start + ROWS, :],
        None, None, refs, out_ref, sens_ref, True,
    )
    send(below).start()

    def step(k, _):
        final_level(
            k, range(1, strips - 1), strips,
            lambda s, j, start: v_ref[k, s, j, start : start + ROWS, :],
            None, None, refs, out_ref, sens_ref, False,
        )
        send(k).start()
        return 0

    lax.fori_loop(0, below, step, 0)
    for k in range(below + 1):
        send(k).wait()


def outer_final_kernel(
    v_ref, vs_ref, vt_ref, left_ref, right_ref, left_top_ref, right_top_ref, seam_ref,
    cx_ref, code_ref, weight_ref, share_ref, inner_ref, done_hbm,
    out_hbm, piece_ref,
    lrow_ref, rrow_ref, ltop_ref, rtop_ref, out_ref, sens_ref, flat_ref, sems,
):
    below, sectors, tiles, padded, _ = v_ref.shape
    strips = (padded - 2 * ROWS) // ROWS
    ends = (0, strips - 1)
    refs = (cx_ref, code_ref, weight_ref, share_ref)
    flip_left, flip_right = flags(seam_ref)
    turned(left_ref, flip_left, lrow_ref)
    turned(right_ref, flip_right, rrow_ref)
    turned(left_top_ref, flip_left, ltop_ref)
    turned(right_top_ref, flip_right, rtop_ref)

    def send(k, i):
        rows = pl.ds(ends[i] * ROWS, ROWS)
        return pltpu.make_async_copy(out_ref.at[k, :, rows], out_hbm.at[:, k, rows], sems.at[i, k])

    send_top = pltpu.make_async_copy(
        out_ref.at[below + 1], out_hbm.at[:, below + 1], sems.at[0, below + 1]
    )
    final_level(
        below + 1, range(strips), strips,
        lambda s, j, start: vt_ref[s, j, start : start + ROWS, :],
        lambda s, j: ltop_ref[j, s : s + 1, :],
        lambda s, j: rtop_ref[j, s : s + 1, :],
        refs, out_ref, sens_ref, True,
    )
    send_top.start()
    final_level(
        below, ends, strips,
        lambda s, j, start: vs_ref[s, j, start : start + ROWS, :],
        lambda s, j: lrow_ref[j, below * sectors + s : below * sectors + s + 1, :],
        lambda s, j: rrow_ref[j, below * sectors + s : below * sectors + s + 1, :],
        refs, out_ref, sens_ref, False,
    )
    for i in range(2):
        send(below, i).start()

    def step(k, _):
        final_level(
            k, ends, strips,
            lambda s, j, start: v_ref[k, s, j, start : start + ROWS, :],
            lambda s, j: lrow_ref[j, pl.ds(k * sectors + s, 1), :],
            lambda s, j: rrow_ref[j, pl.ds(k * sectors + s, 1), :],
            refs, out_ref, sens_ref, False,
        )
        for i in range(2):
            send(k, i).start()
        return 0

    lax.fori_loop(0, below, step, 0)
    inner = slice(ROWS, (strips - 1) * ROWS)
    sens_ref[inner] += inner_ref[inner]
    if len(piece_ref.shape) == 2:
        piece_ref[...] = sens_ref[...]
    else:
        owners, group, copies, depth, _ = piece_ref.shape
        share = strips * ROWS * tiles // owners
        for xt in range(strips):
            for j in range(tiles):
                value = sens_ref[xt * ROWS : (xt + 1) * ROWS, j * LANES : (j + 1) * LANES]
                flat_ref[pl.ds(xt * ROWS * tiles + j, ROWS, stride=tiles), :] = value
        for o in range(owners):
            for piece in range(group):
                start = piece * depth
                used = max(0, min(depth, share - start))
                value = jnp.zeros((depth, LANES), jnp.float32)
                if used:
                    start += o * share
                    value = flat_ref[start : start + depth, :]
                    if used < depth:
                        line = lax.broadcasted_iota(jnp.int32, (depth, LANES), 0)
                        value = jnp.where(line < used, value, 0.0)
                for i in range(copies):
                    piece_ref[o, piece, i] = value
    send_top.wait()
    for k in range(below + 1):
        for i in range(2):
            send(k, i).wait()


def scatter_kernel(cells_ref, *refs):
    *value_refs, out_ref = refs
    rows, lanes = out_ref.shape
    group, owners, depth, _ = cells_ref.shape
    rank = lax.axis_index("lev")
    half = jnp.bfloat16
    zero, one = jnp.zeros((), half), jnp.ones((), half)
    iota = lax.broadcasted_iota(jnp.int32, (lanes, lanes), 0).astype(jnp.float32).astype(half)
    total = jnp.zeros((2 * lanes, lanes), jnp.float32)
    lines = [(i, o, r) for i in range(group) for o in range(owners) for r in range(depth)]
    wide = 8

    def spread(row):
        return jnp.broadcast_to(row, (lanes, lanes)).astype(half)

    for start in range(0, len(lines), wide):
        lefts, rights = [], []
        for part, owner, line in lines[start : start + wide]:
            cells = cells_ref[jnp.bitwise_xor(rank, part), owner, line : line + 1, :]
            value = value_refs[part][owner, line : line + 1, :]
            coarse = value.astype(half).astype(jnp.float32)
            high = spread(jnp.right_shift(cells, 7).astype(jnp.float32)) == iota
            low = spread(jnp.bitwise_and(cells, 127).astype(jnp.float32)) == iota
            lefts.append(
                jnp.concatenate(
                    [
                        jnp.where(high, spread(coarse), zero),
                        jnp.where(high, spread(value - coarse), zero),
                    ],
                    axis=0,
                )
            )
            rights.append(jnp.where(low, one, zero))
        total += lax.dot_general(
            jnp.concatenate(lefts, axis=1),
            jnp.concatenate(rights, axis=1),
            (((1,), (1,)), ((), ())),
            preferred_element_type=jnp.float32,
        )
    out_ref[...] = total[:rows] + total[lanes : lanes + rows]


def exchanged(value, axis, apart):
    count = lax.axis_size(axis)
    return lax.ppermute(value, axis, [(i, i ^ apart) for i in range(count)])


def remapped(pieces, flux_cell):
    owners, share = flux_cell.shape
    _, group, copies, depth, _ = pieces.shape
    sent = pieces.reshape(-1, depth, LANES)
    arrived = lax.all_to_all(
        sent, ("tile", "lev", "sec"), split_axis=0, concat_axis=0, tiled=True
    )
    own = jnp.sum(arrived.reshape(owners, group * copies, depth, LANES), axis=1)
    parts = [own] + [exchanged(own, "lev", d) for d in range(1, group)]
    cells = jnp.pad(flux_cell, ((0, 0), (0, group * depth * LANES - share)))
    cells = cells.reshape(owners, group, depth, LANES).transpose(1, 0, 2, 3)
    out = call(
        scatter_kernel, f32(FL_DEV // LANES, LANES), [VM] * (group + 1), VM, (cells, *parts)
    )
    return out.reshape(-1)


def around(first, last):
    count = lax.axis_size("tile")
    up = [(i, (i + 1) % count) for i in range(count)]
    down = [(j, i) for i, j in up]
    return lax.ppermute(last, "tile", up), lax.ppermute(first, "tile", down)


def from_above(halves):
    count = lax.axis_size("lev")
    return tuple(lax.ppermute(half, "lev", [(i + 1, i) for i in range(count - 1)]) for half in halves)


def shards(
    forcing, courant_x, courant_y, mass_flux, limiter_code, seam_code, level_weight, sector_share, flux_cell
):
    sectors, levels, columns, width = forcing.shape
    tiles, below = width // LANES, levels - 1
    padded = columns + 2 * ROWS
    field = kept(below, sectors, tiles, padded, LANES)
    field_top = kept(sectors, tiles, padded, LANES)
    plane = kept(sectors, columns, width)
    halves = (kept(sectors // 2, columns, width),) * 2
    rim = kept(tiles, below * sectors, LANES)
    rim_top = kept(tiles, sectors, LANES)
    rim_next = kept(tiles, (below - 1) * sectors, LANES)
    rim_scratch = pltpu.VMEM((tiles, below * sectors, LANES), jnp.float32)

    seam = jnp.broadcast_to(seam_code.T[:, :, None], (*seam_code.T.shape, LANES))
    weight = jnp.broadcast_to(level_weight[:, None], (levels, LANES))

    narrow = pltpu.VMEM((levels, columns, width), jnp.bfloat16)
    lowest, mass_flux, courant_y, limiter_code, courant_x = call(
        start_kernel,
        (halves, narrow, narrow, pltpu.VMEM((levels, columns, width), jnp.int32), narrow),
        [HBM] * 5,
        [VM] * 5,
        in_hbm(forcing, mass_flux, courant_y, limiter_code, courant_x),
        [pltpu.SemaphoreType.DMA((6,))],
    )
    above = from_above(lowest)
    v, first, last, top = call(
        lower_kernel,
        (field, rim, rim, plane),
        [VM] * 4,
        [VM] * 4,
        (forcing, mass_flux, courant_y, limiter_code),
    )
    left, right = around(first, last)
    lines = kept(sectors, tiles, columns, LANES)
    inner_field = kept(below - 1, sectors, tiles, padded, LANES)
    a_scratch = pltpu.VMEM((2, sectors, tiles, columns, LANES), jnp.float32)
    inner, inner_lowest, inner_top = call(
        inner_middle_kernel,
        (inner_field, lines, lines),
        [VM] * 5,
        [VM] * 3,
        (v, courant_x, mass_flux, courant_y, limiter_code),
        [a_scratch],
    )
    lowest, vt, first_top, last_top = call(
        ends_kernel,
        (halves, field_top, rim_top, rim_top),
        [VM] * 11,
        [VM] * 4,
        (
            v, inner_lowest, left, right, seam, courant_x, limiter_code, top, above,
            mass_flux, courant_y,
        ),
        [pltpu.VMEM((tiles, ROWS, LANES), jnp.float32)] * 2,
    )
    above = from_above(lowest)
    left_top, right_top = around(first_top, last_top)

    v, first, last, top = call(
        outer_middle_kernel,
        (inner_field, rim_next, rim_next, lines),
        [VM] * 11,
        [VM] * 4,
        (
            v, inner, inner_top, left, right, lowest, seam,
            courant_x, mass_flux, courant_y, limiter_code,
        ),
        [rim_scratch, rim_scratch, a_scratch],
    )
    vs, first, last, top = call(
        second_last_kernel,
        (field_top, rim, rim, kept(sectors, tiles, columns, LANES)),
        [VM] * 11,
        [VM] * 4,
        (
            vt, left_top, right_top, top, first, last, seam,
            courant_x, mass_flux, courant_y, limiter_code,
        ),
        [pltpu.VMEM((tiles, sectors, LANES), jnp.float32)] * 2,
    )
    left, right = around(first, last)
    vt, first_top, last_top = call(
        highest_kernel,
        (field_top, rim_top, rim_top),
        [VM] * 5,
        [VM] * 3,
        (top, above, mass_flux, courant_y, limiter_code),
    )
    left_top, right_top = around(first_top, last_top)

    owners, share = flux_cell.shape
    group, copies = lax.axis_size("lev"), lax.axis_size("sec")
    depth = -(-share // (group * LANES))
    aligned = share % LANES == 0
    packed = (owners, group, copies, depth, LANES)
    stage = pltpu.VMEM((levels, sectors, columns, width), jnp.float32)
    adjoint, inner = call(
        inner_final_kernel,
        (f32(*forcing.shape), kept(columns, width)),
        [VM] * 6,
        [HBM, VM],
        (v, vs, courant_x, limiter_code, weight, sector_share),
        [stage, pltpu.SemaphoreType.DMA((levels,))],
    )
    adjoint, pieces = call(
        outer_final_kernel,
        (f32(*forcing.shape), f32(*packed) if aligned else f32(columns, width)),
        [VM] * 13 + [HBM],
        [HBM, VM],
        (
            v, vs, vt, left, right, left_top, right_top, seam,
            courant_x, limiter_code, weight, sector_share, inner, adjoint,
        ),
        [
            rim_scratch, rim_scratch,
            pltpu.VMEM((tiles, sectors, LANES), jnp.float32),
            pltpu.VMEM((tiles, sectors, LANES), jnp.float32),
            stage,
            pltpu.VMEM((columns, width), jnp.float32),
            pltpu.VMEM((columns * tiles + ROWS, LANES), jnp.float32),
            pltpu.SemaphoreType.DMA((2, levels)),
        ],
        aliases={13: 0},
    )
    if not aligned:
        pieces = jnp.pad(
            pieces.reshape(owners, share), ((0, 0), (0, group * depth * LANES - share))
        ).reshape(owners, group, 1, depth, LANES)
        pieces = jnp.broadcast_to(pieces, packed)
    flux_cell, pieces = lax.optimization_barrier((flux_cell, pieces))
    return (adjoint, remapped(pieces, flux_cell))


def solution(mesh):
    placed = (
        P("sec", "lev", "tile", None),
        P("lev", "tile", None),
        P("lev", "tile", None),
        P("lev", "tile", None),
        P("lev", "tile", None),
        P(),
        P("lev"),
        P("sec", "tile", None),
        P("tile", None),
    )
    return jax.shard_map(
        shards,
        mesh=mesh,
        in_specs=placed,
        out_specs=(P("sec", "lev", "tile", None), P("tile")),
        check_vma=False,
    )
```

```python
import functools

import jax
import jax.numpy as jnp
from jax import lax
from jax.experimental import pallas as pl
from jax.experimental.pallas import tpu as pltpu
from jax.sharding import PartitionSpec as P

FL_DEV = 15360
LANES = 128
ROWS = 8
MIB = 2**20
VM = pl.BlockSpec(memory_space=pltpu.VMEM)
HBM = pl.BlockSpec(memory_space=pltpu.HBM)


def call(kernel, out_shape, in_specs, out_specs, operands, scratch=(), mib=16, aliases={}):
    return pl.pallas_call(
        kernel,
        out_shape=out_shape,
        in_specs=in_specs,
        out_specs=out_specs,
        scratch_shapes=list(scratch),
        input_output_aliases=aliases,
        cost_estimate=pl.CostEstimate(flops=1, transcendentals=0, bytes_accessed=1),
        compiler_params=pltpu.CompilerParams(vmem_limit_bytes=mib * MIB),
    )(*operands)


def in_hbm(*arrays):
    return tuple(pltpu.with_memory_space_constraint(a, pltpu.HBM) for a in arrays)


def kept(*shape):
    return pltpu.VMEM(shape, jnp.float32)


def f32(*shape):
    return jax.ShapeDtypeStruct(shape, jnp.float32)


def cut(value, xt, j):
    return value[xt * ROWS : (xt + 1) * ROWS, j * LANES : (j + 1) * LANES]


def weights(courant, codes, bit):
    size = jnp.abs(courant)
    half = (0.5 * size) * (1.0 - size)
    limited = jnp.where(jnp.bitwise_and(codes, 1 << bit) != 0, half, 0.0)
    ahead = jnp.maximum(courant, 0.0) - limited
    back = jnp.maximum(-courant, 0.0) - limited
    return ahead, back


def second_weights(cy, codes, bit, xt, tiles):
    lane = lax.broadcasted_iota(jnp.int32, (ROWS, LANES), 1)
    out = []
    for j in range(tiles):
        ahead, back = weights(cut(cy, xt, j), cut(codes, xt, j), bit)
        if j == 0:
            back = jnp.where(lane == 0, 0.0, back)
        if j == tiles - 1:
            ahead = jnp.where(lane == LANES - 1, 0.0, ahead)
        out.append((ahead, back, (1.0 - ahead) - back))
    return out


def second_sweep(parts, factors):
    lane = lax.broadcasted_iota(jnp.int32, (ROWS, LANES), 1)
    tiles = len(parts)
    later = [pltpu.roll(part, LANES - 1, 1) for part in parts]
    sooner = [pltpu.roll(part, 1, 1) for part in parts]
    out = []
    for j in range(tiles):
        following, previous = later[j], sooner[j]
        if j + 1 < tiles:
            following = jnp.where(lane == LANES - 1, later[j + 1], following)
        if j > 0:
            previous = jnp.where(lane == 0, sooner[j - 1], previous)
        ahead, back, own = factors[j]
        out.append(own * parts[j] + ahead * following + back * previous)
    return out


def first_sweep(field, s, j, xt, factors, before=None, after=None):
    start = ROWS * (xt + 1)
    sub = lax.broadcasted_iota(jnp.int32, (ROWS, LANES), 0)
    own_value = field(s, j, start)
    following = field(s, j, start + 1)
    previous = field(s, j, start - 1)
    if before is not None:
        previous = jnp.where(sub == 0, before(s, j), previous)
    if after is not None:
        following = jnp.where(sub == ROWS - 1, after(s, j), following)
    ahead, back, own = factors
    return own * own_value + ahead * following + back * previous


def rim_rows(xt, last, left_row, right_row):
    return (left_row if xt == 0 else None, right_row if xt == last else None)


def turned(source_ref, flag, target_ref):
    tiles, rows, _ = source_ref.shape
    for j in range(tiles):
        for start in range(0, rows, ROWS):
            count = min(ROWS, rows - start)
            index = (LANES - 1) - lax.broadcasted_iota(jnp.int32, (count, LANES), 1)
            straight = source_ref[j, start : start + count, :]
            other = source_ref[tiles - 1 - j, start : start + count, :]
            mirrored = jnp.take_along_axis(other, index, axis=1, mode="promise_in_bounds")
            target_ref[j, start : start + count, :] = jnp.where(flag, mirrored, straight)


def store_padded(ref, index, s, j, xt, value):
    start = ROWS * (xt + 1)
    ref[(*index, s, j, slice(start, start + ROWS), slice(None))] = value


def store_rims(first_ref, last_ref, row, j, xt, last, value):
    if xt == 0:
        first_ref[j, pl.ds(row, 1), :] = value[:1]
    if xt == last:
        last_ref[j, pl.ds(row, 1), :] = value[ROWS - 1 :]


def flags(seam_ref):
    tile = lax.axis_index("tile")
    return seam_ref[0, pl.ds(tile, 1), :] == 1, seam_ref[1, pl.ds(tile, 1), :] == 1


def start_kernel(f_hbm, mf_hbm, cy_hbm, code_hbm, cx_hbm, out_ref, mf_ref, cy_ref, code_ref, cx_ref, sems):
    copies = [
        pltpu.make_async_copy(source, target, sems.at[i])
        for i, (source, target) in enumerate(
            (
                (f_hbm.at[:, 0], out_ref),
                (mf_hbm, mf_ref),
                (cy_hbm, cy_ref),
                (code_hbm, code_ref),
                (cx_hbm, cx_ref),
            )
        )
    ]
    for copy in copies:
        copy.start()
    for copy in copies:
        copy.wait()


def lower_kernel(f_ref, mf_ref, cy_ref, code_ref, v_ref, first_ref, last_ref, top_ref):
    sectors, levels, columns, width = f_ref.shape
    tiles, strips = width // LANES, columns // ROWS

    def level(k, _):
        mf = mf_ref[k].astype(jnp.float32)
        cy = cy_ref[k].astype(jnp.float32)
        codes = code_ref[k]
        for xt in range(strips):
            factors = second_weights(cy, codes, 3, xt, tiles)
            rows = slice(xt * ROWS, (xt + 1) * ROWS)
            for s in range(sectors):
                parts = []
                for j in range(tiles):
                    lanes = slice(j * LANES, (j + 1) * LANES)
                    here = f_ref[s, k, rows, lanes]
                    upper = f_ref[s, k + 1, rows, lanes]
                    parts.append(here + cut(mf, xt, j) * (upper - here))
                for j, value in enumerate(second_sweep(parts, factors)):
                    store_padded(v_ref, (k,), s, j, xt, value)
                    store_rims(first_ref, last_ref, k * sectors + s, j, xt, strips - 1, value)
        return 0

    lax.fori_loop(0, levels - 1, level, 0)
    top_ref[...] = f_ref[:, levels - 1]


def first_weights(cx, codes, bit, xt, j):
    ahead, back = weights(cut(cx, xt, j), cut(codes, xt, j), bit)
    return ahead, back, (1.0 - ahead) - back


def ends_kernel(
    v_ref, inner_ref, left_ref, right_ref, seam_ref, cx_ref, code_ref, here_ref, above_ref,
    mf_ref, cy_ref,
    out_ref, top_ref, first_ref, last_ref,
    lrow_ref, rrow_ref,
):
    _, sectors, tiles, _, _ = v_ref.shape
    columns = out_ref.shape[1]
    strips = columns // ROWS
    flip_left, flip_right = flags(seam_ref)
    turned(left_ref.at[:, :ROWS], flip_left, lrow_ref)
    turned(right_ref.at[:, :ROWS], flip_right, rrow_ref)
    cx = cx_ref[0].astype(jnp.float32)
    codes = code_ref[0]
    for s in range(sectors):
        for j in range(tiles):
            lanes = slice(j * LANES, (j + 1) * LANES)
            out_ref[s, ROWS : columns - ROWS, lanes] = inner_ref[s, j, ROWS : columns - ROWS]
    for xt in (0, strips - 1):
        for j in range(tiles):
            factors = first_weights(cx, codes, 2, xt, j)
            for s in range(sectors):
                value = first_sweep(
                    lambda s, j, start: v_ref[0, s, j, start : start + ROWS, :],
                    s, j, xt, factors,
                    *rim_rows(
                        xt, strips - 1,
                        lambda s, j: lrow_ref[j, s : s + 1, :],
                        lambda s, j: rrow_ref[j, s : s + 1, :],
                    ),
                )
                out_ref[s, xt * ROWS : (xt + 1) * ROWS, j * LANES : (j + 1) * LANES] = value

    level = mf_ref.shape[0] - 1
    at_top = lax.axis_index("lev") == lax.axis_size("lev") - 1
    mf = mf_ref[level].astype(jnp.float32)
    cy = cy_ref[level].astype(jnp.float32)
    codes = code_ref[level]
    for xt in range(strips):
        factors = second_weights(cy, codes, 3, xt, tiles)
        rows = slice(xt * ROWS, (xt + 1) * ROWS)
        for s in range(sectors):
            parts = []
            for j in range(tiles):
                lanes = slice(j * LANES, (j + 1) * LANES)
                here = here_ref[s, rows, lanes]
                upper = jnp.where(at_top, here, above_ref[s, rows, lanes])
                parts.append(here + cut(mf, xt, j) * (upper - here))
            for j, value in enumerate(second_sweep(parts, factors)):
                store_padded(top_ref, (), s, j, xt, value)
                store_rims(first_ref, last_ref, s, j, xt, strips - 1, value)


def middle_levels(
    chosen, v_ref, lrow_ref, rrow_ref, cx_ref, mf_ref, cy_ref, code_ref, out_ref, a_ref, rims=None
):
    below, sectors, tiles, padded, _ = v_ref.shape
    strips = (padded - 2 * ROWS) // ROWS

    def level(k, _):
        cx = cx_ref[k + 1].astype(jnp.float32)
        mf = mf_ref[k].astype(jnp.float32)
        cy = cy_ref[k].astype(jnp.float32)
        codes_x = code_ref[k + 1]
        codes_y = code_ref[k]
        slot = lax.rem(k, 2)
        for xt in chosen:
            along = [first_weights(cx, codes_x, 2, xt, j) for j in range(tiles)]
            across = second_weights(cy, codes_y, 1, xt, tiles)
            rows = slice(xt * ROWS, (xt + 1) * ROWS)
            for s in range(sectors):
                parts = []
                for j in range(tiles):
                    upper = first_sweep(
                        lambda s, j, start: v_ref[k + 1, s, j, start : start + ROWS, :],
                        s, j, xt, along[j],
                        *rim_rows(
                            xt, strips - 1,
                            lambda s, j: lrow_ref[j, pl.ds((k + 1) * sectors + s, 1), :],
                            lambda s, j: rrow_ref[j, pl.ds((k + 1) * sectors + s, 1), :],
                        ),
                    )
                    here = a_ref[slot, s, j, rows, :]
                    a_ref[1 - slot, s, j, rows, :] = upper
                    parts.append(here + cut(mf, xt, j) * (upper - here))
                for j, value in enumerate(second_sweep(parts, across)):
                    store_padded(out_ref, (k,), s, j, xt, value)
                    if rims is not None:
                        store_rims(*rims, k * sectors + s, j, xt, strips - 1, value)
        return 0

    lax.fori_loop(0, below - 1, level, 0)


def inner_middle_kernel(
    v_ref, cx_ref, mf_ref, cy_ref, code_ref, out_ref, lowest_ref, top_ref, a_ref
):
    below, sectors, tiles, padded, _ = v_ref.shape
    strips = (padded - 2 * ROWS) // ROWS
    cx = cx_ref[0].astype(jnp.float32)
    for xt in range(1, strips - 1):
        for j in range(tiles):
            factors = first_weights(cx, code_ref[0], 2, xt, j)
            for s in range(sectors):
                value = first_sweep(
                    lambda s, j, start: v_ref[0, s, j, start : start + ROWS, :],
                    s, j, xt, factors,
                )
                a_ref[0, s, j, xt * ROWS : (xt + 1) * ROWS, :] = value
                lowest_ref[s, j, xt * ROWS : (xt + 1) * ROWS, :] = value
    middle_levels(
        range(1, strips - 1), v_ref, None, None, cx_ref, mf_ref, cy_ref, code_ref, out_ref, a_ref
    )
    inner = slice(ROWS, (strips - 1) * ROWS)
    top_ref[:, :, inner] = a_ref[(below - 1) % 2, :, :, inner]


def outer_middle_kernel(
    v_ref, inner_top_ref, left_ref, right_ref, lowest_ref, seam_ref,
    cx_ref, mf_ref, cy_ref, code_ref,
    out_ref, first_ref, last_ref, top_ref,
    lrow_ref, rrow_ref, a_ref,
):
    below, sectors, tiles, padded, _ = v_ref.shape
    strips = (padded - 2 * ROWS) // ROWS
    ends = (0, strips - 1)
    flip_left, flip_right = flags(seam_ref)
    turned(left_ref, flip_left, lrow_ref)
    turned(right_ref, flip_right, rrow_ref)
    for s in range(sectors):
        for j in range(tiles):
            for xt in ends:
                rows = slice(xt * ROWS, (xt + 1) * ROWS)
                a_ref[0, s, j, rows] = lowest_ref[s, rows, j * LANES : (j + 1) * LANES]
    middle_levels(
        ends, v_ref, lrow_ref, rrow_ref, cx_ref, mf_ref, cy_ref, code_ref, out_ref, a_ref,
        (first_ref, last_ref),
    )
    for xt in ends:
        rows = slice(xt * ROWS, (xt + 1) * ROWS)
        top_ref[:, :, rows] = a_ref[(below - 1) % 2, :, :, rows]
    inner = slice(ROWS, (strips - 1) * ROWS)
    top_ref[:, :, inner] = inner_top_ref[:, :, inner]


def second_last_kernel(
    vt_ref, left_ref, right_ref, lower_ref, first_in, last_in, seam_ref, cx_ref, mf_ref, cy_ref, code_ref,
    out_ref, first_ref, last_ref, top_ref,
    lrow_ref, rrow_ref,
):
    sectors, tiles, padded, _ = vt_ref.shape
    strips = (padded - 2 * ROWS) // ROWS
    top = mf_ref.shape[0] - 1
    done = first_in.shape[1]
    flip_left, flip_right = flags(seam_ref)
    turned(left_ref, flip_left, lrow_ref)
    turned(right_ref, flip_right, rrow_ref)
    first_ref[:, :done] = first_in[...]
    last_ref[:, :done] = last_in[...]
    cx = cx_ref[top].astype(jnp.float32)
    mf = mf_ref[top - 1].astype(jnp.float32)
    cy = cy_ref[top - 1].astype(jnp.float32)
    for xt in range(strips):
        along = [first_weights(cx, code_ref[top], 2, xt, j) for j in range(tiles)]
        across = second_weights(cy, code_ref[top - 1], 1, xt, tiles)
        rows = slice(xt * ROWS, (xt + 1) * ROWS)
        for s in range(sectors):
            parts = []
            for j in range(tiles):
                upper = first_sweep(
                    lambda s, j, start: vt_ref[s, j, start : start + ROWS, :],
                    s, j, xt, along[j],
                    *rim_rows(
                        xt, strips - 1,
                        lambda s, j: lrow_ref[j, s : s + 1, :],
                        lambda s, j: rrow_ref[j, s : s + 1, :],
                    ),
                )
                top_ref[s, j, rows, :] = upper
                here = lower_ref[s, j, rows, :]
                parts.append(here + cut(mf, xt, j) * (upper - here))
            for j, value in enumerate(second_sweep(parts, across)):
                store_padded(out_ref, (), s, j, xt, value)
                store_rims(first_ref, last_ref, done + s, j, xt, strips - 1, value)


def highest_kernel(
    here_ref, above_ref, mf_ref, cy_ref, code_ref, done_ref, out_ref, first_ref, last_ref
):
    sectors, tiles, columns, _ = here_ref.shape
    strips = columns // ROWS
    top = mf_ref.shape[0] - 1
    at_top = lax.axis_index("lev") == lax.axis_size("lev") - 1
    mf = mf_ref[top].astype(jnp.float32)
    cy = cy_ref[top].astype(jnp.float32)
    for xt in range(strips):
        across = second_weights(cy, code_ref[top], 1, xt, tiles)
        rows = slice(xt * ROWS, (xt + 1) * ROWS)
        for s in range(sectors):
            parts = []
            for j in range(tiles):
                here = here_ref[s, j, rows, :]
                upper = above_ref[s, rows, j * LANES : (j + 1) * LANES]
                upper = jnp.where(at_top, here, upper)
                parts.append(here + cut(mf, xt, j) * (upper - here))
            for j, value in enumerate(second_sweep(parts, across)):
                store_padded(out_ref, (), s, j, xt, value)
                store_rims(first_ref, last_ref, s, j, xt, strips - 1, value)


def final_level(k, chosen, field, rows_at, refs, out_ref, sens_ref=None, start_sum=False):
    cx_ref, code_ref, weight_ref, share_ref = refs
    sectors, _, width = share_ref.shape
    cx = cx_ref[k].astype(jnp.float32)
    codes = code_ref[k]
    factor = weight_ref[pl.ds(k, 1), :]
    for xt in chosen:
        rows = slice(xt * ROWS, (xt + 1) * ROWS)
        for j in range(width // LANES):
            lanes = slice(j * LANES, (j + 1) * LANES)
            factors = first_weights(cx, codes, 0, xt, j)
            total = 0.0
            for s in range(sectors):
                value = first_sweep(field, s, j, xt, factors, *rows_at(xt))
                out_ref[k, s, rows, lanes] = value
                if sens_ref is not None:
                    total = total + share_ref[s, rows, lanes] * value
            if sens_ref is None:
                continue
            if start_sum:
                sens_ref[rows, lanes] = factor * total
            else:
                sens_ref[rows, lanes] += factor * total


def inner_final_kernel(
    inner_ref, outer_ref, vs_ref, cx_ref, code_ref, weight_ref, share_ref,
    out_hbm, sens_ref, out_ref, sems,
):
    below, _, _, padded, _ = inner_ref.shape
    strips = (padded - 2 * ROWS) // ROWS
    refs = (cx_ref, code_ref, weight_ref, share_ref)
    inner = pl.ds(ROWS, (strips - 2) * ROWS)
    chosen = range(1, strips - 1)

    def send(k):
        return pltpu.make_async_copy(out_ref.at[k, :, inner], out_hbm.at[:, k, inner], sems.at[k])

    final_level(
        below, chosen, lambda s, j, start: vs_ref[s, j, start : start + ROWS, :],
        lambda xt: (None, None), refs, out_ref, sens_ref, True,
    )
    send(below).start()

    def step(k, _):
        low, high = 2 * ROWS - 1, strips * ROWS

        def rows_at(xt):
            return (
                (lambda s, j: outer_ref[k, s, j, low : low + 1, :]) if xt == 1 else None,
                (lambda s, j: outer_ref[k, s, j, high : high + 1, :]) if xt == strips - 2 else None,
            )

        final_level(
            k, chosen, lambda s, j, start: inner_ref[k, s, j, start : start + ROWS, :],
            rows_at, refs, out_ref, sens_ref,
        )
        send(k).start()
        return 0

    lax.fori_loop(0, below, step, 0)
    for k in range(below + 1):
        send(k).wait()


def outer_final_kernel(
    inner_ref, outer_ref, vs_ref, vt_ref, left_ref, right_ref, left_top_ref, right_top_ref, seam_ref,
    cx_ref, code_ref, weight_ref, share_ref, inner_sens_ref, done_hbm,
    out_hbm, piece_ref,
    lrow_ref, rrow_ref, ltop_ref, rtop_ref, out_ref, sens_ref, flat_ref, sems,
):
    below, sectors, tiles, padded, _ = outer_ref.shape
    strips = (padded - 2 * ROWS) // ROWS
    ends = (0, strips - 1)
    refs = (cx_ref, code_ref, weight_ref, share_ref)
    flip_left, flip_right = flags(seam_ref)
    turned(left_ref, flip_left, lrow_ref)
    turned(right_ref, flip_right, rrow_ref)
    turned(left_top_ref, flip_left, ltop_ref)
    turned(right_top_ref, flip_right, rtop_ref)

    def send(k, i):
        rows = pl.ds(ends[i] * ROWS, ROWS)
        return pltpu.make_async_copy(out_ref.at[k, :, rows], out_hbm.at[:, k, rows], sems.at[i, k])

    send_top = pltpu.make_async_copy(
        out_ref.at[below + 1], out_hbm.at[:, below + 1], sems.at[0, below + 1]
    )
    final_level(
        below + 1, range(strips), lambda s, j, start: vt_ref[s, j, start : start + ROWS, :],
        lambda xt: rim_rows(
            xt, strips - 1,
            lambda s, j: ltop_ref[j, s : s + 1, :],
            lambda s, j: rtop_ref[j, s : s + 1, :],
        ),
        refs, out_ref, sens_ref, True,
    )
    send_top.start()
    edge = below * sectors
    final_level(
        below, ends, lambda s, j, start: vs_ref[s, j, start : start + ROWS, :],
        lambda xt: rim_rows(
            xt, strips - 1,
            lambda s, j: lrow_ref[j, edge + s : edge + s + 1, :],
            lambda s, j: rrow_ref[j, edge + s : edge + s + 1, :],
        ),
        refs, out_ref,
    )
    for i in range(2):
        send(below, i).start()

    def step(k, _):
        low, high = 2 * ROWS, strips * ROWS - 1

        def rows_at(xt):
            if xt == 0:
                return (
                    lambda s, j: lrow_ref[j, pl.ds(k * sectors + s, 1), :],
                    lambda s, j: inner_ref[k, s, j, low : low + 1, :],
                )
            return (
                lambda s, j: inner_ref[k, s, j, high : high + 1, :],
                lambda s, j: rrow_ref[j, pl.ds(k * sectors + s, 1), :],
            )

        final_level(
            k, ends, lambda s, j, start: outer_ref[k, s, j, start : start + ROWS, :],
            rows_at, refs, out_ref,
        )
        for i in range(2):
            send(k, i).start()
        return 0

    lax.fori_loop(0, below, step, 0)

    places = [
        (slice(xt * ROWS, (xt + 1) * ROWS), slice(j * LANES, (j + 1) * LANES))
        for xt in ends
        for j in range(tiles)
    ]

    def add(k, sums):
        factor = weight_ref[pl.ds(k, 1), :]
        out = []
        for total, place in zip(sums, places):
            part = share_ref[(0, *place)] * out_ref[(k, 0, *place)]
            for s in range(1, sectors):
                part = part + share_ref[(s, *place)] * out_ref[(k, s, *place)]
            out.append(total + factor * part)
        return tuple(out)

    sums = lax.fori_loop(0, below + 1, add, tuple(sens_ref[place] for place in places))
    for total, place in zip(sums, places):
        sens_ref[place] = total
    inner = slice(ROWS, (strips - 1) * ROWS)
    sens_ref[inner] += inner_sens_ref[inner]
    if len(piece_ref.shape) == 2:
        piece_ref[...] = sens_ref[...]
    else:
        owners, group, copies, depth, _ = piece_ref.shape
        share = strips * ROWS * tiles // owners
        for xt in range(strips):
            for j in range(tiles):
                value = sens_ref[xt * ROWS : (xt + 1) * ROWS, j * LANES : (j + 1) * LANES]
                flat_ref[pl.ds(xt * ROWS * tiles + j, ROWS, stride=tiles), :] = value
        for o in range(owners):
            for piece in range(group):
                start = piece * depth
                used = max(0, min(depth, share - start))
                value = jnp.zeros((depth, LANES), jnp.float32)
                if used:
                    start += o * share
                    value = flat_ref[start : start + depth, :]
                    if used < depth:
                        line = lax.broadcasted_iota(jnp.int32, (depth, LANES), 0)
                        value = jnp.where(line < used, value, 0.0)
                for i in range(copies):
                    piece_ref[o, piece, i] = value
    send_top.wait()
    for k in range(below + 1):
        for i in range(2):
            send(k, i).wait()


def scatter_kernel(cells_ref, *refs):
    *value_refs, out_ref = refs
    rows, lanes = out_ref.shape
    group, owners, depth, _ = cells_ref.shape
    rank = lax.axis_index("lev")
    half = jnp.bfloat16
    zero, one = jnp.zeros((), half), jnp.ones((), half)
    tall, short = 2 * lanes, lanes // 2
    iota = lax.broadcasted_iota(jnp.int32, (tall, lanes), 0).astype(jnp.float32).astype(half)
    total = jnp.zeros((2 * short, tall), jnp.float32)
    lines = [(i, o, r) for i in range(group) for o in range(owners) for r in range(depth)]
    wide = 4

    def spread(row, count):
        return jnp.broadcast_to(row, (count, lanes)).astype(half)

    for start in range(0, len(lines), wide):
        lefts, rights = [], []
        for part, owner, line in lines[start : start + wide]:
            cells = cells_ref[jnp.bitwise_xor(rank, part), owner, line : line + 1, :]
            value = value_refs[part][owner, line : line + 1, :]
            coarse = value.astype(half).astype(jnp.float32)
            high = jnp.right_shift(cells, 8).astype(jnp.float32)
            low = jnp.bitwise_and(cells, 255).astype(jnp.float32)
            high = spread(high, short) == iota[:short]
            lefts.append(
                jnp.concatenate(
                    [
                        jnp.where(high, spread(coarse, short), zero),
                        jnp.where(high, spread(value - coarse, short), zero),
                    ],
                    axis=0,
                )
            )
            rights.append(jnp.where(spread(low, tall) == iota, one, zero))
        total += lax.dot_general(
            jnp.concatenate(lefts, axis=1),
            jnp.concatenate(rights, axis=1),
            (((1,), (1,)), ((), ())),
            preferred_element_type=jnp.float32,
        )
    total = total[:short] + total[short:]
    for i in range(2):
        out_ref[pl.ds(i, rows // 2, stride=2), :] = total[: rows // 2, i * lanes : (i + 1) * lanes]


def exchanged(value, axis, apart):
    count = lax.axis_size(axis)
    return lax.ppermute(value, axis, [(i, i ^ apart) for i in range(count)])


def remapped(pieces, flux_cell):
    owners, share = flux_cell.shape
    _, group, copies, depth, _ = pieces.shape
    sent = pieces.reshape(-1, depth, LANES)
    arrived = lax.all_to_all(
        sent, ("tile", "lev", "sec"), split_axis=0, concat_axis=0, tiled=True
    )
    own = jnp.sum(arrived.reshape(owners, group * copies, depth, LANES), axis=1)
    parts = [own] + [exchanged(own, "lev", d) for d in range(1, group)]
    cells = jnp.pad(flux_cell, ((0, 0), (0, group * depth * LANES - share)))
    cells = cells.reshape(owners, group, depth, LANES).transpose(1, 0, 2, 3)
    out = call(
        scatter_kernel, f32(FL_DEV // LANES, LANES), [VM] * (group + 1), VM, (cells, *parts)
    )
    return out.reshape(-1)


def around(first, last):
    count = lax.axis_size("tile")
    up = [(i, (i + 1) % count) for i in range(count)]
    down = [(j, i) for i, j in up]
    return lax.ppermute(last, "tile", up), lax.ppermute(first, "tile", down)


def from_above(value):
    count = lax.axis_size("lev")
    return lax.ppermute(value, "lev", [(i + 1, i) for i in range(count - 1)])


def shards(
    forcing, courant_x, courant_y, mass_flux, limiter_code, seam_code, level_weight, sector_share, flux_cell
):
    sectors, levels, columns, width = forcing.shape
    tiles, below = width // LANES, levels - 1
    padded = columns + 2 * ROWS
    field = kept(below, sectors, tiles, padded, LANES)
    field_top = kept(sectors, tiles, padded, LANES)
    plane = kept(sectors, columns, width)
    rim = kept(tiles, below * sectors, LANES)
    rim_top = kept(tiles, sectors, LANES)
    rim_next = kept(tiles, (below - 1) * sectors, LANES)
    rim_scratch = pltpu.VMEM((tiles, below * sectors, LANES), jnp.float32)

    seam = jnp.broadcast_to(seam_code.T[:, :, None], (*seam_code.T.shape, LANES))
    weight = jnp.broadcast_to(level_weight[:, None], (levels, LANES))

    narrow = pltpu.VMEM((levels, columns, width), jnp.bfloat16)
    lowest, mass_flux, courant_y, limiter_code, courant_x = call(
        start_kernel,
        (plane, narrow, narrow, pltpu.VMEM((levels, columns, width), jnp.int32), narrow),
        [HBM] * 5,
        [VM] * 5,
        in_hbm(forcing, mass_flux, courant_y, limiter_code, courant_x),
        [pltpu.SemaphoreType.DMA((5,))],
    )
    above = from_above(lowest)
    v, first, last, top = call(
        lower_kernel,
        (field, rim, rim, plane),
        [VM] * 4,
        [VM] * 4,
        (forcing, mass_flux, courant_y, limiter_code),
    )
    left, right = around(first, last)
    lines = kept(sectors, tiles, columns, LANES)
    inner_field = kept(below - 1, sectors, tiles, padded, LANES)
    a_scratch = pltpu.VMEM((2, sectors, tiles, columns, LANES), jnp.float32)
    inner, inner_lowest, inner_top = call(
        inner_middle_kernel,
        (inner_field, lines, lines),
        [VM] * 5,
        [VM] * 3,
        (v, courant_x, mass_flux, courant_y, limiter_code),
        [a_scratch],
    )
    lowest, vt, first_top, last_top = call(
        ends_kernel,
        (plane, field_top, rim_top, rim_top),
        [VM] * 11,
        [VM] * 4,
        (
            v, inner_lowest, left, right, seam, courant_x, limiter_code, top, above,
            mass_flux, courant_y,
        ),
        [pltpu.VMEM((tiles, ROWS, LANES), jnp.float32)] * 2,
    )
    above = from_above(lowest)
    left_top, right_top = around(first_top, last_top)

    outer, first, last, top = call(
        outer_middle_kernel,
        (inner_field, rim_next, rim_next, lines),
        [VM] * 10,
        [VM] * 4,
        (
            v, inner_top, left, right, lowest, seam,
            courant_x, mass_flux, courant_y, limiter_code,
        ),
        [rim_scratch, rim_scratch, a_scratch],
    )
    vs, first, last, top = call(
        second_last_kernel,
        (field_top, rim, rim, kept(sectors, tiles, columns, LANES)),
        [VM] * 11,
        [VM] * 4,
        (
            vt, left_top, right_top, top, first, last, seam,
            courant_x, mass_flux, courant_y, limiter_code,
        ),
        [pltpu.VMEM((tiles, sectors, LANES), jnp.float32)] * 2,
    )
    left, right = around(first, last)
    owners, share = flux_cell.shape
    group, copies = lax.axis_size("lev"), lax.axis_size("sec")
    depth = -(-share // (group * LANES))
    aligned = share % LANES == 0
    packed = (owners, group, copies, depth, LANES)
    stage = pltpu.VMEM((levels, sectors, columns, width), jnp.float32)
    adjoint, inner_sens = call(
        inner_final_kernel,
        (f32(*forcing.shape), kept(columns, width)),
        [VM] * 7,
        [HBM, VM],
        (inner, outer, vs, courant_x, limiter_code, weight, sector_share),
        [stage, pltpu.SemaphoreType.DMA((levels,))],
    )
    vt, first_top, last_top = call(
        highest_kernel,
        (field_top, rim_top, rim_top),
        [VM] * 6,
        [VM] * 3,
        (top, above, mass_flux, courant_y, limiter_code, inner_sens),
    )
    left_top, right_top = around(first_top, last_top)

    adjoint, pieces = call(
        outer_final_kernel,
        (f32(*forcing.shape), f32(*packed) if aligned else f32(columns, width)),
        [VM] * 14 + [HBM],
        [HBM, VM],
        (
            inner, outer, vs, vt, left, right, left_top, right_top, seam,
            courant_x, limiter_code, weight, sector_share, inner_sens, adjoint,
        ),
        [
            rim_scratch, rim_scratch,
            pltpu.VMEM((tiles, sectors, LANES), jnp.float32),
            pltpu.VMEM((tiles, sectors, LANES), jnp.float32),
            stage,
            pltpu.VMEM((columns, width), jnp.float32),
            pltpu.VMEM((columns * tiles + ROWS, LANES), jnp.float32),
            pltpu.SemaphoreType.DMA((2, levels)),
        ],
        aliases={14: 0},
    )
    if not aligned:
        pieces = jnp.pad(
            pieces.reshape(owners, share), ((0, 0), (0, group * depth * LANES - share))
        ).reshape(owners, group, 1, depth, LANES)
        pieces = jnp.broadcast_to(pieces, packed)
    flux_cell, pieces = lax.optimization_barrier((flux_cell, pieces))
    return (adjoint, remapped(pieces, flux_cell))


def solution(mesh):
    placed = (
        P("sec", "lev", "tile", None),
        P("lev", "tile", None),
        P("lev", "tile", None),
        P("lev", "tile", None),
        P("lev", "tile", None),
        P(),
        P("lev"),
        P("sec", "tile", None),
        P("tile", None),
    )
    return jax.shard_map(
        shards,
        mesh=mesh,
        in_specs=placed,
        out_specs=(P("sec", "lev", "tile", None), P("tile")),
        check_vma=False,
    )
```

```python
import functools

import jax
import jax.numpy as jnp
from jax import lax
from jax.experimental import pallas as pl
from jax.experimental.pallas import tpu as pltpu
from jax.sharding import PartitionSpec as P

FL_DEV = 15360
LANES = 128
ROWS = 8
MIB = 2**20
VM = pl.BlockSpec(memory_space=pltpu.VMEM)
HBM = pl.BlockSpec(memory_space=pltpu.HBM)


def call(kernel, out_shape, in_specs, out_specs, operands, scratch=(), mib=16, aliases={}):
    return pl.pallas_call(
        kernel,
        out_shape=out_shape,
        in_specs=in_specs,
        out_specs=out_specs,
        scratch_shapes=list(scratch),
        input_output_aliases=aliases,
        cost_estimate=pl.CostEstimate(flops=1, transcendentals=0, bytes_accessed=1),
        compiler_params=pltpu.CompilerParams(vmem_limit_bytes=mib * MIB),
    )(*operands)


def in_hbm(*arrays):
    return tuple(pltpu.with_memory_space_constraint(a, pltpu.HBM) for a in arrays)


def kept(*shape):
    return pltpu.VMEM(shape, jnp.float32)


def f32(*shape):
    return jax.ShapeDtypeStruct(shape, jnp.float32)


def cut(value, xt, j):
    return value[xt * ROWS : (xt + 1) * ROWS, j * LANES : (j + 1) * LANES]


def weights(courant, codes, bit):
    size = jnp.abs(courant)
    half = (0.5 * size) * (1.0 - size)
    limited = jnp.where(jnp.bitwise_and(codes, 1 << bit) != 0, half, 0.0)
    ahead = jnp.maximum(courant, 0.0) - limited
    back = jnp.maximum(-courant, 0.0) - limited
    return ahead, back


def second_weights(cy, codes, bit, xt, tiles):
    lane = lax.broadcasted_iota(jnp.int32, (ROWS, LANES), 1)
    out = []
    for j in range(tiles):
        ahead, back = weights(cut(cy, xt, j), cut(codes, xt, j), bit)
        if j == 0:
            back = jnp.where(lane == 0, 0.0, back)
        if j == tiles - 1:
            ahead = jnp.where(lane == LANES - 1, 0.0, ahead)
        out.append((ahead, back, (1.0 - ahead) - back))
    return out


def second_sweep(parts, factors):
    lane = lax.broadcasted_iota(jnp.int32, (ROWS, LANES), 1)
    tiles = len(parts)
    later = [pltpu.roll(part, LANES - 1, 1) for part in parts]
    sooner = [pltpu.roll(part, 1, 1) for part in parts]
    out = []
    for j in range(tiles):
        following, previous = later[j], sooner[j]
        if j + 1 < tiles:
            following = jnp.where(lane == LANES - 1, later[j + 1], following)
        if j > 0:
            previous = jnp.where(lane == 0, sooner[j - 1], previous)
        ahead, back, own = factors[j]
        out.append(own * parts[j] + ahead * following + back * previous)
    return out


def first_sweep(field, s, j, xt, factors, before=None, after=None):
    start = ROWS * (xt + 1)
    sub = lax.broadcasted_iota(jnp.int32, (ROWS, LANES), 0)
    own_value = field(s, j, start)
    following = field(s, j, start + 1)
    previous = field(s, j, start - 1)
    if before is not None:
        previous = jnp.where(sub == 0, before(s, j), previous)
    if after is not None:
        following = jnp.where(sub == ROWS - 1, after(s, j), following)
    ahead, back, own = factors
    return own * own_value + ahead * following + back * previous


def rim_rows(xt, last, left_row, right_row):
    return (left_row if xt == 0 else None, right_row if xt == last else None)


def turned(source_ref, flag, target_ref):
    tiles, rows, _ = source_ref.shape
    for j in range(tiles):
        for start in range(0, rows, ROWS):
            count = min(ROWS, rows - start)
            index = (LANES - 1) - lax.broadcasted_iota(jnp.int32, (count, LANES), 1)
            straight = source_ref[j, start : start + count, :]
            other = source_ref[tiles - 1 - j, start : start + count, :]
            mirrored = jnp.take_along_axis(other, index, axis=1, mode="promise_in_bounds")
            target_ref[j, start : start + count, :] = jnp.where(flag, mirrored, straight)


def store_padded(ref, index, s, j, xt, value):
    start = ROWS * (xt + 1)
    ref[(*index, s, j, slice(start, start + ROWS), slice(None))] = value


def store_rims(first_ref, last_ref, row, j, xt, last, value):
    if xt == 0:
        first_ref[j, pl.ds(row, 1), :] = value[:1]
    if xt == last:
        last_ref[j, pl.ds(row, 1), :] = value[ROWS - 1 :]


def flags(seam_ref):
    tile = lax.axis_index("tile")
    return seam_ref[0, pl.ds(tile, 1), :] == 1, seam_ref[1, pl.ds(tile, 1), :] == 1


def start_kernel(f_hbm, mf_hbm, cy_hbm, code_hbm, cx_hbm, out_ref, mf_ref, cy_ref, code_ref, cx_ref, sems):
    copies = [
        pltpu.make_async_copy(source, target, sems.at[i])
        for i, (source, target) in enumerate(
            (
                (f_hbm.at[:, 0], out_ref),
                (mf_hbm, mf_ref),
                (cy_hbm, cy_ref),
                (code_hbm, code_ref),
                (cx_hbm, cx_ref),
            )
        )
    ]
    for copy in copies:
        copy.start()
    for copy in copies:
        copy.wait()


def lower_kernel(f_ref, mf_ref, cy_ref, code_ref, v_ref, first_ref, last_ref, top_ref):
    sectors, levels, columns, width = f_ref.shape
    tiles, strips = width // LANES, columns // ROWS

    def level(k, _):
        mf = mf_ref[k].astype(jnp.float32)
        cy = cy_ref[k].astype(jnp.float32)
        codes = code_ref[k]
        for xt in range(strips):
            factors = second_weights(cy, codes, 3, xt, tiles)
            rows = slice(xt * ROWS, (xt + 1) * ROWS)
            for s in range(sectors):
                parts = []
                for j in range(tiles):
                    lanes = slice(j * LANES, (j + 1) * LANES)
                    here = f_ref[s, k, rows, lanes]
                    upper = f_ref[s, k + 1, rows, lanes]
                    parts.append(here + cut(mf, xt, j) * (upper - here))
                for j, value in enumerate(second_sweep(parts, factors)):
                    store_padded(v_ref, (k,), s, j, xt, value)
                    store_rims(first_ref, last_ref, k * sectors + s, j, xt, strips - 1, value)
        return 0

    lax.fori_loop(0, levels - 1, level, 0)
    top_ref[...] = f_ref[:, levels - 1]


def first_weights(cx, codes, bit, xt, j):
    ahead, back = weights(cut(cx, xt, j), cut(codes, xt, j), bit)
    return ahead, back, (1.0 - ahead) - back


def ends_kernel(
    v_ref, inner_ref, left_ref, right_ref, seam_ref, cx_ref, code_ref, here_ref, above_ref,
    mf_ref, cy_ref,
    out_ref, top_ref, first_ref, last_ref,
    lrow_ref, rrow_ref,
):
    _, sectors, tiles, _, _ = v_ref.shape
    columns = out_ref.shape[1]
    strips = columns // ROWS
    flip_left, flip_right = flags(seam_ref)
    turned(left_ref.at[:, :ROWS], flip_left, lrow_ref)
    turned(right_ref.at[:, :ROWS], flip_right, rrow_ref)
    cx = cx_ref[0].astype(jnp.float32)
    codes = code_ref[0]
    for s in range(sectors):
        for j in range(tiles):
            lanes = slice(j * LANES, (j + 1) * LANES)
            out_ref[s, ROWS : columns - ROWS, lanes] = inner_ref[s, j, ROWS : columns - ROWS]
    for xt in (0, strips - 1):
        for j in range(tiles):
            factors = first_weights(cx, codes, 2, xt, j)
            for s in range(sectors):
                value = first_sweep(
                    lambda s, j, start: v_ref[0, s, j, start : start + ROWS, :],
                    s, j, xt, factors,
                    *rim_rows(
                        xt, strips - 1,
                        lambda s, j: lrow_ref[j, s : s + 1, :],
                        lambda s, j: rrow_ref[j, s : s + 1, :],
                    ),
                )
                out_ref[s, xt * ROWS : (xt + 1) * ROWS, j * LANES : (j + 1) * LANES] = value

    level = mf_ref.shape[0] - 1
    at_top = lax.axis_index("lev") == lax.axis_size("lev") - 1
    mf = mf_ref[level].astype(jnp.float32)
    cy = cy_ref[level].astype(jnp.float32)
    codes = code_ref[level]
    for xt in range(strips):
        factors = second_weights(cy, codes, 3, xt, tiles)
        rows = slice(xt * ROWS, (xt + 1) * ROWS)
        for s in range(sectors):
            parts = []
            for j in range(tiles):
                lanes = slice(j * LANES, (j + 1) * LANES)
                here = here_ref[s, rows, lanes]
                upper = jnp.where(at_top, here, above_ref[s, rows, lanes])
                parts.append(here + cut(mf, xt, j) * (upper - here))
            for j, value in enumerate(second_sweep(parts, factors)):
                store_padded(top_ref, (), s, j, xt, value)
                store_rims(first_ref, last_ref, s, j, xt, strips - 1, value)


def middle_levels(
    chosen, v_ref, lrow_ref, rrow_ref, cx_ref, mf_ref, cy_ref, code_ref, out_ref, a_ref, rims=None
):
    below, sectors, tiles, padded, _ = v_ref.shape
    strips = (padded - 2 * ROWS) // ROWS

    def level(k, _):
        cx = cx_ref[k + 1].astype(jnp.float32)
        mf = mf_ref[k].astype(jnp.float32)
        cy = cy_ref[k].astype(jnp.float32)
        codes_x = code_ref[k + 1]
        codes_y = code_ref[k]
        slot = lax.rem(k, 2)
        for xt in chosen:
            along = [first_weights(cx, codes_x, 2, xt, j) for j in range(tiles)]
            across = second_weights(cy, codes_y, 1, xt, tiles)
            rows = slice(xt * ROWS, (xt + 1) * ROWS)
            for s in range(sectors):
                parts = []
                for j in range(tiles):
                    upper = first_sweep(
                        lambda s, j, start: v_ref[k + 1, s, j, start : start + ROWS, :],
                        s, j, xt, along[j],
                        *rim_rows(
                            xt, strips - 1,
                            lambda s, j: lrow_ref[j, pl.ds((k + 1) * sectors + s, 1), :],
                            lambda s, j: rrow_ref[j, pl.ds((k + 1) * sectors + s, 1), :],
                        ),
                    )
                    here = a_ref[slot, s, j, rows, :]
                    a_ref[1 - slot, s, j, rows, :] = upper
                    parts.append(here + cut(mf, xt, j) * (upper - here))
                for j, value in enumerate(second_sweep(parts, across)):
                    store_padded(out_ref, (k,), s, j, xt, value)
                    if rims is not None:
                        store_rims(*rims, k * sectors + s, j, xt, strips - 1, value)
        return 0

    lax.fori_loop(0, below - 1, level, 0)


def inner_middle_kernel(
    v_ref, cx_ref, mf_ref, cy_ref, code_ref, out_ref, lowest_ref, top_ref, a_ref
):
    below, sectors, tiles, padded, _ = v_ref.shape
    strips = (padded - 2 * ROWS) // ROWS
    cx = cx_ref[0].astype(jnp.float32)
    for xt in range(1, strips - 1):
        for j in range(tiles):
            factors = first_weights(cx, code_ref[0], 2, xt, j)
            for s in range(sectors):
                value = first_sweep(
                    lambda s, j, start: v_ref[0, s, j, start : start + ROWS, :],
                    s, j, xt, factors,
                )
                a_ref[0, s, j, xt * ROWS : (xt + 1) * ROWS, :] = value
                lowest_ref[s, j, xt * ROWS : (xt + 1) * ROWS, :] = value
    middle_levels(
        range(1, strips - 1), v_ref, None, None, cx_ref, mf_ref, cy_ref, code_ref, out_ref, a_ref
    )
    inner = slice(ROWS, (strips - 1) * ROWS)
    top_ref[:, :, inner] = a_ref[(below - 1) % 2, :, :, inner]


def outer_middle_kernel(
    v_ref, inner_top_ref, left_ref, right_ref, lowest_ref, seam_ref,
    cx_ref, mf_ref, cy_ref, code_ref,
    out_ref, first_ref, last_ref, top_ref,
    lrow_ref, rrow_ref, a_ref,
):
    below, sectors, tiles, padded, _ = v_ref.shape
    strips = (padded - 2 * ROWS) // ROWS
    ends = (0, strips - 1)
    flip_left, flip_right = flags(seam_ref)
    turned(left_ref, flip_left, lrow_ref)
    turned(right_ref, flip_right, rrow_ref)
    for s in range(sectors):
        for j in range(tiles):
            for xt in ends:
                rows = slice(xt * ROWS, (xt + 1) * ROWS)
                a_ref[0, s, j, rows] = lowest_ref[s, rows, j * LANES : (j + 1) * LANES]
    middle_levels(
        ends, v_ref, lrow_ref, rrow_ref, cx_ref, mf_ref, cy_ref, code_ref, out_ref, a_ref,
        (first_ref, last_ref),
    )
    for xt in ends:
        rows = slice(xt * ROWS, (xt + 1) * ROWS)
        top_ref[:, :, rows] = a_ref[(below - 1) % 2, :, :, rows]
    inner = slice(ROWS, (strips - 1) * ROWS)
    top_ref[:, :, inner] = inner_top_ref[:, :, inner]


def second_last_kernel(
    vt_ref, left_ref, right_ref, lower_ref, first_in, last_in, seam_ref, cx_ref, mf_ref, cy_ref, code_ref,
    out_ref, first_ref, last_ref, top_ref,
    lrow_ref, rrow_ref,
):
    sectors, tiles, padded, _ = vt_ref.shape
    strips = (padded - 2 * ROWS) // ROWS
    top = mf_ref.shape[0] - 1
    done = first_in.shape[1]
    flip_left, flip_right = flags(seam_ref)
    turned(left_ref, flip_left, lrow_ref)
    turned(right_ref, flip_right, rrow_ref)
    first_ref[:, :done] = first_in[...]
    last_ref[:, :done] = last_in[...]
    cx = cx_ref[top].astype(jnp.float32)
    mf = mf_ref[top - 1].astype(jnp.float32)
    cy = cy_ref[top - 1].astype(jnp.float32)
    for xt in range(strips):
        along = [first_weights(cx, code_ref[top], 2, xt, j) for j in range(tiles)]
        across = second_weights(cy, code_ref[top - 1], 1, xt, tiles)
        rows = slice(xt * ROWS, (xt + 1) * ROWS)
        for s in range(sectors):
            parts = []
            for j in range(tiles):
                upper = first_sweep(
                    lambda s, j, start: vt_ref[s, j, start : start + ROWS, :],
                    s, j, xt, along[j],
                    *rim_rows(
                        xt, strips - 1,
                        lambda s, j: lrow_ref[j, s : s + 1, :],
                        lambda s, j: rrow_ref[j, s : s + 1, :],
                    ),
                )
                top_ref[s, j, rows, :] = upper
                here = lower_ref[s, j, rows, :]
                parts.append(here + cut(mf, xt, j) * (upper - here))
            for j, value in enumerate(second_sweep(parts, across)):
                store_padded(out_ref, (), s, j, xt, value)
                store_rims(first_ref, last_ref, done + s, j, xt, strips - 1, value)


def highest_kernel(here_ref, above_ref, mf_ref, cy_ref, code_ref, out_ref, first_ref, last_ref):
    sectors, tiles, columns, _ = here_ref.shape
    strips = columns // ROWS
    top = mf_ref.shape[0] - 1
    at_top = lax.axis_index("lev") == lax.axis_size("lev") - 1
    mf = mf_ref[top].astype(jnp.float32)
    cy = cy_ref[top].astype(jnp.float32)
    for xt in range(strips):
        across = second_weights(cy, code_ref[top], 1, xt, tiles)
        rows = slice(xt * ROWS, (xt + 1) * ROWS)
        for s in range(sectors):
            parts = []
            for j in range(tiles):
                here = here_ref[s, j, rows, :]
                upper = above_ref[s, rows, j * LANES : (j + 1) * LANES]
                upper = jnp.where(at_top, here, upper)
                parts.append(here + cut(mf, xt, j) * (upper - here))
            for j, value in enumerate(second_sweep(parts, across)):
                store_padded(out_ref, (), s, j, xt, value)
                store_rims(first_ref, last_ref, s, j, xt, strips - 1, value)


def final_level(k, chosen, field, rows_at, refs, out_ref, sens_ref=None, start_sum=False):
    cx_ref, code_ref, weight_ref, share_ref = refs
    sectors, _, width = share_ref.shape
    cx = cx_ref[k].astype(jnp.float32)
    codes = code_ref[k]
    factor = weight_ref[pl.ds(k, 1), :]
    for xt in chosen:
        rows = slice(xt * ROWS, (xt + 1) * ROWS)
        for j in range(width // LANES):
            lanes = slice(j * LANES, (j + 1) * LANES)
            factors = first_weights(cx, codes, 0, xt, j)
            total = 0.0
            for s in range(sectors):
                value = first_sweep(field, s, j, xt, factors, *rows_at(xt))
                out_ref[k, s, rows, lanes] = value
                if sens_ref is not None:
                    total = total + share_ref[s, rows, lanes] * value
            if sens_ref is None:
                continue
            if start_sum:
                sens_ref[rows, lanes] = factor * total
            else:
                sens_ref[rows, lanes] += factor * total


def inner_final_kernel(
    inner_ref, outer_ref, vs_ref, cx_ref, code_ref, weight_ref, share_ref,
    out_hbm, sens_ref, out_ref, sems,
):
    below, _, _, padded, _ = inner_ref.shape
    strips = (padded - 2 * ROWS) // ROWS
    refs = (cx_ref, code_ref, weight_ref, share_ref)
    inner = pl.ds(ROWS, (strips - 2) * ROWS)
    chosen = range(1, strips - 1)

    def send(k):
        return pltpu.make_async_copy(out_ref.at[k, :, inner], out_hbm.at[:, k, inner], sems.at[k])

    final_level(
        below, chosen, lambda s, j, start: vs_ref[s, j, start : start + ROWS, :],
        lambda xt: (None, None), refs, out_ref, sens_ref, True,
    )
    send(below).start()

    def step(k, _):
        low, high = 2 * ROWS - 1, strips * ROWS

        def rows_at(xt):
            return (
                (lambda s, j: outer_ref[k, s, j, low : low + 1, :]) if xt == 1 else None,
                (lambda s, j: outer_ref[k, s, j, high : high + 1, :]) if xt == strips - 2 else None,
            )

        final_level(
            k, chosen, lambda s, j, start: inner_ref[k, s, j, start : start + ROWS, :],
            rows_at, refs, out_ref, sens_ref,
        )
        send(k).start()
        return 0

    lax.fori_loop(0, below, step, 0)
    for k in range(below + 1):
        send(k).wait()


def outer_final_kernel(
    inner_ref, outer_ref, vs_ref, vt_ref, left_ref, right_ref, left_top_ref, right_top_ref, seam_ref,
    cx_ref, code_ref, weight_ref, share_ref, inner_sens_ref, done_hbm,
    out_hbm, piece_ref,
    lrow_ref, rrow_ref, ltop_ref, rtop_ref, out_ref, sens_ref, flat_ref, sems,
):
    below, sectors, tiles, padded, _ = outer_ref.shape
    strips = (padded - 2 * ROWS) // ROWS
    ends = (0, strips - 1)
    refs = (cx_ref, code_ref, weight_ref, share_ref)
    flip_left, flip_right = flags(seam_ref)
    turned(left_ref, flip_left, lrow_ref)
    turned(right_ref, flip_right, rrow_ref)
    turned(left_top_ref, flip_left, ltop_ref)
    turned(right_top_ref, flip_right, rtop_ref)

    def send(k, i):
        rows = pl.ds(ends[i] * ROWS, ROWS)
        return pltpu.make_async_copy(out_ref.at[k, :, rows], out_hbm.at[:, k, rows], sems.at[i, k])

    send_top = pltpu.make_async_copy(
        out_ref.at[below + 1], out_hbm.at[:, below + 1], sems.at[0, below + 1]
    )
    final_level(
        below + 1, range(strips), lambda s, j, start: vt_ref[s, j, start : start + ROWS, :],
        lambda xt: rim_rows(
            xt, strips - 1,
            lambda s, j: ltop_ref[j, s : s + 1, :],
            lambda s, j: rtop_ref[j, s : s + 1, :],
        ),
        refs, out_ref, sens_ref, True,
    )
    send_top.start()
    edge = below * sectors
    final_level(
        below, ends, lambda s, j, start: vs_ref[s, j, start : start + ROWS, :],
        lambda xt: rim_rows(
            xt, strips - 1,
            lambda s, j: lrow_ref[j, edge + s : edge + s + 1, :],
            lambda s, j: rrow_ref[j, edge + s : edge + s + 1, :],
        ),
        refs, out_ref,
    )
    for i in range(2):
        send(below, i).start()

    def step(k, _):
        low, high = 2 * ROWS, strips * ROWS - 1

        def rows_at(xt):
            if xt == 0:
                return (
                    lambda s, j: lrow_ref[j, pl.ds(k * sectors + s, 1), :],
                    lambda s, j: inner_ref[k, s, j, low : low + 1, :],
                )
            return (
                lambda s, j: inner_ref[k, s, j, high : high + 1, :],
                lambda s, j: rrow_ref[j, pl.ds(k * sectors + s, 1), :],
            )

        final_level(
            k, ends, lambda s, j, start: outer_ref[k, s, j, start : start + ROWS, :],
            rows_at, refs, out_ref,
        )
        for i in range(2):
            send(k, i).start()
        return 0

    lax.fori_loop(0, below, step, 0)

    places = [
        (slice(xt * ROWS, (xt + 1) * ROWS), slice(j * LANES, (j + 1) * LANES))
        for xt in ends
        for j in range(tiles)
    ]

    def add(k, sums):
        factor = weight_ref[pl.ds(k, 1), :]
        out = []
        for total, place in zip(sums, places):
            part = share_ref[(0, *place)] * out_ref[(k, 0, *place)]
            for s in range(1, sectors):
                part = part + share_ref[(s, *place)] * out_ref[(k, s, *place)]
            out.append(total + factor * part)
        return tuple(out)

    sums = lax.fori_loop(0, below + 1, add, tuple(sens_ref[place] for place in places))
    for total, place in zip(sums, places):
        sens_ref[place] = total
    inner = slice(ROWS, (strips - 1) * ROWS)
    sens_ref[inner] += inner_sens_ref[inner]
    if len(piece_ref.shape) == 2:
        piece_ref[...] = sens_ref[...]
    else:
        owners, group, copies, depth, _ = piece_ref.shape
        share = strips * ROWS * tiles // owners
        for xt in range(strips):
            for j in range(tiles):
                value = sens_ref[xt * ROWS : (xt + 1) * ROWS, j * LANES : (j + 1) * LANES]
                flat_ref[pl.ds(xt * ROWS * tiles + j, ROWS, stride=tiles), :] = value
        for o in range(owners):
            for piece in range(group):
                start = piece * depth
                used = max(0, min(depth, share - start))
                value = jnp.zeros((depth, LANES), jnp.float32)
                if used:
                    start += o * share
                    value = flat_ref[start : start + depth, :]
                    if used < depth:
                        line = lax.broadcasted_iota(jnp.int32, (depth, LANES), 0)
                        value = jnp.where(line < used, value, 0.0)
                for i in range(copies):
                    piece_ref[o, piece, i] = value
    send_top.wait()
    for k in range(below + 1):
        for i in range(2):
            send(k, i).wait()


def low_kernel(turned_ref, low_ref):
    count = low_ref.shape[0]
    iota = lax.broadcasted_iota(jnp.int32, (LANES, LANES), 1)
    for line in range(count):
        low = jnp.bitwise_and(turned_ref[:, line : line + 1], LANES - 1)
        low_ref[line] = jnp.where(low == iota, 1.0, 0.0).astype(jnp.bfloat16)


def scatter_kernel(cells_ref, low_ref, *refs):
    *value_refs, out_ref = refs
    rows, lanes = out_ref.shape
    group, owners, depth, _ = cells_ref.shape
    each = owners * depth
    rank = lax.axis_index("lev")
    half = jnp.bfloat16
    zero = jnp.zeros((), half)
    iota = lax.broadcasted_iota(jnp.int32, (lanes, lanes), 0).astype(jnp.float32).astype(half)
    total = jnp.zeros((2 * lanes, lanes), jnp.float32)
    wide = 8

    def spread(row):
        return jnp.broadcast_to(row, (lanes, lanes)).astype(half)

    for part in range(group):
        piece = jnp.bitwise_xor(rank, part)
        for start in range(0, each, wide):
            lefts = []
            for place in range(start, start + wide):
                owner, line = divmod(place, depth)
                cells = cells_ref[piece, owner, line : line + 1, :]
                value = value_refs[part][owner, line : line + 1, :]
                coarse = value.astype(half).astype(jnp.float32)
                high = spread(jnp.right_shift(cells, 7).astype(jnp.float32)) == iota
                lefts.append(
                    jnp.concatenate(
                        [
                            jnp.where(high, spread(coarse), zero),
                            jnp.where(high, spread(value - coarse), zero),
                        ],
                        axis=0,
                    )
                )
            low = low_ref[pl.ds(piece * each + start, wide)].reshape(wide * lanes, lanes)
            total += jnp.dot(
                jnp.concatenate(lefts, axis=1), low, preferred_element_type=jnp.float32
            )
    out_ref[...] = total[:rows] + total[lanes : lanes + rows]


def exchanged(value, axis, apart):
    count = lax.axis_size(axis)
    return lax.ppermute(value, axis, [(i, i ^ apart) for i in range(count)])


def remapped(pieces, flux_cell):
    owners, share = flux_cell.shape
    _, group, copies, depth, _ = pieces.shape
    sent = pieces.reshape(-1, depth, LANES)
    arrived = lax.all_to_all(
        sent, ("tile", "lev", "sec"), split_axis=0, concat_axis=0, tiled=True
    )
    own = jnp.sum(arrived.reshape(owners, group * copies, depth, LANES), axis=1)
    arrived = [exchanged(own, "lev", d) for d in range(group - 1, 0, -1)]
    parts = [own, *reversed(arrived)]
    cells = jnp.pad(flux_cell, ((0, 0), (0, group * depth * LANES - share)))
    cells = cells.reshape(owners, group, depth, LANES).transpose(1, 0, 2, 3)
    lines = cells.size // LANES
    low = call(
        low_kernel,
        pltpu.VMEM((lines, LANES, LANES), jnp.bfloat16),
        [VM],
        VM,
        (cells.reshape(lines, LANES).T,),
    )
    out = call(
        scatter_kernel, f32(FL_DEV // LANES, LANES), [VM] * (group + 2), VM, (cells, low, *parts)
    )
    return out.reshape(-1)


def around(first, last):
    count = lax.axis_size("tile")
    up = [(i, (i + 1) % count) for i in range(count)]
    down = [(j, i) for i, j in up]
    return lax.ppermute(last, "tile", up), lax.ppermute(first, "tile", down)


def from_above(value):
    count = lax.axis_size("lev")
    return lax.ppermute(value, "lev", [(i + 1, i) for i in range(count - 1)])


def shards(
    forcing, courant_x, courant_y, mass_flux, limiter_code, seam_code, level_weight, sector_share, flux_cell
):
    sectors, levels, columns, width = forcing.shape
    tiles, below = width // LANES, levels - 1
    padded = columns + 2 * ROWS
    field = kept(below, sectors, tiles, padded, LANES)
    field_top = kept(sectors, tiles, padded, LANES)
    plane = kept(sectors, columns, width)
    rim = kept(tiles, below * sectors, LANES)
    rim_top = kept(tiles, sectors, LANES)
    rim_next = kept(tiles, (below - 1) * sectors, LANES)
    rim_scratch = pltpu.VMEM((tiles, below * sectors, LANES), jnp.float32)

    seam = jnp.broadcast_to(seam_code.T[:, :, None], (*seam_code.T.shape, LANES))
    weight = jnp.broadcast_to(level_weight[:, None], (levels, LANES))

    narrow = pltpu.VMEM((levels, columns, width), jnp.bfloat16)
    lowest, mass_flux, courant_y, limiter_code, courant_x = call(
        start_kernel,
        (plane, narrow, narrow, pltpu.VMEM((levels, columns, width), jnp.int32), narrow),
        [HBM] * 5,
        [VM] * 5,
        in_hbm(forcing, mass_flux, courant_y, limiter_code, courant_x),
        [pltpu.SemaphoreType.DMA((5,))],
    )
    above = from_above(lowest)
    v, first, last, top = call(
        lower_kernel,
        (field, rim, rim, plane),
        [VM] * 4,
        [VM] * 4,
        (forcing, mass_flux, courant_y, limiter_code),
    )
    left, right = around(first, last)
    lines = kept(sectors, tiles, columns, LANES)
    inner_field = kept(below - 1, sectors, tiles, padded, LANES)
    a_scratch = pltpu.VMEM((2, sectors, tiles, columns, LANES), jnp.float32)
    inner, inner_lowest, inner_top = call(
        inner_middle_kernel,
        (inner_field, lines, lines),
        [VM] * 5,
        [VM] * 3,
        (v, courant_x, mass_flux, courant_y, limiter_code),
        [a_scratch],
    )
    lowest, vt, first_top, last_top = call(
        ends_kernel,
        (plane, field_top, rim_top, rim_top),
        [VM] * 11,
        [VM] * 4,
        (
            v, inner_lowest, left, right, seam, courant_x, limiter_code, top, above,
            mass_flux, courant_y,
        ),
        [pltpu.VMEM((tiles, ROWS, LANES), jnp.float32)] * 2,
    )
    above = from_above(lowest)
    left_top, right_top = around(first_top, last_top)

    outer, first, last, top = call(
        outer_middle_kernel,
        (inner_field, rim_next, rim_next, lines),
        [VM] * 10,
        [VM] * 4,
        (
            v, inner_top, left, right, lowest, seam,
            courant_x, mass_flux, courant_y, limiter_code,
        ),
        [rim_scratch, rim_scratch, a_scratch],
    )
    vs, first, last, top = call(
        second_last_kernel,
        (field_top, rim, rim, kept(sectors, tiles, columns, LANES)),
        [VM] * 11,
        [VM] * 4,
        (
            vt, left_top, right_top, top, first, last, seam,
            courant_x, mass_flux, courant_y, limiter_code,
        ),
        [pltpu.VMEM((tiles, sectors, LANES), jnp.float32)] * 2,
    )
    left, right = around(first, last)
    vt, first_top, last_top = call(
        highest_kernel,
        (field_top, rim_top, rim_top),
        [VM] * 5,
        [VM] * 3,
        (top, above, mass_flux, courant_y, limiter_code),
    )
    left_top, right_top = around(first_top, last_top)

    owners, share = flux_cell.shape
    group, copies = lax.axis_size("lev"), lax.axis_size("sec")
    depth = -(-share // (group * LANES))
    aligned = share % LANES == 0
    packed = (owners, group, copies, depth, LANES)
    stage = pltpu.VMEM((levels, sectors, columns, width), jnp.float32)
    adjoint, inner_sens = call(
        inner_final_kernel,
        (f32(*forcing.shape), kept(columns, width)),
        [VM] * 7,
        [HBM, VM],
        (inner, outer, vs, courant_x, limiter_code, weight, sector_share),
        [stage, pltpu.SemaphoreType.DMA((levels,))],
    )
    adjoint, pieces = call(
        outer_final_kernel,
        (f32(*forcing.shape), f32(*packed) if aligned else f32(columns, width)),
        [VM] * 14 + [HBM],
        [HBM, VM],
        (
            inner, outer, vs, vt, left, right, left_top, right_top, seam,
            courant_x, limiter_code, weight, sector_share, inner_sens, adjoint,
        ),
        [
            rim_scratch, rim_scratch,
            pltpu.VMEM((tiles, sectors, LANES), jnp.float32),
            pltpu.VMEM((tiles, sectors, LANES), jnp.float32),
            stage,
            pltpu.VMEM((columns, width), jnp.float32),
            pltpu.VMEM((columns * tiles + ROWS, LANES), jnp.float32),
            pltpu.SemaphoreType.DMA((2, levels)),
        ],
        aliases={14: 0},
    )
    if not aligned:
        pieces = jnp.pad(
            pieces.reshape(owners, share), ((0, 0), (0, group * depth * LANES - share))
        ).reshape(owners, group, 1, depth, LANES)
        pieces = jnp.broadcast_to(pieces, packed)
    flux_cell, pieces = lax.optimization_barrier((flux_cell, pieces))
    return (adjoint, remapped(pieces, flux_cell))


def solution(mesh):
    placed = (
        P("sec", "lev", "tile", None),
        P("lev", "tile", None),
        P("lev", "tile", None),
        P("lev", "tile", None),
        P("lev", "tile", None),
        P(),
        P("lev"),
        P("sec", "tile", None),
        P("tile", None),
    )
    return jax.shard_map(
        shards,
        mesh=mesh,
        in_specs=placed,
        out_specs=(P("sec", "lev", "tile", None), P("tile")),
        check_vma=False,
    )
```

```python
import functools

import jax
import jax.numpy as jnp
from jax import lax
from jax.experimental import pallas as pl
from jax.experimental.pallas import tpu as pltpu
from jax.sharding import PartitionSpec as P

FL_DEV = 15360
LANES = 128
ROWS = 8
MIB = 2**20
VM = pl.BlockSpec(memory_space=pltpu.VMEM)
HBM = pl.BlockSpec(memory_space=pltpu.HBM)


def call(kernel, out_shape, in_specs, out_specs, operands, scratch=(), mib=16, aliases={}):
    return pl.pallas_call(
        kernel,
        out_shape=out_shape,
        in_specs=in_specs,
        out_specs=out_specs,
        scratch_shapes=list(scratch),
        input_output_aliases=aliases,
        cost_estimate=pl.CostEstimate(flops=1, transcendentals=0, bytes_accessed=1),
        compiler_params=pltpu.CompilerParams(vmem_limit_bytes=mib * MIB),
    )(*operands)


def in_hbm(*arrays):
    return tuple(pltpu.with_memory_space_constraint(a, pltpu.HBM) for a in arrays)


def kept(*shape):
    return pltpu.VMEM(shape, jnp.float32)


def f32(*shape):
    return jax.ShapeDtypeStruct(shape, jnp.float32)


def cut(value, xt, j):
    return value[xt * ROWS : (xt + 1) * ROWS, j * LANES : (j + 1) * LANES]


def weights(courant, codes, bit):
    size = jnp.abs(courant)
    half = (0.5 * size) * (1.0 - size)
    limited = jnp.where(jnp.bitwise_and(codes, 1 << bit) != 0, half, 0.0)
    ahead = jnp.maximum(courant, 0.0) - limited
    back = jnp.maximum(-courant, 0.0) - limited
    return ahead, back


def second_weights(cy, codes, bit, xt, tiles):
    lane = lax.broadcasted_iota(jnp.int32, (ROWS, LANES), 1)
    out = []
    for j in range(tiles):
        ahead, back = weights(cut(cy, xt, j), cut(codes, xt, j), bit)
        if j == 0:
            back = jnp.where(lane == 0, 0.0, back)
        if j == tiles - 1:
            ahead = jnp.where(lane == LANES - 1, 0.0, ahead)
        out.append((ahead, back, (1.0 - ahead) - back))
    return out


def second_sweep(parts, factors):
    lane = lax.broadcasted_iota(jnp.int32, (ROWS, LANES), 1)
    tiles = len(parts)
    later = [pltpu.roll(part, LANES - 1, 1) for part in parts]
    sooner = [pltpu.roll(part, 1, 1) for part in parts]
    out = []
    for j in range(tiles):
        following, previous = later[j], sooner[j]
        if j + 1 < tiles:
            following = jnp.where(lane == LANES - 1, later[j + 1], following)
        if j > 0:
            previous = jnp.where(lane == 0, sooner[j - 1], previous)
        ahead, back, own = factors[j]
        out.append(own * parts[j] + ahead * following + back * previous)
    return out


def first_sweep(field, s, j, xt, factors, before=None, after=None):
    start = ROWS * (xt + 1)
    sub = lax.broadcasted_iota(jnp.int32, (ROWS, LANES), 0)
    own_value = field(s, j, start)
    following = field(s, j, start + 1)
    previous = field(s, j, start - 1)
    if before is not None:
        previous = jnp.where(sub == 0, before(s, j), previous)
    if after is not None:
        following = jnp.where(sub == ROWS - 1, after(s, j), following)
    ahead, back, own = factors
    return own * own_value + ahead * following + back * previous


def rim_rows(xt, last, left_row, right_row):
    return (left_row if xt == 0 else None, right_row if xt == last else None)


def turned(source_ref, flag, target_ref):
    tiles, rows, _ = source_ref.shape
    for j in range(tiles):
        for start in range(0, rows, ROWS):
            count = min(ROWS, rows - start)
            index = (LANES - 1) - lax.broadcasted_iota(jnp.int32, (count, LANES), 1)
            straight = source_ref[j, start : start + count, :]
            other = source_ref[tiles - 1 - j, start : start + count, :]
            mirrored = jnp.take_along_axis(other, index, axis=1, mode="promise_in_bounds")
            target_ref[j, start : start + count, :] = jnp.where(flag, mirrored, straight)


def store_padded(ref, index, s, j, xt, value):
    start = ROWS * (xt + 1)
    ref[(*index, s, j, slice(start, start + ROWS), slice(None))] = value


def store_rims(first_ref, last_ref, row, j, xt, last, value):
    if xt == 0:
        first_ref[j, pl.ds(row, 1), :] = value[:1]
    if xt == last:
        last_ref[j, pl.ds(row, 1), :] = value[ROWS - 1 :]


def flags(seam_ref):
    tile = lax.axis_index("tile")
    return seam_ref[0, pl.ds(tile, 1), :] == 1, seam_ref[1, pl.ds(tile, 1), :] == 1


def start_kernel(f_hbm, mf_hbm, cy_hbm, code_hbm, cx_hbm, out_ref, mf_ref, cy_ref, code_ref, cx_ref, sems):
    copies = [
        pltpu.make_async_copy(source, target, sems.at[i])
        for i, (source, target) in enumerate(
            (
                (f_hbm.at[:, 0], out_ref),
                (mf_hbm, mf_ref),
                (cy_hbm, cy_ref),
                (code_hbm, code_ref),
                (cx_hbm, cx_ref),
            )
        )
    ]
    for copy in copies:
        copy.start()
    for copy in copies:
        copy.wait()


def lower_kernel(f_ref, mf_ref, cy_ref, code_ref, v_ref, first_ref, last_ref, top_ref):
    sectors, levels, columns, width = f_ref.shape
    tiles, strips = width // LANES, columns // ROWS

    def level(k, _):
        mf = mf_ref[k].astype(jnp.float32)
        cy = cy_ref[k].astype(jnp.float32)
        codes = code_ref[k]
        for xt in range(strips):
            factors = second_weights(cy, codes, 3, xt, tiles)
            rows = slice(xt * ROWS, (xt + 1) * ROWS)
            for s in range(sectors):
                parts = []
                for j in range(tiles):
                    lanes = slice(j * LANES, (j + 1) * LANES)
                    here = f_ref[s, k, rows, lanes]
                    upper = f_ref[s, k + 1, rows, lanes]
                    parts.append(here + cut(mf, xt, j) * (upper - here))
                for j, value in enumerate(second_sweep(parts, factors)):
                    store_padded(v_ref, (k,), s, j, xt, value)
                    store_rims(first_ref, last_ref, k * sectors + s, j, xt, strips - 1, value)
        return 0

    lax.fori_loop(0, levels - 1, level, 0)
    top_ref[...] = f_ref[:, levels - 1]


def first_weights(cx, codes, bit, xt, j):
    ahead, back = weights(cut(cx, xt, j), cut(codes, xt, j), bit)
    return ahead, back, (1.0 - ahead) - back


def ends_kernel(
    v_ref, inner_ref, left_ref, right_ref, seam_ref, cx_ref, code_ref, here_ref, above_ref,
    mf_ref, cy_ref,
    out_ref, top_ref, first_ref, last_ref,
    lrow_ref, rrow_ref,
):
    _, sectors, tiles, _, _ = v_ref.shape
    columns = out_ref.shape[1]
    strips = columns // ROWS
    flip_left, flip_right = flags(seam_ref)
    turned(left_ref.at[:, :ROWS], flip_left, lrow_ref)
    turned(right_ref.at[:, :ROWS], flip_right, rrow_ref)
    cx = cx_ref[0].astype(jnp.float32)
    codes = code_ref[0]
    for s in range(sectors):
        for j in range(tiles):
            lanes = slice(j * LANES, (j + 1) * LANES)
            out_ref[s, ROWS : columns - ROWS, lanes] = inner_ref[s, j, ROWS : columns - ROWS]
    for xt in (0, strips - 1):
        for j in range(tiles):
            factors = first_weights(cx, codes, 2, xt, j)
            for s in range(sectors):
                value = first_sweep(
                    lambda s, j, start: v_ref[0, s, j, start : start + ROWS, :],
                    s, j, xt, factors,
                    *rim_rows(
                        xt, strips - 1,
                        lambda s, j: lrow_ref[j, s : s + 1, :],
                        lambda s, j: rrow_ref[j, s : s + 1, :],
                    ),
                )
                out_ref[s, xt * ROWS : (xt + 1) * ROWS, j * LANES : (j + 1) * LANES] = value

    level = mf_ref.shape[0] - 1
    at_top = lax.axis_index("lev") == lax.axis_size("lev") - 1
    mf = mf_ref[level].astype(jnp.float32)
    cy = cy_ref[level].astype(jnp.float32)
    codes = code_ref[level]
    for xt in range(strips):
        factors = second_weights(cy, codes, 3, xt, tiles)
        rows = slice(xt * ROWS, (xt + 1) * ROWS)
        for s in range(sectors):
            parts = []
            for j in range(tiles):
                lanes = slice(j * LANES, (j + 1) * LANES)
                here = here_ref[s, rows, lanes]
                upper = jnp.where(at_top, here, above_ref[s, rows, lanes])
                parts.append(here + cut(mf, xt, j) * (upper - here))
            for j, value in enumerate(second_sweep(parts, factors)):
                store_padded(top_ref, (), s, j, xt, value)
                store_rims(first_ref, last_ref, s, j, xt, strips - 1, value)


def middle_levels(
    chosen, v_ref, lrow_ref, rrow_ref, cx_ref, mf_ref, cy_ref, code_ref, out_ref, a_ref, rims=None
):
    below, sectors, tiles, padded, _ = v_ref.shape
    strips = (padded - 2 * ROWS) // ROWS

    def level(k, _):
        cx = cx_ref[k + 1].astype(jnp.float32)
        mf = mf_ref[k].astype(jnp.float32)
        cy = cy_ref[k].astype(jnp.float32)
        codes_x = code_ref[k + 1]
        codes_y = code_ref[k]
        slot = lax.rem(k, 2)
        for xt in chosen:
            along = [first_weights(cx, codes_x, 2, xt, j) for j in range(tiles)]
            across = second_weights(cy, codes_y, 1, xt, tiles)
            rows = slice(xt * ROWS, (xt + 1) * ROWS)
            for s in range(sectors):
                parts = []
                for j in range(tiles):
                    upper = first_sweep(
                        lambda s, j, start: v_ref[k + 1, s, j, start : start + ROWS, :],
                        s, j, xt, along[j],
                        *rim_rows(
                            xt, strips - 1,
                            lambda s, j: lrow_ref[j, pl.ds((k + 1) * sectors + s, 1), :],
                            lambda s, j: rrow_ref[j, pl.ds((k + 1) * sectors + s, 1), :],
                        ),
                    )
                    here = a_ref[slot, s, j, rows, :]
                    a_ref[1 - slot, s, j, rows, :] = upper
                    parts.append(here + cut(mf, xt, j) * (upper - here))
                for j, value in enumerate(second_sweep(parts, across)):
                    store_padded(out_ref, (k,), s, j, xt, value)
                    if rims is not None:
                        store_rims(*rims, k * sectors + s, j, xt, strips - 1, value)
        return 0

    lax.fori_loop(0, below - 1, level, 0)


def inner_middle_kernel(
    v_ref, cx_ref, mf_ref, cy_ref, code_ref, out_ref, lowest_ref, top_ref, a_ref
):
    below, sectors, tiles, padded, _ = v_ref.shape
    strips = (padded - 2 * ROWS) // ROWS
    cx = cx_ref[0].astype(jnp.float32)
    for xt in range(1, strips - 1):
        for j in range(tiles):
            factors = first_weights(cx, code_ref[0], 2, xt, j)
            for s in range(sectors):
                value = first_sweep(
                    lambda s, j, start: v_ref[0, s, j, start : start + ROWS, :],
                    s, j, xt, factors,
                )
                a_ref[0, s, j, xt * ROWS : (xt + 1) * ROWS, :] = value
                lowest_ref[s, j, xt * ROWS : (xt + 1) * ROWS, :] = value
    middle_levels(
        range(1, strips - 1), v_ref, None, None, cx_ref, mf_ref, cy_ref, code_ref, out_ref, a_ref
    )
    inner = slice(ROWS, (strips - 1) * ROWS)
    top_ref[:, :, inner] = a_ref[(below - 1) % 2, :, :, inner]


def outer_middle_kernel(
    v_ref, inner_top_ref, left_ref, right_ref, lowest_ref, seam_ref,
    cx_ref, mf_ref, cy_ref, code_ref,
    out_ref, first_ref, last_ref, top_ref,
    lrow_ref, rrow_ref, a_ref,
):
    below, sectors, tiles, padded, _ = v_ref.shape
    strips = (padded - 2 * ROWS) // ROWS
    ends = (0, strips - 1)
    flip_left, flip_right = flags(seam_ref)
    turned(left_ref, flip_left, lrow_ref)
    turned(right_ref, flip_right, rrow_ref)
    for s in range(sectors):
        for j in range(tiles):
            for xt in ends:
                rows = slice(xt * ROWS, (xt + 1) * ROWS)
                a_ref[0, s, j, rows] = lowest_ref[s, rows, j * LANES : (j + 1) * LANES]
    middle_levels(
        ends, v_ref, lrow_ref, rrow_ref, cx_ref, mf_ref, cy_ref, code_ref, out_ref, a_ref,
        (first_ref, last_ref),
    )
    for xt in ends:
        rows = slice(xt * ROWS, (xt + 1) * ROWS)
        top_ref[:, :, rows] = a_ref[(below - 1) % 2, :, :, rows]
    inner = slice(ROWS, (strips - 1) * ROWS)
    top_ref[:, :, inner] = inner_top_ref[:, :, inner]


def second_last_kernel(
    vt_ref, left_ref, right_ref, lower_ref, first_in, last_in, seam_ref, cx_ref, mf_ref, cy_ref, code_ref,
    out_ref, first_ref, last_ref, top_ref,
    lrow_ref, rrow_ref,
):
    sectors, tiles, padded, _ = vt_ref.shape
    strips = (padded - 2 * ROWS) // ROWS
    top = mf_ref.shape[0] - 1
    done = first_in.shape[1]
    flip_left, flip_right = flags(seam_ref)
    turned(left_ref, flip_left, lrow_ref)
    turned(right_ref, flip_right, rrow_ref)
    first_ref[:, :done] = first_in[...]
    last_ref[:, :done] = last_in[...]
    cx = cx_ref[top].astype(jnp.float32)
    mf = mf_ref[top - 1].astype(jnp.float32)
    cy = cy_ref[top - 1].astype(jnp.float32)
    for xt in range(strips):
        along = [first_weights(cx, code_ref[top], 2, xt, j) for j in range(tiles)]
        across = second_weights(cy, code_ref[top - 1], 1, xt, tiles)
        rows = slice(xt * ROWS, (xt + 1) * ROWS)
        for s in range(sectors):
            parts = []
            for j in range(tiles):
                upper = first_sweep(
                    lambda s, j, start: vt_ref[s, j, start : start + ROWS, :],
                    s, j, xt, along[j],
                    *rim_rows(
                        xt, strips - 1,
                        lambda s, j: lrow_ref[j, s : s + 1, :],
                        lambda s, j: rrow_ref[j, s : s + 1, :],
                    ),
                )
                top_ref[s, j, rows, :] = upper
                here = lower_ref[s, j, rows, :]
                parts.append(here + cut(mf, xt, j) * (upper - here))
            for j, value in enumerate(second_sweep(parts, across)):
                store_padded(out_ref, (), s, j, xt, value)
                store_rims(first_ref, last_ref, done + s, j, xt, strips - 1, value)


def highest_kernel(here_ref, above_ref, mf_ref, cy_ref, code_ref, out_ref, first_ref, last_ref):
    sectors, tiles, columns, _ = here_ref.shape
    strips = columns // ROWS
    top = mf_ref.shape[0] - 1
    at_top = lax.axis_index("lev") == lax.axis_size("lev") - 1
    mf = mf_ref[top].astype(jnp.float32)
    cy = cy_ref[top].astype(jnp.float32)
    for xt in range(strips):
        across = second_weights(cy, code_ref[top], 1, xt, tiles)
        rows = slice(xt * ROWS, (xt + 1) * ROWS)
        for s in range(sectors):
            parts = []
            for j in range(tiles):
                here = here_ref[s, j, rows, :]
                upper = above_ref[s, rows, j * LANES : (j + 1) * LANES]
                upper = jnp.where(at_top, here, upper)
                parts.append(here + cut(mf, xt, j) * (upper - here))
            for j, value in enumerate(second_sweep(parts, across)):
                store_padded(out_ref, (), s, j, xt, value)
                store_rims(first_ref, last_ref, s, j, xt, strips - 1, value)


def final_level(k, chosen, field, rows_at, refs, out_ref, sens_ref=None, start_sum=False):
    cx_ref, code_ref, weight_ref, share_ref = refs
    sectors, _, width = share_ref.shape
    cx = cx_ref[k].astype(jnp.float32)
    codes = code_ref[k]
    factor = weight_ref[pl.ds(k, 1), :]
    for xt in chosen:
        rows = slice(xt * ROWS, (xt + 1) * ROWS)
        for j in range(width // LANES):
            lanes = slice(j * LANES, (j + 1) * LANES)
            factors = first_weights(cx, codes, 0, xt, j)
            total = 0.0
            for s in range(sectors):
                value = first_sweep(field, s, j, xt, factors, *rows_at(xt))
                out_ref[k, s, rows, lanes] = value
                if sens_ref is not None:
                    total = total + share_ref[s, rows, lanes] * value
            if sens_ref is None:
                continue
            if start_sum:
                sens_ref[rows, lanes] = factor * total
            else:
                sens_ref[rows, lanes] += factor * total


def inner_final_kernel(
    inner_ref, outer_ref, vs_ref, cx_ref, code_ref, weight_ref, share_ref,
    out_hbm, sens_ref, out_ref, sems,
):
    below, _, _, padded, _ = inner_ref.shape
    strips = (padded - 2 * ROWS) // ROWS
    refs = (cx_ref, code_ref, weight_ref, share_ref)
    inner = pl.ds(ROWS, (strips - 2) * ROWS)
    chosen = range(1, strips - 1)

    def send(k):
        return pltpu.make_async_copy(out_ref.at[k, :, inner], out_hbm.at[:, k, inner], sems.at[k])

    final_level(
        below, chosen, lambda s, j, start: vs_ref[s, j, start : start + ROWS, :],
        lambda xt: (None, None), refs, out_ref, sens_ref, True,
    )
    send(below).start()

    def step(k, _):
        low, high = 2 * ROWS - 1, strips * ROWS

        def rows_at(xt):
            return (
                (lambda s, j: outer_ref[k, s, j, low : low + 1, :]) if xt == 1 else None,
                (lambda s, j: outer_ref[k, s, j, high : high + 1, :]) if xt == strips - 2 else None,
            )

        final_level(
            k, chosen, lambda s, j, start: inner_ref[k, s, j, start : start + ROWS, :],
            rows_at, refs, out_ref, sens_ref,
        )
        send(k).start()
        return 0

    lax.fori_loop(0, below, step, 0)
    for k in range(below + 1):
        send(k).wait()


def outer_final_kernel(
    inner_ref, outer_ref, vs_ref, vt_ref, left_ref, right_ref, left_top_ref, right_top_ref, seam_ref,
    cx_ref, code_ref, weight_ref, share_ref, inner_sens_ref, done_hbm,
    out_hbm, piece_ref,
    lrow_ref, rrow_ref, ltop_ref, rtop_ref, out_ref, sens_ref, flat_ref, sems,
):
    below, sectors, tiles, padded, _ = outer_ref.shape
    strips = (padded - 2 * ROWS) // ROWS
    ends = (0, strips - 1)
    refs = (cx_ref, code_ref, weight_ref, share_ref)
    flip_left, flip_right = flags(seam_ref)
    turned(left_ref, flip_left, lrow_ref)
    turned(right_ref, flip_right, rrow_ref)
    turned(left_top_ref, flip_left, ltop_ref)
    turned(right_top_ref, flip_right, rtop_ref)

    def send(k, i):
        rows = pl.ds(ends[i] * ROWS, ROWS)
        return pltpu.make_async_copy(out_ref.at[k, :, rows], out_hbm.at[:, k, rows], sems.at[i, k])

    send_top = pltpu.make_async_copy(
        out_ref.at[below + 1], out_hbm.at[:, below + 1], sems.at[0, below + 1]
    )
    final_level(
        below + 1, range(strips), lambda s, j, start: vt_ref[s, j, start : start + ROWS, :],
        lambda xt: rim_rows(
            xt, strips - 1,
            lambda s, j: ltop_ref[j, s : s + 1, :],
            lambda s, j: rtop_ref[j, s : s + 1, :],
        ),
        refs, out_ref, sens_ref, True,
    )
    send_top.start()
    edge = below * sectors
    final_level(
        below, ends, lambda s, j, start: vs_ref[s, j, start : start + ROWS, :],
        lambda xt: rim_rows(
            xt, strips - 1,
            lambda s, j: lrow_ref[j, edge + s : edge + s + 1, :],
            lambda s, j: rrow_ref[j, edge + s : edge + s + 1, :],
        ),
        refs, out_ref,
    )
    for i in range(2):
        send(below, i).start()

    def step(k, _):
        low, high = 2 * ROWS, strips * ROWS - 1

        def rows_at(xt):
            if xt == 0:
                return (
                    lambda s, j: lrow_ref[j, pl.ds(k * sectors + s, 1), :],
                    lambda s, j: inner_ref[k, s, j, low : low + 1, :],
                )
            return (
                lambda s, j: inner_ref[k, s, j, high : high + 1, :],
                lambda s, j: rrow_ref[j, pl.ds(k * sectors + s, 1), :],
            )

        final_level(
            k, ends, lambda s, j, start: outer_ref[k, s, j, start : start + ROWS, :],
            rows_at, refs, out_ref,
        )
        for i in range(2):
            send(k, i).start()
        return 0

    lax.fori_loop(0, below, step, 0)

    places = [
        (slice(xt * ROWS, (xt + 1) * ROWS), slice(j * LANES, (j + 1) * LANES))
        for xt in ends
        for j in range(tiles)
    ]

    def add(k, sums):
        factor = weight_ref[pl.ds(k, 1), :]
        out = []
        for total, place in zip(sums, places):
            part = share_ref[(0, *place)] * out_ref[(k, 0, *place)]
            for s in range(1, sectors):
                part = part + share_ref[(s, *place)] * out_ref[(k, s, *place)]
            out.append(total + factor * part)
        return tuple(out)

    sums = lax.fori_loop(0, below + 1, add, tuple(sens_ref[place] for place in places))
    for total, place in zip(sums, places):
        sens_ref[place] = total
    inner = slice(ROWS, (strips - 1) * ROWS)
    sens_ref[inner] += inner_sens_ref[inner]
    if len(piece_ref.shape) == 2:
        piece_ref[...] = sens_ref[...]
    else:
        owners, group, copies, depth, _ = piece_ref.shape
        share = strips * ROWS * tiles // owners
        for xt in range(strips):
            for j in range(tiles):
                value = sens_ref[xt * ROWS : (xt + 1) * ROWS, j * LANES : (j + 1) * LANES]
                flat_ref[pl.ds(xt * ROWS * tiles + j, ROWS, stride=tiles), :] = value
        for o in range(owners):
            for piece in range(group):
                start = piece * depth
                used = max(0, min(depth, share - start))
                value = jnp.zeros((depth, LANES), jnp.float32)
                if used:
                    start += o * share
                    value = flat_ref[start : start + depth, :]
                    if used < depth:
                        line = lax.broadcasted_iota(jnp.int32, (depth, LANES), 0)
                        value = jnp.where(line < used, value, 0.0)
                for i in range(copies):
                    piece_ref[o, piece, i] = value
    send_top.wait()
    for k in range(below + 1):
        for i in range(2):
            send(k, i).wait()


def scatter_kernel(cells_ref, *refs):
    *value_refs, out_ref = refs
    rows, lanes = out_ref.shape
    group, owners, depth, _ = cells_ref.shape
    rank = lax.axis_index("lev")
    half = jnp.bfloat16
    zero, one = jnp.zeros((), half), jnp.ones((), half)
    iota = lax.broadcasted_iota(jnp.int32, (lanes, lanes), 0).astype(jnp.float32).astype(half)
    total = jnp.zeros((2 * lanes, lanes), jnp.float32)
    lines = [(i, o, r) for i in range(group) for o in range(owners) for r in range(depth)]
    wide = 8

    def spread(row):
        return jnp.broadcast_to(row, (lanes, lanes)).astype(half)

    for start in range(0, len(lines), wide):
        lefts, rights = [], []
        for part, owner, line in lines[start : start + wide]:
            piece = jnp.bitwise_xor(rank, (group - part) % group)
            cells = cells_ref[piece, owner, line : line + 1, :]
            value = value_refs[part][owner, line : line + 1, :]
            coarse = value.astype(half).astype(jnp.float32)
            high = spread(jnp.right_shift(cells, 7).astype(jnp.float32)) == iota
            low = spread(jnp.bitwise_and(cells, 127).astype(jnp.float32)) == iota
            lefts.append(
                jnp.concatenate(
                    [
                        jnp.where(high, spread(coarse), zero),
                        jnp.where(high, spread(value - coarse), zero),
                    ],
                    axis=0,
                )
            )
            rights.append(jnp.where(low, one, zero))
        total += lax.dot_general(
            jnp.concatenate(lefts, axis=1),
            jnp.concatenate(rights, axis=1),
            (((1,), (1,)), ((), ())),
            preferred_element_type=jnp.float32,
        )
    out_ref[...] = total[:rows] + total[lanes : lanes + rows]


def exchanged(value, axis, apart):
    count = lax.axis_size(axis)
    return lax.ppermute(value, axis, [(i, i ^ apart) for i in range(count)])


def remapped(pieces, flux_cell):
    owners, share = flux_cell.shape
    _, group, copies, depth, _ = pieces.shape
    sent = pieces.reshape(-1, depth, LANES)
    arrived = lax.all_to_all(
        sent, ("tile", "lev", "sec"), split_axis=0, concat_axis=0, tiled=True
    )
    own = jnp.sum(arrived.reshape(owners, group * copies, depth, LANES), axis=1)
    parts = [own] + [exchanged(own, "lev", group - d) for d in range(1, group)]
    cells = jnp.pad(flux_cell, ((0, 0), (0, group * depth * LANES - share)))
    cells = cells.reshape(owners, group, depth, LANES).transpose(1, 0, 2, 3)
    out = call(
        scatter_kernel, f32(FL_DEV // LANES, LANES), [VM] * (group + 1), VM, (cells, *parts)
    )
    return out.reshape(-1)


def around(first, last):
    count = lax.axis_size("tile")
    up = [(i, (i + 1) % count) for i in range(count)]
    down = [(j, i) for i, j in up]
    return lax.ppermute(last, "tile", up), lax.ppermute(first, "tile", down)


def from_above(value):
    count = lax.axis_size("lev")
    return lax.ppermute(value, "lev", [(i + 1, i) for i in range(count - 1)])


def shards(
    forcing, courant_x, courant_y, mass_flux, limiter_code, seam_code, level_weight, sector_share, flux_cell
):
    sectors, levels, columns, width = forcing.shape
    tiles, below = width // LANES, levels - 1
    padded = columns + 2 * ROWS
    field = kept(below, sectors, tiles, padded, LANES)
    field_top = kept(sectors, tiles, padded, LANES)
    plane = kept(sectors, columns, width)
    rim = kept(tiles, below * sectors, LANES)
    rim_top = kept(tiles, sectors, LANES)
    rim_next = kept(tiles, (below - 1) * sectors, LANES)
    rim_scratch = pltpu.VMEM((tiles, below * sectors, LANES), jnp.float32)

    seam = jnp.broadcast_to(seam_code.T[:, :, None], (*seam_code.T.shape, LANES))
    weight = jnp.broadcast_to(level_weight[:, None], (levels, LANES))

    narrow = pltpu.VMEM((levels, columns, width), jnp.bfloat16)
    lowest, mass_flux, courant_y, limiter_code, courant_x = call(
        start_kernel,
        (plane, narrow, narrow, pltpu.VMEM((levels, columns, width), jnp.int32), narrow),
        [HBM] * 5,
        [VM] * 5,
        in_hbm(forcing, mass_flux, courant_y, limiter_code, courant_x),
        [pltpu.SemaphoreType.DMA((5,))],
    )
    above = from_above(lowest)
    v, first, last, top = call(
        lower_kernel,
        (field, rim, rim, plane),
        [VM] * 4,
        [VM] * 4,
        (forcing, mass_flux, courant_y, limiter_code),
    )
    left, right = around(first, last)
    lines = kept(sectors, tiles, columns, LANES)
    inner_field = kept(below - 1, sectors, tiles, padded, LANES)
    a_scratch = pltpu.VMEM((2, sectors, tiles, columns, LANES), jnp.float32)
    inner, inner_lowest, inner_top = call(
        inner_middle_kernel,
        (inner_field, lines, lines),
        [VM] * 5,
        [VM] * 3,
        (v, courant_x, mass_flux, courant_y, limiter_code),
        [a_scratch],
    )
    lowest, vt, first_top, last_top = call(
        ends_kernel,
        (plane, field_top, rim_top, rim_top),
        [VM] * 11,
        [VM] * 4,
        (
            v, inner_lowest, left, right, seam, courant_x, limiter_code, top, above,
            mass_flux, courant_y,
        ),
        [pltpu.VMEM((tiles, ROWS, LANES), jnp.float32)] * 2,
    )
    above = from_above(lowest)
    left_top, right_top = around(first_top, last_top)

    outer, first, last, top = call(
        outer_middle_kernel,
        (inner_field, rim_next, rim_next, lines),
        [VM] * 10,
        [VM] * 4,
        (
            v, inner_top, left, right, lowest, seam,
            courant_x, mass_flux, courant_y, limiter_code,
        ),
        [rim_scratch, rim_scratch, a_scratch],
    )
    vs, first, last, top = call(
        second_last_kernel,
        (field_top, rim, rim, kept(sectors, tiles, columns, LANES)),
        [VM] * 11,
        [VM] * 4,
        (
            vt, left_top, right_top, top, first, last, seam,
            courant_x, mass_flux, courant_y, limiter_code,
        ),
        [pltpu.VMEM((tiles, sectors, LANES), jnp.float32)] * 2,
    )
    left, right = around(first, last)
    vt, first_top, last_top = call(
        highest_kernel,
        (field_top, rim_top, rim_top),
        [VM] * 5,
        [VM] * 3,
        (top, above, mass_flux, courant_y, limiter_code),
    )
    left_top, right_top = around(first_top, last_top)

    owners, share = flux_cell.shape
    group, copies = lax.axis_size("lev"), lax.axis_size("sec")
    depth = -(-share // (group * LANES))
    aligned = share % LANES == 0
    packed = (owners, group, copies, depth, LANES)
    stage = pltpu.VMEM((levels, sectors, columns, width), jnp.float32)
    adjoint, inner_sens = call(
        inner_final_kernel,
        (f32(*forcing.shape), kept(columns, width)),
        [VM] * 7,
        [HBM, VM],
        (inner, outer, vs, courant_x, limiter_code, weight, sector_share),
        [stage, pltpu.SemaphoreType.DMA((levels,))],
    )
    adjoint, pieces = call(
        outer_final_kernel,
        (f32(*forcing.shape), f32(*packed) if aligned else f32(columns, width)),
        [VM] * 14 + [HBM],
        [HBM, VM],
        (
            inner, outer, vs, vt, left, right, left_top, right_top, seam,
            courant_x, limiter_code, weight, sector_share, inner_sens, adjoint,
        ),
        [
            rim_scratch, rim_scratch,
            pltpu.VMEM((tiles, sectors, LANES), jnp.float32),
            pltpu.VMEM((tiles, sectors, LANES), jnp.float32),
            stage,
            pltpu.VMEM((columns, width), jnp.float32),
            pltpu.VMEM((columns * tiles + ROWS, LANES), jnp.float32),
            pltpu.SemaphoreType.DMA((2, levels)),
        ],
        aliases={14: 0},
    )
    if not aligned:
        pieces = jnp.pad(
            pieces.reshape(owners, share), ((0, 0), (0, group * depth * LANES - share))
        ).reshape(owners, group, 1, depth, LANES)
        pieces = jnp.broadcast_to(pieces, packed)
    flux_cell, pieces = lax.optimization_barrier((flux_cell, pieces))
    return (adjoint, remapped(pieces, flux_cell))


def solution(mesh):
    placed = (
        P("sec", "lev", "tile", None),
        P("lev", "tile", None),
        P("lev", "tile", None),
        P("lev", "tile", None),
        P("lev", "tile", None),
        P(),
        P("lev"),
        P("sec", "tile", None),
        P("tile", None),
    )
    return jax.shard_map(
        shards,
        mesh=mesh,
        in_specs=placed,
        out_specs=(P("sec", "lev", "tile", None), P("tile")),
        check_vma=False,
    )
```

```python
import functools

import jax
import jax.numpy as jnp
from jax import lax
from jax.experimental import pallas as pl
from jax.experimental.pallas import tpu as pltpu
from jax.sharding import PartitionSpec as P

FL_DEV = 15360
LANES = 128
ROWS = 8
MIB = 2**20
VM = pl.BlockSpec(memory_space=pltpu.VMEM)
HBM = pl.BlockSpec(memory_space=pltpu.HBM)


def call(kernel, out_shape, in_specs, out_specs, operands, scratch=(), mib=16, aliases={}):
    return pl.pallas_call(
        kernel,
        out_shape=out_shape,
        in_specs=in_specs,
        out_specs=out_specs,
        scratch_shapes=list(scratch),
        input_output_aliases=aliases,
        cost_estimate=pl.CostEstimate(flops=1, transcendentals=0, bytes_accessed=1),
        compiler_params=pltpu.CompilerParams(vmem_limit_bytes=mib * MIB),
    )(*operands)


def in_hbm(*arrays):
    return tuple(pltpu.with_memory_space_constraint(a, pltpu.HBM) for a in arrays)


def kept(*shape):
    return pltpu.VMEM(shape, jnp.float32)


def f32(*shape):
    return jax.ShapeDtypeStruct(shape, jnp.float32)


def cut(value, xt, j):
    return value[xt * ROWS : (xt + 1) * ROWS, j * LANES : (j + 1) * LANES]


def weights(courant, codes, bit):
    size = jnp.abs(courant)
    half = (0.5 * size) * (1.0 - size)
    limited = jnp.where(jnp.bitwise_and(codes, 1 << bit) != 0, half, 0.0)
    ahead = jnp.maximum(courant, 0.0) - limited
    back = jnp.maximum(-courant, 0.0) - limited
    return ahead, back


def second_weights(cy, codes, bit, xt, tiles):
    lane = lax.broadcasted_iota(jnp.int32, (ROWS, LANES), 1)
    out = []
    for j in range(tiles):
        ahead, back = weights(cut(cy, xt, j), cut(codes, xt, j), bit)
        if j == 0:
            back = jnp.where(lane == 0, 0.0, back)
        if j == tiles - 1:
            ahead = jnp.where(lane == LANES - 1, 0.0, ahead)
        out.append((ahead, back, (1.0 - ahead) - back))
    return out


def second_sweep(parts, factors):
    lane = lax.broadcasted_iota(jnp.int32, (ROWS, LANES), 1)
    tiles = len(parts)
    later = [pltpu.roll(part, LANES - 1, 1) for part in parts]
    sooner = [pltpu.roll(part, 1, 1) for part in parts]
    out = []
    for j in range(tiles):
        following, previous = later[j], sooner[j]
        if j + 1 < tiles:
            following = jnp.where(lane == LANES - 1, later[j + 1], following)
        if j > 0:
            previous = jnp.where(lane == 0, sooner[j - 1], previous)
        ahead, back, own = factors[j]
        out.append(own * parts[j] + ahead * following + back * previous)
    return out


def first_sweep(field, s, j, xt, factors, before=None, after=None):
    start = ROWS * (xt + 1)
    sub = lax.broadcasted_iota(jnp.int32, (ROWS, LANES), 0)
    own_value = field(s, j, start)
    following = field(s, j, start + 1)
    previous = field(s, j, start - 1)
    if before is not None:
        previous = jnp.where(sub == 0, before(s, j), previous)
    if after is not None:
        following = jnp.where(sub == ROWS - 1, after(s, j), following)
    ahead, back, own = factors
    return own * own_value + ahead * following + back * previous


def rim_rows(xt, last, left_row, right_row):
    return (left_row if xt == 0 else None, right_row if xt == last else None)


def near_rows(other_ref, k, xt, strips, left_row, right_row):
    def row(place):
        return lambda s, j: other_ref[k, s, j, place : place + 1, :]

    first, last = ROWS * (xt + 1), ROWS * (xt + 2)
    if xt == 0:
        return left_row, row(last)
    if xt == strips - 1:
        return row(first - 1), right_row
    return (row(first - 1) if xt == 1 else None, row(last) if xt == strips - 2 else None)


def turned(source_ref, flag, target_ref):
    tiles, rows, _ = source_ref.shape
    for j in range(tiles):
        for start in range(0, rows, ROWS):
            count = min(ROWS, rows - start)
            index = (LANES - 1) - lax.broadcasted_iota(jnp.int32, (count, LANES), 1)
            straight = source_ref[j, start : start + count, :]
            other = source_ref[tiles - 1 - j, start : start + count, :]
            mirrored = jnp.take_along_axis(other, index, axis=1, mode="promise_in_bounds")
            target_ref[j, start : start + count, :] = jnp.where(flag, mirrored, straight)


def store_padded(ref, index, s, j, xt, value):
    start = ROWS * (xt + 1)
    ref[(*index, s, j, slice(start, start + ROWS), slice(None))] = value


def store_rims(first_ref, last_ref, row, j, xt, last, value):
    if xt == 0:
        first_ref[j, pl.ds(row, 1), :] = value[:1]
    if xt == last:
        last_ref[j, pl.ds(row, 1), :] = value[ROWS - 1 :]


def flags(seam_ref):
    tile = lax.axis_index("tile")
    return seam_ref[0, pl.ds(tile, 1), :] == 1, seam_ref[1, pl.ds(tile, 1), :] == 1


def start_kernel(f_hbm, mf_hbm, cy_hbm, code_hbm, cx_hbm, out_ref, mf_ref, cy_ref, code_ref, cx_ref, sems):
    copies = [
        pltpu.make_async_copy(source, target, sems.at[i])
        for i, (source, target) in enumerate(
            (
                (f_hbm.at[:, 0], out_ref),
                (mf_hbm, mf_ref),
                (cy_hbm, cy_ref),
                (code_hbm, code_ref),
                (cx_hbm, cx_ref),
            )
        )
    ]
    for copy in copies:
        copy.start()
    for copy in copies:
        copy.wait()


def lower_levels(chosen, f_ref, mf_ref, cy_ref, code_ref, v_ref, rims=None):
    sectors, levels, columns, width = f_ref.shape
    tiles, strips = width // LANES, columns // ROWS

    def level(k, _):
        mf = mf_ref[k].astype(jnp.float32)
        cy = cy_ref[k].astype(jnp.float32)
        codes = code_ref[k]
        for xt in chosen:
            factors = second_weights(cy, codes, 3, xt, tiles)
            rows = slice(xt * ROWS, (xt + 1) * ROWS)
            for s in range(sectors):
                parts = []
                for j in range(tiles):
                    lanes = slice(j * LANES, (j + 1) * LANES)
                    here = f_ref[s, k, rows, lanes]
                    upper = f_ref[s, k + 1, rows, lanes]
                    parts.append(here + cut(mf, xt, j) * (upper - here))
                for j, value in enumerate(second_sweep(parts, factors)):
                    store_padded(v_ref, (k,), s, j, xt, value)
                    if rims is not None:
                        store_rims(*rims, k * sectors + s, j, xt, strips - 1, value)
        return 0

    lax.fori_loop(0, levels - 1, level, 0)


def outer_lower_kernel(f_ref, mf_ref, cy_ref, code_ref, v_ref, first_ref, last_ref):
    strips = f_ref.shape[2] // ROWS
    rims = (first_ref, last_ref)
    lower_levels((0, strips - 1), f_ref, mf_ref, cy_ref, code_ref, v_ref, rims)


def inner_lower_kernel(f_ref, mf_ref, cy_ref, code_ref, v_ref, top_ref):
    strips = f_ref.shape[2] // ROWS
    lower_levels(range(1, strips - 1), f_ref, mf_ref, cy_ref, code_ref, v_ref)
    top_ref[...] = f_ref[:, f_ref.shape[1] - 1]


def first_weights(cx, codes, bit, xt, j):
    ahead, back = weights(cut(cx, xt, j), cut(codes, xt, j), bit)
    return ahead, back, (1.0 - ahead) - back


def ends_kernel(
    v_ref, next_ref, inner_ref, left_ref, right_ref, seam_ref, cx_ref, code_ref,
    here_ref, above_ref, mf_ref, cy_ref,
    out_ref, top_ref, first_ref, last_ref,
    lrow_ref, rrow_ref,
):
    _, sectors, tiles, _, _ = v_ref.shape
    columns = out_ref.shape[1]
    strips = columns // ROWS
    flip_left, flip_right = flags(seam_ref)
    turned(left_ref.at[:, :ROWS], flip_left, lrow_ref)
    turned(right_ref.at[:, :ROWS], flip_right, rrow_ref)
    cx = cx_ref[0].astype(jnp.float32)
    codes = code_ref[0]
    for s in range(sectors):
        for j in range(tiles):
            lanes = slice(j * LANES, (j + 1) * LANES)
            out_ref[s, ROWS : columns - ROWS, lanes] = inner_ref[s, j, ROWS : columns - ROWS]
    for xt in (0, strips - 1):
        for j in range(tiles):
            factors = first_weights(cx, codes, 2, xt, j)
            for s in range(sectors):
                value = first_sweep(
                    lambda s, j, start: v_ref[0, s, j, start : start + ROWS, :],
                    s, j, xt, factors,
                    *near_rows(
                        next_ref, 0, xt, strips,
                        lambda s, j: lrow_ref[j, s : s + 1, :],
                        lambda s, j: rrow_ref[j, s : s + 1, :],
                    ),
                )
                out_ref[s, xt * ROWS : (xt + 1) * ROWS, j * LANES : (j + 1) * LANES] = value

    level = mf_ref.shape[0] - 1
    at_top = lax.axis_index("lev") == lax.axis_size("lev") - 1
    mf = mf_ref[level].astype(jnp.float32)
    cy = cy_ref[level].astype(jnp.float32)
    codes = code_ref[level]
    for xt in range(strips):
        factors = second_weights(cy, codes, 3, xt, tiles)
        rows = slice(xt * ROWS, (xt + 1) * ROWS)
        for s in range(sectors):
            parts = []
            for j in range(tiles):
                lanes = slice(j * LANES, (j + 1) * LANES)
                here = here_ref[s, rows, lanes]
                upper = jnp.where(at_top, here, above_ref[s, rows, lanes])
                parts.append(here + cut(mf, xt, j) * (upper - here))
            for j, value in enumerate(second_sweep(parts, factors)):
                store_padded(top_ref, (), s, j, xt, value)
                store_rims(first_ref, last_ref, s, j, xt, strips - 1, value)


def middle_levels(
    chosen, v_ref, next_ref, lrow_ref, rrow_ref, cx_ref, mf_ref, cy_ref, code_ref, out_ref, a_ref,
    rims=None,
):
    below, sectors, tiles, padded, _ = v_ref.shape
    strips = (padded - 2 * ROWS) // ROWS

    def level(k, _):
        cx = cx_ref[k + 1].astype(jnp.float32)
        mf = mf_ref[k].astype(jnp.float32)
        cy = cy_ref[k].astype(jnp.float32)
        codes_x = code_ref[k + 1]
        codes_y = code_ref[k]
        slot = lax.rem(k, 2)
        for xt in chosen:
            along = [first_weights(cx, codes_x, 2, xt, j) for j in range(tiles)]
            across = second_weights(cy, codes_y, 1, xt, tiles)
            rows = slice(xt * ROWS, (xt + 1) * ROWS)
            for s in range(sectors):
                parts = []
                for j in range(tiles):
                    upper = first_sweep(
                        lambda s, j, start: v_ref[k + 1, s, j, start : start + ROWS, :],
                        s, j, xt, along[j],
                        *near_rows(
                            next_ref, k + 1, xt, strips,
                            lambda s, j: lrow_ref[j, pl.ds((k + 1) * sectors + s, 1), :],
                            lambda s, j: rrow_ref[j, pl.ds((k + 1) * sectors + s, 1), :],
                        ),
                    )
                    here = a_ref[slot, s, j, rows, :]
                    a_ref[1 - slot, s, j, rows, :] = upper
                    parts.append(here + cut(mf, xt, j) * (upper - here))
                for j, value in enumerate(second_sweep(parts, across)):
                    store_padded(out_ref, (k,), s, j, xt, value)
                    if rims is not None:
                        store_rims(*rims, k * sectors + s, j, xt, strips - 1, value)
        return 0

    lax.fori_loop(0, below - 1, level, 0)


def inner_middle_kernel(
    v_ref, next_ref, cx_ref, mf_ref, cy_ref, code_ref, out_ref, lowest_ref, top_ref, a_ref
):
    below, sectors, tiles, padded, _ = v_ref.shape
    strips = (padded - 2 * ROWS) // ROWS
    cx = cx_ref[0].astype(jnp.float32)
    for xt in range(1, strips - 1):
        for j in range(tiles):
            factors = first_weights(cx, code_ref[0], 2, xt, j)
            for s in range(sectors):
                value = first_sweep(
                    lambda s, j, start: v_ref[0, s, j, start : start + ROWS, :],
                    s, j, xt, factors, *near_rows(next_ref, 0, xt, strips, None, None),
                )
                a_ref[0, s, j, xt * ROWS : (xt + 1) * ROWS, :] = value
                lowest_ref[s, j, xt * ROWS : (xt + 1) * ROWS, :] = value
    middle_levels(
        range(1, strips - 1), v_ref, next_ref, None, None, cx_ref, mf_ref, cy_ref, code_ref,
        out_ref, a_ref,
    )
    inner = slice(ROWS, (strips - 1) * ROWS)
    top_ref[:, :, inner] = a_ref[(below - 1) % 2, :, :, inner]


def outer_middle_kernel(
    v_ref, next_ref, inner_top_ref, left_ref, right_ref, lowest_ref, seam_ref,
    cx_ref, mf_ref, cy_ref, code_ref,
    out_ref, first_ref, last_ref, top_ref,
    lrow_ref, rrow_ref, a_ref,
):
    below, sectors, tiles, padded, _ = v_ref.shape
    strips = (padded - 2 * ROWS) // ROWS
    ends = (0, strips - 1)
    flip_left, flip_right = flags(seam_ref)
    turned(left_ref, flip_left, lrow_ref)
    turned(right_ref, flip_right, rrow_ref)
    for s in range(sectors):
        for j in range(tiles):
            for xt in ends:
                rows = slice(xt * ROWS, (xt + 1) * ROWS)
                a_ref[0, s, j, rows] = lowest_ref[s, rows, j * LANES : (j + 1) * LANES]
    middle_levels(
        ends, v_ref, next_ref, lrow_ref, rrow_ref, cx_ref, mf_ref, cy_ref, code_ref, out_ref, a_ref,
        (first_ref, last_ref),
    )
    for xt in ends:
        rows = slice(xt * ROWS, (xt + 1) * ROWS)
        top_ref[:, :, rows] = a_ref[(below - 1) % 2, :, :, rows]
    inner = slice(ROWS, (strips - 1) * ROWS)
    top_ref[:, :, inner] = inner_top_ref[:, :, inner]


def second_last_kernel(
    vt_ref, left_ref, right_ref, lower_ref, first_in, last_in, seam_ref, cx_ref, mf_ref, cy_ref, code_ref,
    out_ref, first_ref, last_ref, top_ref,
    lrow_ref, rrow_ref,
):
    sectors, tiles, padded, _ = vt_ref.shape
    strips = (padded - 2 * ROWS) // ROWS
    top = mf_ref.shape[0] - 1
    done = first_in.shape[1]
    flip_left, flip_right = flags(seam_ref)
    turned(left_ref, flip_left, lrow_ref)
    turned(right_ref, flip_right, rrow_ref)
    first_ref[:, :done] = first_in[...]
    last_ref[:, :done] = last_in[...]
    cx = cx_ref[top].astype(jnp.float32)
    mf = mf_ref[top - 1].astype(jnp.float32)
    cy = cy_ref[top - 1].astype(jnp.float32)
    for xt in range(strips):
        along = [first_weights(cx, code_ref[top], 2, xt, j) for j in range(tiles)]
        across = second_weights(cy, code_ref[top - 1], 1, xt, tiles)
        rows = slice(xt * ROWS, (xt + 1) * ROWS)
        for s in range(sectors):
            parts = []
            for j in range(tiles):
                upper = first_sweep(
                    lambda s, j, start: vt_ref[s, j, start : start + ROWS, :],
                    s, j, xt, along[j],
                    *rim_rows(
                        xt, strips - 1,
                        lambda s, j: lrow_ref[j, s : s + 1, :],
                        lambda s, j: rrow_ref[j, s : s + 1, :],
                    ),
                )
                top_ref[s, j, rows, :] = upper
                here = lower_ref[s, j, rows, :]
                parts.append(here + cut(mf, xt, j) * (upper - here))
            for j, value in enumerate(second_sweep(parts, across)):
                store_padded(out_ref, (), s, j, xt, value)
                store_rims(first_ref, last_ref, done + s, j, xt, strips - 1, value)


def highest_kernel(here_ref, above_ref, mf_ref, cy_ref, code_ref, out_ref, first_ref, last_ref):
    sectors, tiles, columns, _ = here_ref.shape
    strips = columns // ROWS
    top = mf_ref.shape[0] - 1
    at_top = lax.axis_index("lev") == lax.axis_size("lev") - 1
    mf = mf_ref[top].astype(jnp.float32)
    cy = cy_ref[top].astype(jnp.float32)
    for xt in range(strips):
        across = second_weights(cy, code_ref[top], 1, xt, tiles)
        rows = slice(xt * ROWS, (xt + 1) * ROWS)
        for s in range(sectors):
            parts = []
            for j in range(tiles):
                here = here_ref[s, j, rows, :]
                upper = above_ref[s, rows, j * LANES : (j + 1) * LANES]
                upper = jnp.where(at_top, here, upper)
                parts.append(here + cut(mf, xt, j) * (upper - here))
            for j, value in enumerate(second_sweep(parts, across)):
                store_padded(out_ref, (), s, j, xt, value)
                store_rims(first_ref, last_ref, s, j, xt, strips - 1, value)


def final_level(k, chosen, field, rows_at, refs, out_ref, sens_ref=None, start_sum=False):
    cx_ref, code_ref, weight_ref, share_ref = refs
    sectors, _, width = share_ref.shape
    cx = cx_ref[k].astype(jnp.float32)
    codes = code_ref[k]
    factor = weight_ref[pl.ds(k, 1), :]
    for xt in chosen:
        rows = slice(xt * ROWS, (xt + 1) * ROWS)
        for j in range(width // LANES):
            lanes = slice(j * LANES, (j + 1) * LANES)
            factors = first_weights(cx, codes, 0, xt, j)
            total = 0.0
            for s in range(sectors):
                value = first_sweep(field, s, j, xt, factors, *rows_at(xt))
                out_ref[k, s, rows, lanes] = value
                if sens_ref is not None:
                    total = total + share_ref[s, rows, lanes] * value
            if sens_ref is None:
                continue
            if start_sum:
                sens_ref[rows, lanes] = factor * total
            else:
                sens_ref[rows, lanes] += factor * total


def inner_final_kernel(
    inner_ref, outer_ref, vs_ref, cx_ref, code_ref, weight_ref, share_ref,
    out_hbm, sens_ref, out_ref, sems,
):
    below, _, _, padded, _ = inner_ref.shape
    strips = (padded - 2 * ROWS) // ROWS
    refs = (cx_ref, code_ref, weight_ref, share_ref)
    inner = pl.ds(ROWS, (strips - 2) * ROWS)
    chosen = range(1, strips - 1)

    def send(k):
        return pltpu.make_async_copy(out_ref.at[k, :, inner], out_hbm.at[:, k, inner], sems.at[k])

    final_level(
        below, chosen, lambda s, j, start: vs_ref[s, j, start : start + ROWS, :],
        lambda xt: (None, None), refs, out_ref, sens_ref, True,
    )
    send(below).start()

    def step(k, _):
        low, high = 2 * ROWS - 1, strips * ROWS

        def rows_at(xt):
            return (
                (lambda s, j: outer_ref[k, s, j, low : low + 1, :]) if xt == 1 else None,
                (lambda s, j: outer_ref[k, s, j, high : high + 1, :]) if xt == strips - 2 else None,
            )

        final_level(
            k, chosen, lambda s, j, start: inner_ref[k, s, j, start : start + ROWS, :],
            rows_at, refs, out_ref, sens_ref,
        )
        send(k).start()
        return 0

    lax.fori_loop(0, below, step, 0)
    for k in range(below + 1):
        send(k).wait()


def outer_final_kernel(
    inner_ref, outer_ref, vs_ref, vt_ref, left_ref, right_ref, left_top_ref, right_top_ref, seam_ref,
    cx_ref, code_ref, weight_ref, share_ref, inner_sens_ref, done_hbm,
    out_hbm, piece_ref,
    lrow_ref, rrow_ref, ltop_ref, rtop_ref, out_ref, sens_ref, flat_ref, sems,
):
    below, sectors, tiles, padded, _ = outer_ref.shape
    strips = (padded - 2 * ROWS) // ROWS
    ends = (0, strips - 1)
    refs = (cx_ref, code_ref, weight_ref, share_ref)
    flip_left, flip_right = flags(seam_ref)
    turned(left_ref, flip_left, lrow_ref)
    turned(right_ref, flip_right, rrow_ref)
    turned(left_top_ref, flip_left, ltop_ref)
    turned(right_top_ref, flip_right, rtop_ref)

    def send(k, i):
        rows = pl.ds(ends[i] * ROWS, ROWS)
        return pltpu.make_async_copy(out_ref.at[k, :, rows], out_hbm.at[:, k, rows], sems.at[i, k])

    send_top = pltpu.make_async_copy(
        out_ref.at[below + 1], out_hbm.at[:, below + 1], sems.at[0, below + 1]
    )
    final_level(
        below + 1, range(strips), lambda s, j, start: vt_ref[s, j, start : start + ROWS, :],
        lambda xt: rim_rows(
            xt, strips - 1,
            lambda s, j: ltop_ref[j, s : s + 1, :],
            lambda s, j: rtop_ref[j, s : s + 1, :],
        ),
        refs, out_ref, sens_ref, True,
    )
    send_top.start()
    edge = below * sectors
    final_level(
        below, ends, lambda s, j, start: vs_ref[s, j, start : start + ROWS, :],
        lambda xt: rim_rows(
            xt, strips - 1,
            lambda s, j: lrow_ref[j, edge + s : edge + s + 1, :],
            lambda s, j: rrow_ref[j, edge + s : edge + s + 1, :],
        ),
        refs, out_ref,
    )
    for i in range(2):
        send(below, i).start()

    def step(k, _):
        low, high = 2 * ROWS, strips * ROWS - 1

        def rows_at(xt):
            if xt == 0:
                return (
                    lambda s, j: lrow_ref[j, pl.ds(k * sectors + s, 1), :],
                    lambda s, j: inner_ref[k, s, j, low : low + 1, :],
                )
            return (
                lambda s, j: inner_ref[k, s, j, high : high + 1, :],
                lambda s, j: rrow_ref[j, pl.ds(k * sectors + s, 1), :],
            )

        final_level(
            k, ends, lambda s, j, start: outer_ref[k, s, j, start : start + ROWS, :],
            rows_at, refs, out_ref,
        )
        for i in range(2):
            send(k, i).start()
        return 0

    lax.fori_loop(0, below, step, 0)

    places = [
        (slice(xt * ROWS, (xt + 1) * ROWS), slice(j * LANES, (j + 1) * LANES))
        for xt in ends
        for j in range(tiles)
    ]

    def add(k, sums):
        factor = weight_ref[pl.ds(k, 1), :]
        out = []
        for total, place in zip(sums, places):
            part = share_ref[(0, *place)] * out_ref[(k, 0, *place)]
            for s in range(1, sectors):
                part = part + share_ref[(s, *place)] * out_ref[(k, s, *place)]
            out.append(total + factor * part)
        return tuple(out)

    sums = lax.fori_loop(0, below + 1, add, tuple(sens_ref[place] for place in places))
    for total, place in zip(sums, places):
        sens_ref[place] = total
    inner = slice(ROWS, (strips - 1) * ROWS)
    sens_ref[inner] += inner_sens_ref[inner]
    if len(piece_ref.shape) == 2:
        piece_ref[...] = sens_ref[...]
    else:
        owners, group, copies, depth, _ = piece_ref.shape
        share = strips * ROWS * tiles // owners
        for xt in range(strips):
            for j in range(tiles):
                value = sens_ref[xt * ROWS : (xt + 1) * ROWS, j * LANES : (j + 1) * LANES]
                flat_ref[pl.ds(xt * ROWS * tiles + j, ROWS, stride=tiles), :] = value
        for o in range(owners):
            for piece in range(group):
                start = piece * depth
                used = max(0, min(depth, share - start))
                value = jnp.zeros((depth, LANES), jnp.float32)
                if used:
                    start += o * share
                    value = flat_ref[start : start + depth, :]
                    if used < depth:
                        line = lax.broadcasted_iota(jnp.int32, (depth, LANES), 0)
                        value = jnp.where(line < used, value, 0.0)
                for i in range(copies):
                    piece_ref[o, piece, i] = value
    send_top.wait()
    for k in range(below + 1):
        for i in range(2):
            send(k, i).wait()


def scatter_kernel(cells_ref, *refs):
    *value_refs, out_ref = refs
    rows, lanes = out_ref.shape
    group, owners, depth, _ = cells_ref.shape
    rank = lax.axis_index("lev")
    half = jnp.bfloat16
    zero, one = jnp.zeros((), half), jnp.ones((), half)
    iota = lax.broadcasted_iota(jnp.int32, (lanes, lanes), 0).astype(jnp.float32).astype(half)
    total = jnp.zeros((2 * lanes, lanes), jnp.float32)
    lines = [(i, o, r) for i in range(group) for o in range(owners) for r in range(depth)]
    wide = 8

    def spread(row):
        return jnp.broadcast_to(row, (lanes, lanes)).astype(half)

    for start in range(0, len(lines), wide):
        lefts, rights = [], []
        for part, owner, line in lines[start : start + wide]:
            cells = cells_ref[jnp.bitwise_xor(rank, part), owner, line : line + 1, :]
            value = value_refs[part][owner, line : line + 1, :]
            coarse = value.astype(half).astype(jnp.float32)
            high = spread(jnp.right_shift(cells, 7).astype(jnp.float32)) == iota
            low = spread(jnp.bitwise_and(cells, 127).astype(jnp.float32)) == iota
            lefts.append(
                jnp.concatenate(
                    [
                        jnp.where(high, spread(coarse), zero),
                        jnp.where(high, spread(value - coarse), zero),
                    ],
                    axis=0,
                )
            )
            rights.append(jnp.where(low, one, zero))
        total += lax.dot_general(
            jnp.concatenate(lefts, axis=1),
            jnp.concatenate(rights, axis=1),
            (((1,), (1,)), ((), ())),
            preferred_element_type=jnp.float32,
        )
    out_ref[...] = total[:rows] + total[lanes : lanes + rows]


def exchanged(value, axis, apart):
    count = lax.axis_size(axis)
    return lax.ppermute(value, axis, [(i, i ^ apart) for i in range(count)])


def remapped(pieces, flux_cell):
    owners, share = flux_cell.shape
    _, group, copies, depth, _ = pieces.shape
    sent = pieces.reshape(-1, depth, LANES)
    arrived = lax.all_to_all(
        sent, ("tile", "lev", "sec"), split_axis=0, concat_axis=0, tiled=True
    )
    own = jnp.sum(arrived.reshape(owners, group * copies, depth, LANES), axis=1)
    parts = [own] + [exchanged(own, "lev", d) for d in range(1, group)]
    cells = jnp.pad(flux_cell, ((0, 0), (0, group * depth * LANES - share)))
    cells = cells.reshape(owners, group, depth, LANES).transpose(1, 0, 2, 3)
    out = call(
        scatter_kernel, f32(FL_DEV // LANES, LANES), [VM] * (group + 1), VM, (cells, *parts)
    )
    return out.reshape(-1)


def around(first, last):
    count = lax.axis_size("tile")
    up = [(i, (i + 1) % count) for i in range(count)]
    down = [(j, i) for i, j in up]
    return lax.ppermute(last, "tile", up), lax.ppermute(first, "tile", down)


def from_above(value):
    count = lax.axis_size("lev")
    return lax.ppermute(value, "lev", [(i + 1, i) for i in range(count - 1)])


def shards(
    forcing, courant_x, courant_y, mass_flux, limiter_code, seam_code, level_weight, sector_share, flux_cell
):
    sectors, levels, columns, width = forcing.shape
    tiles, below = width // LANES, levels - 1
    padded = columns + 2 * ROWS
    field = kept(below, sectors, tiles, padded, LANES)
    field_top = kept(sectors, tiles, padded, LANES)
    plane = kept(sectors, columns, width)
    rim = kept(tiles, below * sectors, LANES)
    rim_top = kept(tiles, sectors, LANES)
    rim_next = kept(tiles, (below - 1) * sectors, LANES)
    rim_scratch = pltpu.VMEM((tiles, below * sectors, LANES), jnp.float32)

    seam = jnp.broadcast_to(seam_code.T[:, :, None], (*seam_code.T.shape, LANES))
    weight = jnp.broadcast_to(level_weight[:, None], (levels, LANES))

    narrow = pltpu.VMEM((levels, columns, width), jnp.bfloat16)
    lowest, mass_flux, courant_y, limiter_code, courant_x = call(
        start_kernel,
        (plane, narrow, narrow, pltpu.VMEM((levels, columns, width), jnp.int32), narrow),
        [HBM] * 5,
        [VM] * 5,
        in_hbm(forcing, mass_flux, courant_y, limiter_code, courant_x),
        [pltpu.SemaphoreType.DMA((5,))],
    )
    above = from_above(lowest)
    v, first, last = call(
        outer_lower_kernel,
        (field, rim, rim),
        [VM] * 4,
        [VM] * 3,
        (forcing, mass_flux, courant_y, limiter_code),
    )
    v_inner, top = call(
        inner_lower_kernel,
        (field, plane),
        [VM] * 4,
        [VM] * 2,
        (forcing, mass_flux, courant_y, limiter_code),
    )
    left, right = around(first, last)
    lines = kept(sectors, tiles, columns, LANES)
    inner_field = kept(below - 1, sectors, tiles, padded, LANES)
    a_scratch = pltpu.VMEM((2, sectors, tiles, columns, LANES), jnp.float32)
    inner, inner_lowest, inner_top = call(
        inner_middle_kernel,
        (inner_field, lines, lines),
        [VM] * 6,
        [VM] * 3,
        (v_inner, v, courant_x, mass_flux, courant_y, limiter_code),
        [a_scratch],
    )
    lowest, vt, first_top, last_top = call(
        ends_kernel,
        (plane, field_top, rim_top, rim_top),
        [VM] * 12,
        [VM] * 4,
        (
            v, v_inner, inner_lowest, left, right, seam, courant_x, limiter_code, top, above,
            mass_flux, courant_y,
        ),
        [pltpu.VMEM((tiles, ROWS, LANES), jnp.float32)] * 2,
    )
    above = from_above(lowest)
    left_top, right_top = around(first_top, last_top)

    outer, first, last, top = call(
        outer_middle_kernel,
        (inner_field, rim_next, rim_next, lines),
        [VM] * 11,
        [VM] * 4,
        (
            v, v_inner, inner_top, left, right, lowest, seam,
            courant_x, mass_flux, courant_y, limiter_code,
        ),
        [rim_scratch, rim_scratch, a_scratch],
    )
    vs, first, last, top = call(
        second_last_kernel,
        (field_top, rim, rim, kept(sectors, tiles, columns, LANES)),
        [VM] * 11,
        [VM] * 4,
        (
            vt, left_top, right_top, top, first, last, seam,
            courant_x, mass_flux, courant_y, limiter_code,
        ),
        [pltpu.VMEM((tiles, sectors, LANES), jnp.float32)] * 2,
    )
    left, right = around(first, last)
    vt, first_top, last_top = call(
        highest_kernel,
        (field_top, rim_top, rim_top),
        [VM] * 5,
        [VM] * 3,
        (top, above, mass_flux, courant_y, limiter_code),
    )
    left_top, right_top = around(first_top, last_top)

    owners, share = flux_cell.shape
    group, copies = lax.axis_size("lev"), lax.axis_size("sec")
    depth = -(-share // (group * LANES))
    aligned = share % LANES == 0
    packed = (owners, group, copies, depth, LANES)
    stage = pltpu.VMEM((levels, sectors, columns, width), jnp.float32)
    adjoint, inner_sens = call(
        inner_final_kernel,
        (f32(*forcing.shape), kept(columns, width)),
        [VM] * 7,
        [HBM, VM],
        (inner, outer, vs, courant_x, limiter_code, weight, sector_share),
        [stage, pltpu.SemaphoreType.DMA((levels,))],
    )
    adjoint, pieces = call(
        outer_final_kernel,
        (f32(*forcing.shape), f32(*packed) if aligned else f32(columns, width)),
        [VM] * 14 + [HBM],
        [HBM, VM],
        (
            inner, outer, vs, vt, left, right, left_top, right_top, seam,
            courant_x, limiter_code, weight, sector_share, inner_sens, adjoint,
        ),
        [
            rim_scratch, rim_scratch,
            pltpu.VMEM((tiles, sectors, LANES), jnp.float32),
            pltpu.VMEM((tiles, sectors, LANES), jnp.float32),
            stage,
            pltpu.VMEM((columns, width), jnp.float32),
            pltpu.VMEM((columns * tiles + ROWS, LANES), jnp.float32),
            pltpu.SemaphoreType.DMA((2, levels)),
        ],
        aliases={14: 0},
    )
    if not aligned:
        pieces = jnp.pad(
            pieces.reshape(owners, share), ((0, 0), (0, group * depth * LANES - share))
        ).reshape(owners, group, 1, depth, LANES)
        pieces = jnp.broadcast_to(pieces, packed)
    flux_cell, pieces = lax.optimization_barrier((flux_cell, pieces))
    return (adjoint, remapped(pieces, flux_cell))


def solution(mesh):
    placed = (
        P("sec", "lev", "tile", None),
        P("lev", "tile", None),
        P("lev", "tile", None),
        P("lev", "tile", None),
        P("lev", "tile", None),
        P(),
        P("lev"),
        P("sec", "tile", None),
        P("tile", None),
    )
    return jax.shard_map(
        shards,
        mesh=mesh,
        in_specs=placed,
        out_specs=(P("sec", "lev", "tile", None), P("tile")),
        check_vma=False,
    )
```

```python
import functools

import jax
import jax.numpy as jnp
from jax import lax
from jax.experimental import pallas as pl
from jax.experimental.pallas import tpu as pltpu
from jax.sharding import PartitionSpec as P

FL_DEV = 15360
LANES = 128
ROWS = 8
MIB = 2**20
VM = pl.BlockSpec(memory_space=pltpu.VMEM)
HBM = pl.BlockSpec(memory_space=pltpu.HBM)


def call(kernel, out_shape, in_specs, out_specs, operands, scratch=(), mib=16, aliases={}):
    return pl.pallas_call(
        kernel,
        out_shape=out_shape,
        in_specs=in_specs,
        out_specs=out_specs,
        scratch_shapes=list(scratch),
        input_output_aliases=aliases,
        cost_estimate=pl.CostEstimate(flops=1, transcendentals=0, bytes_accessed=1),
        compiler_params=pltpu.CompilerParams(vmem_limit_bytes=mib * MIB),
    )(*operands)


def in_hbm(*arrays):
    return tuple(pltpu.with_memory_space_constraint(a, pltpu.HBM) for a in arrays)


def kept(*shape):
    return pltpu.VMEM(shape, jnp.float32)


def f32(*shape):
    return jax.ShapeDtypeStruct(shape, jnp.float32)


def cut(value, xt, j):
    return value[xt * ROWS : (xt + 1) * ROWS, j * LANES : (j + 1) * LANES]


def weights(courant, codes, bit):
    size = jnp.abs(courant)
    half = (0.5 * size) * (1.0 - size)
    limited = jnp.where(jnp.bitwise_and(codes, 1 << bit) != 0, half, 0.0)
    ahead = jnp.maximum(courant, 0.0) - limited
    back = jnp.maximum(-courant, 0.0) - limited
    return ahead, back


def second_weights(cy, codes, bit, xt, tiles):
    lane = lax.broadcasted_iota(jnp.int32, (ROWS, LANES), 1)
    out = []
    for j in range(tiles):
        ahead, back = weights(cut(cy, xt, j), cut(codes, xt, j), bit)
        if j == 0:
            back = jnp.where(lane == 0, 0.0, back)
        if j == tiles - 1:
            ahead = jnp.where(lane == LANES - 1, 0.0, ahead)
        out.append((ahead, back, (1.0 - ahead) - back))
    return out


def second_sweep(parts, factors):
    lane = lax.broadcasted_iota(jnp.int32, (ROWS, LANES), 1)
    tiles = len(parts)
    later = [pltpu.roll(part, LANES - 1, 1) for part in parts]
    sooner = [pltpu.roll(part, 1, 1) for part in parts]
    out = []
    for j in range(tiles):
        following, previous = later[j], sooner[j]
        if j + 1 < tiles:
            following = jnp.where(lane == LANES - 1, later[j + 1], following)
        if j > 0:
            previous = jnp.where(lane == 0, sooner[j - 1], previous)
        ahead, back, own = factors[j]
        out.append(own * parts[j] + ahead * following + back * previous)
    return out


def first_sweep(field, s, j, xt, factors, before=None, after=None):
    start = ROWS * (xt + 1)
    sub = lax.broadcasted_iota(jnp.int32, (ROWS, LANES), 0)
    own_value = field(s, j, start)
    following = field(s, j, start + 1)
    previous = field(s, j, start - 1)
    if before is not None:
        previous = jnp.where(sub == 0, before(s, j), previous)
    if after is not None:
        following = jnp.where(sub == ROWS - 1, after(s, j), following)
    ahead, back, own = factors
    return own * own_value + ahead * following + back * previous


def rim_rows(xt, last, left_row, right_row):
    return (left_row if xt == 0 else None, right_row if xt == last else None)


def turned(source_ref, flag, target_ref):
    tiles, rows, _ = source_ref.shape
    for j in range(tiles):
        for start in range(0, rows, ROWS):
            count = min(ROWS, rows - start)
            index = (LANES - 1) - lax.broadcasted_iota(jnp.int32, (count, LANES), 1)
            straight = source_ref[j, start : start + count, :]
            other = source_ref[tiles - 1 - j, start : start + count, :]
            mirrored = jnp.take_along_axis(other, index, axis=1, mode="promise_in_bounds")
            target_ref[j, start : start + count, :] = jnp.where(flag, mirrored, straight)


def store_padded(ref, index, s, j, xt, value):
    start = ROWS * (xt + 1)
    ref[(*index, s, j, slice(start, start + ROWS), slice(None))] = value


def store_rims(first_ref, last_ref, row, j, xt, last, value):
    if xt == 0:
        first_ref[j, pl.ds(row, 1), :] = value[:1]
    if xt == last:
        last_ref[j, pl.ds(row, 1), :] = value[ROWS - 1 :]


def flags(seam_ref):
    tile = lax.axis_index("tile")
    return seam_ref[0, pl.ds(tile, 1), :] == 1, seam_ref[1, pl.ds(tile, 1), :] == 1


def start_kernel(f_hbm, mf_hbm, cy_hbm, code_hbm, cx_hbm, out_ref, mf_ref, cy_ref, code_ref, cx_ref, sems):
    copies = [
        pltpu.make_async_copy(source, target, sems.at[i])
        for i, (source, target) in enumerate(
            (
                (f_hbm.at[:, 0], out_ref),
                (mf_hbm, mf_ref),
                (cy_hbm, cy_ref),
                (code_hbm, code_ref),
                (cx_hbm, cx_ref),
            )
        )
    ]
    for copy in copies:
        copy.start()
    for copy in copies:
        copy.wait()


def lower_kernel(f_ref, mf_ref, cy_ref, code_ref, v_ref, first_ref, last_ref, top_ref):
    sectors, levels, columns, width = f_ref.shape
    tiles, strips = width // LANES, columns // ROWS

    def level(k, _):
        mf = mf_ref[k].astype(jnp.float32)
        cy = cy_ref[k].astype(jnp.float32)
        codes = code_ref[k]
        for xt in range(strips):
            factors = second_weights(cy, codes, 3, xt, tiles)
            rows = slice(xt * ROWS, (xt + 1) * ROWS)
            for s in range(sectors):
                parts = []
                for j in range(tiles):
                    lanes = slice(j * LANES, (j + 1) * LANES)
                    here = f_ref[s, k, rows, lanes]
                    upper = f_ref[s, k + 1, rows, lanes]
                    parts.append(here + cut(mf, xt, j) * (upper - here))
                for j, value in enumerate(second_sweep(parts, factors)):
                    store_padded(v_ref, (k,), s, j, xt, value)
                    store_rims(first_ref, last_ref, k * sectors + s, j, xt, strips - 1, value)
        return 0

    lax.fori_loop(0, levels - 1, level, 0)
    top_ref[...] = f_ref[:, levels - 1]


def first_weights(cx, codes, bit, xt, j):
    ahead, back = weights(cut(cx, xt, j), cut(codes, xt, j), bit)
    return ahead, back, (1.0 - ahead) - back


def ends_kernel(
    v_ref, inner_ref, left_ref, right_ref, seam_ref, cx_ref, code_ref, here_ref, above_ref,
    mf_ref, cy_ref,
    out_ref, top_ref, first_ref, last_ref,
    lrow_ref, rrow_ref,
):
    _, sectors, tiles, _, _ = v_ref.shape
    columns = out_ref.shape[1]
    strips = columns // ROWS
    flip_left, flip_right = flags(seam_ref)
    turned(left_ref.at[:, :ROWS], flip_left, lrow_ref)
    turned(right_ref.at[:, :ROWS], flip_right, rrow_ref)
    cx = cx_ref[0].astype(jnp.float32)
    codes = code_ref[0]
    for s in range(sectors):
        for j in range(tiles):
            lanes = slice(j * LANES, (j + 1) * LANES)
            out_ref[s, ROWS : columns - ROWS, lanes] = inner_ref[s, j, ROWS : columns - ROWS]
    for xt in (0, strips - 1):
        for j in range(tiles):
            factors = first_weights(cx, codes, 2, xt, j)
            for s in range(sectors):
                value = first_sweep(
                    lambda s, j, start: v_ref[0, s, j, start : start + ROWS, :],
                    s, j, xt, factors,
                    *rim_rows(
                        xt, strips - 1,
                        lambda s, j: lrow_ref[j, s : s + 1, :],
                        lambda s, j: rrow_ref[j, s : s + 1, :],
                    ),
                )
                out_ref[s, xt * ROWS : (xt + 1) * ROWS, j * LANES : (j + 1) * LANES] = value

    level = mf_ref.shape[0] - 1
    at_top = lax.axis_index("lev") == lax.axis_size("lev") - 1
    mf = mf_ref[level].astype(jnp.float32)
    cy = cy_ref[level].astype(jnp.float32)
    codes = code_ref[level]
    for xt in range(strips):
        factors = second_weights(cy, codes, 3, xt, tiles)
        rows = slice(xt * ROWS, (xt + 1) * ROWS)
        for s in range(sectors):
            parts = []
            for j in range(tiles):
                lanes = slice(j * LANES, (j + 1) * LANES)
                here = here_ref[s, rows, lanes]
                upper = jnp.where(at_top, here, above_ref[s, rows, lanes])
                parts.append(here + cut(mf, xt, j) * (upper - here))
            for j, value in enumerate(second_sweep(parts, factors)):
                store_padded(top_ref, (), s, j, xt, value)
                store_rims(first_ref, last_ref, s, j, xt, strips - 1, value)


def middle_levels(
    chosen, v_ref, lrow_ref, rrow_ref, cx_ref, mf_ref, cy_ref, code_ref, out_ref, a_ref, rims=None
):
    below, sectors, tiles, padded, _ = v_ref.shape
    strips = (padded - 2 * ROWS) // ROWS

    def level(k, _):
        cx = cx_ref[k + 1].astype(jnp.float32)
        mf = mf_ref[k].astype(jnp.float32)
        cy = cy_ref[k].astype(jnp.float32)
        codes_x = code_ref[k + 1]
        codes_y = code_ref[k]
        slot = lax.rem(k, 2)
        for xt in chosen:
            along = [first_weights(cx, codes_x, 2, xt, j) for j in range(tiles)]
            across = second_weights(cy, codes_y, 1, xt, tiles)
            rows = slice(xt * ROWS, (xt + 1) * ROWS)
            for s in range(sectors):
                parts = []
                for j in range(tiles):
                    upper = first_sweep(
                        lambda s, j, start: v_ref[k + 1, s, j, start : start + ROWS, :],
                        s, j, xt, along[j],
                        *rim_rows(
                            xt, strips - 1,
                            lambda s, j: lrow_ref[j, pl.ds((k + 1) * sectors + s, 1), :],
                            lambda s, j: rrow_ref[j, pl.ds((k + 1) * sectors + s, 1), :],
                        ),
                    )
                    here = a_ref[slot, s, j, rows, :]
                    a_ref[1 - slot, s, j, rows, :] = upper
                    parts.append(here + cut(mf, xt, j) * (upper - here))
                for j, value in enumerate(second_sweep(parts, across)):
                    store_padded(out_ref, (k,), s, j, xt, value)
                    if rims is not None:
                        store_rims(*rims, k * sectors + s, j, xt, strips - 1, value)
        return 0

    lax.fori_loop(0, below - 1, level, 0)


def inner_middle_kernel(
    v_ref, cx_ref, mf_ref, cy_ref, code_ref, out_ref, lowest_ref, top_ref, a_ref
):
    below, sectors, tiles, padded, _ = v_ref.shape
    strips = (padded - 2 * ROWS) // ROWS
    cx = cx_ref[0].astype(jnp.float32)
    for xt in range(1, strips - 1):
        for j in range(tiles):
            factors = first_weights(cx, code_ref[0], 2, xt, j)
            for s in range(sectors):
                value = first_sweep(
                    lambda s, j, start: v_ref[0, s, j, start : start + ROWS, :],
                    s, j, xt, factors,
                )
                a_ref[0, s, j, xt * ROWS : (xt + 1) * ROWS, :] = value
                lowest_ref[s, j, xt * ROWS : (xt + 1) * ROWS, :] = value
    middle_levels(
        range(1, strips - 1), v_ref, None, None, cx_ref, mf_ref, cy_ref, code_ref, out_ref, a_ref
    )
    inner = slice(ROWS, (strips - 1) * ROWS)
    top_ref[:, :, inner] = a_ref[(below - 1) % 2, :, :, inner]


def outer_middle_kernel(
    v_ref, inner_top_ref, left_ref, right_ref, lowest_ref, seam_ref,
    cx_ref, mf_ref, cy_ref, code_ref,
    out_ref, first_ref, last_ref, top_ref,
    lrow_ref, rrow_ref, a_ref,
):
    below, sectors, tiles, padded, _ = v_ref.shape
    strips = (padded - 2 * ROWS) // ROWS
    ends = (0, strips - 1)
    flip_left, flip_right = flags(seam_ref)
    turned(left_ref, flip_left, lrow_ref)
    turned(right_ref, flip_right, rrow_ref)
    for s in range(sectors):
        for j in range(tiles):
            for xt in ends:
                rows = slice(xt * ROWS, (xt + 1) * ROWS)
                a_ref[0, s, j, rows] = lowest_ref[s, rows, j * LANES : (j + 1) * LANES]
    middle_levels(
        ends, v_ref, lrow_ref, rrow_ref, cx_ref, mf_ref, cy_ref, code_ref, out_ref, a_ref,
        (first_ref, last_ref),
    )
    for xt in ends:
        rows = slice(xt * ROWS, (xt + 1) * ROWS)
        top_ref[:, :, rows] = a_ref[(below - 1) % 2, :, :, rows]
    inner = slice(ROWS, (strips - 1) * ROWS)
    top_ref[:, :, inner] = inner_top_ref[:, :, inner]


def second_last_kernel(
    vt_ref, left_ref, right_ref, lower_ref, first_in, last_in, seam_ref, cx_ref, mf_ref, cy_ref, code_ref,
    out_ref, first_ref, last_ref, top_ref,
    lrow_ref, rrow_ref,
):
    sectors, tiles, padded, _ = vt_ref.shape
    strips = (padded - 2 * ROWS) // ROWS
    top = mf_ref.shape[0] - 1
    done = first_in.shape[1]
    flip_left, flip_right = flags(seam_ref)
    turned(left_ref, flip_left, lrow_ref)
    turned(right_ref, flip_right, rrow_ref)
    first_ref[:, :done] = first_in[...]
    last_ref[:, :done] = last_in[...]
    cx = cx_ref[top].astype(jnp.float32)
    mf = mf_ref[top - 1].astype(jnp.float32)
    cy = cy_ref[top - 1].astype(jnp.float32)
    for xt in range(strips):
        along = [first_weights(cx, code_ref[top], 2, xt, j) for j in range(tiles)]
        across = second_weights(cy, code_ref[top - 1], 1, xt, tiles)
        rows = slice(xt * ROWS, (xt + 1) * ROWS)
        for s in range(sectors):
            parts = []
            for j in range(tiles):
                upper = first_sweep(
                    lambda s, j, start: vt_ref[s, j, start : start + ROWS, :],
                    s, j, xt, along[j],
                    *rim_rows(
                        xt, strips - 1,
                        lambda s, j: lrow_ref[j, s : s + 1, :],
                        lambda s, j: rrow_ref[j, s : s + 1, :],
                    ),
                )
                top_ref[s, j, rows, :] = upper
                here = lower_ref[s, j, rows, :]
                parts.append(here + cut(mf, xt, j) * (upper - here))
            for j, value in enumerate(second_sweep(parts, across)):
                store_padded(out_ref, (), s, j, xt, value)
                store_rims(first_ref, last_ref, done + s, j, xt, strips - 1, value)


def highest_kernel(here_ref, above_ref, mf_ref, cy_ref, code_ref, out_ref, first_ref, last_ref):
    sectors, tiles, columns, _ = here_ref.shape
    strips = columns // ROWS
    top = mf_ref.shape[0] - 1
    at_top = lax.axis_index("lev") == lax.axis_size("lev") - 1
    mf = mf_ref[top].astype(jnp.float32)
    cy = cy_ref[top].astype(jnp.float32)
    for xt in range(strips):
        across = second_weights(cy, code_ref[top], 1, xt, tiles)
        rows = slice(xt * ROWS, (xt + 1) * ROWS)
        for s in range(sectors):
            parts = []
            for j in range(tiles):
                here = here_ref[s, j, rows, :]
                upper = above_ref[s, rows, j * LANES : (j + 1) * LANES]
                upper = jnp.where(at_top, here, upper)
                parts.append(here + cut(mf, xt, j) * (upper - here))
            for j, value in enumerate(second_sweep(parts, across)):
                store_padded(out_ref, (), s, j, xt, value)
                store_rims(first_ref, last_ref, s, j, xt, strips - 1, value)


def final_level(k, chosen, field, rows_at, refs, out_ref, sens_ref=None, start_sum=False):
    cx_ref, code_ref, weight_ref, share_ref = refs
    sectors, _, width = share_ref.shape
    cx = cx_ref[k].astype(jnp.float32)
    codes = code_ref[k]
    factor = weight_ref[pl.ds(k, 1), :]
    for xt in chosen:
        rows = slice(xt * ROWS, (xt + 1) * ROWS)
        for j in range(width // LANES):
            lanes = slice(j * LANES, (j + 1) * LANES)
            factors = first_weights(cx, codes, 0, xt, j)
            total = 0.0
            for s in range(sectors):
                value = first_sweep(field, s, j, xt, factors, *rows_at(xt))
                out_ref[k, s, rows, lanes] = value
                if sens_ref is not None:
                    total = total + share_ref[s, rows, lanes] * value
            if sens_ref is None:
                continue
            if start_sum:
                sens_ref[rows, lanes] = factor * total
            else:
                sens_ref[rows, lanes] += factor * total


def inner_final_kernel(
    inner_ref, outer_ref, vs_ref, cx_ref, code_ref, weight_ref, share_ref,
    out_hbm, sens_ref, out_ref, sems,
):
    below, _, _, padded, _ = inner_ref.shape
    strips = (padded - 2 * ROWS) // ROWS
    refs = (cx_ref, code_ref, weight_ref, share_ref)
    inner = pl.ds(ROWS, (strips - 2) * ROWS)
    chosen = range(1, strips - 1)

    def send(k):
        return pltpu.make_async_copy(out_ref.at[k, :, inner], out_hbm.at[:, k, inner], sems.at[k])

    final_level(
        below, chosen, lambda s, j, start: vs_ref[s, j, start : start + ROWS, :],
        lambda xt: (None, None), refs, out_ref, sens_ref, True,
    )
    send(below).start()

    def step(k, _):
        low, high = 2 * ROWS - 1, strips * ROWS

        def rows_at(xt):
            return (
                (lambda s, j: outer_ref[k, s, j, low : low + 1, :]) if xt == 1 else None,
                (lambda s, j: outer_ref[k, s, j, high : high + 1, :]) if xt == strips - 2 else None,
            )

        final_level(
            k, chosen, lambda s, j, start: inner_ref[k, s, j, start : start + ROWS, :],
            rows_at, refs, out_ref, sens_ref,
        )
        send(k).start()
        return 0

    lax.fori_loop(0, below, step, 0)
    for k in range(below + 1):
        send(k).wait()


def outer_final_kernel(
    inner_ref, outer_ref, vs_ref, vt_ref, left_ref, right_ref, left_top_ref, right_top_ref, seam_ref,
    cx_ref, code_ref, weight_ref, share_ref, inner_sens_ref, done_hbm,
    out_hbm, piece_ref,
    lrow_ref, rrow_ref, ltop_ref, rtop_ref, out_ref, sens_ref, flat_ref, sems,
):
    below, sectors, tiles, padded, _ = outer_ref.shape
    strips = (padded - 2 * ROWS) // ROWS
    ends = (0, strips - 1)
    refs = (cx_ref, code_ref, weight_ref, share_ref)
    flip_left, flip_right = flags(seam_ref)
    turned(left_ref, flip_left, lrow_ref)
    turned(right_ref, flip_right, rrow_ref)
    turned(left_top_ref, flip_left, ltop_ref)
    turned(right_top_ref, flip_right, rtop_ref)

    def send(k, i):
        rows = pl.ds(ends[i] * ROWS, ROWS)
        return pltpu.make_async_copy(out_ref.at[k, :, rows], out_hbm.at[:, k, rows], sems.at[i, k])

    send_top = pltpu.make_async_copy(
        out_ref.at[below + 1], out_hbm.at[:, below + 1], sems.at[0, below + 1]
    )
    final_level(
        below + 1, range(strips), lambda s, j, start: vt_ref[s, j, start : start + ROWS, :],
        lambda xt: rim_rows(
            xt, strips - 1,
            lambda s, j: ltop_ref[j, s : s + 1, :],
            lambda s, j: rtop_ref[j, s : s + 1, :],
        ),
        refs, out_ref, sens_ref, True,
    )
    send_top.start()
    edge = below * sectors
    final_level(
        below, ends, lambda s, j, start: vs_ref[s, j, start : start + ROWS, :],
        lambda xt: rim_rows(
            xt, strips - 1,
            lambda s, j: lrow_ref[j, edge + s : edge + s + 1, :],
            lambda s, j: rrow_ref[j, edge + s : edge + s + 1, :],
        ),
        refs, out_ref,
    )
    for i in range(2):
        send(below, i).start()

    def step(k, _):
        low, high = 2 * ROWS, strips * ROWS - 1

        def rows_at(xt):
            if xt == 0:
                return (
                    lambda s, j: lrow_ref[j, pl.ds(k * sectors + s, 1), :],
                    lambda s, j: inner_ref[k, s, j, low : low + 1, :],
                )
            return (
                lambda s, j: inner_ref[k, s, j, high : high + 1, :],
                lambda s, j: rrow_ref[j, pl.ds(k * sectors + s, 1), :],
            )

        final_level(
            k, ends, lambda s, j, start: outer_ref[k, s, j, start : start + ROWS, :],
            rows_at, refs, out_ref,
        )
        for i in range(2):
            send(k, i).start()
        return 0

    lax.fori_loop(0, below, step, 0)

    places = [
        (slice(xt * ROWS, (xt + 1) * ROWS), slice(j * LANES, (j + 1) * LANES))
        for xt in ends
        for j in range(tiles)
    ]

    def add(k, sums):
        factor = weight_ref[pl.ds(k, 1), :]
        out = []
        for total, place in zip(sums, places):
            part = share_ref[(0, *place)] * out_ref[(k, 0, *place)]
            for s in range(1, sectors):
                part = part + share_ref[(s, *place)] * out_ref[(k, s, *place)]
            out.append(total + factor * part)
        return tuple(out)

    sums = lax.fori_loop(0, below + 1, add, tuple(sens_ref[place] for place in places))
    for total, place in zip(sums, places):
        sens_ref[place] = total
    inner = slice(ROWS, (strips - 1) * ROWS)
    sens_ref[inner] += inner_sens_ref[inner]
    if len(piece_ref.shape) == 2:
        piece_ref[...] = sens_ref[...]
    else:
        owners, group, copies, depth, _ = piece_ref.shape
        share = strips * ROWS * tiles // owners
        for xt in range(strips):
            for j in range(tiles):
                value = sens_ref[xt * ROWS : (xt + 1) * ROWS, j * LANES : (j + 1) * LANES]
                flat_ref[pl.ds(xt * ROWS * tiles + j, ROWS, stride=tiles), :] = value
        for o in range(owners):
            for piece in range(group):
                start = piece * depth
                used = max(0, min(depth, share - start))
                value = jnp.zeros((depth, LANES), jnp.float32)
                if used:
                    start += o * share
                    value = flat_ref[start : start + depth, :]
                    if used < depth:
                        line = lax.broadcasted_iota(jnp.int32, (depth, LANES), 0)
                        value = jnp.where(line < used, value, 0.0)
                for i in range(copies):
                    piece_ref[o, piece, i] = value
    send_top.wait()
    for k in range(below + 1):
        for i in range(2):
            send(k, i).wait()


def scatter_kernel(cells_ref, *refs):
    *value_refs, out_ref = refs
    rows, lanes = out_ref.shape
    group, owners, depth, _ = cells_ref.shape
    rank = lax.axis_index("lev")
    half = jnp.bfloat16
    zero, one = jnp.zeros((), half), jnp.ones((), half)
    iota = lax.broadcasted_iota(jnp.int32, (lanes, lanes), 0).astype(jnp.float32).astype(half)
    total = jnp.zeros((2 * lanes, lanes), jnp.float32)
    lines = [(i, o, r) for i in range(group) for o in range(owners) for r in range(depth)]
    wide = 8

    def spread(row):
        return jnp.broadcast_to(row, (lanes, lanes)).astype(half)

    for start in range(0, len(lines), wide):
        lefts, rights = [], []
        for part, owner, line in lines[start : start + wide]:
            cells = cells_ref[jnp.bitwise_xor(rank, part), owner, line : line + 1, :]
            value = value_refs[part][owner, line : line + 1, :]
            coarse = value.astype(half).astype(jnp.float32)
            high = spread(jnp.right_shift(cells, 7).astype(jnp.float32)) == iota
            low = spread(jnp.bitwise_and(cells, 127).astype(jnp.float32)) == iota
            lefts.append(
                jnp.concatenate(
                    [
                        jnp.where(high, spread(coarse), zero),
                        jnp.where(high, spread(value - coarse), zero),
                    ],
                    axis=0,
                )
            )
            rights.append(jnp.where(low, one, zero))
        total += lax.dot_general(
            jnp.concatenate(lefts, axis=1),
            jnp.concatenate(rights, axis=1),
            (((1,), (1,)), ((), ())),
            preferred_element_type=jnp.float32,
        )
    out_ref[...] = total[:rows] + total[lanes : lanes + rows]


def exchanged(value, axis, apart):
    count = lax.axis_size(axis)
    return lax.ppermute(value, axis, [(i, i ^ apart) for i in range(count)])


def remapped(pieces, flux_cell):
    owners, share = flux_cell.shape
    _, group, copies, depth, _ = pieces.shape
    sent = pieces.reshape(-1, depth, LANES)
    arrived = lax.all_to_all(
        sent, ("tile", "lev", "sec"), split_axis=0, concat_axis=0, tiled=True
    )
    own = jnp.sum(arrived.reshape(owners, group * copies, depth, LANES), axis=1)
    parts = [own] + [exchanged(own, "lev", d) for d in range(1, group)]
    cells = jnp.pad(flux_cell, ((0, 0), (0, group * depth * LANES - share)))
    cells = cells.reshape(owners, group, depth, LANES).transpose(1, 0, 2, 3)
    out = call(
        scatter_kernel, f32(FL_DEV // LANES, LANES), [VM] * (group + 1), VM, (cells, *parts)
    )
    return out.reshape(-1)


def around(first, last):
    count = lax.axis_size("tile")
    up = [(i, (i + 1) % count) for i in range(count)]
    down = [(j, i) for i, j in up]
    return lax.ppermute(last, "tile", up), lax.ppermute(first, "tile", down)


def from_above(value):
    count = lax.axis_size("lev")
    return lax.ppermute(value, "lev", [(i + 1, i) for i in range(count - 1)])


def shards(
    forcing, courant_x, courant_y, mass_flux, limiter_code, seam_code, level_weight, sector_share, flux_cell
):
    sectors, levels, columns, width = forcing.shape
    tiles, below = width // LANES, levels - 1
    padded = columns + 2 * ROWS
    field = kept(below, sectors, tiles, padded, LANES)
    field_top = kept(sectors, tiles, padded, LANES)
    plane = kept(sectors, columns, width)
    rim = kept(tiles, below * sectors, LANES)
    rim_top = kept(tiles, sectors, LANES)
    rim_next = kept(tiles, (below - 1) * sectors, LANES)
    rim_scratch = pltpu.VMEM((tiles, below * sectors, LANES), jnp.float32)

    seam = jnp.broadcast_to(seam_code.T[:, :, None], (*seam_code.T.shape, LANES))
    weight = jnp.broadcast_to(level_weight[:, None], (levels, LANES))

    narrow = pltpu.VMEM((levels, columns, width), jnp.bfloat16)
    lowest, mass_flux, courant_y, limiter_code, courant_x = call(
        start_kernel,
        (plane, narrow, narrow, pltpu.VMEM((levels, columns, width), jnp.int32), narrow),
        [HBM] * 5,
        [VM] * 5,
        in_hbm(forcing, mass_flux, courant_y, limiter_code, courant_x),
        [pltpu.SemaphoreType.DMA((5,))],
    )
    above = from_above(lowest)
    v, first, last, top = call(
        lower_kernel,
        (field, rim, rim, plane),
        [VM] * 4,
        [VM] * 4,
        (forcing, mass_flux, courant_y, limiter_code),
    )
    left, right = around(first, last)
    lines = kept(sectors, tiles, columns, LANES)
    inner_field = kept(below - 1, sectors, tiles, padded, LANES)
    a_scratch = pltpu.VMEM((2, sectors, tiles, columns, LANES), jnp.float32)
    inner, inner_lowest, inner_top = call(
        inner_middle_kernel,
        (inner_field, lines, lines),
        [VM] * 5,
        [VM] * 3,
        (v, courant_x, mass_flux, courant_y, limiter_code),
        [a_scratch],
    )
    lowest, vt, first_top, last_top = call(
        ends_kernel,
        (plane, field_top, rim_top, rim_top),
        [VM] * 11,
        [VM] * 4,
        (
            v, inner_lowest, left, right, seam, courant_x, limiter_code, top, above,
            mass_flux, courant_y,
        ),
        [pltpu.VMEM((tiles, ROWS, LANES), jnp.float32)] * 2,
    )
    above = from_above(lowest)
    left_top, right_top = around(first_top, last_top)

    outer, first, last, top = call(
        outer_middle_kernel,
        (inner_field, rim_next, rim_next, lines),
        [VM] * 10,
        [VM] * 4,
        (
            v, inner_top, left, right, lowest, seam,
            courant_x, mass_flux, courant_y, limiter_code,
        ),
        [rim_scratch, rim_scratch, a_scratch],
    )
    vs, first, last, top = call(
        second_last_kernel,
        (field_top, rim, rim, kept(sectors, tiles, columns, LANES)),
        [VM] * 11,
        [VM] * 4,
        (
            vt, left_top, right_top, top, first, last, seam,
            courant_x, mass_flux, courant_y, limiter_code,
        ),
        [pltpu.VMEM((tiles, sectors, LANES), jnp.float32)] * 2,
    )
    left, right = around(first, last)
    vt, first_top, last_top = call(
        highest_kernel,
        (field_top, rim_top, rim_top),
        [VM] * 5,
        [VM] * 3,
        (top, above, mass_flux, courant_y, limiter_code),
    )
    left_top, right_top = around(first_top, last_top)

    owners, share = flux_cell.shape
    group, copies = lax.axis_size("lev"), lax.axis_size("sec")
    depth = -(-share // (group * LANES))
    aligned = share % LANES == 0
    packed = (owners, group, copies, depth, LANES)
    stage = pltpu.VMEM((levels, sectors, columns, width), jnp.float32)
    adjoint, inner_sens = call(
        inner_final_kernel,
        (f32(*forcing.shape), kept(columns, width)),
        [VM] * 7,
        [HBM, VM],
        (inner, outer, vs, courant_x, limiter_code, weight, sector_share),
        [stage, pltpu.SemaphoreType.DMA((levels,))],
    )
    adjoint, pieces = call(
        outer_final_kernel,
        (f32(*forcing.shape), f32(*packed) if aligned else f32(columns, width)),
        [VM] * 14 + [HBM],
        [HBM, VM],
        (
            inner, outer, vs, vt, left, right, left_top, right_top, seam,
            courant_x, limiter_code, weight, sector_share, inner_sens, adjoint,
        ),
        [
            rim_scratch, rim_scratch,
            pltpu.VMEM((tiles, sectors, LANES), jnp.float32),
            pltpu.VMEM((tiles, sectors, LANES), jnp.float32),
            stage,
            pltpu.VMEM((columns, width), jnp.float32),
            pltpu.VMEM((columns * tiles + ROWS, LANES), jnp.float32),
            pltpu.SemaphoreType.DMA((2, levels)),
        ],
        aliases={14: 0},
    )
    if not aligned:
        pieces = jnp.pad(
            pieces.reshape(owners, share), ((0, 0), (0, group * depth * LANES - share))
        ).reshape(owners, group, 1, depth, LANES)
        pieces = jnp.broadcast_to(pieces, packed)
    flux_cell, pieces = lax.optimization_barrier((flux_cell, pieces))
    return (adjoint, remapped(pieces, flux_cell))


def solution(mesh):
    placed = (
        P("sec", "lev", "tile", None),
        P("lev", "tile", None),
        P("lev", "tile", None),
        P("lev", "tile", None),
        P("lev", "tile", None),
        P(),
        P("lev"),
        P("sec", "tile", None),
        P("tile", None),
    )
    return jax.shard_map(
        shards,
        mesh=mesh,
        in_specs=placed,
        out_specs=(P("sec", "lev", "tile", None), P("tile")),
        check_vma=False,
    )
```

```python
import functools

import jax
import jax.numpy as jnp
from jax import lax
from jax.experimental import pallas as pl
from jax.experimental.pallas import tpu as pltpu
from jax.sharding import PartitionSpec as P

FL_DEV = 15360
LANES = 128
ROWS = 8
MIB = 2**20
VM = pl.BlockSpec(memory_space=pltpu.VMEM)
HBM = pl.BlockSpec(memory_space=pltpu.HBM)


def call(kernel, out_shape, in_specs, out_specs, operands, scratch=(), mib=16, aliases={}):
    return pl.pallas_call(
        kernel,
        out_shape=out_shape,
        in_specs=in_specs,
        out_specs=out_specs,
        scratch_shapes=list(scratch),
        input_output_aliases=aliases,
        cost_estimate=pl.CostEstimate(flops=1, transcendentals=0, bytes_accessed=1),
        compiler_params=pltpu.CompilerParams(vmem_limit_bytes=mib * MIB),
    )(*operands)


def in_hbm(*arrays):
    return tuple(pltpu.with_memory_space_constraint(a, pltpu.HBM) for a in arrays)


def kept(*shape):
    return pltpu.VMEM(shape, jnp.float32)


def f32(*shape):
    return jax.ShapeDtypeStruct(shape, jnp.float32)


def cut(value, xt, j):
    return value[xt * ROWS : (xt + 1) * ROWS, j * LANES : (j + 1) * LANES]


def weights(courant, codes, bit):
    size = jnp.abs(courant)
    half = (0.5 * size) * (1.0 - size)
    limited = jnp.where(jnp.bitwise_and(codes, 1 << bit) != 0, half, 0.0)
    ahead = jnp.maximum(courant, 0.0) - limited
    back = jnp.maximum(-courant, 0.0) - limited
    return ahead, back


def second_weights(cy, codes, bit, xt, tiles):
    lane = lax.broadcasted_iota(jnp.int32, (ROWS, LANES), 1)
    out = []
    for j in range(tiles):
        ahead, back = weights(cut(cy, xt, j), cut(codes, xt, j), bit)
        if j == 0:
            back = jnp.where(lane == 0, 0.0, back)
        if j == tiles - 1:
            ahead = jnp.where(lane == LANES - 1, 0.0, ahead)
        out.append((ahead, back, (1.0 - ahead) - back))
    return out


def second_sweep(parts, factors):
    lane = lax.broadcasted_iota(jnp.int32, (ROWS, LANES), 1)
    tiles = len(parts)
    later = [pltpu.roll(part, LANES - 1, 1) for part in parts]
    sooner = [pltpu.roll(part, 1, 1) for part in parts]
    out = []
    for j in range(tiles):
        following, previous = later[j], sooner[j]
        if j + 1 < tiles:
            following = jnp.where(lane == LANES - 1, later[j + 1], following)
        if j > 0:
            previous = jnp.where(lane == 0, sooner[j - 1], previous)
        ahead, back, own = factors[j]
        out.append(own * parts[j] + ahead * following + back * previous)
    return out


def first_sweep(field, s, j, xt, factors, before=None, after=None):
    start = ROWS * (xt + 1)
    sub = lax.broadcasted_iota(jnp.int32, (ROWS, LANES), 0)
    own_value = field(s, j, start)
    following = field(s, j, start + 1)
    previous = field(s, j, start - 1)
    if before is not None:
        previous = jnp.where(sub == 0, before(s, j), previous)
    if after is not None:
        following = jnp.where(sub == ROWS - 1, after(s, j), following)
    ahead, back, own = factors
    return own * own_value + ahead * following + back * previous


def rim_rows(xt, last, left_row, right_row):
    return (left_row if xt == 0 else None, right_row if xt == last else None)


def turned(source_ref, flag, target_ref):
    tiles, rows, _ = source_ref.shape
    for j in range(tiles):
        for start in range(0, rows, ROWS):
            count = min(ROWS, rows - start)
            index = (LANES - 1) - lax.broadcasted_iota(jnp.int32, (count, LANES), 1)
            straight = source_ref[j, start : start + count, :]
            other = source_ref[tiles - 1 - j, start : start + count, :]
            mirrored = jnp.take_along_axis(other, index, axis=1, mode="promise_in_bounds")
            target_ref[j, start : start + count, :] = jnp.where(flag, mirrored, straight)


def store_padded(ref, index, s, j, xt, value):
    start = ROWS * (xt + 1)
    ref[(*index, s, j, slice(start, start + ROWS), slice(None))] = value


def store_rims(first_ref, last_ref, row, j, xt, last, value):
    if xt == 0:
        first_ref[j, pl.ds(row, 1), :] = value[:1]
    if xt == last:
        last_ref[j, pl.ds(row, 1), :] = value[ROWS - 1 :]


def flags(seam_ref):
    tile = lax.axis_index("tile")
    return seam_ref[0, pl.ds(tile, 1), :] == 1, seam_ref[1, pl.ds(tile, 1), :] == 1


def start_kernel(f_hbm, mf_hbm, cy_hbm, code_hbm, out_ref, mf_ref, cy_ref, code_ref, sems):
    copies = [
        pltpu.make_async_copy(source, target, sems.at[i])
        for i, (source, target) in enumerate(
            (
                (f_hbm.at[:, 0], out_ref),
                (mf_hbm, mf_ref),
                (cy_hbm, cy_ref),
                (code_hbm, code_ref),
            )
        )
    ]
    for copy in copies:
        copy.start()
    for copy in copies:
        copy.wait()


def lower_kernel(f_ref, mf_ref, cy_ref, code_ref, v_ref, first_ref, last_ref, top_ref):
    sectors, levels, columns, width = f_ref.shape
    tiles, strips = width // LANES, columns // ROWS

    def level(k, _):
        mf = mf_ref[k].astype(jnp.float32)
        cy = cy_ref[k].astype(jnp.float32)
        codes = code_ref[k]
        for xt in range(strips):
            factors = second_weights(cy, codes, 3, xt, tiles)
            rows = slice(xt * ROWS, (xt + 1) * ROWS)
            for s in range(sectors):
                parts = []
                for j in range(tiles):
                    lanes = slice(j * LANES, (j + 1) * LANES)
                    here = f_ref[s, k, rows, lanes]
                    upper = f_ref[s, k + 1, rows, lanes]
                    parts.append(here + cut(mf, xt, j) * (upper - here))
                for j, value in enumerate(second_sweep(parts, factors)):
                    store_padded(v_ref, (k,), s, j, xt, value)
                    store_rims(first_ref, last_ref, k * sectors + s, j, xt, strips - 1, value)
        return 0

    lax.fori_loop(0, levels - 1, level, 0)
    top_ref[...] = f_ref[:, levels - 1]


def first_weights(cx, codes, bit, xt, j):
    ahead, back = weights(cut(cx, xt, j), cut(codes, xt, j), bit)
    return ahead, back, (1.0 - ahead) - back


def ends_kernel(
    v_ref, inner_ref, left_ref, right_ref, seam_ref, cx_ref, code_ref, here_ref, above_ref,
    mf_ref, cy_ref,
    out_ref, top_ref, first_ref, last_ref,
    lrow_ref, rrow_ref,
):
    _, sectors, tiles, _, _ = v_ref.shape
    columns = out_ref.shape[1]
    strips = columns // ROWS
    flip_left, flip_right = flags(seam_ref)
    turned(left_ref.at[:, :ROWS], flip_left, lrow_ref)
    turned(right_ref.at[:, :ROWS], flip_right, rrow_ref)
    cx = cx_ref[0].astype(jnp.float32)
    codes = code_ref[0]
    for s in range(sectors):
        for j in range(tiles):
            lanes = slice(j * LANES, (j + 1) * LANES)
            out_ref[s, ROWS : columns - ROWS, lanes] = inner_ref[s, j, ROWS : columns - ROWS]
    for xt in (0, strips - 1):
        for j in range(tiles):
            factors = first_weights(cx, codes, 2, xt, j)
            for s in range(sectors):
                value = first_sweep(
                    lambda s, j, start: v_ref[0, s, j, start : start + ROWS, :],
                    s, j, xt, factors,
                    *rim_rows(
                        xt, strips - 1,
                        lambda s, j: lrow_ref[j, s : s + 1, :],
                        lambda s, j: rrow_ref[j, s : s + 1, :],
                    ),
                )
                out_ref[s, xt * ROWS : (xt + 1) * ROWS, j * LANES : (j + 1) * LANES] = value

    level = mf_ref.shape[0] - 1
    at_top = lax.axis_index("lev") == lax.axis_size("lev") - 1
    mf = mf_ref[level].astype(jnp.float32)
    cy = cy_ref[level].astype(jnp.float32)
    codes = code_ref[level]
    for xt in range(strips):
        factors = second_weights(cy, codes, 3, xt, tiles)
        rows = slice(xt * ROWS, (xt + 1) * ROWS)
        for s in range(sectors):
            parts = []
            for j in range(tiles):
                lanes = slice(j * LANES, (j + 1) * LANES)
                here = here_ref[s, rows, lanes]
                upper = jnp.where(at_top, here, above_ref[s, rows, lanes])
                parts.append(here + cut(mf, xt, j) * (upper - here))
            for j, value in enumerate(second_sweep(parts, factors)):
                store_padded(top_ref, (), s, j, xt, value)
                store_rims(first_ref, last_ref, s, j, xt, strips - 1, value)


def middle_levels(
    chosen, v_ref, lrow_ref, rrow_ref, cx_ref, mf_ref, cy_ref, code_ref, out_ref, a_ref, rims=None
):
    below, sectors, tiles, padded, _ = v_ref.shape
    strips = (padded - 2 * ROWS) // ROWS

    def level(k, _):
        cx = cx_ref[k + 1].astype(jnp.float32)
        mf = mf_ref[k].astype(jnp.float32)
        cy = cy_ref[k].astype(jnp.float32)
        codes_x = code_ref[k + 1]
        codes_y = code_ref[k]
        slot = lax.rem(k, 2)
        for xt in chosen:
            along = [first_weights(cx, codes_x, 2, xt, j) for j in range(tiles)]
            across = second_weights(cy, codes_y, 1, xt, tiles)
            rows = slice(xt * ROWS, (xt + 1) * ROWS)
            for s in range(sectors):
                parts = []
                for j in range(tiles):
                    upper = first_sweep(
                        lambda s, j, start: v_ref[k + 1, s, j, start : start + ROWS, :],
                        s, j, xt, along[j],
                        *rim_rows(
                            xt, strips - 1,
                            lambda s, j: lrow_ref[j, pl.ds((k + 1) * sectors + s, 1), :],
                            lambda s, j: rrow_ref[j, pl.ds((k + 1) * sectors + s, 1), :],
                        ),
                    )
                    here = a_ref[slot, s, j, rows, :]
                    a_ref[1 - slot, s, j, rows, :] = upper
                    parts.append(here + cut(mf, xt, j) * (upper - here))
                for j, value in enumerate(second_sweep(parts, across)):
                    store_padded(out_ref, (k,), s, j, xt, value)
                    if rims is not None:
                        store_rims(*rims, k * sectors + s, j, xt, strips - 1, value)
        return 0

    lax.fori_loop(0, below - 1, level, 0)


def inner_middle_kernel(
    v_ref, cx_ref, mf_ref, cy_ref, code_ref, out_ref, lowest_ref, top_ref, a_ref
):
    below, sectors, tiles, padded, _ = v_ref.shape
    strips = (padded - 2 * ROWS) // ROWS
    cx = cx_ref[0].astype(jnp.float32)
    for xt in range(1, strips - 1):
        for j in range(tiles):
            factors = first_weights(cx, code_ref[0], 2, xt, j)
            for s in range(sectors):
                value = first_sweep(
                    lambda s, j, start: v_ref[0, s, j, start : start + ROWS, :],
                    s, j, xt, factors,
                )
                a_ref[0, s, j, xt * ROWS : (xt + 1) * ROWS, :] = value
                lowest_ref[s, j, xt * ROWS : (xt + 1) * ROWS, :] = value
    middle_levels(
        range(1, strips - 1), v_ref, None, None, cx_ref, mf_ref, cy_ref, code_ref, out_ref, a_ref
    )
    inner = slice(ROWS, (strips - 1) * ROWS)
    top_ref[:, :, inner] = a_ref[(below - 1) % 2, :, :, inner]


def outer_middle_kernel(
    v_ref, inner_top_ref, left_ref, right_ref, lowest_ref, seam_ref,
    cx_ref, mf_ref, cy_ref, code_ref,
    out_ref, first_ref, last_ref, top_ref,
    lrow_ref, rrow_ref, a_ref,
):
    below, sectors, tiles, padded, _ = v_ref.shape
    strips = (padded - 2 * ROWS) // ROWS
    ends = (0, strips - 1)
    flip_left, flip_right = flags(seam_ref)
    turned(left_ref, flip_left, lrow_ref)
    turned(right_ref, flip_right, rrow_ref)
    for s in range(sectors):
        for j in range(tiles):
            for xt in ends:
                rows = slice(xt * ROWS, (xt + 1) * ROWS)
                a_ref[0, s, j, rows] = lowest_ref[s, rows, j * LANES : (j + 1) * LANES]
    middle_levels(
        ends, v_ref, lrow_ref, rrow_ref, cx_ref, mf_ref, cy_ref, code_ref, out_ref, a_ref,
        (first_ref, last_ref),
    )
    for xt in ends:
        rows = slice(xt * ROWS, (xt + 1) * ROWS)
        top_ref[:, :, rows] = a_ref[(below - 1) % 2, :, :, rows]
    inner = slice(ROWS, (strips - 1) * ROWS)
    top_ref[:, :, inner] = inner_top_ref[:, :, inner]


def second_last_kernel(
    vt_ref, left_ref, right_ref, lower_ref, first_in, last_in, seam_ref, cx_ref, mf_ref, cy_ref, code_ref,
    out_ref, first_ref, last_ref, top_ref,
    lrow_ref, rrow_ref,
):
    sectors, tiles, padded, _ = vt_ref.shape
    strips = (padded - 2 * ROWS) // ROWS
    top = mf_ref.shape[0] - 1
    done = first_in.shape[1]
    flip_left, flip_right = flags(seam_ref)
    turned(left_ref, flip_left, lrow_ref)
    turned(right_ref, flip_right, rrow_ref)
    first_ref[:, :done] = first_in[...]
    last_ref[:, :done] = last_in[...]
    cx = cx_ref[top].astype(jnp.float32)
    mf = mf_ref[top - 1].astype(jnp.float32)
    cy = cy_ref[top - 1].astype(jnp.float32)
    for xt in range(strips):
        along = [first_weights(cx, code_ref[top], 2, xt, j) for j in range(tiles)]
        across = second_weights(cy, code_ref[top - 1], 1, xt, tiles)
        rows = slice(xt * ROWS, (xt + 1) * ROWS)
        for s in range(sectors):
            parts = []
            for j in range(tiles):
                upper = first_sweep(
                    lambda s, j, start: vt_ref[s, j, start : start + ROWS, :],
                    s, j, xt, along[j],
                    *rim_rows(
                        xt, strips - 1,
                        lambda s, j: lrow_ref[j, s : s + 1, :],
                        lambda s, j: rrow_ref[j, s : s + 1, :],
                    ),
                )
                top_ref[s, j, rows, :] = upper
                here = lower_ref[s, j, rows, :]
                parts.append(here + cut(mf, xt, j) * (upper - here))
            for j, value in enumerate(second_sweep(parts, across)):
                store_padded(out_ref, (), s, j, xt, value)
                store_rims(first_ref, last_ref, done + s, j, xt, strips - 1, value)


def highest_kernel(here_ref, above_ref, mf_ref, cy_ref, code_ref, out_ref, first_ref, last_ref):
    sectors, tiles, columns, _ = here_ref.shape
    strips = columns // ROWS
    top = mf_ref.shape[0] - 1
    at_top = lax.axis_index("lev") == lax.axis_size("lev") - 1
    mf = mf_ref[top].astype(jnp.float32)
    cy = cy_ref[top].astype(jnp.float32)
    for xt in range(strips):
        across = second_weights(cy, code_ref[top], 1, xt, tiles)
        rows = slice(xt * ROWS, (xt + 1) * ROWS)
        for s in range(sectors):
            parts = []
            for j in range(tiles):
                here = here_ref[s, j, rows, :]
                upper = above_ref[s, rows, j * LANES : (j + 1) * LANES]
                upper = jnp.where(at_top, here, upper)
                parts.append(here + cut(mf, xt, j) * (upper - here))
            for j, value in enumerate(second_sweep(parts, across)):
                store_padded(out_ref, (), s, j, xt, value)
                store_rims(first_ref, last_ref, s, j, xt, strips - 1, value)


def final_level(k, chosen, field, rows_at, refs, out_ref, sens_ref=None, start_sum=False):
    cx_ref, code_ref, weight_ref, share_ref = refs
    sectors, _, width = share_ref.shape
    cx = cx_ref[k].astype(jnp.float32)
    codes = code_ref[k]
    factor = weight_ref[pl.ds(k, 1), :]
    for xt in chosen:
        rows = slice(xt * ROWS, (xt + 1) * ROWS)
        for j in range(width // LANES):
            lanes = slice(j * LANES, (j + 1) * LANES)
            factors = first_weights(cx, codes, 0, xt, j)
            total = 0.0
            for s in range(sectors):
                value = first_sweep(field, s, j, xt, factors, *rows_at(xt))
                out_ref[k, s, rows, lanes] = value
                if sens_ref is not None:
                    total = total + share_ref[s, rows, lanes] * value
            if sens_ref is None:
                continue
            if start_sum:
                sens_ref[rows, lanes] = factor * total
            else:
                sens_ref[rows, lanes] += factor * total


def inner_final_kernel(
    inner_ref, outer_ref, vs_ref, cx_ref, code_ref, weight_ref, share_ref,
    out_hbm, sens_ref, out_ref, sems,
):
    below, _, _, padded, _ = inner_ref.shape
    strips = (padded - 2 * ROWS) // ROWS
    refs = (cx_ref, code_ref, weight_ref, share_ref)
    inner = pl.ds(ROWS, (strips - 2) * ROWS)
    chosen = range(1, strips - 1)

    def send(k):
        return pltpu.make_async_copy(out_ref.at[k, :, inner], out_hbm.at[:, k, inner], sems.at[k])

    final_level(
        below, chosen, lambda s, j, start: vs_ref[s, j, start : start + ROWS, :],
        lambda xt: (None, None), refs, out_ref, sens_ref, True,
    )
    send(below).start()

    def step(k, _):
        low, high = 2 * ROWS - 1, strips * ROWS

        def rows_at(xt):
            return (
                (lambda s, j: outer_ref[k, s, j, low : low + 1, :]) if xt == 1 else None,
                (lambda s, j: outer_ref[k, s, j, high : high + 1, :]) if xt == strips - 2 else None,
            )

        final_level(
            k, chosen, lambda s, j, start: inner_ref[k, s, j, start : start + ROWS, :],
            rows_at, refs, out_ref, sens_ref,
        )
        send(k).start()
        return 0

    lax.fori_loop(0, below, step, 0)
    for k in range(below + 1):
        send(k).wait()


def outer_final_kernel(
    inner_ref, outer_ref, vs_ref, vt_ref, left_ref, right_ref, left_top_ref, right_top_ref, seam_ref,
    cx_ref, code_ref, weight_ref, share_ref, inner_sens_ref, done_hbm,
    out_hbm, piece_ref,
    lrow_ref, rrow_ref, ltop_ref, rtop_ref, out_ref, sens_ref, flat_ref, sems,
):
    below, sectors, tiles, padded, _ = outer_ref.shape
    strips = (padded - 2 * ROWS) // ROWS
    ends = (0, strips - 1)
    refs = (cx_ref, code_ref, weight_ref, share_ref)
    flip_left, flip_right = flags(seam_ref)
    turned(left_ref, flip_left, lrow_ref)
    turned(right_ref, flip_right, rrow_ref)
    turned(left_top_ref, flip_left, ltop_ref)
    turned(right_top_ref, flip_right, rtop_ref)

    def send(k, i):
        rows = pl.ds(ends[i] * ROWS, ROWS)
        return pltpu.make_async_copy(out_ref.at[k, :, rows], out_hbm.at[:, k, rows], sems.at[i, k])

    send_top = pltpu.make_async_copy(
        out_ref.at[below + 1], out_hbm.at[:, below + 1], sems.at[0, below + 1]
    )
    final_level(
        below + 1, range(strips), lambda s, j, start: vt_ref[s, j, start : start + ROWS, :],
        lambda xt: rim_rows(
            xt, strips - 1,
            lambda s, j: ltop_ref[j, s : s + 1, :],
            lambda s, j: rtop_ref[j, s : s + 1, :],
        ),
        refs, out_ref, sens_ref, True,
    )
    send_top.start()
    edge = below * sectors
    final_level(
        below, ends, lambda s, j, start: vs_ref[s, j, start : start + ROWS, :],
        lambda xt: rim_rows(
            xt, strips - 1,
            lambda s, j: lrow_ref[j, edge + s : edge + s + 1, :],
            lambda s, j: rrow_ref[j, edge + s : edge + s + 1, :],
        ),
        refs, out_ref,
    )
    for i in range(2):
        send(below, i).start()

    def step(k, _):
        low, high = 2 * ROWS, strips * ROWS - 1

        def rows_at(xt):
            if xt == 0:
                return (
                    lambda s, j: lrow_ref[j, pl.ds(k * sectors + s, 1), :],
                    lambda s, j: inner_ref[k, s, j, low : low + 1, :],
                )
            return (
                lambda s, j: inner_ref[k, s, j, high : high + 1, :],
                lambda s, j: rrow_ref[j, pl.ds(k * sectors + s, 1), :],
            )

        final_level(
            k, ends, lambda s, j, start: outer_ref[k, s, j, start : start + ROWS, :],
            rows_at, refs, out_ref,
        )
        for i in range(2):
            send(k, i).start()
        return 0

    lax.fori_loop(0, below, step, 0)

    places = [
        (slice(xt * ROWS, (xt + 1) * ROWS), slice(j * LANES, (j + 1) * LANES))
        for xt in ends
        for j in range(tiles)
    ]

    def add(k, sums):
        factor = weight_ref[pl.ds(k, 1), :]
        out = []
        for total, place in zip(sums, places):
            part = share_ref[(0, *place)] * out_ref[(k, 0, *place)]
            for s in range(1, sectors):
                part = part + share_ref[(s, *place)] * out_ref[(k, s, *place)]
            out.append(total + factor * part)
        return tuple(out)

    sums = lax.fori_loop(0, below + 1, add, tuple(sens_ref[place] for place in places))
    for total, place in zip(sums, places):
        sens_ref[place] = total
    inner = slice(ROWS, (strips - 1) * ROWS)
    sens_ref[inner] += inner_sens_ref[inner]
    if len(piece_ref.shape) == 2:
        piece_ref[...] = sens_ref[...]
    else:
        owners, group, copies, depth, _ = piece_ref.shape
        share = strips * ROWS * tiles // owners
        for xt in range(strips):
            for j in range(tiles):
                value = sens_ref[xt * ROWS : (xt + 1) * ROWS, j * LANES : (j + 1) * LANES]
                flat_ref[pl.ds(xt * ROWS * tiles + j, ROWS, stride=tiles), :] = value
        for o in range(owners):
            for piece in range(group):
                start = piece * depth
                used = max(0, min(depth, share - start))
                value = jnp.zeros((depth, LANES), jnp.float32)
                if used:
                    start += o * share
                    value = flat_ref[start : start + depth, :]
                    if used < depth:
                        line = lax.broadcasted_iota(jnp.int32, (depth, LANES), 0)
                        value = jnp.where(line < used, value, 0.0)
                for i in range(copies):
                    piece_ref[o, piece, i] = value
    send_top.wait()
    for k in range(below + 1):
        for i in range(2):
            send(k, i).wait()


def scatter_kernel(cells_ref, *refs):
    *value_refs, out_ref = refs
    rows, lanes = out_ref.shape
    group, owners, depth, _ = cells_ref.shape
    rank = lax.axis_index("lev")
    half = jnp.bfloat16
    zero, one = jnp.zeros((), half), jnp.ones((), half)
    iota = lax.broadcasted_iota(jnp.int32, (lanes, lanes), 0).astype(jnp.float32).astype(half)
    total = jnp.zeros((2 * lanes, lanes), jnp.float32)
    lines = [(i, o, r) for i in range(group) for o in range(owners) for r in range(depth)]
    wide = 8

    def spread(row):
        return jnp.broadcast_to(row, (lanes, lanes)).astype(half)

    for start in range(0, len(lines), wide):
        lefts, rights = [], []
        for part, owner, line in lines[start : start + wide]:
            cells = cells_ref[jnp.bitwise_xor(rank, part), owner, line : line + 1, :]
            value = value_refs[part][owner, line : line + 1, :]
            coarse = value.astype(half).astype(jnp.float32)
            high = spread(jnp.right_shift(cells, 7).astype(jnp.float32)) == iota
            low = spread(jnp.bitwise_and(cells, 127).astype(jnp.float32)) == iota
            lefts.append(
                jnp.concatenate(
                    [
                        jnp.where(high, spread(coarse), zero),
                        jnp.where(high, spread(value - coarse), zero),
                    ],
                    axis=0,
                )
            )
            rights.append(jnp.where(low, one, zero))
        total += lax.dot_general(
            jnp.concatenate(lefts, axis=1),
            jnp.concatenate(rights, axis=1),
            (((1,), (1,)), ((), ())),
            preferred_element_type=jnp.float32,
        )
    out_ref[...] = total[:rows] + total[lanes : lanes + rows]


def exchanged(value, axis, apart):
    count = lax.axis_size(axis)
    return lax.ppermute(value, axis, [(i, i ^ apart) for i in range(count)])


def remapped(pieces, flux_cell):
    owners, share = flux_cell.shape
    _, group, copies, depth, _ = pieces.shape
    sent = pieces.reshape(-1, depth, LANES)
    arrived = lax.all_to_all(
        sent, ("tile", "lev", "sec"), split_axis=0, concat_axis=0, tiled=True
    )
    own = jnp.sum(arrived.reshape(owners, group * copies, depth, LANES), axis=1)
    parts = [own] + [exchanged(own, "lev", d) for d in range(1, group)]
    cells = jnp.pad(flux_cell, ((0, 0), (0, group * depth * LANES - share)))
    cells = cells.reshape(owners, group, depth, LANES).transpose(1, 0, 2, 3)
    out = call(
        scatter_kernel, f32(FL_DEV // LANES, LANES), [VM] * (group + 1), VM, (cells, *parts)
    )
    return out.reshape(-1)


def around(first, last):
    count = lax.axis_size("tile")
    up = [(i, (i + 1) % count) for i in range(count)]
    down = [(j, i) for i, j in up]
    return lax.ppermute(last, "tile", up), lax.ppermute(first, "tile", down)


def from_above(value):
    count = lax.axis_size("lev")
    return lax.ppermute(value, "lev", [(i + 1, i) for i in range(count - 1)])


def shards(
    forcing, courant_x, courant_y, mass_flux, limiter_code, seam_code, level_weight, sector_share, flux_cell
):
    sectors, levels, columns, width = forcing.shape
    tiles, below = width // LANES, levels - 1
    padded = columns + 2 * ROWS
    field = kept(below, sectors, tiles, padded, LANES)
    field_top = kept(sectors, tiles, padded, LANES)
    plane = kept(sectors, columns, width)
    rim = kept(tiles, below * sectors, LANES)
    rim_top = kept(tiles, sectors, LANES)
    rim_next = kept(tiles, (below - 1) * sectors, LANES)
    rim_scratch = pltpu.VMEM((tiles, below * sectors, LANES), jnp.float32)

    seam = jnp.broadcast_to(seam_code.T[:, :, None], (*seam_code.T.shape, LANES))
    weight = jnp.broadcast_to(level_weight[:, None], (levels, LANES))

    narrow = pltpu.VMEM((levels, columns, width), jnp.bfloat16)
    lowest, mass_flux, courant_y, limiter_code = call(
        start_kernel,
        (plane, narrow, narrow, pltpu.VMEM((levels, columns, width), jnp.int32)),
        [HBM] * 4,
        [VM] * 4,
        in_hbm(forcing, mass_flux, courant_y, limiter_code),
        [pltpu.SemaphoreType.DMA((4,))],
    )
    above = from_above(lowest)
    v, first, last, top = call(
        lower_kernel,
        (field, rim, rim, plane),
        [VM] * 4,
        [VM] * 4,
        (forcing, mass_flux, courant_y, limiter_code),
    )
    left, right = around(first, last)
    lines = kept(sectors, tiles, columns, LANES)
    inner_field = kept(below - 1, sectors, tiles, padded, LANES)
    a_scratch = pltpu.VMEM((2, sectors, tiles, columns, LANES), jnp.float32)
    inner, inner_lowest, inner_top = call(
        inner_middle_kernel,
        (inner_field, lines, lines),
        [VM] * 5,
        [VM] * 3,
        (v, courant_x, mass_flux, courant_y, limiter_code),
        [a_scratch],
    )
    lowest, vt, first_top, last_top = call(
        ends_kernel,
        (plane, field_top, rim_top, rim_top),
        [VM] * 11,
        [VM] * 4,
        (
            v, inner_lowest, left, right, seam, courant_x, limiter_code, top, above,
            mass_flux, courant_y,
        ),
        [pltpu.VMEM((tiles, ROWS, LANES), jnp.float32)] * 2,
    )
    above = from_above(lowest)
    left_top, right_top = around(first_top, last_top)

    outer, first, last, top = call(
        outer_middle_kernel,
        (inner_field, rim_next, rim_next, lines),
        [VM] * 10,
        [VM] * 4,
        (
            v, inner_top, left, right, lowest, seam,
            courant_x, mass_flux, courant_y, limiter_code,
        ),
        [rim_scratch, rim_scratch, a_scratch],
    )
    vs, first, last, top = call(
        second_last_kernel,
        (field_top, rim, rim, kept(sectors, tiles, columns, LANES)),
        [VM] * 11,
        [VM] * 4,
        (
            vt, left_top, right_top, top, first, last, seam,
            courant_x, mass_flux, courant_y, limiter_code,
        ),
        [pltpu.VMEM((tiles, sectors, LANES), jnp.float32)] * 2,
    )
    left, right = around(first, last)
    vt, first_top, last_top = call(
        highest_kernel,
        (field_top, rim_top, rim_top),
        [VM] * 5,
        [VM] * 3,
        (top, above, mass_flux, courant_y, limiter_code),
    )
    left_top, right_top = around(first_top, last_top)

    owners, share = flux_cell.shape
    group, copies = lax.axis_size("lev"), lax.axis_size("sec")
    depth = -(-share // (group * LANES))
    aligned = share % LANES == 0
    packed = (owners, group, copies, depth, LANES)
    stage = pltpu.VMEM((levels, sectors, columns, width), jnp.float32)
    adjoint, inner_sens = call(
        inner_final_kernel,
        (f32(*forcing.shape), kept(columns, width)),
        [VM] * 7,
        [HBM, VM],
        (inner, outer, vs, courant_x, limiter_code, weight, sector_share),
        [stage, pltpu.SemaphoreType.DMA((levels,))],
    )
    adjoint, pieces = call(
        outer_final_kernel,
        (f32(*forcing.shape), f32(*packed) if aligned else f32(columns, width)),
        [VM] * 14 + [HBM],
        [HBM, VM],
        (
            inner, outer, vs, vt, left, right, left_top, right_top, seam,
            courant_x, limiter_code, weight, sector_share, inner_sens, adjoint,
        ),
        [
            rim_scratch, rim_scratch,
            pltpu.VMEM((tiles, sectors, LANES), jnp.float32),
            pltpu.VMEM((tiles, sectors, LANES), jnp.float32),
            stage,
            pltpu.VMEM((columns, width), jnp.float32),
            pltpu.VMEM((columns * tiles + ROWS, LANES), jnp.float32),
            pltpu.SemaphoreType.DMA((2, levels)),
        ],
        aliases={14: 0},
    )
    if not aligned:
        pieces = jnp.pad(
            pieces.reshape(owners, share), ((0, 0), (0, group * depth * LANES - share))
        ).reshape(owners, group, 1, depth, LANES)
        pieces = jnp.broadcast_to(pieces, packed)
    flux_cell, pieces = lax.optimization_barrier((flux_cell, pieces))
    return (adjoint, remapped(pieces, flux_cell))


def solution(mesh):
    placed = (
        P("sec", "lev", "tile", None),
        P("lev", "tile", None),
        P("lev", "tile", None),
        P("lev", "tile", None),
        P("lev", "tile", None),
        P(),
        P("lev"),
        P("sec", "tile", None),
        P("tile", None),
    )
    return jax.shard_map(
        shards,
        mesh=mesh,
        in_specs=placed,
        out_specs=(P("sec", "lev", "tile", None), P("tile")),
        check_vma=False,
    )
```
